32 devices in a mesh: dp: 8 (over z, x), heads: 4 (over y, core).
Axes of the slice: x: 2, y: 2, z: 4, core: 2. Of those that a mesh axis runs over, the one named last changes fastest.
Arguments:
- token_ids: int32 [32, 512], P('dp'), may hold values from 0 to 50687
- row_lengths: int32 [32], P('dp'), may hold values from 64 to 512, as said below
- replaced: int32 [32, 512], P('dp'), may hold values 0 or 1
- embedding: float32 [768, 50688], P('dp', 'heads'), may hold values from -0.3 to 0.3
- relative: float32 [512, 768], P(None, 'dp'), may hold values from -0.12 to 0.12
- project: float32 [768, 3, 768], P('dp', None, 'heads'), may hold values from -0.21875 to 0.21875
- combine: float32 [768, 768], P('heads', 'dp'), may hold values from -0.625 to 0.625
- expand: float32 [768, 3072], P('dp', 'heads'), may hold values from -0.21875 to 0.21875
- contract: float32 [3072, 768], P('heads', 'dp'), may hold values from -0.109375 to 0.109375
- readout: float32 [768, 768], P('dp'), may hold values from -0.21875 to 0.21875
- vectors: float32 [11, 768], P(None, 'dp')
- embedding_mean: float32 [768, 50688], P('dp', 'heads'), may hold values from -4.4703484e-08 to 4.4703484e-08
- relative_mean: float32 [512, 768], P(None, 'dp'), may hold values from -4.7683716e-07 to 4.7683716e-07
- project_mean: float32 [768, 3, 768], P('dp', None, 'heads'), may hold values from -4.7683716e-07 to 4.7683716e-07
- combine_mean: float32 [768, 768], P('heads', 'dp'), may hold values from -4.7683716e-07 to 4.7683716e-07
- expand_mean: float32 [768, 3072], P('dp', 'heads'), may hold values from -4.7683716e-07 to 4.7683716e-07
- contract_mean: float32 [3072, 768], P('heads', 'dp'), may hold values from -4.7683716e-07 to 4.7683716e-07
- readout_mean: float32 [768, 768], P('dp'), may hold values from -4.7683716e-07 to 4.7683716e-07
- vectors_mean: float32 [11, 768], P(None, 'dp'), may hold values from -1.9073486e-06 to 1.9073486e-06
- embedding_square: float32 [768, 50688], P('dp', 'heads'), may hold values from 5.3194024e-16 to 2.127761e-15
- relative_square: float32 [512, 768], P(None, 'dp'), may hold values from 5.3194024e-16 to 2.127761e-15
- project_square: float32 [768, 3, 768], P('dp', None, 'heads'), may hold values from 5.3194024e-16 to 2.127761e-15
- combine_square: float32 [768, 768], P('heads', 'dp'), may hold values from 5.3194024e-16 to 2.127761e-15
- expand_square: float32 [768, 3072], P('dp', 'heads'), may hold values from 5.3194024e-16 to 2.127761e-15
- contract_square: float32 [3072, 768], P('heads', 'dp'), may hold values from 5.3194024e-16 to 2.127761e-15
- readout_square: float32 [768, 768], P('dp'), may hold values from 5.3194024e-16 to 2.127761e-15
- vectors_square: float32 [11, 768], P(None, 'dp'), may hold values from 1.0638805e-12 to 4.255522e-12
Outputs:
- loss_sum: float32 [], replicated
- token_total: float32 [], replicated
- grad_norm: float32 [], replicated
- embedding_first: float32 [768, 50688], P('dp', 'heads')
- embedding_second: float32 [768, 50688], P('dp', 'heads')
- embedding_master: float32 [768, 50688], P('dp', 'heads')
- relative_first: float32 [512, 768], P(None, 'dp')
- relative_second: float32 [512, 768], P(None, 'dp')
- relative_master: float32 [512, 768], P(None, 'dp')
- project_first: float32 [768, 3, 768], P('dp', None, 'heads')
- project_second: float32 [768, 3, 768], P('dp', None, 'heads')
- project_master: float32 [768, 3, 768], P('dp', None, 'heads')
- combine_first: float32 [768, 768], P('heads', 'dp')
- combine_second: float32 [768, 768], P('heads', 'dp')
- combine_master: float32 [768, 768], P('heads', 'dp')
- expand_first: float32 [768, 3072], P('dp', 'heads')
- expand_second: float32 [768, 3072], P('dp', 'heads')
- expand_master: float32 [768, 3072], P('dp', 'heads')
- contract_first: float32 [3072, 768], P('heads', 'dp')
- contract_second: float32 [3072, 768], P('heads', 'dp')
- contract_master: float32 [3072, 768], P('heads', 'dp')
- readout_first: float32 [768, 768], P('dp')
- readout_second: float32 [768, 768], P('dp')
- readout_master: float32 [768, 768], P('dp')
- vectors_first: float32 [11, 768], P(None, 'dp')
- vectors_second: float32 [11, 768], P(None, 'dp')
- vectors_master: float32 [11, 768], P(None, 'dp')
- relative_bias_grad: float32 [768], P('dp')
The draws below stay inside these ranges and needn't reach their ends.
Inputs may be any that keep to these rules, and one draw needn't show every extreme that they name: `row_lengths`: one row among the last 4 rows has length 512; lengths tend to grow with the row's index.
All inputs are finite; a program needn't handle non-finite values. No bound on the sum of `replaced` on one device may be relied on, other than what follows from the above.
Results may differ from the reference program's by a relative error of at most 0.0091.
Values may be sent and summed in bfloat16 or wider, within the bound.
A program may use at most 320 MiB of HBM per device.

```python
import math
import jax
import jax.numpy as jnp
import numpy as np
from jax import lax

D = 768
HEADS = 12
HEAD_DIM = 64
FF = 3072
VOCAB = 50688
SPAN = 256
LEN = 512
ROWS = 4
STEP = 10
BATCH = 32
PARAMS = 46997760


def draw_row_lengths(key, part):
    key = jax.random.fold_in(key, 3)
    first_key, second_key = jax.random.split(key)
    groups = BATCH // ROWS
    places = jnp.arange(BATCH, dtype=jnp.int32)
    group_of = places // ROWS
    shortest = LEN // 8
    ceiling = LEN // 4 + (LEN - LEN // 4) * group_of // max(groups - 1, 1)
    raw_draw = jax.random.randint(first_key, (BATCH,), 0, 1 << 20, dtype=jnp.int32)
    lengths = shortest + raw_draw % (ceiling - shortest + 1)
    longest_row = jax.random.randint(second_key, (), BATCH - ROWS, BATCH, dtype=jnp.int32)
    return jnp.where(places == longest_row, LEN, lengths).astype(jnp.int32)


def draw_vectors(key, part):
    key = jax.random.fold_in(key, 5)
    noise = jnp.clip(jax.random.normal(key, (11, D), jnp.float32), -3.0, 3.0)
    columns = jnp.arange(D, dtype=jnp.float32) / (D - 1)
    ramp = 0.6 + 1.2 * columns
    gains = ramp[None, :] * (1.0 + 0.15 * noise)
    biases = 0.3 * noise
    rows_kind = jnp.arange(11)[:, None]
    table = jnp.where(rows_kind % 2 == 0, gains, biases)
    return jnp.where(rows_kind == 10, 2.0 * D ** (-0.5) * noise, table).astype(jnp.float32)


def touch_ends(array, stream_key, low, largest):
    dims = array.shape
    index_at = [jax.random.randint(jax.random.fold_in(stream_key, axis), (), 0, dims[axis]) for axis in range(len(dims))]
    array = array.at[tuple(index_at)].set(low)
    longest = dims.index(max(dims))
    index_at[longest] = (index_at[longest] + 1) % dims[longest]
    return array.at[tuple(index_at)].set(largest)


def block_scale(stream_key, extent, cuts, least, top_value):
    def one(dim, shards_of):
        steps = jax.random.uniform(jax.random.fold_in(jax.random.fold_in(stream_key, 6), dim), (shards_of,), jnp.float32, least / len(cuts), top_value / len(cuts))
        return jnp.repeat(jnp.exp(steps), extent[dim] // shards_of).reshape((-1,) + (1,) * (len(extent) - dim - 1))

    level = one(*cuts[0])
    for cut in cuts[1:]:
        level = level * one(*cut)
    return level


def cumulative_ranks(count, lean):
    weights = [(1 << 20) // math.isqrt(rank ** lean) + 1 for rank in range(1, count + 1)]
    spread = 1 + sum(weights) // (1 << 30)
    return np.cumsum(np.array([max(1, weight // spread) for weight in weights]))


def ranked(rng, dims, amount, slope):
    table = cumulative_ranks(amount, slope)
    pick = jax.random.randint(jax.random.fold_in(rng, 1), dims, 0, int(table[amount - 1]))
    standing = jnp.searchsorted(jnp.asarray(table, jnp.int32), pick, side="right")
    return jax.random.permutation(jax.random.fold_in(rng, 2), amount)[standing].astype(jnp.int32)


def gaussian(rng, extent, width, most, cuts=(), kind=jnp.bfloat16):
    result = jax.random.normal(rng, extent, jnp.float32) * width
    if len(cuts) > 0:
        result = block_scale(rng, extent, cuts, -0.22, 0.18) * result
    return jnp.clip(result, min=-most, max=most).astype(kind)


def setup_inputs(seed: int = 0) -> dict:
    streams_of = jax.random.split(jax.random.key(seed), 28)
    token_ids = touch_ends(ranked(streams_of[0], (BATCH, LEN), VOCAB, 2), jax.random.fold_in(streams_of[0], 3), 0, VOCAB - 1).astype(jnp.int32)
    row_lengths = draw_row_lengths(jax.random.fold_in(streams_of[27], 71), 0)
    replaced = touch_ends((jax.random.randint(streams_of[2], (BATCH, LEN), 0, 7) < 1).astype(jnp.int32), jax.random.fold_in(streams_of[2], 1), 0, 1)
    embedding = gaussian(streams_of[3], (D, VOCAB), 0.05, 0.3, ((0, 8), (1, 4)), jnp.float32)
    relative = gaussian(streams_of[4], (2 * SPAN, D), 0.02, 0.12, ((1, 8),), jnp.float32)
    project = gaussian(streams_of[5], (D, 3, D), D ** -0.5, 0.21875, ((0, 8), (2, 4)), jnp.float32)
    combine = gaussian(streams_of[6], (D, D), (D // 8) ** -0.5, 0.625, ((0, 4), (1, 8)), jnp.float32)
    expand = gaussian(streams_of[7], (D, FF), D ** -0.5, 0.21875, ((0, 8), (1, 4)), jnp.float32)
    contract = gaussian(streams_of[8], (FF, D), FF ** -0.5, 0.109375, ((0, 4), (1, 8)), jnp.float32)
    readout = gaussian(streams_of[9], (D, D), D ** -0.5, 0.21875, ((0, 8),), jnp.float32)
    vectors = draw_vectors(jax.random.fold_in(streams_of[27], 71), 0)
    embedding_mean = gaussian(streams_of[11], (D, VOCAB), (0.011 * 0.005 / PARAMS ** 0.5), 4.470348358154297e-08, ((0, 8), (1, 4)), jnp.float32)
    relative_mean = gaussian(streams_of[12], (2 * SPAN, D), (0.11 * 0.005 / PARAMS ** 0.5), 4.76837158203125e-07, ((1, 8),), jnp.float32)
    project_mean = gaussian(streams_of[13], (D, 3, D), (0.11 * 0.005 / PARAMS ** 0.5), 4.76837158203125e-07, ((0, 8), (2, 4)), jnp.float32)
    combine_mean = gaussian(streams_of[14], (D, D), (0.11 * 0.005 / PARAMS ** 0.5), 4.76837158203125e-07, ((0, 4), (1, 8)), jnp.float32)
    expand_mean = gaussian(streams_of[15], (D, FF), (0.11 * 0.005 / PARAMS ** 0.5), 4.76837158203125e-07, ((0, 8), (1, 4)), jnp.float32)
    contract_mean = gaussian(streams_of[16], (FF, D), (0.11 * 0.005 / PARAMS ** 0.5), 4.76837158203125e-07, ((0, 4), (1, 8)), jnp.float32)
    readout_mean = gaussian(streams_of[17], (D, D), (0.11 * 0.005 / PARAMS ** 0.5), 4.76837158203125e-07, ((0, 8),), jnp.float32)
    vectors_mean = gaussian(streams_of[18], (11, D), (0.44 * 0.005 / PARAMS ** 0.5), 1.9073486328125e-06, ((1, 8),), jnp.float32)
    embedding_square = jnp.clip(jnp.exp(math.log(2.127760951304669e-15) - 1.3862944 * jax.random.uniform(streams_of[19], (D, VOCAB), jnp.float32) ** block_scale(streams_of[19], (D, VOCAB), ((0, 8), (1, 4)), -0.2, 0.2)), 5.319402378261672e-16, 2.127760951304669e-15)
    relative_square = jnp.clip(jnp.exp(math.log(2.127760951304669e-15) - 1.3862944 * jax.random.uniform(streams_of[20], (2 * SPAN, D), jnp.float32) ** block_scale(streams_of[20], (2 * SPAN, D), ((1, 8),), -0.2, 0.2)), 5.319402378261672e-16, 2.127760951304669e-15)
    project_square = jnp.clip(jnp.exp(math.log(2.127760951304669e-15) - 1.3862944 * jax.random.uniform(streams_of[21], (D, 3, D), jnp.float32) ** block_scale(streams_of[21], (D, 3, D), ((0, 8), (2, 4)), -0.2, 0.2)), 5.319402378261672e-16, 2.127760951304669e-15)
    combine_square = jnp.clip(jnp.exp(math.log(2.127760951304669e-15) - 1.3862944 * jax.random.uniform(streams_of[22], (D, D), jnp.float32) ** block_scale(streams_of[22], (D, D), ((0, 4), (1, 8)), -0.2, 0.2)), 5.319402378261672e-16, 2.127760951304669e-15)
    expand_square = jnp.clip(jnp.exp(math.log(2.127760951304669e-15) - 1.3862944 * jax.random.uniform(streams_of[23], (D, FF), jnp.float32) ** block_scale(streams_of[23], (D, FF), ((0, 8), (1, 4)), -0.2, 0.2)), 5.319402378261672e-16, 2.127760951304669e-15)
    contract_square = jnp.clip(jnp.exp(math.log(2.127760951304669e-15) - 1.3862944 * jax.random.uniform(streams_of[24], (FF, D), jnp.float32) ** block_scale(streams_of[24], (FF, D), ((0, 4), (1, 8)), -0.2, 0.2)), 5.319402378261672e-16, 2.127760951304669e-15)
    readout_square = jnp.clip(jnp.exp(math.log(2.127760951304669e-15) - 1.3862944 * jax.random.uniform(streams_of[25], (D, D), jnp.float32) ** block_scale(streams_of[25], (D, D), ((0, 8),), -0.2, 0.2)), 5.319402378261672e-16, 2.127760951304669e-15)
    vectors_square = jnp.clip(jnp.exp(math.log(4.2555221499429585e-12) - 1.3862944 * jax.random.uniform(streams_of[26], (11, D), jnp.float32) ** block_scale(streams_of[26], (11, D), ((1, 8),), -0.2, 0.2)), 1.0638805374857396e-12, 4.2555221499429585e-12)
    return {"token_ids": token_ids, "row_lengths": row_lengths, "replaced": replaced, "embedding": embedding, "relative": relative, "project": project, "combine": combine, "expand": expand, "contract": contract, "readout": readout, "vectors": vectors, "embedding_mean": embedding_mean, "relative_mean": relative_mean, "project_mean": project_mean, "combine_mean": combine_mean, "expand_mean": expand_mean, "contract_mean": contract_mean, "readout_mean": readout_mean, "vectors_mean": vectors_mean, "embedding_square": embedding_square, "relative_square": relative_square, "project_square": project_square, "combine_square": combine_square, "expand_square": expand_square, "contract_square": contract_square, "readout_square": readout_square, "vectors_square": vectors_square}


layer_eps = 1e-07
clip_level = 0.005
rate_steps = (0.1, 0.05, 0.05, 0.05, 0.05, 0.05, 0.05, 1.0)
beta_first = 0.9
beta_second = 0.999
adam_eps = 1e-08
weight_decay = 0.01

@jax.custom_vjp
def low(v):
    return lax.optimization_barrier(v.astype(jnp.bfloat16)).astype(jnp.float32)

@jax.custom_vjp
def low_back(v):
    return v

def low_keep(v):
    return (low(v), None)

def low_pass(kept, grad):
    return (grad,)

def back_keep(v):
    return (v, None)

def back_low(kept, grad):
    return (low(grad),)
low.defvjp(low_keep, low_pass)
low_back.defvjp(back_keep, back_low)

def matmul(matrix, operand):
    return jnp.dot(matrix, operand, precision=lax.Precision.HIGHEST, preferred_element_type=jnp.float32)

def einsum_high(form, matrix, operand):
    return jnp.einsum(form, matrix, operand, precision=lax.Precision.HIGHEST)

def normalize(values, gain_row, bias_row):
    center = values - lax.optimization_barrier(jnp.mean(values, -1, keepdims=True))
    spread_sq = lax.optimization_barrier(jnp.mean(center * center, -1, keepdims=True))
    return center * lax.rsqrt(spread_sq + layer_eps) * gain_row + bias_row

def gelu(values):
    return jax.nn.gelu(values, approximate=False)

def offsets(length):
    places = jnp.arange(length, dtype=jnp.int32)
    return (jnp.clip(places[:, None] - places[None, :], -SPAN, SPAN - 1) + SPAN).astype(jnp.int32)

def row_attention(queries, key_rows, value_rows, rel_q, rel_k, length):
    offset_idx = jnp.broadcast_to(offsets(LEN)[None], (HEADS, LEN, LEN))
    direct_scores = low_back(einsum_high('ihe,jhe->hij', queries, key_rows))
    near_scores = low_back(einsum_high('ihe,rhe->hir', queries, rel_k))
    far_scores = low_back(einsum_high('jhe,rhe->hjr', key_rows, rel_q))
    scores = (direct_scores + jnp.take_along_axis(near_scores, offset_idx, 2) + jnp.swapaxes(jnp.take_along_axis(far_scores, offset_idx, 2), 1, 2)) * (3 * HEAD_DIM) ** (-0.5)
    valid = jnp.arange(LEN) < length
    scores = jnp.where(valid[None, None, :], scores, -1000000000.0)
    probs = jax.nn.softmax(scores, -1)
    return einsum_high('hij,jhe->ihe', low(probs), value_rows)

def group_loss(params, group_ids, group_lengths, group_flags):
    embedding, relative, project, combine, expand, contract, readout, vectors = params
    word_rows = jnp.take(low(embedding), group_ids.reshape(-1), axis=1).T
    hidden_in = normalize(word_rows, vectors[0], vectors[1])
    weights_in = low(project)
    hidden_low = low(hidden_in)
    queries = low_back(low(matmul(hidden_low, weights_in[:, 0])))
    key_rows = low_back(low(matmul(hidden_low, weights_in[:, 1])))
    value_rows = low_back(low(matmul(hidden_low, weights_in[:, 2])))
    rel_norm = low(normalize(relative, vectors[2], vectors[3]))
    rel_q = low_back(low(matmul(rel_norm, weights_in[:, 0]))).reshape(2 * SPAN, HEADS, HEAD_DIM)
    rel_k = low_back(low(matmul(rel_norm, weights_in[:, 1]))).reshape(2 * SPAN, HEADS, HEAD_DIM)

    def head_split(matrix):
        return matrix.reshape(ROWS, LEN, HEADS, HEAD_DIM)

    def one_row(blocks):
        return jax.checkpoint(row_attention)(blocks[0], blocks[1], blocks[2], rel_q, rel_k, blocks[3])
    attn_mixed = lax.map(one_row, (head_split(queries), head_split(key_rows), head_split(value_rows), group_lengths))
    attn_mixed = low_back(low(attn_mixed.reshape(ROWS * LEN, D)))
    attended = low_back(matmul(attn_mixed, low(combine)))
    hidden_mid = normalize(hidden_in + attended, vectors[4], vectors[5])
    gate_in = low_back(matmul(low(hidden_mid), low(expand)))
    ffn_out = low_back(matmul(low(gelu(gate_in)), low(contract)))
    hidden_out = normalize(hidden_mid + ffn_out, vectors[6], vectors[7])
    dense_out = low_back(matmul(low(hidden_out), low(readout)))
    head_norm = normalize(gelu(dense_out), vectors[8], vectors[9])
    logits = lax.optimization_barrier(jnp.sum(head_norm * vectors[10], -1))
    live = (jnp.arange(LEN)[None, :] < group_lengths[:, None]).reshape(-1)
    losses = jax.nn.softplus(logits) - group_flags.reshape(-1).astype(logits.dtype) * logits
    return jnp.sum(jnp.where(live, losses, 0.0))

def adamw(weight, gradient, mean, square, rate_now):
    first = beta_first * mean + (1.0 - beta_first) * gradient
    second = beta_second * square + (1.0 - beta_second) * gradient * gradient
    mean_hat = first / (1.0 - beta_first ** STEP)
    square_hat = second / (1.0 - beta_second ** STEP)
    master = weight - rate_now * (mean_hat / (jnp.sqrt(square_hat) + adam_eps) + weight_decay * weight)
    return (first, second, master)

def reference(token_ids, row_lengths, replaced, embedding, relative, project, combine, expand, contract, readout, vectors, embedding_mean, relative_mean, project_mean, combine_mean, expand_mean, contract_mean, readout_mean, vectors_mean, embedding_square, relative_square, project_square, combine_square, expand_square, contract_square, readout_square, vectors_square):
    params = (embedding, relative, project, combine, expand, contract, readout, vectors)
    means = (embedding_mean, relative_mean, project_mean, combine_mean, expand_mean, contract_mean, readout_mean, vectors_mean)
    squares = (embedding_square, relative_square, project_square, combine_square, expand_square, contract_square, readout_square, vectors_square)
    groups = token_ids.shape[0] // ROWS
    id_groups = token_ids.reshape(groups, ROWS, LEN)
    length_groups = row_lengths.reshape(groups, ROWS)
    flag_groups = replaced.reshape(groups, ROWS, LEN)
    token_total = jnp.sum(row_lengths).astype(jnp.float32)

    def total_loss(weights):

        def step_group(running, blocks):
            return (running + jax.checkpoint(group_loss)(weights, blocks[0], blocks[1], blocks[2]), None)
        summed, unused = lax.scan(step_group, jnp.zeros((), jnp.float32), (id_groups, length_groups, flag_groups))
        return summed
    loss_sum, pull_back = jax.vjp(total_loss, params)
    gradients = pull_back(jnp.ones((), jnp.float32) / token_total)[0]
    squared = sum((jnp.sum(gradient * gradient) for gradient in gradients))
    grad_norm = jnp.sqrt(squared)
    factor = jnp.minimum(1.0, clip_level / grad_norm)
    updates = [adamw(weight, gradient * factor, mean, square, rate_now) for weight, gradient, mean, square, rate_now in zip(params, gradients, means, squares, rate_steps)]
    return (loss_sum, token_total, grad_norm, updates[0][0], updates[0][1], updates[0][2], updates[1][0], updates[1][1], updates[1][2], updates[2][0], updates[2][1], updates[2][2], updates[3][0], updates[3][1], updates[3][2], updates[4][0], updates[4][1], updates[4][2], updates[5][0], updates[5][1], updates[5][2], updates[6][0], updates[6][1], updates[6][2], updates[7][0], updates[7][1], updates[7][2], gradients[7][3] * factor)
```

```python
import jax
import jax.numpy as jnp
from jax import lax
from jax.experimental import pallas as pl
from jax.experimental.pallas import tpu as pltpu
from jax.sharding import PartitionSpec as P

HEAD_DIM = 64
STEP = 10
BLOCK = 128
UNROLL = 8

low = jnp.bfloat16
f32 = jnp.float32

layer_eps = 1e-07
clip_level = 0.005
rate_steps = (0.1, 0.05, 0.05, 0.05, 0.05, 0.05, 0.05, 1.0)
beta_first = 0.9
beta_second = 0.999
adam_eps = 1e-08
weight_decay = 0.01

def dot_rows(a,b):
    return lax.dot_general(a,b,(((1,),(1,)),((),())),preferred_element_type=f32)
def dot_plain(a,b):
    return lax.dot_general(a,b,(((1,),(0,)),((),())),preferred_element_type=f32)
def dot_left(a,b):
    return lax.dot_general(a,b,(((0,),(0,)),((),())),preferred_element_type=f32)

def attend_kernel(length_ref, qkv_ref, table_ref, probs_ref, mixed_ref, far_ref):
    seq=qkv_ref.shape[1]; width=qkv_ref.shape[2]//3; heads=width//HEAD_DIM
    blocks=seq//BLOCK
    scale=(3*HEAD_DIM)**-0.5
    length=length_ref[0]
    live=lax.broadcasted_iota(jnp.int32,(BLOCK,seq),1)<length
    for head in range(heads):
        at=head*HEAD_DIM
        q=qkv_ref[0,:,at:at+HEAD_DIM]
        k=qkv_ref[0,:,width+at:width+at+HEAD_DIM]
        v=qkv_ref[0,:,2*width+at:2*width+at+HEAD_DIM]
        for block in range(blocks):
            rows=slice(block*BLOCK,(block+1)*BLOCK)
            start=seq-BLOCK*(block+1)
            far=dot_rows(k[rows],table_ref[0,start:start+seq+BLOCK,at:at+HEAD_DIM])
            far=pltpu.roll(far,seq,1,stride=1,stride_axis=0)[:,:seq]
            far_ref[head,:,rows]=far.T
        for block in range(blocks):
            rows=slice(block*BLOCK,(block+1)*BLOCK)
            start=seq-BLOCK*(block+1)
            near=dot_rows(q[rows],table_ref[0,start:start+seq+BLOCK,width+at:width+at+HEAD_DIM])
            near=pltpu.roll(near,seq,1,stride=1,stride_axis=0)[:,:seq]
            scores=(dot_rows(q[rows],k)+near+far_ref[head,rows,:])*scale
            scores=jnp.where(live,scores,-1e9)
            top=jnp.max(scores,-1,keepdims=True)
            expo=jnp.exp(scores-top)
            probs=(expo*(1.0/jnp.sum(expo,-1,keepdims=True))).astype(low)
            probs_ref[head,rows,:]=probs
            mixed_ref[0,rows,at:at+HEAD_DIM]=dot_plain(probs,v).astype(low)

def attend(length,qkv,table):
    groups,seq,width3=qkv.shape
    width=width3//3; heads=width//HEAD_DIM
    return pl.pallas_call(
        attend_kernel,
        grid=(groups,),
        in_specs=[pl.BlockSpec(memory_space=pltpu.SMEM),
            pl.BlockSpec((1,seq,width3),lambda g:(g,0,0)),
            pl.BlockSpec((1,2*seq,2*width),lambda g:(g,0,0))],
        out_specs=[pl.BlockSpec((heads,seq,seq),lambda g:(g,0,0)),
            pl.BlockSpec((1,seq,width),lambda g:(g,0,0))],
        out_shape=[jax.ShapeDtypeStruct((groups*heads,seq,seq),low),jax.ShapeDtypeStruct((groups,seq,width),low)],
        scratch_shapes=[pltpu.VMEM((heads,seq,seq),f32)],
        compiler_params=pltpu.CompilerParams(vmem_limit_bytes=48<<20),
        name="attend",
    )(length,qkv,table)

def attend_back_kernel(qkv_ref, table_ref, probs_ref, up_ref, grad_ref, rel_ref, low_ref, sum_ref):
    seq=qkv_ref.shape[1]; width=qkv_ref.shape[2]//3; heads=width//HEAD_DIM
    blocks=seq//BLOCK; reach=seq+BLOCK
    scale=(3*HEAD_DIM)**-0.5
    flip=(lax.broadcasted_iota(jnp.int32,(BLOCK,BLOCK),0)+lax.broadcasted_iota(jnp.int32,(BLOCK,BLOCK),1)==BLOCK-1).astype(f32).astype(low)
    edge=jnp.zeros((BLOCK,BLOCK),f32)
    def shear(rows):
        return pltpu.roll(jnp.concatenate([rows,edge],1),1,1,stride=1,stride_axis=0).astype(low)
    for head in range(heads):
        at=head*HEAD_DIM
        q=qkv_ref[0,:,at:at+HEAD_DIM]
        k=qkv_ref[0,:,width+at:width+at+HEAD_DIM]
        v=qkv_ref[0,:,2*width+at:2*width+at+HEAD_DIM]
        up=up_ref[0,:,at:at+HEAD_DIM]
        for block in range(blocks):
            rows=slice(block*BLOCK,(block+1)*BLOCK)
            probs=probs_ref[head,rows,:].astype(f32)
            pull=dot_rows(up[rows],v)
            inner=jnp.sum(probs*pull,-1,keepdims=True)
            low_ref[head,rows,:]=(probs*(pull-inner)*scale).astype(low)
        grad_ref[0,:,2*width+at:2*width+at+HEAD_DIM]=dot_left(up,probs_ref[head]).T.astype(low)
        sum_ref[2*head]=jnp.zeros(sum_ref.shape[1:],f32)
        sum_ref[2*head+1]=jnp.zeros(sum_ref.shape[1:],f32)
        for block in range(blocks):
            rows=slice(block*BLOCK,(block+1)*BLOCK)
            start=seq-BLOCK*(block+1)
            window=slice(start,start+reach)
            turned=dot_plain(flip,low_ref[head,rows,:])
            near=shear(turned)
            grad_q=dot_plain(turned.astype(low),k)+dot_plain(near,table_ref[0,window,width+at:width+at+HEAD_DIM])
            grad_ref[0,rows,at:at+HEAD_DIM]=dot_plain(flip,grad_q.astype(low)).astype(low)
            q_turned=dot_plain(flip,q[rows]).astype(low)
            sum_ref[2*head+1,:,window]+=dot_left(q_turned,near)
            turned=dot_rows(flip,low_ref[head,:,rows])
            far=shear(turned)
            grad_k=dot_plain(turned.astype(low),q)+dot_plain(far,table_ref[0,window,at:at+HEAD_DIM])
            grad_ref[0,rows,width+at:width+at+HEAD_DIM]=dot_plain(flip,grad_k.astype(low)).astype(low)
            k_turned=dot_plain(flip,k[rows]).astype(low)
            sum_ref[2*head,:,window]+=dot_left(k_turned,far)
        rel_ref[0,:,at:at+HEAD_DIM]=sum_ref[2*head].T.astype(low)
        rel_ref[0,:,width+at:width+at+HEAD_DIM]=sum_ref[2*head+1].T.astype(low)

def attend_back(qkv,table,probs,up):
    groups,seq,width3=qkv.shape
    width=width3//3; heads=width//HEAD_DIM
    return pl.pallas_call(
        attend_back_kernel,
        grid=(groups,),
        in_specs=[
            pl.BlockSpec((1,seq,width3),lambda g:(g,0,0)),
            pl.BlockSpec((1,2*seq,2*width),lambda g:(g,0,0)),
            pl.BlockSpec((heads,seq,seq),lambda g:(g,0,0)),
            pl.BlockSpec((1,seq,width),lambda g:(g,0,0))],
        out_specs=[pl.BlockSpec((1,seq,width3),lambda g:(g,0,0)),
            pl.BlockSpec((1,2*seq,2*width),lambda g:(g,0,0))],
        out_shape=[jax.ShapeDtypeStruct((groups,seq,width3),low),jax.ShapeDtypeStruct((groups,2*seq,2*width),low)],
        scratch_shapes=[pltpu.VMEM((heads,seq,seq),low),pltpu.VMEM((2*heads,HEAD_DIM,2*seq),f32)],
        compiler_params=pltpu.CompilerParams(vmem_limit_bytes=48<<20),
        name="attend_back",
    )(qkv,table,probs,up)


def lookup_kernel(lengths_ref, places_ref, table_ref, words_ref, rows_ref):
    rows_ref[...] = jnp.zeros_like(rows_ref)

    def step(index, carry):
        first = pl.multiple_of(index * UNROLL, UNROLL)
        for offset in range(UNROLL):
            place = places_ref[0, 0, first + offset]
            rows_ref[pl.ds(first + offset, 1), :] = table_ref[pl.ds(place, 1), :]
        return carry

    lax.fori_loop(0, pl.cdiv(lengths_ref[pl.program_id(0)], UNROLL), step, 0)
    words_ref[0] = rows_ref[...].astype(low)


def lookup(lengths, places, table):
    rows, seq = places.shape
    width = table.shape[1]
    return pl.pallas_call(
        lookup_kernel,
        grid=(rows,),
        in_specs=[
            pl.BlockSpec(memory_space=pltpu.SMEM),
            pl.BlockSpec((1, 1, seq), lambda row: (row, 0, 0), memory_space=pltpu.SMEM),
            pl.BlockSpec(table.shape, lambda row: (0, 0)),
        ],
        out_specs=pl.BlockSpec((1, seq, width), lambda row: (row, 0, 0)),
        out_shape=jax.ShapeDtypeStruct((rows, seq, width), low),
        scratch_shapes=[pltpu.VMEM((seq, width), f32)],
        compiler_params=pltpu.CompilerParams(vmem_limit_bytes=48 << 20),
        name="lookup",
    )(lengths, places[:, None], table)


def deposit_kernel(lengths_ref, places_ref, grads_ref, total_ref, rows_ref, *parts):
    tables = (total_ref,) + parts

    @pl.when(pl.program_id(0) == 0)
    def clear():
        for table in tables:
            table[...] = jnp.zeros_like(table)

    rows_ref[...] = grads_ref[0].astype(f32)

    def step(index, carry):
        first = pl.multiple_of(index * UNROLL, UNROLL)
        for offset in range(0, UNROLL, len(tables)):
            places = [places_ref[0, 0, first + offset + part] for part in range(len(tables))]
            sums = [
                table[pl.ds(place, 1), :] + rows_ref[pl.ds(first + offset + part, 1), :]
                for part, (place, table) in enumerate(zip(places, tables))
            ]
            for place, table, value in zip(places, tables, sums):
                table[pl.ds(place, 1), :] = value
        return carry

    lax.fori_loop(0, pl.cdiv(lengths_ref[pl.program_id(0)], UNROLL), step, 0)

    @pl.when(pl.program_id(0) == pl.num_programs(0) - 1)
    def finish():
        for part in parts:
            total_ref[...] += part[...]


def deposit(lengths, places, grads, slots):
    rows, seq = places.shape
    width = grads.shape[2]
    return pl.pallas_call(
        deposit_kernel,
        grid=(rows,),
        in_specs=[
            pl.BlockSpec(memory_space=pltpu.SMEM),
            pl.BlockSpec((1, 1, seq), lambda row: (row, 0, 0), memory_space=pltpu.SMEM),
            pl.BlockSpec((1, seq, width), lambda row: (row, 0, 0)),
        ],
        out_specs=pl.BlockSpec((slots, width), lambda row: (0, 0)),
        out_shape=jax.ShapeDtypeStruct((slots, width), f32),
        scratch_shapes=[pltpu.VMEM((seq, width), f32)] + [pltpu.VMEM((slots, width), f32)] * 3,
        compiler_params=pltpu.CompilerParams(vmem_limit_bytes=56 << 20),
        name="deposit",
    )(lengths, places[:, None], grads)


def matmul(matrix, operand):
    return jnp.dot(matrix, operand, preferred_element_type=f32)


def product(form, matrix, operand):
    return jnp.einsum(form, matrix, operand, preferred_element_type=f32)


def normalize(values, gain_row, bias_row):
    center = values - jnp.mean(values, -1, keepdims=True)
    spread_sq = jnp.mean(center * center, -1, keepdims=True)
    return center * lax.rsqrt(spread_sq + layer_eps) * gain_row + bias_row


def gelu(values):
    return jax.nn.gelu(values, approximate=False)


def norm_at(first_row):
    def apply_norm(values, gain_rows):
        return normalize(values, gain_rows[first_row], gain_rows[first_row + 1])

    return apply_norm


def split_terms(values, count):
    terms = []
    for _ in range(count):
        term = lax.reduce_precision(values, 8, 7)
        terms.append(term.astype(low))
        values = values - term
    return terms


def adamw(weight, gradient, mean, square, rate_now):
    first = beta_first * mean + (1.0 - beta_first) * gradient
    second = beta_second * square + (1.0 - beta_second) * gradient * gradient
    mean_hat = first / (1.0 - beta_first**STEP)
    square_hat = second / (1.0 - beta_second**STEP)
    master = weight - rate_now * (
        mean_hat / (jnp.sqrt(square_hat) + adam_eps) + weight_decay * weight
    )
    return (first, second, master)


def per_device(
    token_ids,
    row_lengths,
    replaced,
    embedding,
    relative,
    project,
    combine,
    expand,
    contract,
    readout,
    vectors,
    embedding_mean,
    relative_mean,
    project_mean,
    combine_mean,
    expand_mean,
    contract_mean,
    readout_mean,
    vectors_mean,
    embedding_square,
    relative_square,
    project_square,
    combine_square,
    expand_square,
    contract_square,
    readout_square,
    vectors_square,
):
    pieces = lax.axis_size("heads")
    holder = lax.axis_index("heads")
    owner = lax.axis_index("dp")
    owners = lax.axis_size("dp")
    row_count, seq_len = token_ids.shape
    width = vectors.shape[1]
    model = width * owners
    everyone = ("heads", "dp")
    head_width = project.shape[2]
    hidden = expand.shape[1]
    vocab_slab = embedding.shape[1]
    span_part = relative.shape[0] // pieces
    vector_count = vectors.shape[0]

    row_facts = lax.all_gather(
        jnp.concatenate([token_ids, row_lengths[:, None]], 1), "dp", axis=0, tiled=True
    )
    all_ids, all_lengths = row_facts[:, :seq_len], row_facts[:, seq_len]
    token_total = jnp.sum(all_lengths).astype(f32)
    local_ids = all_ids - holder * vocab_slab
    inside = (local_ids >= 0) & (local_ids < vocab_slab)
    places = jnp.where(inside, local_ids, vocab_slab)
    slots = vocab_slab + 8

    own_relative = lax.dynamic_slice_in_dim(relative, holder * span_part, span_part, 0).T
    own_readout = lax.dynamic_slice_in_dim(readout, holder * head_width, head_width, 1)
    vector_terms = jnp.concatenate(split_terms(vectors.T, 3), 1)
    first_pack = jnp.concatenate(
        [
            project.reshape(width, 3 * head_width).astype(low),
            combine.T.astype(low),
            *split_terms(own_relative, 2),
            jnp.pad(vector_terms, ((0, 0), (0, BLOCK - 3 * vector_count))),
        ],
        1,
    )
    second_pack = jnp.concatenate(
        [expand.astype(low), contract.T.astype(low), own_readout.astype(low)], 1
    )
    first_all = lax.all_gather(first_pack, everyone, axis=0, tiled=True)
    first_all = first_all.reshape(pieces, model, -1)
    second_all = lax.all_gather(second_pack, everyone, axis=0, tiled=True)
    second_all = second_all.reshape(pieces, model, -1)

    w_project = first_all[:, :, : 3 * head_width]
    w_combine = first_all[:, :, 3 * head_width : 4 * head_width]
    at = 4 * head_width
    rel_terms = first_all[:, :, at : at + 2 * span_part].astype(f32)
    rel_full = rel_terms[:, :, :span_part] + rel_terms[:, :, span_part:]
    rel_full = rel_full.transpose(0, 2, 1).reshape(pieces * span_part, model)
    at = at + 2 * span_part
    vec_terms = first_all[0, :, at : at + 3 * vector_count].astype(f32)
    vec_full = (
        vec_terms[:, :vector_count]
        + vec_terms[:, vector_count : 2 * vector_count]
        + vec_terms[:, 2 * vector_count :]
    ).T
    w_expand = second_all[:, :, :hidden]
    w_contract = second_all[:, :, hidden : 2 * hidden]
    w_readout = second_all[:, :, 2 * hidden :]

    table = jnp.pad(embedding.T, ((0, 8), (0, 0)))
    found = lookup(all_lengths, places, table).reshape(owners, row_count, seq_len, width)
    found = lax.psum_scatter(found, "heads", scatter_dimension=1, tiled=True)
    found = found.reshape(owners, seq_len, width)
    found = lax.all_to_all(found, "dp", 0, 0, tiled=True)
    word_rows = found.transpose(1, 0, 2).reshape(seq_len, model).astype(f32)

    own_length = lax.dynamic_slice_in_dim(row_lengths, holder, 1)
    own_live = jnp.arange(seq_len) < own_length
    own_flags = lax.dynamic_slice_in_dim(replaced, holder, 1)[0].astype(f32)

    hidden_in, back_in = jax.vjp(norm_at(0), word_rows, vec_full)
    hidden_low = hidden_in.astype(low)
    qkv = product("td,hdc->htc", hidden_low, w_project).astype(low)
    rel_norm, back_rel = jax.vjp(norm_at(2), rel_full, vec_full)
    rel_low = rel_norm.astype(low)
    entries = rel_full.shape[0]
    reach = jnp.clip(seq_len + entries // 2 - jnp.arange(2 * seq_len), 0, entries - 1)
    spread = (reach[:, None] == jnp.arange(entries)[None, :]).astype(low)
    rel_rows = matmul(spread, rel_low).astype(low)
    rel_table = product("ud,hdc->huc", rel_rows, w_project[:, :, : 2 * head_width]).astype(low)
    probs, mixed = attend(own_length, qkv, rel_table)
    attended = product("htc,hdc->td", mixed, w_combine)
    hidden_mid, back_mid = jax.vjp(norm_at(4), hidden_in + attended, vec_full)
    mid_low = hidden_mid.astype(low)
    gate_in = product("td,hdf->htf", mid_low, w_expand)
    gate_act, back_gate = jax.vjp(gelu, gate_in)
    gate_low = gate_act.astype(low)
    ffn_out = product("htf,hdf->td", gate_low, w_contract)
    hidden_out, back_out = jax.vjp(norm_at(6), hidden_mid + ffn_out, vec_full)
    out_low = hidden_out.astype(low)
    w_readout = w_readout.transpose(1, 0, 2).reshape(model, model)
    dense_out = matmul(out_low, w_readout)

    def head_loss(dense_rows, gain_rows):
        head_norm = normalize(gelu(dense_rows), gain_rows[8], gain_rows[9])
        logits = jnp.sum(head_norm * gain_rows[10], -1)
        losses = jax.nn.softplus(logits) - own_flags * logits
        return jnp.sum(jnp.where(own_live, losses, 0.0))

    loss_part, back_head = jax.vjp(head_loss, dense_out, vec_full)
    grad_dense, grad_vec = back_head(1.0 / token_total)
    dense_low = grad_dense.astype(low)
    grad_readout = product(
        "td,thc->hdc", out_low, dense_low.reshape(seq_len, pieces, head_width)
    ).astype(low)
    grad_sum, grad_gain = back_out(product("tc,dc->td", dense_low, w_readout))
    grad_vec = grad_vec + grad_gain
    ffn_low = grad_sum.astype(low)
    grad_contract = product("td,htf->hdf", ffn_low, gate_low).astype(low)
    gate_grad = back_gate(product("td,hdf->htf", ffn_low, w_contract))[0].astype(low)
    grad_expand = product("td,htf->hdf", mid_low, gate_grad).astype(low)
    grad_mid = grad_sum + product("htf,hdf->td", gate_grad, w_expand)
    grad_sum, grad_gain = back_mid(grad_mid)
    grad_vec = grad_vec + grad_gain
    attend_low = grad_sum.astype(low)
    grad_mixed = product("td,hdc->htc", attend_low, w_combine).astype(low)
    grad_combine = product("td,htc->hdc", attend_low, mixed).astype(low)

    early = jnp.concatenate([grad_expand, grad_contract, grad_readout, grad_combine], 2)
    early = lax.psum_scatter(
        early.reshape(pieces * model, -1), everyone, scatter_dimension=0, tiled=True
    )

    qkv_grads, rel_table_grads = attend_back(qkv, rel_table, probs, grad_mixed)
    rel_grads = product("ur,huc->hrc", spread, rel_table_grads).astype(low)
    grad_hidden = grad_sum + product("htc,hdc->td", qkv_grads, w_project)
    grad_words, grad_gain = back_in(grad_hidden)
    grad_vec = grad_vec + grad_gain
    sent = grad_words.astype(low).reshape(seq_len, owners, width).transpose(1, 0, 2)
    sent = lax.all_to_all(sent, "dp", 0, 0, tiled=True)
    sent = lax.all_gather(sent[:, None], "heads", axis=1, tiled=True)
    sent = sent.reshape(owners * row_count, seq_len, width)
    grad_project = product("td,htc->hdc", hidden_low, qkv_grads)
    grad_rel_part = product("rd,hrc->hdc", rel_low, rel_grads)
    grad_project = jnp.concatenate(
        [
            grad_project[:, :, : 2 * head_width] + grad_rel_part,
            grad_project[:, :, 2 * head_width :],
        ],
        2,
    ).astype(low)
    grad_rel_norm = product("hrc,hdc->rd", rel_grads, w_project[:, :, : 2 * head_width])
    grad_relative, grad_gain = back_rel(grad_rel_norm)
    grad_vec = grad_vec + grad_gain
    grad_relative = grad_relative.reshape(pieces, span_part, model).transpose(0, 2, 1).astype(low)
    late = jnp.concatenate([grad_project, grad_relative], 2)
    late = lax.psum_scatter(
        late.reshape(pieces * model, -1), everyone, scatter_dimension=0, tiled=True
    )
    grad_vec = lax.psum(grad_vec, everyone)
    grad_embedding = deposit(all_lengths, places, sent, slots)[:vocab_slab].T

    early = early.astype(f32)
    late = late.astype(f32)
    squares_local = sum(jnp.sum(part * part) for part in (early, late, grad_embedding))
    squares_total, loss_sum = lax.psum((squares_local, loss_part), everyone)
    grad_norm = jnp.sqrt(squares_total + jnp.sum(grad_vec * grad_vec))
    factor = jnp.minimum(1.0, clip_level / grad_norm)

    grad_expand = early[:, :hidden]
    grad_contract = early[:, hidden : 2 * hidden].T
    grad_combine = early[:, 2 * hidden + head_width :].T
    grad_project = late[:, : 3 * head_width].reshape(width, 3, head_width)
    shared = jnp.concatenate(
        [early[:, 2 * hidden : 2 * hidden + head_width], late[:, 3 * head_width :]], 1
    )
    shared = lax.all_gather(shared, "heads", axis=0, tiled=True).reshape(pieces, width, -1)
    grad_readout = shared[:, :, :head_width].transpose(1, 0, 2).reshape(width, model)
    grad_relative = shared[:, :, head_width:].transpose(0, 2, 1).reshape(entries, width)
    grad_vec = lax.dynamic_slice_in_dim(grad_vec, owner * width, width, 1)
    weights = (embedding, relative, project, combine, expand, contract, readout, vectors)
    gradients = (
        grad_embedding,
        grad_relative,
        grad_project,
        grad_combine,
        grad_expand,
        grad_contract,
        grad_readout,
        grad_vec,
    )
    means = (
        embedding_mean,
        relative_mean,
        project_mean,
        combine_mean,
        expand_mean,
        contract_mean,
        readout_mean,
        vectors_mean,
    )
    squares = (
        embedding_square,
        relative_square,
        project_square,
        combine_square,
        expand_square,
        contract_square,
        readout_square,
        vectors_square,
    )
    updates = [
        adamw(weight, gradient * factor, mean, square, rate_now)
        for weight, gradient, mean, square, rate_now in zip(
            weights, gradients, means, squares, rate_steps
        )
    ]
    return (
        loss_sum,
        token_total,
        grad_norm,
        updates[0][0],
        updates[0][1],
        updates[0][2],
        updates[1][0],
        updates[1][1],
        updates[1][2],
        updates[2][0],
        updates[2][1],
        updates[2][2],
        updates[3][0],
        updates[3][1],
        updates[3][2],
        updates[4][0],
        updates[4][1],
        updates[4][2],
        updates[5][0],
        updates[5][1],
        updates[5][2],
        updates[6][0],
        updates[6][1],
        updates[6][2],
        updates[7][0],
        updates[7][1],
        updates[7][2],
        grad_vec[3] * factor,
    )


def solution(mesh):
    placed = (
        P("dp", None),
        P("dp"),
        P("dp", None),
        P("dp", "heads"),
        P(None, "dp"),
        P("dp", None, "heads"),
        P("heads", "dp"),
        P("dp", "heads"),
        P("heads", "dp"),
        P("dp", None),
        P(None, "dp"),
        P("dp", "heads"),
        P(None, "dp"),
        P("dp", None, "heads"),
        P("heads", "dp"),
        P("dp", "heads"),
        P("heads", "dp"),
        P("dp", None),
        P(None, "dp"),
        P("dp", "heads"),
        P(None, "dp"),
        P("dp", None, "heads"),
        P("heads", "dp"),
        P("dp", "heads"),
        P("heads", "dp"),
        P("dp", None),
        P(None, "dp"),
    )
    return jax.shard_map(
        per_device,
        mesh=mesh,
        in_specs=placed,
        out_specs=(
            P(),
            P(),
            P(),
            P("dp", "heads"),
            P("dp", "heads"),
            P("dp", "heads"),
            P(None, "dp"),
            P(None, "dp"),
            P(None, "dp"),
            P("dp", None, "heads"),
            P("dp", None, "heads"),
            P("dp", None, "heads"),
            P("heads", "dp"),
            P("heads", "dp"),
            P("heads", "dp"),
            P("dp", "heads"),
            P("dp", "heads"),
            P("dp", "heads"),
            P("heads", "dp"),
            P("heads", "dp"),
            P("heads", "dp"),
            P("dp", None),
            P("dp", None),
            P("dp", None),
            P(None, "dp"),
            P(None, "dp"),
            P(None, "dp"),
            P("dp"),
        ),
        check_vma=False,
    )
```

```python
import functools

import jax
import jax.numpy as jnp
from jax import lax
from jax.experimental import pallas as pl
from jax.experimental.pallas import tpu as pltpu
from jax.sharding import PartitionSpec as P

HEAD_DIM = 64
STEP = 10
BLOCK = 128
UNROLL = 8

low = jnp.bfloat16
f32 = jnp.float32

layer_eps = 1e-07
clip_level = 0.005
rate_steps = (0.1, 0.05, 0.05, 0.05, 0.05, 0.05, 0.05, 1.0)
beta_first = 0.9
beta_second = 0.999
adam_eps = 1e-08
weight_decay = 0.01


def dot_rows(a,b):
    return lax.dot_general(a,b,(((1,),(1,)),((),())),preferred_element_type=f32)
def dot_plain(a,b):
    return lax.dot_general(a,b,(((1,),(0,)),((),())),preferred_element_type=f32)
def dot_left(a,b):
    return lax.dot_general(a,b,(((0,),(0,)),((),())),preferred_element_type=f32)

def attend_kernel(length_ref, qkv_ref, table_ref, probs_ref, mixed_ref, far_ref):
    seq=qkv_ref.shape[1]; width=qkv_ref.shape[2]//3; heads=width//HEAD_DIM
    blocks=seq//BLOCK
    scale=(3*HEAD_DIM)**-0.5
    length=length_ref[0]
    live=lax.broadcasted_iota(jnp.int32,(BLOCK,seq),1)<length
    for head in range(heads):
        at=head*HEAD_DIM
        q=qkv_ref[0,:,at:at+HEAD_DIM]
        k=qkv_ref[0,:,width+at:width+at+HEAD_DIM]
        v=qkv_ref[0,:,2*width+at:2*width+at+HEAD_DIM]
        for block in range(blocks):
            rows=slice(block*BLOCK,(block+1)*BLOCK)
            start=seq-BLOCK*(block+1)
            far=dot_rows(k[rows],table_ref[0,start:start+seq+BLOCK,at:at+HEAD_DIM])
            far=pltpu.roll(far,seq,1,stride=1,stride_axis=0)[:,:seq]
            far_ref[head,:,rows]=far.T
        for block in range(blocks):
            rows=slice(block*BLOCK,(block+1)*BLOCK)
            start=seq-BLOCK*(block+1)
            near=dot_rows(q[rows],table_ref[0,start:start+seq+BLOCK,width+at:width+at+HEAD_DIM])
            near=pltpu.roll(near,seq,1,stride=1,stride_axis=0)[:,:seq]
            scores=(dot_rows(q[rows],k)+near+far_ref[head,rows,:])*scale
            scores=jnp.where(live,scores,-1e9)
            top=jnp.max(scores,-1,keepdims=True)
            expo=jnp.exp(scores-top)
            probs=(expo*(1.0/jnp.sum(expo,-1,keepdims=True))).astype(low)
            probs_ref[head,rows,:]=probs
            mixed_ref[0,rows,at:at+HEAD_DIM]=dot_plain(probs,v).astype(low)

def attend(length,qkv,table):
    groups,seq,width3=qkv.shape
    width=width3//3; heads=width//HEAD_DIM
    return pl.pallas_call(
        attend_kernel,
        grid=(groups,),
        in_specs=[pl.BlockSpec(memory_space=pltpu.SMEM),
            pl.BlockSpec((1,seq,width3),lambda g:(g,0,0)),
            pl.BlockSpec((1,2*seq,2*width),lambda g:(g,0,0))],
        out_specs=[pl.BlockSpec((heads,seq,seq),lambda g:(g,0,0)),
            pl.BlockSpec((1,seq,width),lambda g:(g,0,0))],
        out_shape=[jax.ShapeDtypeStruct((groups*heads,seq,seq),low),jax.ShapeDtypeStruct((groups,seq,width),low)],
        scratch_shapes=[pltpu.VMEM((heads,seq,seq),f32)],
        compiler_params=pltpu.CompilerParams(vmem_limit_bytes=48<<20),
        name="attend",
    )(length,qkv,table)

def attend_back_kernel(qkv_ref, table_ref, probs_ref, up_ref, grad_ref, rel_ref, low_ref, sum_ref):
    seq=qkv_ref.shape[1]; width=qkv_ref.shape[2]//3; heads=width//HEAD_DIM
    blocks=seq//BLOCK; reach=seq+BLOCK
    scale=(3*HEAD_DIM)**-0.5
    flip=(lax.broadcasted_iota(jnp.int32,(BLOCK,BLOCK),0)+lax.broadcasted_iota(jnp.int32,(BLOCK,BLOCK),1)==BLOCK-1).astype(f32).astype(low)
    edge=jnp.zeros((BLOCK,BLOCK),f32)
    def shear(rows):
        return pltpu.roll(jnp.concatenate([rows,edge],1),1,1,stride=1,stride_axis=0).astype(low)
    for head in range(heads):
        at=head*HEAD_DIM
        q=qkv_ref[0,:,at:at+HEAD_DIM]
        k=qkv_ref[0,:,width+at:width+at+HEAD_DIM]
        v=qkv_ref[0,:,2*width+at:2*width+at+HEAD_DIM]
        up=up_ref[0,:,at:at+HEAD_DIM]
        for block in range(blocks):
            rows=slice(block*BLOCK,(block+1)*BLOCK)
            probs=probs_ref[head,rows,:].astype(f32)
            pull=dot_rows(up[rows],v)
            inner=jnp.sum(probs*pull,-1,keepdims=True)
            low_ref[head,rows,:]=(probs*(pull-inner)*scale).astype(low)
        grad_ref[0,:,2*width+at:2*width+at+HEAD_DIM]=dot_left(up,probs_ref[head]).T.astype(low)
        sum_ref[2*head]=jnp.zeros(sum_ref.shape[1:],f32)
        sum_ref[2*head+1]=jnp.zeros(sum_ref.shape[1:],f32)
        for block in range(blocks):
            rows=slice(block*BLOCK,(block+1)*BLOCK)
            start=seq-BLOCK*(block+1)
            window=slice(start,start+reach)
            turned=dot_plain(flip,low_ref[head,rows,:])
            near=shear(turned)
            grad_q=dot_plain(turned.astype(low),k)+dot_plain(near,table_ref[0,window,width+at:width+at+HEAD_DIM])
            grad_ref[0,rows,at:at+HEAD_DIM]=dot_plain(flip,grad_q.astype(low)).astype(low)
            q_turned=dot_plain(flip,q[rows]).astype(low)
            sum_ref[2*head+1,:,window]+=dot_left(q_turned,near)
            turned=dot_rows(flip,low_ref[head,:,rows])
            far=shear(turned)
            grad_k=dot_plain(turned.astype(low),q)+dot_plain(far,table_ref[0,window,at:at+HEAD_DIM])
            grad_ref[0,rows,width+at:width+at+HEAD_DIM]=dot_plain(flip,grad_k.astype(low)).astype(low)
            k_turned=dot_plain(flip,k[rows]).astype(low)
            sum_ref[2*head,:,window]+=dot_left(k_turned,far)
        rel_ref[0,:,at:at+HEAD_DIM]=sum_ref[2*head].T.astype(low)
        rel_ref[0,:,width+at:width+at+HEAD_DIM]=sum_ref[2*head+1].T.astype(low)

def attend_back(qkv,table,probs,up):
    groups,seq,width3=qkv.shape
    width=width3//3; heads=width//HEAD_DIM
    return pl.pallas_call(
        attend_back_kernel,
        grid=(groups,),
        in_specs=[
            pl.BlockSpec((1,seq,width3),lambda g:(g,0,0)),
            pl.BlockSpec((1,2*seq,2*width),lambda g:(g,0,0)),
            pl.BlockSpec((heads,seq,seq),lambda g:(g,0,0)),
            pl.BlockSpec((1,seq,width),lambda g:(g,0,0))],
        out_specs=[pl.BlockSpec((1,seq,width3),lambda g:(g,0,0)),
            pl.BlockSpec((1,2*seq,2*width),lambda g:(g,0,0))],
        out_shape=[jax.ShapeDtypeStruct((groups,seq,width3),low),jax.ShapeDtypeStruct((groups,2*seq,2*width),low)],
        scratch_shapes=[pltpu.VMEM((heads,seq,seq),low),pltpu.VMEM((2*heads,HEAD_DIM,2*seq),f32)],
        compiler_params=pltpu.CompilerParams(vmem_limit_bytes=48<<20),
        name="attend_back",
    )(qkv,table,probs,up)


MESH = pl.DeviceIdType.MESH
ANYWHERE = pl.BlockSpec(memory_space=pl.ANY)
IN_VMEM = pl.BlockSpec(memory_space=pltpu.VMEM)


def place():
    owner, holder = lax.axis_index("dp"), lax.axis_index("heads")
    return owner // 2, owner % 2, holder // 2, holder % 2


def device(z, x, y, c):
    return (z * 2 + x, y * 2 + c)


def signal(target):
    pl.semaphore_signal(
        pltpu.get_barrier_semaphore(), inc=1, device_id=target, device_id_type=MESH
    )


def greet(z, x, y, c, line):
    signal(device(z, x, y, 1 - c))
    signal(device(z, x, 1 - y, c))
    if line:
        signal(device(z, 1 - x, y, c))

        @pl.when(z < 3)
        def above():
            signal(device(z + 1, x, y, c))

        @pl.when(z > 0)
        def below():
            signal(device(z - 1, x, y, c))

        pl.semaphore_wait(pltpu.get_barrier_semaphore(), jnp.where((z == 0) | (z == 3), 4, 5))


def remote(source, target, send, recv, to):
    return pltpu.make_async_remote_copy(
        src_ref=source, dst_ref=target, send_sem=send, recv_sem=recv, device_id=to, device_id_type=MESH
    )


def scatter_sums_kernel(count, *refs):
    grads, totals = refs[:count], refs[count : 2 * count]
    refs = refs[2 * count :]
    own, pair, first_a, first_b, second_a, second_b, rise, fall = [
        refs[count * part : count * (part + 1)] for part in range(8)
    ]
    local_sem, send_sem, recv_sem = refs[8 * count :]
    z, x, y, c = place()
    greet(z, x, y, c, True)
    half = grads[0].shape[3] // 2
    upper, lower = pl.ds(0, half), pl.ds(half, half)
    core_to, y_to, x_to = device(z, x, y, 1 - c), device(z, x, 1 - y, c), device(z, 1 - x, y, c)
    up_to, down_to = device(z + 1, x, y, c), device(z - 1, x, y, c)

    def link(part, slot, source, target, to):
        return remote(source, target, send_sem.at[part, slot], recv_sem.at[part, slot], to)

    def local(part, side):
        return pltpu.make_async_copy(
            grads[part].at[side * 2 + c], own[part].at[side], local_sem.at[part, side]
        )

    def pair_copy(part, side):
        return link(part, side, grads[part].at[side * 2 + 1 - c], pair[part].at[side], core_to)

    def first_copies(part):
        block = own[part]
        return (
            link(part, 2, block.at[1 - y, :, :, upper], first_a[part], y_to),
            link(part, 3, block.at[:, :, 1 - x, lower], first_b[part], x_to),
        )

    def second_copies(part):
        block = own[part]
        return (
            link(part, 4, block.at[y, :, 1 - x, upper], second_a[part], x_to),
            link(part, 5, block.at[1 - y, :, x, lower], second_b[part], y_to),
        )

    def rise_copy(part, turn):
        block = own[part].at[y, lax.clamp(0, 3 + z - turn, 3), x]
        return link(part, 6 + turn, block, rise[part].at[turn], up_to)

    def fall_copy(part, turn):
        block = own[part].at[y, lax.clamp(0, turn - 3 + z, 3), x]
        return link(part, 9 + turn, block, fall[part].at[turn], down_to)

    def add(target, source):
        target[...] = (target[...].astype(f32) + source[...].astype(f32)).astype(low)

    def start(part):
        for side in range(2):
            pair_copy(part, side).start()
            local(part, side).start()

    def stage_pair(part):
        for side in range(2):
            local(part, side).wait()
            pair_copy(part, side).wait()

        def step(index, carry):
            side, rest = index // 8, index % 8
            add(own[part].at[side, rest // 2, rest % 2], pair[part].at[side, rest // 2, rest % 2])
            return carry

        lax.fori_loop(0, 16, step, 0)
        for copy in first_copies(part):
            copy.start()

    def stage_first(part):
        for copy in first_copies(part):
            copy.wait()

        def step(index, carry):
            add(own[part].at[y, index // 2, index % 2, upper], first_a[part].at[index // 2, index % 2])
            add(own[part].at[index % 2, index // 2, x, lower], first_b[part].at[index % 2, index // 2])
            return carry

        lax.fori_loop(0, 8, step, 0)
        for copy in second_copies(part):
            copy.start()

    def stage_second(part):
        for copy in second_copies(part):
            copy.wait()

        def step(index, carry):
            add(own[part].at[y, index, x, upper], second_a[part].at[index])
            add(own[part].at[y, index, x, lower], second_b[part].at[index])
            return carry

        lax.fori_loop(0, 4, step, 0)

    def stage_line(part, turn):
        @pl.when((z <= turn) & (z < 3))
        def rises():
            if turn > 0:

                @pl.when(z > 0)
                def joined():
                    rise_copy(part, turn - 1).wait_recv()
                    add(own[part].at[y, 3 + z - turn, x], rise[part].at[turn - 1])

            rise_copy(part, turn).start()

        @pl.when((3 - z <= turn) & (z > 0))
        def falls():
            if turn > 0:

                @pl.when(z < 3)
                def joined():
                    fall_copy(part, turn - 1).wait_recv()
                    add(own[part].at[y, turn - 3 + z, x], fall[part].at[turn - 1])

            fall_copy(part, turn).start()

    def stage_total(part):
        totals[part][...] = own[part][y, z, x].astype(f32)

        @pl.when(z > 0)
        def risen():
            rise_copy(part, 2).wait_recv()
            totals[part][...] += rise[part][2].astype(f32)

        @pl.when(z < 3)
        def fallen():
            fall_copy(part, 2).wait_recv()
            totals[part][...] += fall[part][2].astype(f32)

        for turn in range(3):

            @pl.when((z <= turn) & (z < 3))
            def risen_out():
                rise_copy(part, turn).wait_send()

            @pl.when((3 - z <= turn) & (z > 0))
            def fallen_out():
                fall_copy(part, turn).wait_send()

    stages = [
        stage_pair,
        stage_first,
        stage_second,
        functools.partial(stage_line, turn=0),
        functools.partial(stage_line, turn=1),
        functools.partial(stage_line, turn=2),
        stage_total,
    ]
    for part in range(count):
        start(part)
    for tick in range(count + len(stages) - 1):
        for index, stage in enumerate(stages):
            if 0 <= tick - index < count:
                stage(tick - index)


def scatter_sums(grads, tag):
    count = len(grads)
    width = grads[0].shape[2]
    sizes = [grad.shape[3] for grad in grads]
    half = width // 2
    scratch = []
    for lead in (
        (2, 4, 2, width),
        (2, 4, 2, width),
        (4, 2, half),
        (2, 4, half),
        (4, half),
        (4, half),
        (3, width),
        (3, width),
    ):
        scratch += [pltpu.VMEM(lead + (size,), low) for size in sizes]
    return pl.pallas_call(
        functools.partial(scatter_sums_kernel, count),
        in_specs=[ANYWHERE] * count,
        out_specs=[IN_VMEM] * count,
        out_shape=[jax.ShapeDtypeStruct((width, size), f32) for size in sizes],
        scratch_shapes=scratch
        + [
            pltpu.SemaphoreType.DMA((count, 2)),
            pltpu.SemaphoreType.DMA((count, 12)),
            pltpu.SemaphoreType.DMA((count, 12)),
        ],
        compiler_params=pltpu.CompilerParams(
            collective_id=tag, has_side_effects=True, vmem_limit_bytes=56 << 20
        ),
        name="scatter_sums",
    )(*[grad.reshape(4, 4, 2, width, size) for grad, size in zip(grads, sizes)])


def peers(z, x):
    return [((z + 2 - far) % 4, x if same else 1 - x) for far, same in PEER_ORDER]


PEER_ORDER = ((0, False), (0, True), (1, False), (1, True), (3, False), (3, True), (2, False))


def meet_owners(z, x, y, c):
    for peer_z, peer_x in peers(z, x):
        signal(device(peer_z, peer_x, y, c))


def share_facts_kernel(facts_ref, all_ref, local_sem, send_sem, recv_sem):
    z, x, y, c = place()
    meet_owners(z, x, y, c)
    pl.semaphore_wait(pltpu.get_barrier_semaphore(), 7)
    here = z * 2 + x
    keep = pltpu.make_async_copy(facts_ref, all_ref.at[here], local_sem)
    keep.start()
    copies = []
    for index, (peer_z, peer_x) in enumerate(peers(z, x)):
        copy = remote(
            facts_ref,
            all_ref.at[here],
            send_sem.at[index],
            recv_sem.at[here],
            device(peer_z, peer_x, y, c),
        )
        copy.start()
        copies.append(copy)
    for index, (peer_z, peer_x) in enumerate(peers(z, x)):
        there = peer_z * 2 + peer_x
        copies[index].wait_send()
        remote(
            facts_ref, all_ref.at[there], send_sem.at[index], recv_sem.at[there], device(z, x, y, c)
        ).wait_recv()
    keep.wait()


def share_facts(facts, tag):
    return pl.pallas_call(
        share_facts_kernel,
        in_specs=[IN_VMEM],
        out_specs=IN_VMEM,
        out_shape=jax.ShapeDtypeStruct((8,) + facts.shape, facts.dtype),
        scratch_shapes=[
            pltpu.SemaphoreType.DMA,
            pltpu.SemaphoreType.DMA((7,)),
            pltpu.SemaphoreType.DMA((8,)),
        ],
        compiler_params=pltpu.CompilerParams(collective_id=tag, has_side_effects=True),
        name="share_facts",
    )(facts)


def exchange_words_kernel(found_ref, words_ref, pair, side, send_sem, recv_sem, out_sem, in_sem):
    z, x, y, c = place()
    meet_owners(z, x, y, c)
    greet(z, x, y, c, False)
    pl.semaphore_wait(pltpu.get_barrier_semaphore(), 9)
    here = z * 2 + x
    targets = [(z, x)] + peers(z, x)
    targets = targets[1:] + targets[:1]
    core_to, y_to = device(z, x, y, 1 - c), device(z, x, 1 - y, c)

    def pair_copy(part, row):
        to = targets[part][0] * 2 + targets[part][1]
        return remote(
            found_ref.at[row * 2 + 1 - c, to],
            pair.at[row, to],
            send_sem.at[part, row],
            recv_sem.at[part, row],
            core_to,
        )

    def side_copy(part):
        to = targets[part][0] * 2 + targets[part][1]
        return remote(
            pair.at[1 - y, to], side.at[to], send_sem.at[part, 2], recv_sem.at[part, 2], y_to
        )

    def out_copy(part):
        to = targets[part][0] * 2 + targets[part][1]
        return remote(
            pair.at[y, to],
            words_ref.at[here],
            out_sem.at[part],
            in_sem.at[here],
            device(targets[part][0], targets[part][1], y, c),
        )

    def at_home(part):
        return targets[part][0] * 2 + targets[part][1]

    for part in range(8):
        for row in range(2):
            pair_copy(part, row).start()
    for part in range(8):
        to = at_home(part)
        for row in range(2):
            pair_copy(part, row).wait_recv()
            pair[row, to] = pair[row, to] + found_ref[row * 2 + c, to]
        side_copy(part).start()
    for part in range(8):
        to = at_home(part)
        side_copy(part).wait_recv()
        pair[y, to] = pair[y, to] + side[to]
        if part < 7:
            out_copy(part).start()
        else:
            words_ref[here] = pair[y, to]
    for part in range(8):
        for row in range(2):
            pair_copy(part, row).wait_send()
        side_copy(part).wait_send()
        if part < 7:
            out_copy(part).wait_send()
            there = at_home(part)
            remote(
                pair.at[y, there], words_ref.at[there], out_sem.at[part], in_sem.at[there], core_to
            ).wait_recv()


def exchange_words(found, tag):
    piece = found.shape[2:]
    return pl.pallas_call(
        exchange_words_kernel,
        in_specs=[IN_VMEM],
        out_specs=IN_VMEM,
        out_shape=jax.ShapeDtypeStruct((8,) + piece, low),
        scratch_shapes=[
            pltpu.VMEM((2, 8) + piece, low),
            pltpu.VMEM((8,) + piece, low),
            pltpu.SemaphoreType.DMA((8, 3)),
            pltpu.SemaphoreType.DMA((8, 3)),
            pltpu.SemaphoreType.DMA((8,)),
            pltpu.SemaphoreType.DMA((8,)),
        ],
        compiler_params=pltpu.CompilerParams(
            collective_id=tag, has_side_effects=True, vmem_limit_bytes=40 << 20
        ),
        name="exchange_words",
    )(found)


def return_words_kernel(grads_ref, sent_ref, local_sem, out_sem, in_sem, send_sem, recv_sem):
    z, x, y, c = place()
    meet_owners(z, x, y, c)
    greet(z, x, y, c, False)
    pl.semaphore_wait(pltpu.get_barrier_semaphore(), 9)
    here = z * 2 + x
    own = y * 2 + c
    other = (1 - y) * 2 + c
    core_to, y_to = device(z, x, y, 1 - c), device(z, x, 1 - y, c)
    near_first = peers(z, x)[::-1]
    keep = pltpu.make_async_copy(grads_ref.at[here], sent_ref.at[own, here], local_sem)
    keep.start()

    def out_copy(part, peer):
        return remote(
            grads_ref.at[peer[0] * 2 + peer[1]],
            sent_ref.at[own, here],
            out_sem.at[part],
            in_sem.at[here],
            device(peer[0], peer[1], y, c),
        )

    def in_copy(part, peer):
        there = peer[0] * 2 + peer[1]
        return remote(
            grads_ref.at[there], sent_ref.at[own, there], out_sem.at[part], in_sem.at[there], core_to
        )

    def pass_on(slot, row, there, to):
        block = sent_ref.at[row, there]
        return remote(block, block, send_sem.at[slot, there], recv_sem.at[row, there], to)

    for part, peer in enumerate(peers(z, x)):
        out_copy(part, peer).start()
    keep.wait()
    order = [(z, x)] + near_first
    for part, (peer_z, peer_x) in enumerate(order):
        there = peer_z * 2 + peer_x
        if part > 0:
            in_copy(part - 1, (peer_z, peer_x)).wait_recv()
        pass_on(0, own, there, y_to).start()
        pass_on(1, own, there, core_to).start()
    for peer_z, peer_x in order:
        there = peer_z * 2 + peer_x
        pass_on(0, other, there, y_to).wait_recv()
        pass_on(2, other, there, core_to).start()
    for part, peer in enumerate(peers(z, x)):
        out_copy(part, peer).wait_send()
    for peer_z, peer_x in order:
        there = peer_z * 2 + peer_x
        pass_on(0, own, there, y_to).wait_send()
        pass_on(1, own, there, core_to).wait_send()
        pass_on(2, other, there, core_to).wait_send()
        pass_on(1, y * 2 + 1 - c, there, core_to).wait_recv()
        pass_on(2, (1 - y) * 2 + 1 - c, there, core_to).wait_recv()


def return_words(grads, tag):
    piece = grads.shape[1:]
    return pl.pallas_call(
        return_words_kernel,
        in_specs=[IN_VMEM],
        out_specs=IN_VMEM,
        out_shape=jax.ShapeDtypeStruct((4, 8) + piece, low),
        scratch_shapes=[
            pltpu.SemaphoreType.DMA,
            pltpu.SemaphoreType.DMA((7,)),
            pltpu.SemaphoreType.DMA((8,)),
            pltpu.SemaphoreType.DMA((3, 8)),
            pltpu.SemaphoreType.DMA((4, 8)),
        ],
        compiler_params=pltpu.CompilerParams(
            collective_id=tag, has_side_effects=True, vmem_limit_bytes=40 << 20
        ),
        name="return_words",
    )(grads)


def finish_sums_kernel(facts_ref, shared_ref, total_ref, all_ref, pair, side, cross, line, local_sem, send_sem, recv_sem, line_send, line_recv):
    z, x, y, c = place()
    core_to, y_to, x_to = device(z, x, y, 1 - c), device(z, x, 1 - y, c), device(z, 1 - x, y, c)
    column = [(z + step) % 4 for step in range(1, 4)]
    for target in (core_to, y_to, x_to, *[device(other, x, y, c) for other in column]):
        signal(target)
    pl.semaphore_wait(pltpu.get_barrier_semaphore(), 6)
    own, other = y * 2 + c, (1 - y) * 2 + c
    keep = pltpu.make_async_copy(shared_ref, all_ref.at[own], local_sem)
    keep.start()
    swap_pair = remote(facts_ref, pair, send_sem.at[0], recv_sem.at[0], core_to)
    swap_pair.start()
    shared_side = remote(shared_ref, all_ref.at[own], send_sem.at[3], recv_sem.at[3], y_to)
    shared_pair = remote(shared_ref, all_ref.at[own], send_sem.at[4], recv_sem.at[4], core_to)
    shared_side.start()
    shared_pair.start()
    swap_pair.wait()
    total_ref[...] = facts_ref[...] + pair[...]
    swap_side = remote(total_ref, side, send_sem.at[1], recv_sem.at[1], y_to)
    swap_side.start()
    swap_side.wait()
    total_ref[...] += side[...]
    swap_cross = remote(total_ref, cross, send_sem.at[2], recv_sem.at[2], x_to)
    swap_cross.start()
    swap_cross.wait()
    total_ref[...] += cross[...]
    line[z] = total_ref[...]
    lines = [
        remote(line.at[z], line.at[z], line_send.at[step], line_recv.at[z], device(to, x, y, c))
        for step, to in enumerate(column)
    ]
    for copy in lines:
        copy.start()
    shared_side.wait()
    relay = remote(all_ref.at[other], all_ref.at[other], send_sem.at[5], recv_sem.at[5], core_to)
    relay.start()
    for step, to in enumerate(column):
        lines[step].wait_send()
        remote(line.at[to], line.at[to], line_send.at[step], line_recv.at[to], core_to).wait_recv()
    total_ref[...] = (line[0] + line[1]) + (line[2] + line[3])
    shared_pair.wait()
    relay.wait()
    keep.wait()


def finish_sums(facts, shared, tag):
    return pl.pallas_call(
        finish_sums_kernel,
        in_specs=[IN_VMEM] * 2,
        out_specs=[IN_VMEM] * 2,
        out_shape=[
            jax.ShapeDtypeStruct(facts.shape, f32),
            jax.ShapeDtypeStruct((4,) + shared.shape, f32),
        ],
        scratch_shapes=[pltpu.VMEM(facts.shape, f32)] * 3
        + [
            pltpu.VMEM((4,) + facts.shape, f32),
            pltpu.SemaphoreType.DMA,
            pltpu.SemaphoreType.DMA((6,)),
            pltpu.SemaphoreType.DMA((6,)),
            pltpu.SemaphoreType.DMA((3,)),
            pltpu.SemaphoreType.DMA((4,)),
        ],
        compiler_params=pltpu.CompilerParams(collective_id=tag, has_side_effects=True),
        name="finish_sums",
    )(facts, shared)


def identity(size):
    rows = lax.broadcasted_iota(jnp.int32, (size, size), 0)
    columns = lax.broadcasted_iota(jnp.int32, (size, size), 1)
    return (rows == columns).astype(f32).astype(low)


def turn(values):
    return dot_rows(identity(values.shape[1]), values)


def lookup_kernel(lengths_ref, places_ref, weights_ref, words_ref, table_ref, rows_ref):
    width, slab = weights_ref.shape

    @pl.when(pl.program_id(0) == 0)
    def fill():
        def step(index, carry):
            first = pl.multiple_of(index * BLOCK, BLOCK)
            table_ref[pl.ds(first, BLOCK), :] = turn(weights_ref[:, pl.ds(first, BLOCK)].astype(low))
            return carry

        lax.fori_loop(0, slab // BLOCK, step, 0)
        table_ref[pl.ds(slab, 8), :] = jnp.zeros((8, width), f32)

    rows_ref[...] = jnp.zeros_like(rows_ref)

    def step(index, carry):
        first = pl.multiple_of(index * UNROLL, UNROLL)
        for offset in range(UNROLL):
            spot = places_ref[0, 0, first + offset]
            rows_ref[pl.ds(first + offset, 1), :] = table_ref[pl.ds(spot, 1), :]
        return carry

    lax.fori_loop(0, pl.cdiv(lengths_ref[pl.program_id(0)], UNROLL), step, 0)
    seq = rows_ref.shape[0]
    for first in range(0, seq, BLOCK):
        words_ref[0, 0, :, first : first + BLOCK] = turn_block(rows_ref[first : first + BLOCK, :])


def turn_block(rows):
    return dot_rows(identity(rows.shape[1]), rows.astype(low)).astype(low)


def lookup(lengths, places, weights, row_count):
    rows, seq = places.shape
    width, slab = weights.shape
    return pl.pallas_call(
        lookup_kernel,
        grid=(rows,),
        in_specs=[
            pl.BlockSpec(memory_space=pltpu.SMEM),
            pl.BlockSpec((1, 1, seq), lambda row: (row, 0, 0), memory_space=pltpu.SMEM),
            pl.BlockSpec(weights.shape, lambda row: (0, 0)),
        ],
        out_specs=pl.BlockSpec(
            (1, 1, width, seq), lambda row: (row % row_count, row // row_count, 0, 0)
        ),
        out_shape=jax.ShapeDtypeStruct((row_count, rows // row_count, width, seq), low),
        scratch_shapes=[pltpu.VMEM((slab + 8, width), f32), pltpu.VMEM((seq, width), f32)],
        compiler_params=pltpu.CompilerParams(vmem_limit_bytes=48 << 20),
        name="lookup",
    )(lengths, places[:, None], weights)


def deposit_kernel(lengths_ref, places_ref, grads_ref, total_ref, squares_ref, rows_ref, *tables):
    width, slab = total_ref.shape

    @pl.when(pl.program_id(0) == 0)
    def clear():
        for table in tables:
            table[...] = jnp.zeros_like(table)

    for first in range(0, rows_ref.shape[0], BLOCK):
        rows_ref[first : first + BLOCK, :] = turn(grads_ref[0, 0, :, first : first + BLOCK])

    def step(index, carry):
        first = pl.multiple_of(index * UNROLL, UNROLL)
        for offset in range(0, UNROLL, len(tables)):
            places = [places_ref[0, 0, first + offset + part] for part in range(len(tables))]
            sums = [
                table[pl.ds(place, 1), :] + rows_ref[pl.ds(first + offset + part, 1), :]
                for part, (place, table) in enumerate(zip(places, tables))
            ]
            for place, table, value in zip(places, tables, sums):
                table[pl.ds(place, 1), :] = value
        return carry

    lax.fori_loop(0, pl.cdiv(lengths_ref[pl.program_id(0)], UNROLL), step, 0)

    @pl.when(pl.program_id(0) == pl.num_programs(0) - 1)
    def finish():
        squares_ref[...] = jnp.zeros_like(squares_ref)

        def step(index, carry):
            first = pl.multiple_of(index * BLOCK, BLOCK)
            block = sum(table[pl.ds(first, BLOCK), :] for table in tables).T
            total_ref[:, pl.ds(first, BLOCK)] = block
            squares_ref[...] += block * block
            return carry

        lax.fori_loop(0, slab // BLOCK, step, 0)


def deposit(lengths, places, grads, slab):
    rows, seq = places.shape
    row_count, width = grads.shape[0], grads.shape[2]
    return pl.pallas_call(
        deposit_kernel,
        grid=(rows,),
        in_specs=[
            pl.BlockSpec(memory_space=pltpu.SMEM),
            pl.BlockSpec((1, 1, seq), lambda row: (row, 0, 0), memory_space=pltpu.SMEM),
            pl.BlockSpec(
                (1, 1, width, seq), lambda row: (row % row_count, row // row_count, 0, 0)
            ),
        ],
        out_specs=[
            pl.BlockSpec((width, slab), lambda row: (0, 0)),
            pl.BlockSpec((width, BLOCK), lambda row: (0, 0)),
        ],
        out_shape=[
            jax.ShapeDtypeStruct((width, slab), f32),
            jax.ShapeDtypeStruct((width, BLOCK), f32),
        ],
        scratch_shapes=[pltpu.VMEM((seq, width), f32)] + [pltpu.VMEM((slab + 8, width), f32)] * 4,
        compiler_params=pltpu.CompilerParams(vmem_limit_bytes=56 << 20),
        name="deposit",
    )(lengths, places[:, None], grads)


def matmul(matrix, operand):
    return jnp.dot(matrix, operand, preferred_element_type=f32)


def product(form, matrix, operand):
    return jnp.einsum(form, matrix, operand, preferred_element_type=f32)


def normalize(values, gain_row, bias_row):
    center = values - jnp.mean(values, -1, keepdims=True)
    spread_sq = jnp.mean(center * center, -1, keepdims=True)
    return center * lax.rsqrt(spread_sq + layer_eps) * gain_row + bias_row


def gelu(values):
    return jax.nn.gelu(values, approximate=False)


def norm_at(first_row):
    def apply_norm(values, gain_rows):
        return normalize(values, gain_rows[first_row], gain_rows[first_row + 1])

    return apply_norm


def split_terms(values, count):
    terms = []
    for _ in range(count):
        term = lax.reduce_precision(values, 8, 7)
        terms.append(term.astype(low))
        values = values - term
    return terms


def adamw(weight, gradient, mean, square, rate_now):
    first = beta_first * mean + (1.0 - beta_first) * gradient
    second = beta_second * square + (1.0 - beta_second) * gradient * gradient
    mean_hat = first / (1.0 - beta_first**STEP)
    square_hat = second / (1.0 - beta_second**STEP)
    master = weight - rate_now * (
        mean_hat / (jnp.sqrt(square_hat) + adam_eps) + weight_decay * weight
    )
    return (first, second, master)


def per_device(
    token_ids,
    row_lengths,
    replaced,
    embedding,
    relative,
    project,
    combine,
    expand,
    contract,
    readout,
    vectors,
    embedding_mean,
    relative_mean,
    project_mean,
    combine_mean,
    expand_mean,
    contract_mean,
    readout_mean,
    vectors_mean,
    embedding_square,
    relative_square,
    project_square,
    combine_square,
    expand_square,
    contract_square,
    readout_square,
    vectors_square,
):
    pieces = lax.axis_size("heads")
    holder = lax.axis_index("heads")
    owners = lax.axis_size("dp")
    row_count, seq_len = token_ids.shape
    width = vectors.shape[1]
    model = width * owners
    everyone = ("heads", "dp")
    head_width = project.shape[2]
    hidden = expand.shape[1]
    vocab_slab = embedding.shape[1]
    span_part = relative.shape[0] // pieces
    vector_count = vectors.shape[0]
    vector_part = pl.cdiv(vector_count, pieces)
    direct = owners == 8 and pieces == 4

    own_relative = lax.dynamic_slice_in_dim(relative, holder * span_part, span_part, 0).T
    own_readout = lax.dynamic_slice_in_dim(readout, holder * head_width, head_width, 1)
    vector_terms = jnp.concatenate(split_terms(vectors.T, 3), 1)
    first_pack = jnp.concatenate(
        [
            project.reshape(width, 3 * head_width).astype(low),
            combine.T.astype(low),
            *split_terms(own_relative, 2),
            jnp.pad(vector_terms, ((0, 0), (0, BLOCK - 3 * vector_count))),
        ],
        1,
    )
    second_pack = jnp.concatenate(
        [expand.astype(low), contract.T.astype(low), own_readout.astype(low)], 1
    )
    first_all = lax.all_gather(first_pack, everyone, axis=0, tiled=True)
    first_all = first_all.reshape(pieces, model, -1)
    second_all = lax.all_gather(second_pack, everyone, axis=0, tiled=True)
    second_all = second_all.reshape(pieces, model, -1)

    length_row = jnp.pad(row_lengths[None, :], ((0, 0), (0, seq_len - row_count)))
    facts = jnp.concatenate([token_ids, jnp.pad(length_row, ((0, 8 - 1 - row_count), (0, 0)))], 0)
    all_facts = share_facts(facts, 1) if direct else lax.all_gather(facts, "dp")
    all_ids = all_facts[:, :row_count].reshape(owners * row_count, seq_len)
    all_lengths = all_facts[:, row_count, :row_count].reshape(-1)
    token_total = jnp.sum(all_lengths).astype(f32)
    local_ids = all_ids - holder * vocab_slab
    inside = (local_ids >= 0) & (local_ids < vocab_slab)
    places = jnp.where(inside, local_ids, vocab_slab)

    w_project = first_all[:, :, : 3 * head_width]
    w_combine = first_all[:, :, 3 * head_width : 4 * head_width]
    at = 4 * head_width
    rel_terms = first_all[:, :, at : at + 2 * span_part].astype(f32)
    rel_full = rel_terms[:, :, :span_part] + rel_terms[:, :, span_part:]
    rel_full = rel_full.transpose(0, 2, 1).reshape(pieces * span_part, model)
    at = at + 2 * span_part
    vec_terms = first_all[0, :, at : at + 3 * vector_count].astype(f32)
    vec_full = (
        vec_terms[:, :vector_count]
        + vec_terms[:, vector_count : 2 * vector_count]
        + vec_terms[:, 2 * vector_count :]
    ).T
    w_expand = second_all[:, :, :hidden]
    w_contract = second_all[:, :, hidden : 2 * hidden]
    w_readout = second_all[:, :, 2 * hidden :]

    found = lookup(all_lengths, places, embedding, row_count)
    if direct:
        found = exchange_words(found, 2)
    else:
        found = lax.psum_scatter(found, "heads", scatter_dimension=0, tiled=True)[0]
        found = lax.all_to_all(found, "dp", 0, 0, tiled=True)
    word_rows = found.reshape(model, seq_len).T.astype(f32)

    own_length = lax.dynamic_slice_in_dim(row_lengths, holder, 1)
    own_live = jnp.arange(seq_len) < own_length
    own_flags = lax.dynamic_slice_in_dim(replaced, holder, 1)[0].astype(f32)

    hidden_in, back_in = jax.vjp(norm_at(0), word_rows, vec_full)
    hidden_low = hidden_in.astype(low)
    qkv = product("td,hdc->htc", hidden_low, w_project).astype(low)
    rel_norm, back_rel = jax.vjp(norm_at(2), rel_full, vec_full)
    rel_low = rel_norm.astype(low)
    entries = rel_full.shape[0]
    reach = jnp.clip(seq_len + entries // 2 - jnp.arange(2 * seq_len), 0, entries - 1)
    spread = (reach[:, None] == jnp.arange(entries)[None, :]).astype(low)
    rel_rows = matmul(spread, rel_low).astype(low)
    rel_table = product("ud,hdc->huc", rel_rows, w_project[:, :, : 2 * head_width]).astype(low)
    probs, mixed = attend(own_length, qkv, rel_table)
    attended = product("htc,hdc->td", mixed, w_combine)
    hidden_mid, back_mid = jax.vjp(norm_at(4), hidden_in + attended, vec_full)
    mid_low = hidden_mid.astype(low)
    gate_in = product("td,hdf->htf", mid_low, w_expand)
    gate_act, back_gate = jax.vjp(gelu, gate_in)
    gate_low = gate_act.astype(low)
    ffn_out = product("htf,hdf->td", gate_low, w_contract)
    hidden_out, back_out = jax.vjp(norm_at(6), hidden_mid + ffn_out, vec_full)
    out_low = hidden_out.astype(low)
    w_readout = w_readout.transpose(1, 0, 2).reshape(model, model)
    dense_out = matmul(out_low, w_readout)

    def head_loss(dense_rows, gain_rows):
        head_norm = normalize(gelu(dense_rows), gain_rows[8], gain_rows[9])
        logits = jnp.sum(head_norm * gain_rows[10], -1)
        losses = jax.nn.softplus(logits) - own_flags * logits
        return jnp.sum(jnp.where(own_live, losses, 0.0))

    loss_part, back_head = jax.vjp(head_loss, dense_out, vec_full)
    grad_dense, grad_vec = back_head(1.0 / token_total)
    dense_low = grad_dense.astype(low)
    grad_readout = product(
        "td,thc->hdc", out_low, dense_low.reshape(seq_len, pieces, head_width)
    ).astype(low)
    grad_sum, grad_gain = back_out(product("tc,dc->td", dense_low, w_readout))
    grad_vec = grad_vec + grad_gain
    ffn_low = grad_sum.astype(low)
    grad_contract = product("td,htf->hdf", ffn_low, gate_low).astype(low)
    gate_grad = back_gate(product("td,hdf->htf", ffn_low, w_contract))[0].astype(low)
    grad_expand = product("td,htf->hdf", mid_low, gate_grad).astype(low)
    grad_mid = grad_sum + product("htf,hdf->td", gate_grad, w_expand)
    grad_sum, grad_gain = back_mid(grad_mid)
    grad_vec = grad_vec + grad_gain
    attend_low = grad_sum.astype(low)
    grad_mixed = product("td,hdc->htc", attend_low, w_combine).astype(low)
    grad_combine = product("td,htc->hdc", attend_low, mixed).astype(low)

    qkv_grads, rel_table_grads = attend_back(qkv, rel_table, probs, grad_mixed)
    grad_hidden = grad_sum + product("htc,hdc->td", qkv_grads, w_project)
    grad_words, grad_gain = back_in(grad_hidden)
    grad_vec = grad_vec + grad_gain
    sent = grad_words.astype(low).T.reshape(owners, width, seq_len)
    if direct:
        sent = return_words(sent, 3)
    else:
        sent = lax.all_to_all(sent, "dp", 0, 0, tiled=True)
        sent = lax.all_gather(sent, "heads", axis=0)

    rel_grads = product("ur,huc->hrc", spread, rel_table_grads).astype(low)
    grad_project = product("td,htc->hdc", hidden_low, qkv_grads)
    grad_rel_part = product("rd,hrc->hdc", rel_low, rel_grads)
    grad_project = jnp.concatenate(
        [
            grad_project[:, :, : 2 * head_width] + grad_rel_part,
            grad_project[:, :, 2 * head_width :],
        ],
        2,
    ).astype(low)
    grad_rel_norm = product("hrc,hdc->rd", rel_grads, w_project[:, :, : 2 * head_width])
    grad_relative, grad_gain = back_rel(grad_rel_norm)
    grad_vec = grad_vec + grad_gain
    grad_relative = grad_relative.reshape(pieces, span_part, model).transpose(0, 2, 1).astype(low)
    grad_vec = jnp.pad(grad_vec, ((0, pieces * vector_part - vector_count), (0, 0)))
    grad_vec = grad_vec.reshape(pieces, vector_part, model).transpose(0, 2, 1).astype(low)
    grad_vec = jnp.pad(grad_vec, ((0, 0), (0, 0), (0, BLOCK - vector_part)))

    partial_grads = [
        grad_contract,
        grad_expand,
        jnp.concatenate([grad_readout, grad_combine], 2),
        grad_project,
        jnp.concatenate([grad_relative, grad_vec], 2),
    ]
    if direct:
        sums = scatter_sums(
            [part.reshape(pieces, owners, width, -1) for part in partial_grads], 4
        )
    else:
        sums = [
            lax.psum_scatter(
                part.reshape(pieces * model, -1), everyone, scatter_dimension=0, tiled=True
            ).astype(f32)
            for part in partial_grads
        ]
    grad_embedding, own_squares = deposit(all_lengths, places, sent, vocab_slab)

    squares_local = sum(jnp.sum(part * part) for part in sums) + jnp.sum(own_squares)
    shared = jnp.concatenate([sums[2][:, :head_width], sums[4]], 1)
    if direct:
        column = lax.broadcasted_iota(jnp.int32, (8, BLOCK), 1)
        own_facts = jnp.where(column == 0, squares_local, jnp.where(column == 1, loss_part, 0.0))
        all_facts, shared = finish_sums(own_facts, shared, 5)
        squares_total, loss_sum = all_facts[0, 0], all_facts[0, 1]
    else:
        squares_total, loss_sum = lax.psum((squares_local, loss_part), everyone)
        shared = lax.all_gather(shared, "heads", axis=0)
    grad_norm = jnp.sqrt(squares_total)
    factor = jnp.minimum(1.0, clip_level / grad_norm)

    grad_contract = sums[0].T
    grad_expand = sums[1]
    grad_combine = sums[2][:, head_width:].T
    grad_project = sums[3].reshape(width, 3, head_width)
    grad_readout = shared[:, :, :head_width].transpose(1, 0, 2).reshape(width, model)
    at = head_width + span_part
    grad_relative = shared[:, :, head_width:at].transpose(0, 2, 1).reshape(entries, width)
    grad_vec = shared[:, :, at : at + vector_part].transpose(0, 2, 1).reshape(-1, width)
    grad_vec = grad_vec[:vector_count]
    weights = (embedding, relative, project, combine, expand, contract, readout, vectors)
    gradients = (
        grad_embedding,
        grad_relative,
        grad_project,
        grad_combine,
        grad_expand,
        grad_contract,
        grad_readout,
        grad_vec,
    )
    means = (
        embedding_mean,
        relative_mean,
        project_mean,
        combine_mean,
        expand_mean,
        contract_mean,
        readout_mean,
        vectors_mean,
    )
    squares = (
        embedding_square,
        relative_square,
        project_square,
        combine_square,
        expand_square,
        contract_square,
        readout_square,
        vectors_square,
    )
    updates = [
        adamw(weight, gradient * factor, mean, square, rate_now)
        for weight, gradient, mean, square, rate_now in zip(
            weights, gradients, means, squares, rate_steps
        )
    ]
    return (
        loss_sum,
        token_total,
        grad_norm,
        updates[0][0],
        updates[0][1],
        updates[0][2],
        updates[1][0],
        updates[1][1],
        updates[1][2],
        updates[2][0],
        updates[2][1],
        updates[2][2],
        updates[3][0],
        updates[3][1],
        updates[3][2],
        updates[4][0],
        updates[4][1],
        updates[4][2],
        updates[5][0],
        updates[5][1],
        updates[5][2],
        updates[6][0],
        updates[6][1],
        updates[6][2],
        updates[7][0],
        updates[7][1],
        updates[7][2],
        grad_vec[3] * factor,
    )


def solution(mesh):
    placed = (
        P("dp", None),
        P("dp"),
        P("dp", None),
        P("dp", "heads"),
        P(None, "dp"),
        P("dp", None, "heads"),
        P("heads", "dp"),
        P("dp", "heads"),
        P("heads", "dp"),
        P("dp", None),
        P(None, "dp"),
        P("dp", "heads"),
        P(None, "dp"),
        P("dp", None, "heads"),
        P("heads", "dp"),
        P("dp", "heads"),
        P("heads", "dp"),
        P("dp", None),
        P(None, "dp"),
        P("dp", "heads"),
        P(None, "dp"),
        P("dp", None, "heads"),
        P("heads", "dp"),
        P("dp", "heads"),
        P("heads", "dp"),
        P("dp", None),
        P(None, "dp"),
    )
    return jax.shard_map(
        per_device,
        mesh=mesh,
        in_specs=placed,
        out_specs=(
            P(),
            P(),
            P(),
            P("dp", "heads"),
            P("dp", "heads"),
            P("dp", "heads"),
            P(None, "dp"),
            P(None, "dp"),
            P(None, "dp"),
            P("dp", None, "heads"),
            P("dp", None, "heads"),
            P("dp", None, "heads"),
            P("heads", "dp"),
            P("heads", "dp"),
            P("heads", "dp"),
            P("dp", "heads"),
            P("dp", "heads"),
            P("dp", "heads"),
            P("heads", "dp"),
            P("heads", "dp"),
            P("heads", "dp"),
            P("dp", None),
            P("dp", None),
            P("dp", None),
            P(None, "dp"),
            P(None, "dp"),
            P(None, "dp"),
            P("dp"),
        ),
        check_vma=False,
    )
```

```python
import functools

import jax
import jax.numpy as jnp
from jax import lax
from jax.experimental import pallas as pl
from jax.experimental.pallas import tpu as pltpu
from jax.sharding import PartitionSpec as P

HEAD_DIM = 64
STEP = 10
BLOCK = 128
UNROLL = 16

low = jnp.bfloat16
f32 = jnp.float32

layer_eps = 1e-07
clip_level = 0.005
rate_steps = (0.1, 0.05, 0.05, 0.05, 0.05, 0.05, 0.05, 1.0)
beta_first = 0.9
beta_second = 0.999
adam_eps = 1e-08
weight_decay = 0.01


def dot_rows(a,b):
    return lax.dot_general(a,b,(((1,),(1,)),((),())),preferred_element_type=f32)
def dot_plain(a,b):
    return lax.dot_general(a,b,(((1,),(0,)),((),())),preferred_element_type=f32)
def dot_left(a,b):
    return lax.dot_general(a,b,(((0,),(0,)),((),())),preferred_element_type=f32)

def attend_kernel(length_ref, qkv_ref, table_ref, probs_ref, mixed_ref, far_ref):
    seq=qkv_ref.shape[1]; width=qkv_ref.shape[2]//3; heads=width//HEAD_DIM
    blocks=seq//BLOCK
    scale=(3*HEAD_DIM)**-0.5
    length=length_ref[0]
    live=lax.broadcasted_iota(jnp.int32,(BLOCK,seq),1)<length
    for head in range(heads):
        at=head*HEAD_DIM
        q=qkv_ref[0,:,at:at+HEAD_DIM]
        k=qkv_ref[0,:,width+at:width+at+HEAD_DIM]
        v=qkv_ref[0,:,2*width+at:2*width+at+HEAD_DIM]
        for block in range(blocks):
            rows=slice(block*BLOCK,(block+1)*BLOCK)
            start=seq-BLOCK*(block+1)
            far=dot_rows(k[rows],table_ref[0,start:start+seq+BLOCK,at:at+HEAD_DIM])
            far=pltpu.roll(far,seq,1,stride=1,stride_axis=0)[:,:seq]
            far_ref[head,:,rows]=far.T
        for block in range(blocks):
            rows=slice(block*BLOCK,(block+1)*BLOCK)
            start=seq-BLOCK*(block+1)
            near=dot_rows(q[rows],table_ref[0,start:start+seq+BLOCK,width+at:width+at+HEAD_DIM])
            near=pltpu.roll(near,seq,1,stride=1,stride_axis=0)[:,:seq]
            scores=(dot_rows(q[rows],k)+near+far_ref[head,rows,:])*scale
            scores=jnp.where(live,scores,-1e9)
            top=jnp.max(scores,-1,keepdims=True)
            expo=jnp.exp(scores-top)
            probs=(expo*(1.0/jnp.sum(expo,-1,keepdims=True))).astype(low)
            probs_ref[head,rows,:]=probs
            mixed_ref[0,rows,at:at+HEAD_DIM]=dot_plain(probs,v).astype(low)

def attend(length,qkv,table):
    groups,seq,width3=qkv.shape
    width=width3//3; heads=width//HEAD_DIM
    return pl.pallas_call(
        attend_kernel,
        grid=(groups,),
        in_specs=[pl.BlockSpec(memory_space=pltpu.SMEM),
            pl.BlockSpec((1,seq,width3),lambda g:(g,0,0)),
            pl.BlockSpec((1,2*seq,2*width),lambda g:(g,0,0))],
        out_specs=[pl.BlockSpec((heads,seq,seq),lambda g:(g,0,0)),
            pl.BlockSpec((1,seq,width),lambda g:(g,0,0))],
        out_shape=[jax.ShapeDtypeStruct((groups*heads,seq,seq),low),jax.ShapeDtypeStruct((groups,seq,width),low)],
        scratch_shapes=[pltpu.VMEM((heads,seq,seq),f32)],
        compiler_params=pltpu.CompilerParams(vmem_limit_bytes=48<<20),
        name="attend",
    )(length,qkv,table)

def attend_back_kernel(qkv_ref, table_ref, probs_ref, up_ref, grad_ref, rel_ref, low_ref, sum_ref):
    seq=qkv_ref.shape[1]; width=qkv_ref.shape[2]//3; heads=width//HEAD_DIM
    blocks=seq//BLOCK; reach=seq+BLOCK
    scale=(3*HEAD_DIM)**-0.5
    flip=(lax.broadcasted_iota(jnp.int32,(BLOCK,BLOCK),0)+lax.broadcasted_iota(jnp.int32,(BLOCK,BLOCK),1)==BLOCK-1).astype(f32).astype(low)
    edge=jnp.zeros((BLOCK,BLOCK),f32)
    def shear(rows):
        return pltpu.roll(jnp.concatenate([rows,edge],1),1,1,stride=1,stride_axis=0).astype(low)
    for head in range(heads):
        at=head*HEAD_DIM
        q=qkv_ref[0,:,at:at+HEAD_DIM]
        k=qkv_ref[0,:,width+at:width+at+HEAD_DIM]
        v=qkv_ref[0,:,2*width+at:2*width+at+HEAD_DIM]
        up=up_ref[0,:,at:at+HEAD_DIM]
        for block in range(blocks):
            rows=slice(block*BLOCK,(block+1)*BLOCK)
            probs=probs_ref[head,rows,:].astype(f32)
            pull=dot_rows(up[rows],v)
            inner=jnp.sum(probs*pull,-1,keepdims=True)
            low_ref[head,rows,:]=(probs*(pull-inner)*scale).astype(low)
        grad_ref[0,:,2*width+at:2*width+at+HEAD_DIM]=dot_left(up,probs_ref[head]).T.astype(low)
        sum_ref[2*head]=jnp.zeros(sum_ref.shape[1:],f32)
        sum_ref[2*head+1]=jnp.zeros(sum_ref.shape[1:],f32)
        for block in range(blocks):
            rows=slice(block*BLOCK,(block+1)*BLOCK)
            start=seq-BLOCK*(block+1)
            window=slice(start,start+reach)
            turned=dot_plain(flip,low_ref[head,rows,:])
            near=shear(turned)
            grad_q=dot_plain(turned.astype(low),k)+dot_plain(near,table_ref[0,window,width+at:width+at+HEAD_DIM])
            grad_ref[0,rows,at:at+HEAD_DIM]=dot_plain(flip,grad_q.astype(low)).astype(low)
            q_turned=dot_plain(flip,q[rows]).astype(low)
            sum_ref[2*head+1,:,window]+=dot_left(q_turned,near)
            turned=dot_rows(flip,low_ref[head,:,rows])
            far=shear(turned)
            grad_k=dot_plain(turned.astype(low),q)+dot_plain(far,table_ref[0,window,at:at+HEAD_DIM])
            grad_ref[0,rows,width+at:width+at+HEAD_DIM]=dot_plain(flip,grad_k.astype(low)).astype(low)
            k_turned=dot_plain(flip,k[rows]).astype(low)
            sum_ref[2*head,:,window]+=dot_left(k_turned,far)
        rel_ref[0,:,at:at+HEAD_DIM]=sum_ref[2*head].T.astype(low)
        rel_ref[0,:,width+at:width+at+HEAD_DIM]=sum_ref[2*head+1].T.astype(low)

def attend_back(qkv,table,probs,up):
    groups,seq,width3=qkv.shape
    width=width3//3; heads=width//HEAD_DIM
    return pl.pallas_call(
        attend_back_kernel,
        grid=(groups,),
        in_specs=[
            pl.BlockSpec((1,seq,width3),lambda g:(g,0,0)),
            pl.BlockSpec((1,2*seq,2*width),lambda g:(g,0,0)),
            pl.BlockSpec((heads,seq,seq),lambda g:(g,0,0)),
            pl.BlockSpec((1,seq,width),lambda g:(g,0,0))],
        out_specs=[pl.BlockSpec((1,seq,width3),lambda g:(g,0,0)),
            pl.BlockSpec((1,2*seq,2*width),lambda g:(g,0,0))],
        out_shape=[jax.ShapeDtypeStruct((groups,seq,width3),low),jax.ShapeDtypeStruct((groups,2*seq,2*width),low)],
        scratch_shapes=[pltpu.VMEM((heads,seq,seq),low),pltpu.VMEM((2*heads,HEAD_DIM,2*seq),f32)],
        compiler_params=pltpu.CompilerParams(vmem_limit_bytes=48<<20),
        name="attend_back",
    )(qkv,table,probs,up)


MESH = pl.DeviceIdType.MESH
ANYWHERE = pl.BlockSpec(memory_space=pl.ANY)
IN_VMEM = pl.BlockSpec(memory_space=pltpu.VMEM)


def place():
    owner, holder = lax.axis_index("dp"), lax.axis_index("heads")
    return owner // 2, owner % 2, holder // 2, holder % 2


def device(z, x, y, c):
    return (z * 2 + x, y * 2 + c)


def signal(target):
    pl.semaphore_signal(
        pltpu.get_barrier_semaphore(), inc=1, device_id=target, device_id_type=MESH
    )


def greet(z, x, y, c, line):
    signal(device(z, x, y, 1 - c))
    signal(device(z, x, 1 - y, c))
    if line:
        signal(device(z, 1 - x, y, c))

        @pl.when(z < 3)
        def above():
            signal(device(z + 1, x, y, c))

        @pl.when(z > 0)
        def below():
            signal(device(z - 1, x, y, c))

        pl.semaphore_wait(pltpu.get_barrier_semaphore(), jnp.where((z == 0) | (z == 3), 4, 5))


def remote(source, target, send, recv, to):
    return pltpu.make_async_remote_copy(
        src_ref=source, dst_ref=target, send_sem=send, recv_sem=recv, device_id=to, device_id_type=MESH
    )


def scatter_sums_kernel(count, *refs):
    grads, totals = refs[:count], refs[count : 2 * count]
    refs = refs[2 * count :]
    own, pair, first_a, first_b, second_a, second_b, rise, fall = [
        refs[count * part : count * (part + 1)] for part in range(8)
    ]
    local_sem, send_sem, recv_sem = refs[8 * count :]
    z, x, y, c = place()
    greet(z, x, y, c, True)
    half = grads[0].shape[3] // 2
    upper, lower = pl.ds(0, half), pl.ds(half, half)
    core_to, y_to, x_to = device(z, x, y, 1 - c), device(z, x, 1 - y, c), device(z, 1 - x, y, c)
    up_to, down_to = device(z + 1, x, y, c), device(z - 1, x, y, c)

    def link(part, slot, source, target, to):
        return remote(source, target, send_sem.at[part, slot], recv_sem.at[part, slot], to)

    def local(part, side):
        return pltpu.make_async_copy(
            grads[part].at[side * 2 + c], own[part].at[side], local_sem.at[part, side]
        )

    def pair_copy(part, side):
        return link(part, side, grads[part].at[side * 2 + 1 - c], pair[part].at[side], core_to)

    def first_copies(part):
        block = own[part]
        return (
            link(part, 2, block.at[1 - y, :, :, upper], first_a[part], y_to),
            link(part, 3, block.at[:, :, 1 - x, lower], first_b[part], x_to),
        )

    def second_copies(part):
        block = own[part]
        return (
            link(part, 4, block.at[y, :, 1 - x, upper], second_a[part], x_to),
            link(part, 5, block.at[1 - y, :, x, lower], second_b[part], y_to),
        )

    def rise_copy(part, turn):
        block = own[part].at[y, lax.clamp(0, 3 + z - turn, 3), x]
        return link(part, 6 + turn, block, rise[part].at[turn], up_to)

    def fall_copy(part, turn):
        block = own[part].at[y, lax.clamp(0, turn - 3 + z, 3), x]
        return link(part, 9 + turn, block, fall[part].at[turn], down_to)

    def add(target, source):
        target[...] = (target[...].astype(f32) + source[...].astype(f32)).astype(low)

    def start(part):
        for side in range(2):
            pair_copy(part, side).start()
            local(part, side).start()

    def stage_pair(part):
        for side in range(2):
            local(part, side).wait()
            pair_copy(part, side).wait()

        def step(index, carry):
            side, rest = index // 8, index % 8
            add(own[part].at[side, rest // 2, rest % 2], pair[part].at[side, rest // 2, rest % 2])
            return carry

        lax.fori_loop(0, 16, step, 0)
        for copy in first_copies(part):
            copy.start()

    def stage_first(part):
        for copy in first_copies(part):
            copy.wait()

        def step(index, carry):
            add(own[part].at[y, index // 2, index % 2, upper], first_a[part].at[index // 2, index % 2])
            add(own[part].at[index % 2, index // 2, x, lower], first_b[part].at[index % 2, index // 2])
            return carry

        lax.fori_loop(0, 8, step, 0)
        for copy in second_copies(part):
            copy.start()

    def stage_second(part):
        for copy in second_copies(part):
            copy.wait()

        def step(index, carry):
            add(own[part].at[y, index, x, upper], second_a[part].at[index])
            add(own[part].at[y, index, x, lower], second_b[part].at[index])
            return carry

        lax.fori_loop(0, 4, step, 0)

    def stage_line(part, turn):
        @pl.when((z <= turn) & (z < 3))
        def rises():
            if turn > 0:

                @pl.when(z > 0)
                def joined():
                    rise_copy(part, turn - 1).wait_recv()
                    add(own[part].at[y, 3 + z - turn, x], rise[part].at[turn - 1])

            rise_copy(part, turn).start()

        @pl.when((3 - z <= turn) & (z > 0))
        def falls():
            if turn > 0:

                @pl.when(z < 3)
                def joined():
                    fall_copy(part, turn - 1).wait_recv()
                    add(own[part].at[y, turn - 3 + z, x], fall[part].at[turn - 1])

            fall_copy(part, turn).start()

    def stage_total(part):
        totals[part][...] = own[part][y, z, x].astype(f32)

        @pl.when(z > 0)
        def risen():
            rise_copy(part, 2).wait_recv()
            totals[part][...] += rise[part][2].astype(f32)

        @pl.when(z < 3)
        def fallen():
            fall_copy(part, 2).wait_recv()
            totals[part][...] += fall[part][2].astype(f32)

        for turn in range(3):

            @pl.when((z <= turn) & (z < 3))
            def risen_out():
                rise_copy(part, turn).wait_send()

            @pl.when((3 - z <= turn) & (z > 0))
            def fallen_out():
                fall_copy(part, turn).wait_send()

    stages = [
        stage_pair,
        stage_first,
        stage_second,
        functools.partial(stage_line, turn=0),
        functools.partial(stage_line, turn=1),
        functools.partial(stage_line, turn=2),
        stage_total,
    ]
    for part in range(count):
        start(part)
    for tick in range(count + len(stages) - 1):
        for index, stage in enumerate(stages):
            if 0 <= tick - index < count:
                stage(tick - index)


def scatter_sums(grads, tag):
    count = len(grads)
    width = grads[0].shape[2]
    sizes = [grad.shape[3] for grad in grads]
    half = width // 2
    scratch = []
    for lead in (
        (2, 4, 2, width),
        (2, 4, 2, width),
        (4, 2, half),
        (2, 4, half),
        (4, half),
        (4, half),
        (3, width),
        (3, width),
    ):
        scratch += [pltpu.VMEM(lead + (size,), low) for size in sizes]
    return pl.pallas_call(
        functools.partial(scatter_sums_kernel, count),
        in_specs=[ANYWHERE] * count,
        out_specs=[IN_VMEM] * count,
        out_shape=[jax.ShapeDtypeStruct((width, size), f32) for size in sizes],
        scratch_shapes=scratch
        + [
            pltpu.SemaphoreType.DMA((count, 2)),
            pltpu.SemaphoreType.DMA((count, 12)),
            pltpu.SemaphoreType.DMA((count, 12)),
        ],
        compiler_params=pltpu.CompilerParams(
            collective_id=tag, has_side_effects=True, vmem_limit_bytes=56 << 20
        ),
        name="scatter_sums",
    )(*[grad.reshape(4, 4, 2, width, size) for grad, size in zip(grads, sizes)])


def peers(z, x):
    return [((z + 2 - far) % 4, x if same else 1 - x) for far, same in PEER_ORDER]


PEER_ORDER = ((0, False), (0, True), (1, False), (1, True), (3, False), (3, True), (2, False))


def meet_owners(z, x, y, c):
    for peer_z, peer_x in peers(z, x):
        signal(device(peer_z, peer_x, y, c))


def share_facts_kernel(facts_ref, all_ref, local_sem, send_sem, recv_sem):
    z, x, y, c = place()
    meet_owners(z, x, y, c)
    pl.semaphore_wait(pltpu.get_barrier_semaphore(), 7)
    here = z * 2 + x
    keep = pltpu.make_async_copy(facts_ref, all_ref.at[here], local_sem)
    keep.start()
    copies = []
    for index, (peer_z, peer_x) in enumerate(peers(z, x)):
        copy = remote(
            facts_ref,
            all_ref.at[here],
            send_sem.at[index],
            recv_sem.at[here],
            device(peer_z, peer_x, y, c),
        )
        copy.start()
        copies.append(copy)
    for index, (peer_z, peer_x) in enumerate(peers(z, x)):
        there = peer_z * 2 + peer_x
        copies[index].wait_send()
        remote(
            facts_ref, all_ref.at[there], send_sem.at[index], recv_sem.at[there], device(z, x, y, c)
        ).wait_recv()
    keep.wait()


def share_facts(facts, tag):
    return pl.pallas_call(
        share_facts_kernel,
        in_specs=[IN_VMEM],
        out_specs=IN_VMEM,
        out_shape=jax.ShapeDtypeStruct((8,) + facts.shape, facts.dtype),
        scratch_shapes=[
            pltpu.SemaphoreType.DMA,
            pltpu.SemaphoreType.DMA((7,)),
            pltpu.SemaphoreType.DMA((8,)),
        ],
        compiler_params=pltpu.CompilerParams(collective_id=tag, has_side_effects=True),
        name="share_facts",
    )(facts)


def exchange_words_kernel(found_ref, words_ref, pair, side, send_sem, recv_sem, out_sem, in_sem):
    z, x, y, c = place()
    meet_owners(z, x, y, c)
    greet(z, x, y, c, False)
    pl.semaphore_wait(pltpu.get_barrier_semaphore(), 9)
    here = z * 2 + x
    targets = [(z, x)] + peers(z, x)
    targets = targets[1:] + targets[:1]
    core_to, y_to = device(z, x, y, 1 - c), device(z, x, 1 - y, c)

    def pair_copy(part, row):
        to = targets[part][0] * 2 + targets[part][1]
        return remote(
            found_ref.at[to, row * 2 + 1 - c],
            pair.at[row, to],
            send_sem.at[part, row],
            recv_sem.at[part, row],
            core_to,
        )

    def side_copy(part):
        to = targets[part][0] * 2 + targets[part][1]
        return remote(
            pair.at[1 - y, to], side.at[to], send_sem.at[part, 2], recv_sem.at[part, 2], y_to
        )

    def out_copy(part):
        to = targets[part][0] * 2 + targets[part][1]
        return remote(
            pair.at[y, to],
            words_ref.at[here],
            out_sem.at[part],
            in_sem.at[here],
            device(targets[part][0], targets[part][1], y, c),
        )

    def at_home(part):
        return targets[part][0] * 2 + targets[part][1]

    for part in range(8):
        for row in range(2):
            pair_copy(part, row).start()
    for part in range(8):
        to = at_home(part)
        for row in range(2):
            pair_copy(part, row).wait_recv()
            pair[row, to] = pair[row, to] + found_ref[to, row * 2 + c]
        side_copy(part).start()
    for part in range(8):
        to = at_home(part)
        side_copy(part).wait_recv()
        pair[y, to] = pair[y, to] + side[to]
        if part < 7:
            out_copy(part).start()
        else:
            words_ref[here] = pair[y, to]
    for part in range(8):
        for row in range(2):
            pair_copy(part, row).wait_send()
        side_copy(part).wait_send()
        if part < 7:
            out_copy(part).wait_send()
            there = at_home(part)
            remote(
                pair.at[y, there], words_ref.at[there], out_sem.at[part], in_sem.at[there], core_to
            ).wait_recv()


def exchange_words(found, tag):
    piece = found.shape[2:]
    return pl.pallas_call(
        exchange_words_kernel,
        in_specs=[IN_VMEM],
        out_specs=IN_VMEM,
        out_shape=jax.ShapeDtypeStruct((8,) + piece, low),
        scratch_shapes=[
            pltpu.VMEM((2, 8) + piece, low),
            pltpu.VMEM((8,) + piece, low),
            pltpu.SemaphoreType.DMA((8, 3)),
            pltpu.SemaphoreType.DMA((8, 3)),
            pltpu.SemaphoreType.DMA((8,)),
            pltpu.SemaphoreType.DMA((8,)),
        ],
        compiler_params=pltpu.CompilerParams(
            collective_id=tag, has_side_effects=True, vmem_limit_bytes=40 << 20
        ),
        name="exchange_words",
    )(found)


def return_words_kernel(grads_ref, sent_ref, local_sem, out_sem, in_sem, send_sem, recv_sem):
    z, x, y, c = place()
    meet_owners(z, x, y, c)
    greet(z, x, y, c, False)
    pl.semaphore_wait(pltpu.get_barrier_semaphore(), 9)
    here = z * 2 + x
    own = y * 2 + c
    other = (1 - y) * 2 + c
    core_to, y_to = device(z, x, y, 1 - c), device(z, x, 1 - y, c)
    near_first = peers(z, x)[::-1]
    keep = pltpu.make_async_copy(grads_ref.at[here], sent_ref.at[here, own], local_sem)
    keep.start()

    def out_copy(part, peer):
        return remote(
            grads_ref.at[peer[0] * 2 + peer[1]],
            sent_ref.at[here, own],
            out_sem.at[part],
            in_sem.at[here],
            device(peer[0], peer[1], y, c),
        )

    def in_copy(part, peer):
        there = peer[0] * 2 + peer[1]
        return remote(
            grads_ref.at[there], sent_ref.at[there, own], out_sem.at[part], in_sem.at[there], core_to
        )

    def pass_on(slot, row, there, to):
        block = sent_ref.at[there, row]
        return remote(block, block, send_sem.at[slot, there], recv_sem.at[row, there], to)

    for part, peer in enumerate(peers(z, x)):
        out_copy(part, peer).start()
    keep.wait()
    order = [(z, x)] + near_first
    for part, (peer_z, peer_x) in enumerate(order):
        there = peer_z * 2 + peer_x
        if part > 0:
            in_copy(part - 1, (peer_z, peer_x)).wait_recv()
        pass_on(0, own, there, y_to).start()
        pass_on(1, own, there, core_to).start()
    for peer_z, peer_x in order:
        there = peer_z * 2 + peer_x
        pass_on(0, other, there, y_to).wait_recv()
        pass_on(2, other, there, core_to).start()
    for part, peer in enumerate(peers(z, x)):
        out_copy(part, peer).wait_send()
    for peer_z, peer_x in order:
        there = peer_z * 2 + peer_x
        pass_on(0, own, there, y_to).wait_send()
        pass_on(1, own, there, core_to).wait_send()
        pass_on(2, other, there, core_to).wait_send()
        pass_on(1, y * 2 + 1 - c, there, core_to).wait_recv()
        pass_on(2, (1 - y) * 2 + 1 - c, there, core_to).wait_recv()


def return_words(grads, tag):
    piece = grads.shape[1:]
    return pl.pallas_call(
        return_words_kernel,
        in_specs=[IN_VMEM],
        out_specs=IN_VMEM,
        out_shape=jax.ShapeDtypeStruct((8, 4) + piece, low),
        scratch_shapes=[
            pltpu.SemaphoreType.DMA,
            pltpu.SemaphoreType.DMA((7,)),
            pltpu.SemaphoreType.DMA((8,)),
            pltpu.SemaphoreType.DMA((3, 8)),
            pltpu.SemaphoreType.DMA((4, 8)),
        ],
        compiler_params=pltpu.CompilerParams(
            collective_id=tag, has_side_effects=True, vmem_limit_bytes=40 << 20
        ),
        name="return_words",
    )(grads)


def finish_sums_kernel(facts_ref, shared_ref, total_ref, all_ref, pair, side, cross, line, local_sem, send_sem, recv_sem, line_send, line_recv):
    z, x, y, c = place()
    core_to, y_to, x_to = device(z, x, y, 1 - c), device(z, x, 1 - y, c), device(z, 1 - x, y, c)
    column = [(z + step) % 4 for step in range(1, 4)]
    for target in (core_to, y_to, x_to, *[device(other, x, y, c) for other in column]):
        signal(target)
    pl.semaphore_wait(pltpu.get_barrier_semaphore(), 6)
    own, other = y * 2 + c, (1 - y) * 2 + c
    keep = pltpu.make_async_copy(shared_ref, all_ref.at[own], local_sem)
    keep.start()
    swap_pair = remote(facts_ref, pair, send_sem.at[0], recv_sem.at[0], core_to)
    swap_pair.start()
    shared_side = remote(shared_ref, all_ref.at[own], send_sem.at[3], recv_sem.at[3], y_to)
    shared_pair = remote(shared_ref, all_ref.at[own], send_sem.at[4], recv_sem.at[4], core_to)
    shared_side.start()
    shared_pair.start()
    swap_pair.wait()
    total_ref[...] = facts_ref[...] + pair[...]
    swap_side = remote(total_ref, side, send_sem.at[1], recv_sem.at[1], y_to)
    swap_side.start()
    swap_side.wait()
    total_ref[...] += side[...]
    swap_cross = remote(total_ref, cross, send_sem.at[2], recv_sem.at[2], x_to)
    swap_cross.start()
    swap_cross.wait()
    total_ref[...] += cross[...]
    line[z] = total_ref[...]
    lines = [
        remote(line.at[z], line.at[z], line_send.at[step], line_recv.at[z], device(to, x, y, c))
        for step, to in enumerate(column)
    ]
    for copy in lines:
        copy.start()
    shared_side.wait()
    relay = remote(all_ref.at[other], all_ref.at[other], send_sem.at[5], recv_sem.at[5], core_to)
    relay.start()
    for step, to in enumerate(column):
        lines[step].wait_send()
        remote(line.at[to], line.at[to], line_send.at[step], line_recv.at[to], core_to).wait_recv()
    total_ref[...] = (line[0] + line[1]) + (line[2] + line[3])
    shared_pair.wait()
    relay.wait()
    keep.wait()


def finish_sums(facts, shared, tag):
    return pl.pallas_call(
        finish_sums_kernel,
        in_specs=[IN_VMEM] * 2,
        out_specs=[IN_VMEM] * 2,
        out_shape=[
            jax.ShapeDtypeStruct(facts.shape, f32),
            jax.ShapeDtypeStruct((4,) + shared.shape, f32),
        ],
        scratch_shapes=[pltpu.VMEM(facts.shape, f32)] * 3
        + [
            pltpu.VMEM((4,) + facts.shape, f32),
            pltpu.SemaphoreType.DMA,
            pltpu.SemaphoreType.DMA((6,)),
            pltpu.SemaphoreType.DMA((6,)),
            pltpu.SemaphoreType.DMA((3,)),
            pltpu.SemaphoreType.DMA((4,)),
        ],
        compiler_params=pltpu.CompilerParams(collective_id=tag, has_side_effects=True),
        name="finish_sums",
    )(facts, shared)


def identity(size):
    rows = lax.broadcasted_iota(jnp.int32, (size, size), 0)
    columns = lax.broadcasted_iota(jnp.int32, (size, size), 1)
    return (rows == columns).astype(f32).astype(low)


def turn(values):
    return dot_rows(identity(values.shape[1]), values)


def row_sets(rows):
    return 8 if rows % 8 == 0 else 1


def lookup_kernel(lengths_ref, places_ref, weights_ref, words_ref, table_ref, rows_ref):
    width, slab = weights_ref.shape
    count = places_ref.shape[1]
    seq = rows_ref.shape[0]

    @pl.when(pl.program_id(0) == 0)
    def fill():
        def step(index, carry):
            first = pl.multiple_of(index * 3 * BLOCK, BLOCK)
            for part in range(3):
                at = first + part * BLOCK
                table_ref[pl.ds(at, BLOCK), :] = turn(weights_ref[:, pl.ds(at, BLOCK)].astype(low))
            return carry

        lax.fori_loop(0, slab // (3 * BLOCK), step, 0)
        table_ref[pl.ds(slab, 8), :] = jnp.zeros((8, width), f32)

    def one_row(row, carry):
        rows_ref[...] = jnp.zeros_like(rows_ref)

        def step(index, carry):
            first = pl.multiple_of(index * UNROLL, UNROLL)
            for offset in range(UNROLL):
                spot = places_ref[0, row, first + offset]
                rows_ref[pl.ds(first + offset, 1), :] = table_ref[pl.ds(spot, 1), :]
            return carry

        length = lengths_ref[pl.program_id(0) * count + row]
        lax.fori_loop(0, pl.cdiv(length, UNROLL), step, 0)
        words_ref[row] = dot_rows(identity(width), rows_ref[...].astype(low)).astype(low)
        return carry

    lax.fori_loop(0, count, one_row, 0)


def lookup(lengths, places, weights):
    rows, seq = places.shape
    width, slab = weights.shape
    count = row_sets(rows)
    return pl.pallas_call(
        lookup_kernel,
        grid=(rows // count,),
        in_specs=[
            pl.BlockSpec(memory_space=pltpu.SMEM),
            pl.BlockSpec((1, count, seq), lambda step: (step, 0, 0), memory_space=pltpu.SMEM),
            pl.BlockSpec(weights.shape, lambda step: (0, 0)),
        ],
        out_specs=pl.BlockSpec((count, width, seq), lambda step: (step, 0, 0)),
        out_shape=jax.ShapeDtypeStruct((rows, width, seq), low),
        scratch_shapes=[pltpu.VMEM((slab + 8, width), f32), pltpu.VMEM((seq, width), f32)],
        compiler_params=pltpu.CompilerParams(vmem_limit_bytes=48 << 20),
        name="lookup",
    )(lengths, places.reshape(rows // count, count, seq), weights)


def deposit_kernel(lengths_ref, places_ref, grads_ref, total_ref, squares_ref, rows_ref, *tables):
    width, slab = total_ref.shape
    count = places_ref.shape[1]

    @pl.when(pl.program_id(0) == 0)
    def clear():
        for table in tables:
            table[...] = jnp.zeros_like(table)

    def one_row(row, carry):
        for first in range(0, rows_ref.shape[0], BLOCK):
            rows_ref[first : first + BLOCK, :] = turn(grads_ref[row, :, first : first + BLOCK])

        def step(index, carry):
            first = pl.multiple_of(index * UNROLL, UNROLL)
            for offset in range(0, UNROLL, len(tables)):
                places = [places_ref[0, row, first + offset + part] for part in range(len(tables))]
                sums = [
                    table[pl.ds(place, 1), :] + rows_ref[pl.ds(first + offset + part, 1), :]
                    for part, (place, table) in enumerate(zip(places, tables))
                ]
                for place, table, value in zip(places, tables, sums):
                    table[pl.ds(place, 1), :] = value
            return carry

        length = lengths_ref[pl.program_id(0) * count + row]
        lax.fori_loop(0, pl.cdiv(length, UNROLL), step, 0)
        return carry

    lax.fori_loop(0, count, one_row, 0)

    @pl.when(pl.program_id(0) == pl.num_programs(0) - 1)
    def finish():
        squares_ref[...] = jnp.zeros_like(squares_ref)

        def step(index, carry):
            first = pl.multiple_of(index * 3 * BLOCK, BLOCK)
            squares = jnp.zeros((width, BLOCK), f32)
            for part in range(3):
                at = pl.ds(first + part * BLOCK, BLOCK)
                block = sum(table[at, :] for table in tables).T
                total_ref[:, at] = block
                squares += block * block
            squares_ref[...] += squares
            return carry

        lax.fori_loop(0, slab // (3 * BLOCK), step, 0)


def deposit(lengths, places, grads, slab):
    rows, seq = places.shape
    width = grads.shape[1]
    count = row_sets(rows)
    return pl.pallas_call(
        deposit_kernel,
        grid=(rows // count,),
        in_specs=[
            pl.BlockSpec(memory_space=pltpu.SMEM),
            pl.BlockSpec((1, count, seq), lambda step: (step, 0, 0), memory_space=pltpu.SMEM),
            pl.BlockSpec((count, width, seq), lambda step: (step, 0, 0)),
        ],
        out_specs=[
            pl.BlockSpec((width, slab), lambda step: (0, 0)),
            pl.BlockSpec((width, BLOCK), lambda step: (0, 0)),
        ],
        out_shape=[
            jax.ShapeDtypeStruct((width, slab), f32),
            jax.ShapeDtypeStruct((width, BLOCK), f32),
        ],
        scratch_shapes=[pltpu.VMEM((seq, width), f32)] + [pltpu.VMEM((slab + 8, width), f32)] * 4,
        compiler_params=pltpu.CompilerParams(vmem_limit_bytes=60 << 20),
        name="deposit",
    )(lengths, places.reshape(rows // count, count, seq), grads)


def whiten(values):
    center = values - jnp.mean(values, -1, keepdims=True)
    rate = lax.rsqrt(jnp.mean(center * center, -1, keepdims=True) + layer_eps)
    return center * rate, rate


def unwhiten(upstream, gain, white, rate):
    scaled = upstream * gain
    inner = jnp.mean(scaled, -1, keepdims=True)
    along = jnp.mean(scaled * white, -1, keepdims=True)
    return (
        rate * (scaled - inner - white * along),
        jnp.sum(upstream * white, 0, keepdims=True),
        jnp.sum(upstream, 0, keepdims=True),
    )


def selection(length, entries):
    rows = lax.broadcasted_iota(jnp.int32, (2 * length, entries), 0)
    columns = lax.broadcasted_iota(jnp.int32, (2 * length, entries), 1)
    return (jnp.clip(length + entries // 2 - rows, 0, entries - 1) == columns).astype(f32).astype(low)


def prepare_kernel(
    weights_ref, words_ref, vec_ref, white_ref, rate_ref, qkv_ref, rel_white_ref, rel_rate_ref, table_ref, low_ref, rel_ref
):
    groups, model = weights_ref.shape[:2]
    seq = words_ref.shape[1]
    part = rel_ref.shape[0] // groups
    width = qkv_ref.shape[2] // 3
    terms = turn(weights_ref[0, :, 4 * BLOCK : 5 * BLOCK])
    half = BLOCK // 2
    vec_ref[...] = terms[half : half + 16] + terms[half + 16 : half + 32] + terms[half + 32 : half + 48]
    for group in range(groups):
        rows = slice(group * part, (group + 1) * part)
        entries = turn(weights_ref[group, :, 5 * BLOCK : 6 * BLOCK]) + turn(
            weights_ref[group, :, 8 * BLOCK : 9 * BLOCK]
        )
        white, rate = whiten(entries)
        rel_white_ref[rows, :] = white
        rel_rate_ref[rows, :] = rate
        rel_ref[rows, :] = (white * vec_ref[2:3] + vec_ref[3:4]).astype(low)
    for first in range(0, seq, BLOCK):
        rows = slice(first, first + BLOCK)
        white, rate = whiten(turn(words_ref[:, rows]))
        white_ref[rows, :] = white
        rate_ref[rows, :] = rate
        low_ref[rows, :] = (white * vec_ref[0:1] + vec_ref[1:2]).astype(low)
    chosen = selection(seq, rel_ref.shape[0])

    def step(group, carry):
        qkv_ref[group] = dot_plain(low_ref[...], weights_ref[group, :, : 3 * width]).astype(low)
        keys = dot_plain(rel_ref[...], weights_ref[group, :, : 2 * width]).astype(low)
        table_ref[group] = dot_plain(chosen, keys).astype(low)
        return carry

    lax.fori_loop(0, groups, step, 0)


def prepare(weights, words, width, entries):
    groups, model = weights.shape[:2]
    seq = words.shape[1]
    return pl.pallas_call(
        prepare_kernel,
        in_specs=[IN_VMEM] * 2,
        out_specs=[IN_VMEM] * 7,
        out_shape=[
            jax.ShapeDtypeStruct((16, model), f32),
            jax.ShapeDtypeStruct((seq, model), f32),
            jax.ShapeDtypeStruct((seq, 1), f32),
            jax.ShapeDtypeStruct((groups, seq, 3 * width), low),
            jax.ShapeDtypeStruct((entries, model), f32),
            jax.ShapeDtypeStruct((entries, 1), f32),
            jax.ShapeDtypeStruct((groups, 2 * seq, 2 * width), low),
        ],
        scratch_shapes=[pltpu.VMEM((seq, model), low), pltpu.VMEM((entries, model), low)],
        compiler_params=pltpu.CompilerParams(vmem_limit_bytes=56 << 20),
        name="prepare",
    )(weights, words)


def middle_kernel(
    combine_ref,
    weights_ref,
    vec_ref,
    white_ref,
    mixed_ref,
    marks_ref,
    contract_out,
    expand_out,
    joint_out,
    mixed_out,
    sum_out,
    vec_out,
    loss_out,
    readout_ref,
    slope_ref,
    acts_ref,
    mid_ref,
    mid_white_ref,
    out_white_ref,
    gate_ref,
):
    groups, model = weights_ref.shape[:2]
    seq = white_ref.shape[0]
    width = mixed_ref.shape[2]
    hidden = acts_ref.shape[2]
    vec = [vec_ref[row : row + 1] for row in range(11)]
    for group in range(groups):
        readout_ref[:, group * width : (group + 1) * width] = weights_ref[group, :, 2 * hidden :]
    total = white_ref[...] * vec[0] + vec[1]
    for group in range(groups):
        total += dot_rows(mixed_ref[group], combine_ref[group, :, :width])
    mid_white, mid_rate = whiten(total)
    mid_white_ref[...] = mid_white
    hidden_mid = mid_white * vec[4] + vec[5]
    sum_out[...] = hidden_mid
    mid_ref[...] = hidden_mid.astype(low)

    def forward(group, carry):
        gate = dot_plain(mid_ref[...], weights_ref[group, :, :hidden])
        share = 0.5 + 0.5 * lax.erf(gate * 0.5**0.5)
        acts_ref[group] = (gate * share).astype(low)
        slope_ref[group] = share + gate * jnp.exp(-0.5 * gate * gate) * (2.0 * jnp.pi) ** -0.5
        sum_out[...] += dot_rows(acts_ref[group], weights_ref[group, :, hidden : 2 * hidden])
        return carry

    lax.fori_loop(0, groups, forward, 0)
    out_white, out_rate = whiten(sum_out[...])
    out_white_ref[...] = out_white
    gate_ref[...] = (out_white * vec[6] + vec[7]).astype(low)
    dense = dot_plain(gate_ref[...], readout_ref[...])
    share = 0.5 + 0.5 * lax.erf(dense * 0.5**0.5)
    slope = share + dense * jnp.exp(-0.5 * dense * dense) * (2.0 * jnp.pi) ** -0.5
    white, rate = whiten(dense * share)
    head = white * vec[8] + vec[9]
    logits = jnp.sum(head * vec[10], -1, keepdims=True)
    weight, flags = marks_ref[:, 0:1], marks_ref[:, 1:2]
    losses = jnp.maximum(logits, 0.0) + jnp.log1p(jnp.exp(-jnp.abs(logits))) - flags * logits
    loss_out[...] = jnp.where(weight > 0.0, losses, 0.0)
    pull = (1.0 / (1.0 + jnp.exp(-logits)) - flags) * weight
    vec_out[6:7, :] = jnp.sum(head * pull, 0, keepdims=True)
    upstream, vec_out[4:5, :], vec_out[5:6, :] = unwhiten(pull * vec[10], vec[8], white, rate)
    dense_low = (upstream * slope).astype(low)
    turned = gate_ref[...].astype(f32).T.astype(low)
    for group in range(groups):
        joint_out[group, :, :width] = dot_plain(
            turned, dense_low[:, group * width : (group + 1) * width]
        ).astype(low)
    upstream, vec_out[2:3, :], vec_out[3:4, :] = unwhiten(
        dot_rows(dense_low, readout_ref[...]), vec[6], out_white_ref[...], out_rate
    )
    sum_out[...] = upstream
    gate_ref[...] = upstream.astype(low)
    upstream_turned = upstream.T.astype(low)
    mid_turned = mid_ref[...].astype(f32).T.astype(low)

    def backward(group, carry):
        contract_out[group] = dot_plain(upstream_turned, acts_ref[group]).astype(low)
        acts_ref[group] = (
            dot_plain(gate_ref[...], weights_ref[group, :, hidden : 2 * hidden]) * slope_ref[group]
        ).astype(low)
        expand_out[group] = dot_plain(mid_turned, acts_ref[group]).astype(low)
        sum_out[...] += dot_rows(acts_ref[group], weights_ref[group, :, :hidden])
        return carry

    lax.fori_loop(0, groups, backward, 0)
    upstream, vec_out[0:1, :], vec_out[1:2, :] = unwhiten(
        sum_out[...], vec[4], mid_white_ref[...], mid_rate
    )
    vec_out[7:8, :] = jnp.zeros((1, model), f32)
    sum_out[...] = upstream
    gate_ref[...] = upstream.astype(low)
    turned = upstream.T.astype(low)
    for group in range(groups):
        mixed_out[group] = dot_plain(gate_ref[...], combine_ref[group, :, :width]).astype(low)
        joint_out[group, :, width:] = dot_plain(turned, mixed_ref[group]).astype(low)


def middle(first_weights, weights, vec, white, mixed, marks):
    groups, model = weights.shape[:2]
    seq, width = mixed.shape[1:]
    hidden = (weights.shape[2] - width) // 2
    wide = pltpu.VMEM((seq, model), f32)
    outputs = [
        ((groups, model, hidden), low),
        ((groups, model, hidden), low),
        ((groups, model, 2 * width), low),
        ((groups, seq, width), low),
        ((seq, model), f32),
        ((8, model), f32),
        ((seq, 1), f32),
    ]
    return pl.pallas_call(
        middle_kernel,
        grid=(1,),
        in_specs=[
            pl.BlockSpec(
                (groups, model, 2 * BLOCK), lambda step: (0, 0, 3), pipeline_mode=pl.Buffered(1)
            )
        ]
        + [
            pl.BlockSpec(
                array.shape,
                functools.partial(lambda rank, step: (0,) * rank, array.ndim),
                pipeline_mode=pl.Buffered(1),
            )
            for array in (weights, vec, white, mixed, marks)
        ],
        out_specs=[
            pl.BlockSpec(
                shape,
                functools.partial(lambda rank, step: (0,) * rank, len(shape)),
                pipeline_mode=pl.Buffered(1),
            )
            for shape, _ in outputs
        ],
        out_shape=[jax.ShapeDtypeStruct(*output) for output in outputs],
        scratch_shapes=[
            pltpu.VMEM((model, model), low),
            pltpu.VMEM((groups, seq, hidden), f32),
            pltpu.VMEM((groups, seq, hidden), low),
            pltpu.VMEM((seq, model), low),
            wide,
            wide,
            pltpu.VMEM((seq, model), low),
        ],
        compiler_params=pltpu.CompilerParams(vmem_limit_bytes=60 << 20),
        name="middle",
    )(first_weights, weights, vec, white, mixed, marks)


def project_back_kernel(
    weights_ref,
    vec_ref,
    white_ref,
    rate_ref,
    rel_white_ref,
    rel_rate_ref,
    sum_ref,
    grads_ref,
    tables_ref,
    vec_grads_ref,
    words_out,
    project_out,
    total_ref,
    fold_ref,
):
    groups, model = weights_ref.shape[:2]
    seq = white_ref.shape[0]
    width = grads_ref.shape[2] // 3
    entries = rel_white_ref.shape[0]
    part = entries // groups
    vec = [vec_ref[row : row + 1] for row in range(4)]
    turned = (white_ref[...] * vec[0] + vec[1]).T.astype(low)
    rel_turned = (rel_white_ref[...] * vec[2] + vec[3]).T.astype(low)
    chosen = selection(seq, entries)
    total_ref[...] = sum_ref[...]
    rel_total = jnp.zeros((entries, model), f32)
    for group in range(groups):
        fold_ref[...] = dot_left(chosen, tables_ref[group]).astype(low)
        total_ref[...] += dot_rows(grads_ref[group], weights_ref[group, :, : 3 * width])
        rel_total += dot_rows(fold_ref[...], weights_ref[group, :, : 2 * width])
        project_out[group, :, : 2 * width] = (
            dot_plain(turned, grads_ref[group, :, : 2 * width]) + dot_plain(rel_turned, fold_ref[...])
        ).astype(low)
        project_out[group, :, 2 * width : 3 * width] = dot_plain(
            turned, grads_ref[group, :, 2 * width :]
        ).astype(low)
    upstream, gain_grad, bias_grad = unwhiten(total_ref[...], vec[0], white_ref[...], rate_ref[...])
    words_out[...] = upstream.T.astype(low)
    rel_up, rel_gain_grad, rel_bias_grad = unwhiten(
        rel_total, vec[2], rel_white_ref[...], rel_rate_ref[...]
    )
    turned = rel_up.T.astype(low)
    for group in range(groups):
        project_out[group, :, 3 * width + BLOCK // 2 :] = turned[:, group * part : (group + 1) * part]
    rows = [gain_grad, bias_grad, rel_gain_grad, rel_bias_grad]
    rows += [vec_grads_ref[row : row + 1] for row in range(7)]
    rows += [jnp.zeros((1, model), f32)]
    for group in range(groups):
        three = jnp.concatenate(rows[3 * group : 3 * group + 3] + [jnp.zeros((BLOCK - 3, model), f32)], 0)
        project_out[group, :, 3 * width : 3 * width + BLOCK // 2] = three.T.astype(low)[:, : BLOCK // 2]


def project_back(weights, vec, white, rate, rel_white, rel_rate, total, grads, tables, vec_grads):
    groups, model = weights.shape[:2]
    seq = white.shape[0]
    width = grads.shape[2] // 3
    entries = rel_white.shape[0]
    return pl.pallas_call(
        project_back_kernel,
        in_specs=[IN_VMEM] * 10,
        out_specs=[IN_VMEM] * 2,
        out_shape=[
            jax.ShapeDtypeStruct((model, seq), low),
            jax.ShapeDtypeStruct((groups, model, 3 * width + BLOCK // 2 + entries // groups), low),
        ],
        scratch_shapes=[pltpu.VMEM((seq, model), f32), pltpu.VMEM((entries, 2 * width), low)],
        compiler_params=pltpu.CompilerParams(vmem_limit_bytes=56 << 20),
        name="project_back",
    )(weights, vec, white, rate, rel_white, rel_rate, total, grads, tables, vec_grads)


def split_terms(values, count):
    terms = []
    for _ in range(count):
        term = lax.reduce_precision(values, 8, 7)
        terms.append(term.astype(low))
        values = values - term
    return terms


def adamw(weight, gradient, mean, square, rate_now):
    first = beta_first * mean + (1.0 - beta_first) * gradient
    second = beta_second * square + (1.0 - beta_second) * gradient * gradient
    mean_hat = first / (1.0 - beta_first**STEP)
    square_hat = second / (1.0 - beta_second**STEP)
    master = weight - rate_now * (
        mean_hat / (jnp.sqrt(square_hat) + adam_eps) + weight_decay * weight
    )
    return (first, second, master)


def per_device(
    token_ids,
    row_lengths,
    replaced,
    embedding,
    relative,
    project,
    combine,
    expand,
    contract,
    readout,
    vectors,
    embedding_mean,
    relative_mean,
    project_mean,
    combine_mean,
    expand_mean,
    contract_mean,
    readout_mean,
    vectors_mean,
    embedding_square,
    relative_square,
    project_square,
    combine_square,
    expand_square,
    contract_square,
    readout_square,
    vectors_square,
):
    pieces = lax.axis_size("heads")
    holder = lax.axis_index("heads")
    owners = lax.axis_size("dp")
    row_count, seq_len = token_ids.shape
    width = vectors.shape[1]
    model = width * owners
    everyone = ("heads", "dp")
    head_width = project.shape[2]
    hidden = expand.shape[1]
    vocab_slab = embedding.shape[1]
    span_part = relative.shape[0] // pieces
    vector_count = vectors.shape[0]
    direct = owners == 8 and pieces == 4

    own_relative = lax.dynamic_slice_in_dim(relative, holder * span_part, span_part, 0).T
    own_readout = lax.dynamic_slice_in_dim(readout, holder * head_width, head_width, 1)
    vector_terms = [
        jnp.pad(term, ((0, 0), (0, 16 - vector_count))) for term in split_terms(vectors.T, 3)
    ]
    high, rest = split_terms(own_relative, 2)
    blank = jnp.zeros((width, 16), low)
    first_pack = jnp.concatenate(
        [
            project.reshape(width, 3 * head_width).astype(low),
            *vector_terms,
            blank,
            high,
            combine.T.astype(low),
            jnp.pad(blank, ((0, 0), (0, 48))),
            rest,
        ],
        1,
    )
    second_pack = jnp.concatenate(
        [expand.astype(low), contract.T.astype(low), own_readout.astype(low)], 1
    )
    first_all = lax.all_gather(first_pack, everyone, axis=0, tiled=True)
    first_all = first_all.reshape(pieces, model, -1)
    second_all = lax.all_gather(second_pack, everyone, axis=0, tiled=True)
    second_all = second_all.reshape(pieces, model, -1)

    length_row = jnp.pad(row_lengths[None, :], ((0, 0), (0, seq_len - row_count)))
    facts = jnp.concatenate([token_ids, jnp.pad(length_row, ((0, 8 - 1 - row_count), (0, 0)))], 0)
    all_facts = share_facts(facts, 1) if direct else lax.all_gather(facts, "dp")
    all_ids = all_facts[:, :row_count].reshape(owners * row_count, seq_len)
    all_lengths = all_facts[:, row_count, :row_count].reshape(-1)
    token_total = jnp.sum(all_lengths).astype(f32)
    local_ids = all_ids - holder * vocab_slab
    inside = (local_ids >= 0) & (local_ids < vocab_slab)
    places = jnp.where(inside, local_ids, vocab_slab)

    found = lookup(all_lengths, places, embedding)
    found = found.reshape(owners, row_count, width, seq_len)
    if direct:
        found = exchange_words(found, 2)
    else:
        found = lax.psum_scatter(found, "heads", scatter_dimension=1, tiled=True)[:, 0]
        found = lax.all_to_all(found, "dp", 0, 0, tiled=True)
    own_length = lax.dynamic_slice_in_dim(row_lengths, holder, 1)
    own_live = jnp.arange(seq_len) < own_length
    own_flags = lax.dynamic_slice_in_dim(replaced, holder, 1)[0].astype(f32)
    marks = jnp.stack([jnp.where(own_live, 1.0 / token_total, 0.0), own_flags], 1)

    entries = relative.shape[0]
    vec_full, white, rate, qkv, rel_white, rel_rate, rel_table = prepare(
        first_all, found.reshape(model, seq_len), head_width, entries
    )
    probs, mixed = attend(own_length, qkv, rel_table)
    grad_contract, grad_expand, grad_joint, grad_mixed, grad_sum, grad_vec, losses = middle(
        first_all, second_all, vec_full, white, mixed, marks
    )
    loss_part = jnp.sum(losses)
    qkv_grads, rel_table_grads = attend_back(qkv, rel_table, probs, grad_mixed)
    sent, grad_project = project_back(
        first_all,
        vec_full,
        white,
        rate,
        rel_white,
        rel_rate,
        grad_sum,
        qkv_grads,
        rel_table_grads,
        grad_vec,
    )
    sent = sent.reshape(owners, width, seq_len)
    if direct:
        sent = return_words(sent, 3)
    else:
        sent = lax.all_to_all(sent, "dp", 0, 0, tiled=True)
        sent = lax.all_gather(sent, "heads", axis=0)
        sent = sent.transpose(1, 0, 2, 3)
    sent = sent.reshape(owners * row_count, width, seq_len)

    partial_grads = [grad_contract, grad_expand, grad_joint, grad_project]
    if direct:
        sums = scatter_sums(
            [part.reshape(pieces, owners, width, -1) for part in partial_grads], 4
        )
    else:
        sums = [
            lax.psum_scatter(
                part.reshape(pieces * model, -1), everyone, scatter_dimension=0, tiled=True
            ).astype(f32)
            for part in partial_grads
        ]
    grad_embedding, own_squares = deposit(all_lengths, places, sent, vocab_slab)

    squares_local = sum(jnp.sum(part * part) for part in sums) + jnp.sum(own_squares)
    shared = jnp.concatenate([sums[2][:, :head_width], sums[3][:, 3 * head_width :]], 1)
    if direct:
        column = lax.broadcasted_iota(jnp.int32, (8, BLOCK), 1)
        own_facts = jnp.where(column == 0, squares_local, jnp.where(column == 1, loss_part, 0.0))
        all_facts, shared = finish_sums(own_facts, shared, 5)
        squares_total, loss_sum = all_facts[0, 0], all_facts[0, 1]
    else:
        squares_total, loss_sum = lax.psum((squares_local, loss_part), everyone)
        shared = lax.all_gather(shared, "heads", axis=0)
    grad_norm = jnp.sqrt(squares_total)
    factor = jnp.minimum(1.0, clip_level / grad_norm)

    grad_contract = sums[0].T
    grad_expand = sums[1]
    grad_combine = sums[2][:, head_width:].T
    grad_project = sums[3][:, : 3 * head_width].reshape(width, 3, head_width)
    grad_readout = shared[:, :, :head_width].transpose(1, 0, 2).reshape(width, model)
    at = head_width + BLOCK // 2
    grad_relative = shared[:, :, at:].transpose(0, 2, 1).reshape(entries, width)
    grad_vec = shared[:, :, head_width : head_width + 3].transpose(0, 2, 1).reshape(-1, width)
    grad_vec = grad_vec[:vector_count]
    weights = (embedding, relative, project, combine, expand, contract, readout, vectors)
    gradients = (
        grad_embedding,
        grad_relative,
        grad_project,
        grad_combine,
        grad_expand,
        grad_contract,
        grad_readout,
        grad_vec,
    )
    means = (
        embedding_mean,
        relative_mean,
        project_mean,
        combine_mean,
        expand_mean,
        contract_mean,
        readout_mean,
        vectors_mean,
    )
    squares = (
        embedding_square,
        relative_square,
        project_square,
        combine_square,
        expand_square,
        contract_square,
        readout_square,
        vectors_square,
    )
    updates = [
        adamw(weight, gradient * factor, mean, square, rate_now)
        for weight, gradient, mean, square, rate_now in zip(
            weights, gradients, means, squares, rate_steps
        )
    ]
    return (
        loss_sum,
        token_total,
        grad_norm,
        updates[0][0],
        updates[0][1],
        updates[0][2],
        updates[1][0],
        updates[1][1],
        updates[1][2],
        updates[2][0],
        updates[2][1],
        updates[2][2],
        updates[3][0],
        updates[3][1],
        updates[3][2],
        updates[4][0],
        updates[4][1],
        updates[4][2],
        updates[5][0],
        updates[5][1],
        updates[5][2],
        updates[6][0],
        updates[6][1],
        updates[6][2],
        updates[7][0],
        updates[7][1],
        updates[7][2],
        grad_vec[3] * factor,
    )


def solution(mesh):
    placed = (
        P("dp", None),
        P("dp"),
        P("dp", None),
        P("dp", "heads"),
        P(None, "dp"),
        P("dp", None, "heads"),
        P("heads", "dp"),
        P("dp", "heads"),
        P("heads", "dp"),
        P("dp", None),
        P(None, "dp"),
        P("dp", "heads"),
        P(None, "dp"),
        P("dp", None, "heads"),
        P("heads", "dp"),
        P("dp", "heads"),
        P("heads", "dp"),
        P("dp", None),
        P(None, "dp"),
        P("dp", "heads"),
        P(None, "dp"),
        P("dp", None, "heads"),
        P("heads", "dp"),
        P("dp", "heads"),
        P("heads", "dp"),
        P("dp", None),
        P(None, "dp"),
    )
    return jax.shard_map(
        per_device,
        mesh=mesh,
        in_specs=placed,
        out_specs=(
            P(),
            P(),
            P(),
            P("dp", "heads"),
            P("dp", "heads"),
            P("dp", "heads"),
            P(None, "dp"),
            P(None, "dp"),
            P(None, "dp"),
            P("dp", None, "heads"),
            P("dp", None, "heads"),
            P("dp", None, "heads"),
            P("heads", "dp"),
            P("heads", "dp"),
            P("heads", "dp"),
            P("dp", "heads"),
            P("dp", "heads"),
            P("dp", "heads"),
            P("heads", "dp"),
            P("heads", "dp"),
            P("heads", "dp"),
            P("dp", None),
            P("dp", None),
            P("dp", None),
            P(None, "dp"),
            P(None, "dp"),
            P(None, "dp"),
            P("dp"),
        ),
        check_vma=False,
    )
```

```python
import functools

import jax
import jax.numpy as jnp
from jax import lax
from jax.experimental import pallas as pl
from jax.experimental.pallas import tpu as pltpu
from jax.sharding import PartitionSpec as P

HEAD_DIM = 64
STEP = 10
BLOCK = 128
UNROLL = 16
ROW_SET = 8

low = jnp.bfloat16
f32 = jnp.float32

layer_eps = 1e-07
clip_level = 0.005
rate_steps = (0.1, 0.05, 0.05, 0.05, 0.05, 0.05, 0.05, 1.0)
beta_first = 0.9
beta_second = 0.999
adam_eps = 1e-08
weight_decay = 0.01


def dot_rows(a,b):
    return lax.dot_general(a,b,(((1,),(1,)),((),())),preferred_element_type=f32)
def dot_plain(a,b):
    return lax.dot_general(a,b,(((1,),(0,)),((),())),preferred_element_type=f32)
def dot_left(a,b):
    return lax.dot_general(a,b,(((0,),(0,)),((),())),preferred_element_type=f32)

def attend_head(group, head, length, qkv_ref, table_ref, probs_ref, mixed_ref, far_ref):
    seq = qkv_ref.shape[1]
    width = qkv_ref.shape[2] // 3
    heads = width // HEAD_DIM
    scale = (3 * HEAD_DIM) ** -0.5
    live = lax.broadcasted_iota(jnp.int32, (BLOCK, seq), 1) < length
    at = head * HEAD_DIM
    q = qkv_ref[group, :, at : at + HEAD_DIM]
    k = qkv_ref[group, :, width + at : width + at + HEAD_DIM]
    v = qkv_ref[group, :, 2 * width + at : 2 * width + at + HEAD_DIM]
    for block in range(seq // BLOCK):
        rows = slice(block * BLOCK, (block + 1) * BLOCK)
        window = slice(seq - BLOCK * (block + 1), 2 * seq - BLOCK * block)
        far = dot_rows(k[rows], table_ref[group, window, at : at + HEAD_DIM])
        far = pltpu.roll(far, seq, 1, stride=1, stride_axis=0)[:, :seq]
        far_ref[head, :, rows] = far.T
    for block in range(seq // BLOCK):
        rows = slice(block * BLOCK, (block + 1) * BLOCK)
        window = slice(seq - BLOCK * (block + 1), 2 * seq - BLOCK * block)
        near = dot_rows(q[rows], table_ref[group, window, width + at : width + at + HEAD_DIM])
        near = pltpu.roll(near, seq, 1, stride=1, stride_axis=0)[:, :seq]
        scores = (dot_rows(q[rows], k) + near + far_ref[head, rows, :]) * scale
        scores = jnp.where(live, scores, -1e9)
        top = jnp.max(scores, -1, keepdims=True)
        expo = jnp.exp(scores - top)
        probs = (expo * (1.0 / jnp.sum(expo, -1, keepdims=True))).astype(low)
        probs_ref[group * heads + head, rows, :] = probs
        mixed_ref[group, rows, at : at + HEAD_DIM] = dot_plain(probs, v).astype(low)


def attend_kernel(length_ref, qkv_ref, table_ref, probs_ref, mixed_ref, far_ref):
    for head in range(far_ref.shape[0]):
        attend_head(0, head, length_ref[0], qkv_ref, table_ref, probs_ref, mixed_ref, far_ref)


def attend(length, qkv, table):
    groups, seq, width3 = qkv.shape
    width = width3 // 3
    heads = width // HEAD_DIM
    return pl.pallas_call(
        attend_kernel,
        grid=(groups,),
        in_specs=[
            pl.BlockSpec(memory_space=pltpu.SMEM),
            pl.BlockSpec((1, seq, width3), lambda g: (g, 0, 0)),
            pl.BlockSpec((1, 2 * seq, 2 * width), lambda g: (g, 0, 0)),
        ],
        out_specs=[
            pl.BlockSpec((heads, seq, seq), lambda g: (g, 0, 0)),
            pl.BlockSpec((1, seq, width), lambda g: (g, 0, 0)),
        ],
        out_shape=[
            jax.ShapeDtypeStruct((groups * heads, seq, seq), low),
            jax.ShapeDtypeStruct((groups, seq, width), low),
        ],
        scratch_shapes=[pltpu.VMEM((heads, seq, seq), f32)],
        compiler_params=pltpu.CompilerParams(vmem_limit_bytes=48 << 20),
        name="attend",
    )(length, qkv, table)


def attend_back_head(
    group, head, qkv_ref, table_ref, probs_ref, up_ref, grad_ref, rel_ref, low_ref, sum_ref
):
    seq = qkv_ref.shape[1]
    width = qkv_ref.shape[2] // 3
    heads = width // HEAD_DIM
    scale = (3 * HEAD_DIM) ** -0.5
    row = lax.broadcasted_iota(jnp.int32, (BLOCK, BLOCK), 0)
    flip = row + lax.broadcasted_iota(jnp.int32, (BLOCK, BLOCK), 1) == BLOCK - 1
    flip = flip.astype(f32).astype(low)
    edge = jnp.zeros((BLOCK, BLOCK), f32)

    def shear(rows):
        return pltpu.roll(jnp.concatenate([rows, edge], 1), 1, 1, stride=1, stride_axis=0).astype(low)

    at = head * HEAD_DIM
    q = qkv_ref[group, :, at : at + HEAD_DIM]
    k = qkv_ref[group, :, width + at : width + at + HEAD_DIM]
    v = qkv_ref[group, :, 2 * width + at : 2 * width + at + HEAD_DIM]
    up = up_ref[group, :, at : at + HEAD_DIM]
    source = group * heads + head
    for block in range(seq // BLOCK):
        rows = slice(block * BLOCK, (block + 1) * BLOCK)
        probs = probs_ref[source, rows, :].astype(f32)
        pull = dot_rows(up[rows], v)
        inner = jnp.sum(probs * pull, -1, keepdims=True)
        low_ref[head, rows, :] = (probs * (pull - inner) * scale).astype(low)
    grad_v = dot_left(up, probs_ref[source]).T.astype(low)
    grad_ref[group, :, 2 * width + at : 2 * width + at + HEAD_DIM] = grad_v
    sum_ref[2 * head] = jnp.zeros(sum_ref.shape[1:], f32)
    sum_ref[2 * head + 1] = jnp.zeros(sum_ref.shape[1:], f32)
    for block in range(seq // BLOCK):
        rows = slice(block * BLOCK, (block + 1) * BLOCK)
        window = slice(seq - BLOCK * (block + 1), 2 * seq - BLOCK * block)
        turned = dot_plain(flip, low_ref[head, rows, :])
        near = shear(turned)
        grad_q = dot_plain(turned.astype(low), k) + dot_plain(
            near, table_ref[group, window, width + at : width + at + HEAD_DIM]
        )
        grad_ref[group, rows, at : at + HEAD_DIM] = dot_plain(flip, grad_q.astype(low)).astype(low)
        q_turned = dot_plain(flip, q[rows]).astype(low)
        sum_ref[2 * head + 1, :, window] += dot_left(q_turned, near)
        turned = dot_rows(flip, low_ref[head, :, rows])
        far = shear(turned)
        grad_k = dot_plain(turned.astype(low), q) + dot_plain(
            far, table_ref[group, window, at : at + HEAD_DIM]
        )
        grad_ref[group, rows, width + at : width + at + HEAD_DIM] = dot_plain(
            flip, grad_k.astype(low)
        ).astype(low)
        k_turned = dot_plain(flip, k[rows]).astype(low)
        sum_ref[2 * head, :, window] += dot_left(k_turned, far)
    rel_ref[group, :, at : at + HEAD_DIM] = sum_ref[2 * head].T.astype(low)
    rel_ref[group, :, width + at : width + at + HEAD_DIM] = sum_ref[2 * head + 1].T.astype(low)


def attend_back_kernel(*refs):
    for head in range(refs[-2].shape[0]):
        attend_back_head(0, head, *refs)


def attend_back(qkv, table, probs, up):
    groups, seq, width3 = qkv.shape
    width = width3 // 3
    heads = width // HEAD_DIM
    block = lambda *shape: pl.BlockSpec(shape, lambda g: (g, 0, 0))
    return pl.pallas_call(
        attend_back_kernel,
        grid=(groups,),
        in_specs=[
            block(1, seq, width3),
            block(1, 2 * seq, 2 * width),
            block(heads, seq, seq),
            block(1, seq, width),
        ],
        out_specs=[block(1, seq, width3), block(1, 2 * seq, 2 * width)],
        out_shape=[
            jax.ShapeDtypeStruct((groups, seq, width3), low),
            jax.ShapeDtypeStruct((groups, 2 * seq, 2 * width), low),
        ],
        scratch_shapes=[
            pltpu.VMEM((heads, seq, seq), low),
            pltpu.VMEM((2 * heads, HEAD_DIM, 2 * seq), f32),
        ],
        compiler_params=pltpu.CompilerParams(vmem_limit_bytes=48 << 20),
        name="attend_back",
    )(qkv, table, probs, up)


MESH = pl.DeviceIdType.MESH
ANYWHERE = pl.BlockSpec(memory_space=pl.ANY)
IN_VMEM = pl.BlockSpec(memory_space=pltpu.VMEM)


def place():
    owner, holder = lax.axis_index("dp"), lax.axis_index("heads")
    return owner // 2, owner % 2, holder // 2, holder % 2


def device(z, x, y, c):
    return (z * 2 + x, y * 2 + c)


def signal(target):
    pl.semaphore_signal(
        pltpu.get_barrier_semaphore(), inc=1, device_id=target, device_id_type=MESH
    )


def greet(z, x, y, c, line):
    signal(device(z, x, y, 1 - c))
    signal(device(z, x, 1 - y, c))
    if line:
        signal(device(z, 1 - x, y, c))

        @pl.when(z < 3)
        def above():
            signal(device(z + 1, x, y, c))

        @pl.when(z > 0)
        def below():
            signal(device(z - 1, x, y, c))

        pl.semaphore_wait(pltpu.get_barrier_semaphore(), jnp.where((z == 0) | (z == 3), 4, 5))


def remote(source, target, send, recv, to):
    return pltpu.make_async_remote_copy(
        src_ref=source, dst_ref=target, send_sem=send, recv_sem=recv, device_id=to, device_id_type=MESH
    )


def sum_scratch(width, sizes):
    half = width // 2
    leads = (
        (2, 4, 2, width),
        (2, 4, 2, width),
        (4, 2, half),
        (2, 4, half),
        (4, half),
        (4, half),
        (3, width),
        (3, width),
    )
    shapes = [pltpu.VMEM(lead + (size,), low) for lead in leads for size in sizes]
    count = len(sizes)
    return shapes + [
        pltpu.SemaphoreType.DMA((count, 2)),
        pltpu.SemaphoreType.DMA((count, 12)),
        pltpu.SemaphoreType.DMA((count, 12)),
    ]


def sum_stages(spot, grads, totals, chunks, refs):
    count = len(chunks)
    pair, own, first_a, first_b, second_a, second_b, rise, fall = [
        refs[count * part : count * (part + 1)] for part in range(8)
    ]
    local_sem, send_sem, recv_sem = refs[8 * count :]
    z, x, y, c = spot
    half = grads[0].shape[3] // 2
    upper, lower = pl.ds(0, half), pl.ds(half, half)
    core_to, y_to, x_to = device(z, x, y, 1 - c), device(z, x, 1 - y, c), device(z, 1 - x, y, c)
    up_to, down_to = device(z + 1, x, y, c), device(z - 1, x, y, c)

    def columns(part):
        return pl.ds(chunks[part][1], chunks[part][2])

    def source(part, row):
        return grads[chunks[part][0]].at[row, :, :, :, columns(part)]

    def link(part, slot, source, target, to):
        return remote(source, target, send_sem.at[part, slot], recv_sem.at[part, slot], to)

    def local(part, side):
        return pltpu.make_async_copy(
            source(part, side * 2 + c), own[part].at[side], local_sem.at[part, side]
        )

    def pair_copy(part, side):
        return link(part, side, source(part, side * 2 + 1 - c), pair[part].at[side], core_to)

    def first_copies(part):
        block = own[part]
        return (
            link(part, 2, block.at[1 - y, :, :, upper], first_a[part], y_to),
            link(part, 3, block.at[:, :, 1 - x, lower], first_b[part], x_to),
        )

    def second_copies(part):
        block = own[part]
        return (
            link(part, 4, block.at[y, :, 1 - x, upper], second_a[part], x_to),
            link(part, 5, block.at[1 - y, :, x, lower], second_b[part], y_to),
        )

    def rise_copy(part, turn):
        block = own[part].at[y, lax.clamp(0, 3 + z - turn, 3), x]
        return link(part, 6 + turn, block, rise[part].at[turn], up_to)

    def fall_copy(part, turn):
        block = own[part].at[y, lax.clamp(0, turn - 3 + z, 3), x]
        return link(part, 9 + turn, block, fall[part].at[turn], down_to)

    def add(target, source):
        target[...] = (target[...].astype(f32) + source[...].astype(f32)).astype(low)

    def start_pair(part):
        for side in range(2):
            pair_copy(part, side).start()
            local(part, side).start()

    def start():
        for part in range(min(2, count)):
            start_pair(part)

    def stage_pair(part):
        for side in range(2):
            local(part, side).wait()
            pair_copy(part, side).wait()
        if part + 2 < count:
            start_pair(part + 2)

        def step(index, carry):
            side, rest = index // 8, index % 8
            add(own[part].at[side, rest // 2, rest % 2], pair[part].at[side, rest // 2, rest % 2])
            return carry

        lax.fori_loop(0, 16, step, 0)
        for copy in first_copies(part):
            copy.start()

    def stage_first(part):
        for copy in first_copies(part):
            copy.wait()

        def step(index, carry):
            add(own[part].at[y, index // 2, index % 2, upper], first_a[part].at[index // 2, index % 2])
            add(own[part].at[index % 2, index // 2, x, lower], first_b[part].at[index % 2, index // 2])
            return carry

        lax.fori_loop(0, 8, step, 0)
        for copy in second_copies(part):
            copy.start()

    def stage_second(part):
        for copy in second_copies(part):
            copy.wait()

        def step(index, carry):
            add(own[part].at[y, index, x, upper], second_a[part].at[index])
            add(own[part].at[y, index, x, lower], second_b[part].at[index])
            return carry

        lax.fori_loop(0, 4, step, 0)

    def stage_line(part, turn):
        @pl.when((z <= turn) & (z < 3))
        def rises():
            if turn > 0:

                @pl.when(z > 0)
                def joined():
                    rise_copy(part, turn - 1).wait_recv()
                    add(own[part].at[y, 3 + z - turn, x], rise[part].at[turn - 1])

            rise_copy(part, turn).start()

        @pl.when((3 - z <= turn) & (z > 0))
        def falls():
            if turn > 0:

                @pl.when(z < 3)
                def joined():
                    fall_copy(part, turn - 1).wait_recv()
                    add(own[part].at[y, turn - 3 + z, x], fall[part].at[turn - 1])

            fall_copy(part, turn).start()

    def stage_total(part):
        total = totals[chunks[part][0]].at[:, columns(part)]
        total[...] = own[part][y, z, x].astype(f32)

        @pl.when(z > 0)
        def risen():
            rise_copy(part, 2).wait_recv()
            total[...] += rise[part][2].astype(f32)

        @pl.when(z < 3)
        def fallen():
            fall_copy(part, 2).wait_recv()
            total[...] += fall[part][2].astype(f32)

        for turn in range(3):

            @pl.when((z <= turn) & (z < 3))
            def risen_out():
                rise_copy(part, turn).wait_send()

            @pl.when((3 - z <= turn) & (z > 0))
            def fallen_out():
                fall_copy(part, turn).wait_send()

    return start, {
        "pair": stage_pair,
        "first": stage_first,
        "second": stage_second,
        "line0": functools.partial(stage_line, turn=0),
        "line1": functools.partial(stage_line, turn=1),
        "line2": functools.partial(stage_line, turn=2),
        "total": stage_total,
    }


def chunked(sizes, most=3 * BLOCK):
    return [
        (array, first, min(most, size - first))
        for array, size in enumerate(sizes)
        for first in range(0, size, most)
    ]


BACK_START = (("pair", 0),)
BACK_SLOTS = {
    0: (("pair", 1),),
    2: (("first", 0), ("pair", 2)),
    3: (("first", 1),),
    4: (("pair", 3), ("second", 0), ("line0", 0)),
    5: (("first", 2), ("second", 1), ("line0", 1), ("line1", 0)),
    6: (("line1", 1), ("line2", 0)),
    7: (("first", 3), ("second", 2), ("line0", 2), ("line2", 1), ("total", 0)),
    8: (("line1", 2), ("total", 1)),
    9: (("second", 3), ("line0", 3), ("line2", 2)),
    10: (("line1", 3), ("total", 2)),
    11: (("line2", 3),),
}
BACK_END = (("total", 3),)


def run_all(stages, steps):
    for name, chunk in steps:
        stages[name](chunk)


def attend_back_sums_kernel(count, chunks, *refs):
    inputs, grads = refs[:4], refs[4 : 4 + count]
    outputs, totals = refs[4 + count : 6 + count], refs[6 + count : 6 + 2 * count]
    work, rest = refs[6 + 2 * count : 8 + 2 * count], refs[8 + 2 * count :]
    groups, heads = inputs[0].shape[0], work[0].shape[0]
    spot = place()
    greet(*spot, True)
    start, stages = sum_stages(spot, grads, totals, chunks, rest)
    start()
    run_all(stages, BACK_START)

    def step(group, carry):
        for head in range(heads):
            attend_back_head(group, head, *inputs, *outputs, *work)
            for slot, steps in BACK_SLOTS.items():
                if slot % heads == head:
                    pl.when(group == slot // heads)(functools.partial(run_all, stages, steps))
        return carry

    lax.fori_loop(0, groups, step, 0)
    run_all(stages, BACK_END)


def attend_back_sums(qkv, table, probs, up, grads, tag):
    groups, seq, width3 = qkv.shape
    width = width3 // 3
    heads = width // HEAD_DIM
    part = grads[0].shape[1] // 8
    sizes = [grad.shape[2] for grad in grads]
    chunks = chunked(sizes)
    return pl.pallas_call(
        functools.partial(attend_back_sums_kernel, len(grads), chunks),
        in_specs=[IN_VMEM] * 4 + [ANYWHERE] * len(grads),
        out_specs=[IN_VMEM] * (2 + len(grads)),
        out_shape=[
            jax.ShapeDtypeStruct((groups, seq, width3), low),
            jax.ShapeDtypeStruct((groups, 2 * seq, 2 * width), low),
        ]
        + [jax.ShapeDtypeStruct((part, size), f32) for size in sizes],
        scratch_shapes=[
            pltpu.VMEM((heads, seq, seq), low),
            pltpu.VMEM((2 * heads, HEAD_DIM, 2 * seq), f32),
        ]
        + sum_scratch(part, [chunk[2] for chunk in chunks]),
        compiler_params=pltpu.CompilerParams(
            collective_id=tag, has_side_effects=True, vmem_limit_bytes=60 << 20
        ),
        name="attend_back_sums",
    )(qkv, table, probs, up, *[grad.reshape(4, 4, 2, part, -1) for grad in grads])


def peers(z, x):
    return [((z + 2 - far) % 4, x if same else 1 - x) for far, same in PEER_ORDER]


PEER_ORDER = ((0, False), (0, True), (1, False), (1, True), (3, False), (3, True), (2, False))


def meet_owners(z, x, y, c):
    for peer_z, peer_x in peers(z, x):
        signal(device(peer_z, peer_x, y, c))


def share_facts_kernel(facts_ref, all_ref, local_sem, send_sem, recv_sem):
    z, x, y, c = place()
    meet_owners(z, x, y, c)
    pl.semaphore_wait(pltpu.get_barrier_semaphore(), 7)
    here = z * 2 + x
    keep = pltpu.make_async_copy(facts_ref, all_ref.at[here], local_sem)
    keep.start()
    copies = []
    for index, (peer_z, peer_x) in enumerate(peers(z, x)):
        copy = remote(
            facts_ref,
            all_ref.at[here],
            send_sem.at[index],
            recv_sem.at[here],
            device(peer_z, peer_x, y, c),
        )
        copy.start()
        copies.append(copy)
    for index, (peer_z, peer_x) in enumerate(peers(z, x)):
        there = peer_z * 2 + peer_x
        copies[index].wait_send()
        remote(
            facts_ref, all_ref.at[there], send_sem.at[index], recv_sem.at[there], device(z, x, y, c)
        ).wait_recv()
    keep.wait()


def share_facts(facts, tag):
    return pl.pallas_call(
        share_facts_kernel,
        in_specs=[IN_VMEM],
        out_specs=IN_VMEM,
        out_shape=jax.ShapeDtypeStruct((8,) + facts.shape, facts.dtype),
        scratch_shapes=[
            pltpu.SemaphoreType.DMA,
            pltpu.SemaphoreType.DMA((7,)),
            pltpu.SemaphoreType.DMA((8,)),
        ],
        compiler_params=pltpu.CompilerParams(collective_id=tag, has_side_effects=True),
        name="share_facts",
    )(facts)


def word_stages(spot, found_ref, words_ref, pair, side, send_sem, recv_sem, out_sem, in_sem):
    z, x, y, c = spot
    here = z * 2 + x
    targets = peers(z, x) + [(z, x)]
    core_to, y_to = device(z, x, y, 1 - c), device(z, x, 1 - y, c)

    def at_home(part):
        return targets[part][0] * 2 + targets[part][1]

    def pair_copy(part, row):
        to = at_home(part)
        return remote(
            found_ref.at[to, row * 2 + 1 - c],
            pair.at[row, to],
            send_sem.at[part, row],
            recv_sem.at[part, row],
            core_to,
        )

    def side_copy(part):
        to = at_home(part)
        return remote(
            pair.at[1 - y, to], side.at[to], send_sem.at[part, 2], recv_sem.at[part, 2], y_to
        )

    def out_copy(part):
        return remote(
            pair.at[y, at_home(part)],
            words_ref.at[here],
            out_sem.at[part],
            in_sem.at[here],
            device(targets[part][0], targets[part][1], y, c),
        )

    def start():
        for part in range(8):
            for row in range(2):
                pair_copy(part, row).start()

    def sideways(first, last):
        for part in range(first, last):
            to = at_home(part)
            for row in range(2):
                pair_copy(part, row).wait_recv()
                pair[row, to] = pair[row, to] + found_ref[to, row * 2 + c]
            side_copy(part).start()

    def outward(first, last):
        for part in range(first, last):
            to = at_home(part)
            side_copy(part).wait_recv()
            pair[y, to] = pair[y, to] + side[to]
            if part < 7:
                out_copy(part).start()
            else:
                words_ref[here] = pair[y, to]

    def finish():
        for part in range(8):
            for row in range(2):
                pair_copy(part, row).wait_send()
            side_copy(part).wait_send()
            if part < 7:
                out_copy(part).wait_send()
                there = at_home(part)
                remote(
                    pair.at[y, there], words_ref.at[there], out_sem.at[part], in_sem.at[there], core_to
                ).wait_recv()

    return start, sideways, outward, finish


def exchange_words_kernel(found_ref, words_ref, *refs):
    spot = place()
    meet_owners(*spot)
    greet(*spot, False)
    pl.semaphore_wait(pltpu.get_barrier_semaphore(), 9)
    start, sideways, outward, finish = word_stages(spot, found_ref, words_ref, *refs)
    start()
    sideways(0, 8)
    outward(0, 8)
    finish()


def exchange_words(found, tag):
    piece = found.shape[2:]
    return pl.pallas_call(
        exchange_words_kernel,
        in_specs=[IN_VMEM],
        out_specs=IN_VMEM,
        out_shape=jax.ShapeDtypeStruct((8,) + piece, low),
        scratch_shapes=[
            pltpu.VMEM((2, 8) + piece, low),
            pltpu.VMEM((8,) + piece, low),
            pltpu.SemaphoreType.DMA((8, 3)),
            pltpu.SemaphoreType.DMA((8, 3)),
            pltpu.SemaphoreType.DMA((8,)),
            pltpu.SemaphoreType.DMA((8,)),
        ],
        compiler_params=pltpu.CompilerParams(
            collective_id=tag, has_side_effects=True, vmem_limit_bytes=40 << 20
        ),
        name="exchange_words",
    )(found)


def return_stages(spot, grads_ref, sent_ref, refs):
    local_sem, out_sem, in_sem, send_sem, recv_sem = refs
    z, x, y, c = spot
    here = z * 2 + x
    own = y * 2 + c
    other = (1 - y) * 2 + c
    core_to, y_to = device(z, x, y, 1 - c), device(z, x, 1 - y, c)
    order = [(z, x)] + peers(z, x)[::-1]
    keep = pltpu.make_async_copy(grads_ref.at[here], sent_ref.at[here, own], local_sem)

    def out_copy(part, peer):
        return remote(
            grads_ref.at[peer[0] * 2 + peer[1]],
            sent_ref.at[here, own],
            out_sem.at[part],
            in_sem.at[here],
            device(peer[0], peer[1], y, c),
        )

    def in_copy(part, peer):
        there = peer[0] * 2 + peer[1]
        return remote(
            grads_ref.at[there], sent_ref.at[there, own], out_sem.at[part], in_sem.at[there], core_to
        )

    def pass_on(slot, row, there, to):
        block = sent_ref.at[there, row]
        return remote(block, block, send_sem.at[slot, there], recv_sem.at[row, there], to)

    def start():
        keep.start()
        for part, peer in enumerate(peers(z, x)):
            out_copy(part, peer).start()

    def forward(first, last):
        for part in range(first, last):
            there = order[part][0] * 2 + order[part][1]
            if part == 0:
                keep.wait()
            else:
                in_copy(part - 1, order[part]).wait_recv()
            pass_on(0, own, there, y_to).start()
            pass_on(1, own, there, core_to).start()

    def relay(first, last):
        for part in range(first, last):
            there = order[part][0] * 2 + order[part][1]
            pass_on(0, other, there, y_to).wait_recv()
            pass_on(2, other, there, core_to).start()

    def finish():
        for part, peer in enumerate(peers(z, x)):
            out_copy(part, peer).wait_send()
        for peer_z, peer_x in order:
            there = peer_z * 2 + peer_x
            pass_on(0, own, there, y_to).wait_send()
            pass_on(1, own, there, core_to).wait_send()
            pass_on(2, other, there, core_to).wait_send()
            pass_on(1, y * 2 + 1 - c, there, core_to).wait_recv()
            pass_on(2, (1 - y) * 2 + 1 - c, there, core_to).wait_recv()

    return start, forward, relay, finish


def return_sums_kernel(chunks, words_ref, grads_ref, sent_ref, total_ref, *refs):
    spot = place()
    z, x, y, c = spot
    meet_owners(*spot)
    greet(*spot, False)
    pl.semaphore_wait(pltpu.get_barrier_semaphore(), 9)
    start_words, forward, relay, finish = return_stages(spot, words_ref, sent_ref, refs[:5])
    start_sums, stages = sum_stages(spot, [grads_ref], [total_ref], chunks, refs[5:])
    start_words()
    start_sums()
    forward(0, 1)
    run_all(stages, (("pair", 0), ("pair", 1)))
    forward(1, 8)
    run_all(stages, (("first", 0),))
    relay(0, 4)
    run_all(stages, (("first", 1), ("second", 0), ("line0", 0)))
    relay(4, 8)
    run_all(stages, (("second", 1), ("line0", 1)))
    for turn in ("line1", "line2", "total"):
        run_all(stages, ((turn, 0), (turn, 1)))
    finish()


def return_sums(words, grads, tag):
    piece = words.shape[1:]
    size = grads.shape[2]
    part = grads.shape[1] // 8
    chunks = chunked([size])
    return pl.pallas_call(
        functools.partial(return_sums_kernel, chunks),
        in_specs=[IN_VMEM, ANYWHERE],
        out_specs=[IN_VMEM] * 2,
        out_shape=[
            jax.ShapeDtypeStruct((8, 4) + piece, low),
            jax.ShapeDtypeStruct((part, size), f32),
        ],
        scratch_shapes=[
            pltpu.SemaphoreType.DMA,
            pltpu.SemaphoreType.DMA((7,)),
            pltpu.SemaphoreType.DMA((8,)),
            pltpu.SemaphoreType.DMA((3, 8)),
            pltpu.SemaphoreType.DMA((4, 8)),
        ]
        + sum_scratch(part, [chunk[2] for chunk in chunks]),
        compiler_params=pltpu.CompilerParams(
            collective_id=tag, has_side_effects=True, vmem_limit_bytes=48 << 20
        ),
        name="return_sums",
    )(words, grads.reshape(4, 4, 2, part, size))


def gather_stages(spot, pack_ref, all_ref, local_sem, send_sem, recv_sem):
    z, x, y, c = spot
    half = pack_ref.shape[0] // 2
    core_to, y_to, x_to = device(z, x, y, 1 - c), device(z, x, 1 - y, c), device(z, 1 - x, y, c)
    up_to, down_to = device(z + 1, x, y, c), device(z - 1, x, y, c)
    keep = pltpu.make_async_copy(pack_ref, all_ref.at[y * 2 + c, z * 2 + x], local_sem)
    UP, DOWN, CROSS, SIDE, CORE = range(5)
    targets = (up_to, down_to, x_to, y_to, core_to)

    def copy(kind, part, zz, xx, yy, column=c):
        zz = lax.clamp(0, zz, 3)
        block = all_ref.at[yy * 2 + column, zz * 2 + xx, pl.ds(part * half, half)]
        return remote(
            block,
            block,
            send_sem.at[kind, part, yy, zz * 2 + xx],
            recv_sem.at[column, part, yy, zz * 2 + xx],
            targets[kind],
        )

    def distances(far):
        if far == 0:
            return [(z, z >= 0, None)]
        return [(z - far, z >= far, UP), (z + far, z <= 3 - far, DOWN)]

    def spread_block(zz):
        for part in range(2):
            copy(CROSS if part == 0 else SIDE, part, zz, x, y).start()
        for part in range(2):
            copy(SIDE if part == 0 else CROSS, part, zz, x, y).start()
            copy(CORE, part, zz, x, y).start()

    def along(zz, way):
        if way is None:
            return [(UP, z < 3), (DOWN, z > 0)]
        return [(way, z < 3 if way == UP else z > 0)]

    def line(far):
        for zz, exists, way in distances(far):

            @pl.when(exists)
            def arrived():
                if way is None:
                    keep.wait()
                else:
                    for part in range(2):
                        copy(way, part, zz, x, y).wait_recv()
                for on, possible in along(zz, way):

                    @pl.when(possible)
                    def onward():
                        for part in range(2):
                            copy(on, part, zz, x, y).start()

                spread_block(zz)

    def sides(far):
        for zz, exists, way in distances(far):

            @pl.when(exists)
            def arrived():
                copy(CROSS, 0, zz, 1 - x, y).wait_recv()
                copy(SIDE, 0, zz, 1 - x, y).start()
                copy(CORE, 0, zz, 1 - x, y).start()
                copy(SIDE, 1, zz, x, 1 - y).wait_recv()
                copy(CROSS, 1, zz, x, 1 - y).start()
                copy(CORE, 1, zz, x, 1 - y).start()

    def corners(far):
        for zz, exists, way in distances(far):

            @pl.when(exists)
            def arrived():
                for part, xx, yy in ((0, x, 1 - y), (1, 1 - x, y), (0, 1 - x, 1 - y), (1, 1 - x, 1 - y)):
                    copy(CORE, part, zz, xx, yy).wait_recv()
                    copy(CORE, part, zz, xx, yy).start()

    def finish():
        for far in range(4):
            for zz, exists, way in distances(far):

                @pl.when(exists)
                def drained():
                    for on, possible in along(zz, way):

                        @pl.when(possible)
                        def onward():
                            for part in range(2):
                                copy(on, part, zz, x, y).wait_send()

                    for part in range(2):
                        copy(CROSS, part, zz, x, y).wait_send()
                        copy(SIDE, part, zz, x, y).wait_send()
                        for xx in range(2):
                            for yy in range(2):
                                copy(CORE, part, zz, xx, yy).wait_send()
                                copy(CORE, part, zz, xx, yy, 1 - c).wait_recv()
                    copy(SIDE, 0, zz, 1 - x, y).wait_send()
                    copy(CROSS, 1, zz, x, 1 - y).wait_send()

    return keep.start, {"line": line, "sides": sides, "corners": corners, "finish": lambda far: finish()}


def gather_scratch():
    return [
        pltpu.SemaphoreType.DMA,
        pltpu.SemaphoreType.DMA((5, 2, 2, 8)),
        pltpu.SemaphoreType.DMA((2, 2, 2, 8)),
    ]


def finish_sums_kernel(
    width,
    losses_ref,
    squares_ref,
    *refs,
):
    sums, refs = refs[:4], refs[4:]
    total_ref, all_ref, facts, pair, side, cross, line, local_sem, send_sem, recv_sem, line_send, line_recv = refs
    z, x, y, c = place()
    core_to, y_to, x_to = device(z, x, y, 1 - c), device(z, x, 1 - y, c), device(z, 1 - x, y, c)
    column = [(z + step) % 4 for step in range(1, 4)]
    for target in (core_to, y_to, x_to, *[device(other, x, y, c) for other in column]):
        signal(target)
    own, other = y * 2 + c, (1 - y) * 2 + c
    all_ref[own, :, :width] = sums[2][:, :width]
    all_ref[own, :, width:] = sums[3][:, 3 * width :]
    squares = jnp.sum(squares_ref[...], 0, keepdims=True)
    for part in sums:
        for first in range(0, part.shape[1], BLOCK):
            values = part[:, first : first + BLOCK]
            squares += jnp.sum(values * values, 0, keepdims=True)
    facts[0:1] = squares
    facts[1:2] = jnp.broadcast_to(jnp.sum(losses_ref[...], 0, keepdims=True), squares.shape)
    facts[2:8] = jnp.zeros((6, BLOCK), f32)
    pl.semaphore_wait(pltpu.get_barrier_semaphore(), 6)
    swap_pair = remote(facts, pair, send_sem.at[0], recv_sem.at[0], core_to)
    swap_pair.start()
    block = all_ref.at[own]
    shared_side = remote(block, block, send_sem.at[3], recv_sem.at[3], y_to)
    shared_pair = remote(block, block, send_sem.at[4], recv_sem.at[4], core_to)
    swap_pair.wait()
    total_ref[...] = facts[...] + pair[...]
    swap_side = remote(total_ref, side, send_sem.at[1], recv_sem.at[1], y_to)
    swap_side.start()
    shared_side.start()
    shared_pair.start()
    swap_side.wait()
    total_ref[...] += side[...]
    swap_cross = remote(total_ref, cross, send_sem.at[2], recv_sem.at[2], x_to)
    swap_cross.start()
    swap_cross.wait()
    total_ref[...] += cross[...]
    line[z] = total_ref[...]
    lines = [
        remote(line.at[z], line.at[z], line_send.at[step], line_recv.at[z], device(to, x, y, c))
        for step, to in enumerate(column)
    ]
    for copy in lines:
        copy.start()
    shared_side.wait()
    relay = remote(all_ref.at[other], all_ref.at[other], send_sem.at[5], recv_sem.at[5], core_to)
    relay.start()
    for step, to in enumerate(column):
        lines[step].wait_send()
        remote(line.at[to], line.at[to], line_send.at[step], line_recv.at[to], core_to).wait_recv()
    total_ref[...] = (line[0] + line[1]) + (line[2] + line[3])
    shared_pair.wait()
    relay.wait()


def finish_sums(losses, squares, sums, width, tag):
    small = (8, BLOCK)
    return pl.pallas_call(
        functools.partial(finish_sums_kernel, width),
        in_specs=[IN_VMEM] * 6,
        out_specs=[IN_VMEM] * 2,
        out_shape=[
            jax.ShapeDtypeStruct(small, f32),
            jax.ShapeDtypeStruct((4, squares.shape[0], 2 * width), f32),
        ],
        scratch_shapes=[pltpu.VMEM(small, f32)] * 4
        + [
            pltpu.VMEM((4,) + small, f32),
            pltpu.SemaphoreType.DMA,
            pltpu.SemaphoreType.DMA((6,)),
            pltpu.SemaphoreType.DMA((6,)),
            pltpu.SemaphoreType.DMA((3,)),
            pltpu.SemaphoreType.DMA((4,)),
        ],
        compiler_params=pltpu.CompilerParams(collective_id=tag, has_side_effects=True),
        name="finish_sums",
    )(losses, squares, *sums)


def identity(size):
    rows = lax.broadcasted_iota(jnp.int32, (size, size), 0)
    columns = lax.broadcasted_iota(jnp.int32, (size, size), 1)
    return (rows == columns).astype(f32).astype(low)


def turn(values):
    return dot_rows(identity(values.shape[1]), values)


TABLES = 2


def lookup_kernel(counts_ref, keys_ref, weights_ref, words_ref, table_ref, rows_ref):
    width, slab = weights_ref.shape
    rows, _, seq = words_ref.shape
    shift = slab.bit_length()

    @pl.when(pl.program_id(0) == 0)
    def fill():
        def step(index, carry):
            first = pl.multiple_of(index * 9 * BLOCK, BLOCK)
            for part in range(9):
                at = first + part * BLOCK
                table_ref[pl.ds(at, BLOCK), :] = turn(weights_ref[:, pl.ds(at, BLOCK)].astype(low))
            return carry

        lax.fori_loop(0, slab // (9 * BLOCK), step, 0)
        table_ref[pl.ds(slab, 8), :] = jnp.zeros((8, width), f32)

    rows_ref[...] = jnp.zeros_like(rows_ref)

    def step(index, carry):
        for offset in range(UNROLL):
            key = keys_ref[0, 0, index * UNROLL + offset]
            spot, token = key & ((1 << shift) - 1), key >> shift
            rows_ref[pl.ds(token, 1), :] = table_ref[pl.ds(spot, 1), :]
        return carry

    lax.fori_loop(0, pl.cdiv(counts_ref[pl.program_id(0)], UNROLL), step, 0)
    for row in range(rows):
        values = rows_ref[row * seq : (row + 1) * seq, :].astype(low)
        words_ref[row] = dot_rows(identity(width), values).astype(low)


def lookup(counts, keys, weights, seq):
    steps, tokens = keys.shape
    width, slab = weights.shape
    rows = tokens // seq
    return pl.pallas_call(
        lookup_kernel,
        grid=(steps,),
        in_specs=[
            pl.BlockSpec(memory_space=pltpu.SMEM),
            pl.BlockSpec((1, 1, tokens), lambda step: (step, 0, 0), memory_space=pltpu.SMEM),
            pl.BlockSpec(weights.shape, lambda step: (0, 0)),
        ],
        out_specs=pl.BlockSpec((rows, width, seq), lambda step: (step, 0, 0)),
        out_shape=jax.ShapeDtypeStruct((steps * rows, width, seq), low),
        scratch_shapes=[pltpu.VMEM((slab + 8, width), f32), pltpu.VMEM((tokens + 8, width), f32)],
        compiler_params=pltpu.CompilerParams(vmem_limit_bytes=48 << 20),
        name="lookup",
    )(counts, keys[:, None], weights)


def deposit_kernel(counts_ref, keys_ref, grads_ref, total_ref, squares_ref, rows_ref, *tables):
    width, slab = total_ref.shape
    rows, _, seq = grads_ref.shape
    shift = slab.bit_length()

    @pl.when(pl.program_id(0) == 0)
    def clear():
        for table in tables:
            table[...] = jnp.zeros_like(table)
        rows_ref[pl.ds(rows * seq, 8), :] = jnp.zeros((8, width), f32)

    for row in range(rows):
        for first in range(0, seq, BLOCK):
            at = row * seq + first
            rows_ref[at : at + BLOCK, :] = turn(grads_ref[row, :, first : first + BLOCK])

    def step(index, carry):
        for offset in range(0, UNROLL, len(tables)):
            keys = [keys_ref[0, 0, index * UNROLL + offset + part] for part in range(len(tables))]
            spots = [key & ((1 << shift) - 1) for key in keys]
            sums = [
                table[pl.ds(spot, 1), :] + rows_ref[pl.ds(key >> shift, 1), :]
                for key, spot, table in zip(keys, spots, tables)
            ]
            for spot, table, value in zip(spots, tables, sums):
                table[pl.ds(spot, 1), :] = value
        return carry

    lax.fori_loop(0, pl.cdiv(counts_ref[pl.program_id(0)], UNROLL), step, 0)

    @pl.when(pl.program_id(0) == pl.num_programs(0) - 1)
    def finish():
        squares_ref[...] = jnp.zeros_like(squares_ref)

        def step(index, carry):
            first = pl.multiple_of(index * 9 * BLOCK, BLOCK)
            squares = jnp.zeros((width, BLOCK), f32)
            for part in range(9):
                at = pl.ds(first + part * BLOCK, BLOCK)
                block = sum(table[at, :] for table in tables).T
                total_ref[:, at] = block
                squares += block * block
            squares_ref[...] += squares
            return carry

        lax.fori_loop(0, slab // (9 * BLOCK), step, 0)


def deposit(counts, keys, grads, slab):
    steps, tokens = keys.shape
    _, width, seq = grads.shape
    rows = tokens // seq
    return pl.pallas_call(
        deposit_kernel,
        grid=(steps,),
        in_specs=[
            pl.BlockSpec(memory_space=pltpu.SMEM),
            pl.BlockSpec((1, 1, tokens), lambda step: (step, 0, 0), memory_space=pltpu.SMEM),
            pl.BlockSpec((rows, width, seq), lambda step: (step, 0, 0)),
        ],
        out_specs=[
            pl.BlockSpec((width, slab), lambda step: (0, 0)),
            pl.BlockSpec((width, BLOCK), lambda step: (0, 0)),
        ],
        out_shape=[
            jax.ShapeDtypeStruct((width, slab), f32),
            jax.ShapeDtypeStruct((width, BLOCK), f32),
        ],
        scratch_shapes=[pltpu.VMEM((tokens + 8, width), f32)]
        + [pltpu.VMEM((slab + 8, width), f32)] * TABLES,
        compiler_params=pltpu.CompilerParams(vmem_limit_bytes=60 << 20),
        name="deposit",
    )(counts, keys[:, None], grads)


def whiten(values):
    center = values - jnp.mean(values, -1, keepdims=True)
    rate = lax.rsqrt(jnp.mean(center * center, -1, keepdims=True) + layer_eps)
    return center * rate, rate


def unwhiten(upstream, gain, white, rate):
    scaled = upstream * gain
    inner = jnp.mean(scaled, -1, keepdims=True)
    along = jnp.mean(scaled * white, -1, keepdims=True)
    return (
        rate * (scaled - inner - white * along),
        jnp.sum(upstream * white, 0, keepdims=True),
        jnp.sum(upstream, 0, keepdims=True),
    )


def selection(length, entries):
    rows = lax.broadcasted_iota(jnp.int32, (2 * length, entries), 0)
    columns = lax.broadcasted_iota(jnp.int32, (2 * length, entries), 1)
    return (jnp.clip(length + entries // 2 - rows, 0, entries - 1) == columns).astype(f32).astype(low)


def prepare_kernel(*refs, between=lambda group: None):
    weights_ref, words_ref, vec_ref, white_ref, rate_ref, qkv_ref = refs[:6]
    rel_white_ref, rel_rate_ref, table_ref, low_ref, rel_ref = refs[6:]
    groups, model = weights_ref.shape[:2]
    seq = words_ref.shape[1]
    part = rel_ref.shape[0] // groups
    width = qkv_ref.shape[2] // 3
    terms = turn(weights_ref[0, :, 4 * BLOCK : 5 * BLOCK])
    half = BLOCK // 2
    vec_ref[...] = terms[half : half + 16] + terms[half + 16 : half + 32] + terms[half + 32 : half + 48]
    for group in range(groups):
        rows = slice(group * part, (group + 1) * part)
        entries = turn(weights_ref[group, :, 5 * BLOCK : 6 * BLOCK]) + turn(
            weights_ref[group, :, 6 * BLOCK : 7 * BLOCK]
        )
        white, rate = whiten(entries)
        rel_white_ref[rows, :] = white
        rel_rate_ref[rows, :] = rate
        rel_ref[rows, :] = (white * vec_ref[2:3] + vec_ref[3:4]).astype(low)
    for first in range(0, seq, BLOCK):
        rows = slice(first, first + BLOCK)
        white, rate = whiten(turn(words_ref[:, rows]))
        white_ref[rows, :] = white
        rate_ref[rows, :] = rate
        low_ref[rows, :] = (white * vec_ref[0:1] + vec_ref[1:2]).astype(low)
    chosen = selection(seq, rel_ref.shape[0])

    def step(group, carry):
        between(group)
        qkv_ref[group] = dot_plain(low_ref[...], weights_ref[group, :, : 3 * width]).astype(low)
        keys = dot_plain(rel_ref[...], weights_ref[group, :, : 2 * width]).astype(low)
        table_ref[group] = dot_plain(chosen, keys).astype(low)
        return carry

    lax.fori_loop(0, groups, step, 0)


def prepared(weights, seq, width, entries):
    groups, model = weights.shape[:2]
    outputs = [
        jax.ShapeDtypeStruct((16, model), f32),
        jax.ShapeDtypeStruct((seq, model), f32),
        jax.ShapeDtypeStruct((seq, 1), f32),
        jax.ShapeDtypeStruct((groups, seq, 3 * width), low),
        jax.ShapeDtypeStruct((entries, model), f32),
        jax.ShapeDtypeStruct((entries, 1), f32),
        jax.ShapeDtypeStruct((groups, 2 * seq, 2 * width), low),
    ]
    return outputs, [pltpu.VMEM((seq, model), low), pltpu.VMEM((entries, model), low)]


def prepare(weights, words, width, entries):
    outputs, scratch = prepared(weights, words.shape[1], width, entries)
    return pl.pallas_call(
        prepare_kernel,
        in_specs=[IN_VMEM] * 2,
        out_specs=[IN_VMEM] * 7,
        out_shape=outputs,
        scratch_shapes=scratch,
        compiler_params=pltpu.CompilerParams(vmem_limit_bytes=56 << 20),
        name="prepare",
    )(weights, words)


GATHER_SLOTS = {
    1: (("line", 2),),
    4: (("line", 3), ("sides", 1)),
    8: (("sides", 2),),
    9: (("sides", 3), ("corners", 0)),
    11: (("corners", 1),),
}
GATHER_END = (("corners", 2), ("corners", 3), ("finish", 0))


def attend_gather_kernel(length_ref, weights_ref, words_ref, pack_ref, *refs):
    outputs, probs_ref, mixed_ref, all_ref = refs[:7], refs[7], refs[8], refs[9]
    low_ref, rel_ref, far_ref, *sems = refs[10:]
    qkv_ref, table_ref = outputs[3], outputs[6]
    groups, heads = qkv_ref.shape[0], far_ref.shape[0]
    spot = place()
    greet(*spot, True)
    start, steps = gather_stages(spot, pack_ref, all_ref, *sems)
    start()
    run_all(steps, (("line", 0),))

    def between(group):
        pl.when(group == 2)(lambda: run_all(steps, (("line", 1), ("sides", 0))))

    prepare_kernel(weights_ref, words_ref, *outputs, low_ref, rel_ref, between=between)

    def step(group, carry):
        for head in range(heads):
            attend_head(group, head, length_ref[0], qkv_ref, table_ref, probs_ref, mixed_ref, far_ref)
            for slot, timed in GATHER_SLOTS.items():
                if slot % heads == head:
                    pl.when(group == slot // heads)(functools.partial(run_all, steps, timed))
        return carry

    lax.fori_loop(0, groups, step, 0)
    run_all(steps, GATHER_END)


def attend_gather(length, weights, words, pack, width, entries, tag):
    groups = weights.shape[0]
    seq = words.shape[1]
    heads = width // HEAD_DIM
    outputs, scratch = prepared(weights, seq, width, entries)
    return pl.pallas_call(
        attend_gather_kernel,
        in_specs=[pl.BlockSpec(memory_space=pltpu.SMEM), IN_VMEM, IN_VMEM, ANYWHERE],
        out_specs=[IN_VMEM] * 9 + [ANYWHERE],
        out_shape=outputs
        + [
            jax.ShapeDtypeStruct((groups * heads, seq, seq), low),
            jax.ShapeDtypeStruct((groups, seq, width), low),
            jax.ShapeDtypeStruct((4, 8) + pack.shape, low),
        ],
        scratch_shapes=scratch + [pltpu.VMEM((heads, seq, seq), f32)] + gather_scratch(),
        compiler_params=pltpu.CompilerParams(
            collective_id=tag, has_side_effects=True, vmem_limit_bytes=56 << 20
        ),
        name="attend_gather",
    )(length, weights, words, pack)


def middle_kernel(
    weights_ref,
    vec_ref,
    white_ref,
    mixed_ref,
    marks_ref,
    contract_out,
    expand_out,
    joint_out,
    mixed_out,
    sum_out,
    vec_out,
    loss_out,
    combine_ref,
    readout_ref,
    slope_ref,
    acts_ref,
    mid_ref,
    mid_white_ref,
    out_white_ref,
    gate_ref,
):
    groups, model = weights_ref.shape[:2]
    seq = white_ref.shape[0]
    width = mixed_ref.shape[2]
    hidden = acts_ref.shape[2]
    vec = [vec_ref[row : row + 1] for row in range(11)]
    for group in range(groups):
        joint = weights_ref[group, :, 2 * hidden :]
        readout_ref[:, group * width : (group + 1) * width] = joint[:, :width]
        combine_ref[group] = joint[:, width:]
    total = white_ref[...] * vec[0] + vec[1]
    for group in range(groups):
        total += dot_rows(mixed_ref[group], combine_ref[group])
    mid_white, mid_rate = whiten(total)
    mid_white_ref[...] = mid_white
    hidden_mid = mid_white * vec[4] + vec[5]
    sum_out[...] = hidden_mid
    mid_ref[...] = hidden_mid.astype(low)

    def forward(group, carry):
        gate = dot_plain(mid_ref[...], weights_ref[group, :, :hidden])
        share = 0.5 + 0.5 * lax.erf(gate * 0.5**0.5)
        acts_ref[group] = (gate * share).astype(low)
        slope_ref[group] = share + gate * jnp.exp(-0.5 * gate * gate) * (2.0 * jnp.pi) ** -0.5
        sum_out[...] += dot_rows(acts_ref[group], weights_ref[group, :, hidden : 2 * hidden])
        return carry

    lax.fori_loop(0, groups, forward, 0)
    out_white, out_rate = whiten(sum_out[...])
    out_white_ref[...] = out_white
    gate_ref[...] = (out_white * vec[6] + vec[7]).astype(low)
    dense = dot_plain(gate_ref[...], readout_ref[...])
    share = 0.5 + 0.5 * lax.erf(dense * 0.5**0.5)
    slope = share + dense * jnp.exp(-0.5 * dense * dense) * (2.0 * jnp.pi) ** -0.5
    white, rate = whiten(dense * share)
    head = white * vec[8] + vec[9]
    logits = jnp.sum(head * vec[10], -1, keepdims=True)
    weight, flags = marks_ref[:, 0:1], marks_ref[:, 1:2]
    losses = jnp.maximum(logits, 0.0) + jnp.log1p(jnp.exp(-jnp.abs(logits))) - flags * logits
    loss_out[...] = jnp.where(weight > 0.0, losses, 0.0)
    pull = (1.0 / (1.0 + jnp.exp(-logits)) - flags) * weight
    vec_out[6:7, :] = jnp.sum(head * pull, 0, keepdims=True)
    upstream, vec_out[4:5, :], vec_out[5:6, :] = unwhiten(pull * vec[10], vec[8], white, rate)
    dense_low = (upstream * slope).astype(low)
    turned = gate_ref[...].astype(f32).T.astype(low)
    for group in range(groups):
        joint_out[group, :, :width] = dot_plain(
            turned, dense_low[:, group * width : (group + 1) * width]
        ).astype(low)
    upstream, vec_out[2:3, :], vec_out[3:4, :] = unwhiten(
        dot_rows(dense_low, readout_ref[...]), vec[6], out_white_ref[...], out_rate
    )
    sum_out[...] = upstream
    gate_ref[...] = upstream.astype(low)
    upstream_turned = upstream.T.astype(low)
    mid_turned = mid_ref[...].astype(f32).T.astype(low)

    def backward(group, carry):
        contract_out[group] = dot_plain(upstream_turned, acts_ref[group]).astype(low)
        acts_ref[group] = (
            dot_plain(gate_ref[...], weights_ref[group, :, hidden : 2 * hidden]) * slope_ref[group]
        ).astype(low)
        expand_out[group] = dot_plain(mid_turned, acts_ref[group]).astype(low)
        sum_out[...] += dot_rows(acts_ref[group], weights_ref[group, :, :hidden])
        return carry

    lax.fori_loop(0, groups, backward, 0)
    upstream, vec_out[0:1, :], vec_out[1:2, :] = unwhiten(
        sum_out[...], vec[4], mid_white_ref[...], mid_rate
    )
    vec_out[7:8, :] = jnp.zeros((1, model), f32)
    sum_out[...] = upstream
    gate_ref[...] = upstream.astype(low)
    turned = upstream.T.astype(low)
    for group in range(groups):
        mixed_out[group] = dot_plain(gate_ref[...], combine_ref[group]).astype(low)
        joint_out[group, :, width:] = dot_plain(turned, mixed_ref[group]).astype(low)


def middle(weights, vec, white, mixed, marks):
    groups, model = weights.shape[:2]
    seq, width = mixed.shape[1:]
    hidden = weights.shape[2] // 2 - width
    wide = pltpu.VMEM((seq, model), f32)
    outputs = [
        ((groups, model, hidden), low),
        ((groups, model, hidden), low),
        ((groups, model, 2 * width), low),
        ((groups, seq, width), low),
        ((seq, model), f32),
        ((8, model), f32),
        ((seq, 1), f32),
    ]
    return pl.pallas_call(
        middle_kernel,
        grid=(1,),
        in_specs=[
            pl.BlockSpec(
                array.shape,
                functools.partial(lambda rank, step: (0,) * rank, array.ndim),
                pipeline_mode=pl.Buffered(1),
            )
            for array in (weights, vec, white, mixed, marks)
        ],
        out_specs=[
            pl.BlockSpec(
                shape,
                functools.partial(lambda rank, step: (0,) * rank, len(shape)),
                pipeline_mode=pl.Buffered(1),
            )
            for shape, _ in outputs
        ],
        out_shape=[jax.ShapeDtypeStruct(*output) for output in outputs],
        scratch_shapes=[
            pltpu.VMEM((groups, model, width), low),
            pltpu.VMEM((model, model), low),
            pltpu.VMEM((groups, seq, hidden), f32),
            pltpu.VMEM((groups, seq, hidden), low),
            pltpu.VMEM((seq, model), low),
            wide,
            wide,
            pltpu.VMEM((seq, model), low),
        ],
        compiler_params=pltpu.CompilerParams(vmem_limit_bytes=60 << 20),
        name="middle",
    )(weights, vec, white, mixed, marks)


def project_back_kernel(
    weights_ref,
    vec_ref,
    white_ref,
    rate_ref,
    rel_white_ref,
    rel_rate_ref,
    sum_ref,
    grads_ref,
    tables_ref,
    vec_grads_ref,
    words_out,
    project_out,
    total_ref,
    fold_ref,
    between=lambda point: None,
):
    groups, model = weights_ref.shape[:2]
    seq = white_ref.shape[0]
    width = grads_ref.shape[2] // 3
    entries = rel_white_ref.shape[0]
    part = entries // groups
    vec = [vec_ref[row : row + 1] for row in range(4)]
    turned = (white_ref[...] * vec[0] + vec[1]).T.astype(low)
    rel_turned = (rel_white_ref[...] * vec[2] + vec[3]).T.astype(low)
    chosen = selection(seq, entries)
    total_ref[...] = sum_ref[...]
    between(-1)
    rel_total = jnp.zeros((entries, model), f32)
    for group in range(groups):
        fold_ref[...] = dot_left(chosen, tables_ref[group]).astype(low)
        total_ref[...] += dot_rows(grads_ref[group], weights_ref[group, :, : 3 * width])
        rel_total += dot_rows(fold_ref[...], weights_ref[group, :, : 2 * width])
        project_out[group, :, : 2 * width] = (
            dot_plain(turned, grads_ref[group, :, : 2 * width]) + dot_plain(rel_turned, fold_ref[...])
        ).astype(low)
        project_out[group, :, 2 * width : 3 * width] = dot_plain(
            turned, grads_ref[group, :, 2 * width :]
        ).astype(low)
        between(group)
    upstream, gain_grad, bias_grad = unwhiten(total_ref[...], vec[0], white_ref[...], rate_ref[...])
    words_out[...] = upstream.T.astype(low)
    between(groups)
    rel_up, rel_gain_grad, rel_bias_grad = unwhiten(
        rel_total, vec[2], rel_white_ref[...], rel_rate_ref[...]
    )
    turned = rel_up.T.astype(low)
    for group in range(groups):
        project_out[group, :, 3 * width + BLOCK // 2 :] = turned[:, group * part : (group + 1) * part]
    rows = [gain_grad, bias_grad, rel_gain_grad, rel_bias_grad]
    rows += [vec_grads_ref[row : row + 1] for row in range(7)]
    rows += [jnp.zeros((1, model), f32)]
    for group in range(groups):
        three = jnp.concatenate(rows[3 * group : 3 * group + 3] + [jnp.zeros((BLOCK - 3, model), f32)], 0)
        project_out[group, :, 3 * width : 3 * width + BLOCK // 2] = three.T.astype(low)[:, : BLOCK // 2]


def projected_back(weights, white, grads, rel_white):
    groups, model = weights.shape[:2]
    seq = white.shape[0]
    width = grads.shape[2] // 3
    entries = rel_white.shape[0]
    outputs = [
        jax.ShapeDtypeStruct((model, seq), low),
        jax.ShapeDtypeStruct((groups, model, 3 * width + BLOCK // 2 + entries // groups), low),
    ]
    return outputs, [pltpu.VMEM((seq, model), f32), pltpu.VMEM((entries, 2 * width), low)]


def project_back(weights, vec, white, rate, rel_white, rel_rate, total, grads, tables, vec_grads):
    outputs, scratch = projected_back(weights, white, grads, rel_white)
    return pl.pallas_call(
        project_back_kernel,
        in_specs=[IN_VMEM] * 10,
        out_specs=[IN_VMEM] * 2,
        out_shape=outputs,
        scratch_shapes=scratch,
        compiler_params=pltpu.CompilerParams(vmem_limit_bytes=56 << 20),
        name="project_back",
    )(weights, vec, white, rate, rel_white, rel_rate, total, grads, tables, vec_grads)


PROJECT_STEPS = {
    -1: ("pair",),
    1: ("first",),
    2: ("second", "line0"),
    3: ("line1",),
    4: ("line2",),
}


def project_back_sums_kernel(count, chunks, *refs):
    inputs, grads = refs[:10], refs[10 : 10 + count]
    outputs, totals = refs[10 + count : 12 + count], refs[12 + count : 12 + 2 * count]
    work, rest = refs[12 + 2 * count : 14 + 2 * count], refs[14 + 2 * count :]
    spot = place()
    greet(*spot, True)
    start, stages = sum_stages(spot, grads, totals, chunks, rest)
    start()

    def between(point):
        for name in PROJECT_STEPS.get(point, ()):
            run_all(stages, [(name, chunk) for chunk in range(len(chunks))])

    project_back_kernel(*inputs, *outputs, *work, between=between)
    run_all(stages, [("total", chunk) for chunk in range(len(chunks))])


def project_back_sums(*inputs, grads, tag):
    weights, white, rel_white, upstream = inputs[0], inputs[2], inputs[4], inputs[7]
    outputs, scratch = projected_back(weights, white, upstream, rel_white)
    part = grads[0].shape[1] // 8
    sizes = [grad.shape[2] for grad in grads]
    chunks = chunked(sizes)
    return pl.pallas_call(
        functools.partial(project_back_sums_kernel, len(grads), chunks),
        in_specs=[IN_VMEM] * 10 + [ANYWHERE] * len(grads),
        out_specs=[IN_VMEM] * (2 + len(grads)),
        out_shape=outputs + [jax.ShapeDtypeStruct((part, size), f32) for size in sizes],
        scratch_shapes=scratch + sum_scratch(part, [chunk[2] for chunk in chunks]),
        compiler_params=pltpu.CompilerParams(
            collective_id=tag, has_side_effects=True, vmem_limit_bytes=56 << 20
        ),
        name="project_back_sums",
    )(*inputs, *[grad.reshape(4, 4, 2, part, -1) for grad in grads])


def split_terms(values, count):
    terms = []
    for _ in range(count):
        term = lax.reduce_precision(values, 8, 7)
        terms.append(term.astype(low))
        values = values - term
    return terms


def adamw(weight, gradient, mean, square, rate_now):
    first = beta_first * mean + (1.0 - beta_first) * gradient
    second = beta_second * square + (1.0 - beta_second) * gradient * gradient
    mean_hat = first / (1.0 - beta_first**STEP)
    square_hat = second / (1.0 - beta_second**STEP)
    master = weight - rate_now * (
        mean_hat / (jnp.sqrt(square_hat) + adam_eps) + weight_decay * weight
    )
    return (first, second, master)


def update_kernel(width, *refs):
    facts_ref, shared_ref, *grads = refs[:7]
    weights, refs = refs[7:31], refs[31:]
    outputs, (factor_ref, bias_ref) = refs[:24], refs[24:26]
    squares = jnp.sum(facts_ref[0:1, :], 1, keepdims=True)
    factor = jnp.minimum(1.0, clip_level / jnp.sqrt(squares))

    def update(index, spot, gradient):
        weight, mean, square = [part.at[spot] for part in weights[3 * index : 3 * index + 3]]
        results = adamw(
            weight[...], gradient * factor, mean[...], square[...], rate_steps[index]
        )
        for part, value in zip(outputs[3 * index : 3 * index + 3], results):
            part.at[spot][...] = value

    everything = slice(None)
    update(0, (everything, everything), grads[0][...])

    @pl.when(pl.program_id(0) == 0)
    def small():
        contract, expand, joint, project = grads[1:]
        factor_ref[...] = jnp.broadcast_to(jnp.sqrt(squares), factor_ref.shape)
        for group in range(4):
            part = slice(group * BLOCK, (group + 1) * BLOCK)
            update(1, (everything, part), shared_ref[group, :, width + BLOCK // 2 :])
            part = slice(group * width, (group + 1) * width)
            update(6, (everything, part), shared_ref[group, :, :width])
        for kind in range(3):
            part = slice(kind * width, (kind + 1) * width)
            update(2, (kind,), project[:, part])
        update(3, (everything, everything), joint[:, width:].T)
        update(4, (everything, everything), expand[...])
        update(5, (everything, everything), contract[...])
        count = weights[21].shape[0]
        for group in range(4):
            rows = shared_ref[group, :, BLOCK : 2 * BLOCK].T[BLOCK // 2 :]
            first = 3 * group
            last = min(first + 3, count)
            update(7, (slice(first, last), everything), rows[: last - first])
            if group == 1:
                bias_ref[...] = rows[0:1] * factor


def update_all(facts, shared, grads, weights, width):
    rows, slab = grads[0].shape
    columns = 11 * BLOCK
    stripe = pl.BlockSpec((rows, columns), lambda step: (0, step))

    def full(array):
        return pl.BlockSpec(array.shape, functools.partial(lambda rank, step: (0,) * rank, array.ndim))

    in_specs = [full(facts), full(shared), stripe] + [full(grad) for grad in grads[1:]]
    in_specs += [stripe] * 3 + [full(weight) for weight in weights[3:]]
    results = [jax.ShapeDtypeStruct(weight.shape, f32) for weight in weights]
    results += [jax.ShapeDtypeStruct((1, BLOCK), f32), jax.ShapeDtypeStruct((1, rows), f32)]
    return pl.pallas_call(
        functools.partial(update_kernel, width),
        grid=(slab // columns,),
        in_specs=in_specs,
        out_specs=[stripe] * 3 + [full(result) for result in results[3:]],
        out_shape=results,
        compiler_params=pltpu.CompilerParams(vmem_limit_bytes=62 << 20),
        name="update_all",
    )(facts, shared, *grads, *weights)


def per_device(
    token_ids,
    row_lengths,
    replaced,
    embedding,
    relative,
    project,
    combine,
    expand,
    contract,
    readout,
    vectors,
    embedding_mean,
    relative_mean,
    project_mean,
    combine_mean,
    expand_mean,
    contract_mean,
    readout_mean,
    vectors_mean,
    embedding_square,
    relative_square,
    project_square,
    combine_square,
    expand_square,
    contract_square,
    readout_square,
    vectors_square,
):
    pieces = lax.axis_size("heads")
    holder = lax.axis_index("heads")
    owners = lax.axis_size("dp")
    row_count, seq_len = token_ids.shape
    width = vectors.shape[1]
    model = width * owners
    everyone = ("heads", "dp")
    head_width = project.shape[2]
    hidden = expand.shape[1]
    vocab_slab = embedding.shape[1]
    span_part = relative.shape[0] // pieces
    vector_count = vectors.shape[0]
    direct = owners == 8 and pieces == 4

    own_relative = lax.dynamic_slice_in_dim(relative, holder * span_part, span_part, 0).T
    own_readout = lax.dynamic_slice_in_dim(readout, holder * head_width, head_width, 1)
    vector_terms = [
        jnp.pad(term, ((0, 0), (0, 16 - vector_count))) for term in split_terms(vectors.T, 3)
    ]
    high, rest = split_terms(own_relative, 2)
    first_pack = jnp.concatenate(
        [
            project.reshape(width, 3 * head_width).astype(low),
            *vector_terms,
            jnp.zeros((width, 16), low),
            high,
            rest,
        ],
        1,
    )
    second_pack = jnp.concatenate(
        [
            expand.astype(low),
            contract.T.astype(low),
            own_readout.astype(low),
            combine.T.astype(low),
        ],
        1,
    )
    first_all = lax.all_gather(first_pack, everyone, axis=0, tiled=True)
    first_all = first_all.reshape(pieces, model, -1)

    length_row = jnp.pad(row_lengths[None, :], ((0, 0), (0, seq_len - row_count)))
    facts = jnp.concatenate([token_ids, jnp.pad(length_row, ((0, 8 - 1 - row_count), (0, 0)))], 0)
    all_facts = share_facts(facts, 1) if direct else lax.all_gather(facts, "dp")
    all_ids = all_facts[:, :row_count].reshape(owners * row_count, seq_len)
    all_lengths = all_facts[:, row_count, :row_count].reshape(-1)
    token_total = jnp.sum(all_lengths).astype(f32)
    local_ids = all_ids - holder * vocab_slab
    inside = (local_ids >= 0) & (local_ids < vocab_slab)
    inside = inside & (jnp.arange(seq_len)[None] < all_lengths[:, None])
    inside = inside.reshape(-1, ROW_SET * seq_len)
    counts = jnp.sum(inside.astype(jnp.int32), 1)
    shift = vocab_slab.bit_length()
    keys = jnp.arange(ROW_SET * seq_len, dtype=jnp.int32)[None] << shift
    keys = jnp.where(
        inside,
        keys + local_ids.reshape(inside.shape),
        ((ROW_SET * seq_len) << shift) + vocab_slab,
    )
    keys = lax.sort(keys.T, dimension=0, is_stable=False).T

    found = lookup(counts, keys, embedding, seq_len)
    found = found.reshape(owners, row_count, width, seq_len)
    if direct:
        found = exchange_words(found, 2)
    else:
        found = lax.psum_scatter(found, "heads", scatter_dimension=1, tiled=True)[:, 0]
        found = lax.all_to_all(found, "dp", 0, 0, tiled=True)
    own_length = lax.dynamic_slice_in_dim(row_lengths, holder, 1)
    own_live = jnp.arange(seq_len) < own_length
    own_flags = lax.dynamic_slice_in_dim(replaced, holder, 1)[0].astype(f32)
    marks = jnp.stack([jnp.where(own_live, 1.0 / token_total, 0.0), own_flags], 1)

    entries = relative.shape[0]
    words = found.reshape(model, seq_len)
    if direct:
        *ready, probs, mixed, second_all = attend_gather(
            own_length, first_all, words, second_pack, head_width, entries, 3
        )
    else:
        ready = prepare(first_all, words, head_width, entries)
        probs, mixed = attend(own_length, ready[3], ready[6])
        second_all = lax.all_gather(second_pack, everyone, axis=0, tiled=True)
    vec_full, white, rate, qkv, rel_white, rel_rate, rel_table = ready
    second_all = second_all.reshape(pieces, model, -1)
    grad_contract, grad_expand, grad_joint, grad_mixed, grad_sum, grad_vec, losses = middle(
        second_all, vec_full, white, mixed, marks
    )
    back = (first_all, vec_full, white, rate, rel_white, rel_rate, grad_sum)
    if direct:
        qkv_grads, rel_table_grads, *sums = attend_back_sums(
            qkv, rel_table, probs, grad_mixed, [grad_contract, grad_expand], 4
        )
        sent, grad_project, joint_sum = project_back_sums(
            *back, qkv_grads, rel_table_grads, grad_vec, grads=[grad_joint], tag=7
        )
        sums.append(joint_sum)
    else:
        qkv_grads, rel_table_grads = attend_back(qkv, rel_table, probs, grad_mixed)
        sent, grad_project = project_back(*back, qkv_grads, rel_table_grads, grad_vec)
    sent = sent.reshape(owners, width, seq_len)
    if direct:
        sent, late_sum = return_sums(sent, grad_project, 5)
        sums.append(late_sum)
    else:
        sent = lax.all_to_all(sent, "dp", 0, 0, tiled=True)
        sent = lax.all_gather(sent, "heads", axis=0)
        sent = sent.transpose(1, 0, 2, 3)
        sums = [
            lax.psum_scatter(
                part.reshape(pieces * model, -1), everyone, scatter_dimension=0, tiled=True
            ).astype(f32)
            for part in (grad_contract, grad_expand, grad_joint, grad_project)
        ]
    sent = sent.reshape(owners * row_count, width, seq_len)
    grad_embedding, own_squares = deposit(counts, keys, sent, vocab_slab)

    weights = (embedding, relative, project, combine, expand, contract, readout, vectors)
    means = (
        embedding_mean,
        relative_mean,
        project_mean,
        combine_mean,
        expand_mean,
        contract_mean,
        readout_mean,
        vectors_mean,
    )
    squares = (
        embedding_square,
        relative_square,
        project_square,
        combine_square,
        expand_square,
        contract_square,
        readout_square,
        vectors_square,
    )
    if direct:
        turns = {1: (1, 0), 2: (1, 0, 2), 5: (1, 0)}
        flat = [
            part.transpose(turns[index]) if index in turns else part
            for index, parts in enumerate(zip(weights, means, squares))
            for part in parts
        ]
        all_facts, shared = finish_sums(losses, own_squares, sums, head_width, 6)
        *flat, norm_row, bias_row = update_all(
            all_facts, shared, [grad_embedding, *sums], flat, head_width
        )
        flat = [
            part.transpose(turns[index // 3]) if index // 3 in turns else part
            for index, part in enumerate(flat)
        ]
        return (all_facts[1, 0], token_total, norm_row[0, 0], *flat, bias_row[0])

    squares_local = sum(jnp.sum(part * part) for part in sums) + jnp.sum(own_squares)
    shared = jnp.concatenate([sums[2][:, :head_width], sums[3][:, 3 * head_width :]], 1)
    squares_total, loss_sum = lax.psum((squares_local, jnp.sum(losses)), everyone)
    shared = lax.all_gather(shared, "heads", axis=0)
    grad_norm = jnp.sqrt(squares_total)
    factor = jnp.minimum(1.0, clip_level / grad_norm)
    grad_readout = shared[:, :, :head_width].transpose(1, 0, 2).reshape(width, model)
    at = head_width + BLOCK // 2
    grad_relative = shared[:, :, at:].transpose(0, 2, 1).reshape(entries, width)
    grad_vec = shared[:, :, head_width : head_width + 3].transpose(0, 2, 1).reshape(-1, width)
    grad_vec = grad_vec[:vector_count]
    gradients = (
        grad_embedding,
        grad_relative,
        sums[3][:, : 3 * head_width].reshape(width, 3, head_width),
        sums[2][:, head_width:].T,
        sums[1],
        sums[0].T,
        grad_readout,
        grad_vec,
    )
    updates = [
        adamw(weight, gradient * factor, mean, square, rate_now)
        for weight, gradient, mean, square, rate_now in zip(
            weights, gradients, means, squares, rate_steps
        )
    ]
    flat = [part for parts in updates for part in parts]
    return (loss_sum, token_total, grad_norm, *flat, grad_vec[3] * factor)


def solution(mesh):
    placed = (
        P("dp", None),
        P("dp"),
        P("dp", None),
        P("dp", "heads"),
        P(None, "dp"),
        P("dp", None, "heads"),
        P("heads", "dp"),
        P("dp", "heads"),
        P("heads", "dp"),
        P("dp", None),
        P(None, "dp"),
        P("dp", "heads"),
        P(None, "dp"),
        P("dp", None, "heads"),
        P("heads", "dp"),
        P("dp", "heads"),
        P("heads", "dp"),
        P("dp", None),
        P(None, "dp"),
        P("dp", "heads"),
        P(None, "dp"),
        P("dp", None, "heads"),
        P("heads", "dp"),
        P("dp", "heads"),
        P("heads", "dp"),
        P("dp", None),
        P(None, "dp"),
    )
    return jax.shard_map(
        per_device,
        mesh=mesh,
        in_specs=placed,
        out_specs=(
            P(),
            P(),
            P(),
            P("dp", "heads"),
            P("dp", "heads"),
            P("dp", "heads"),
            P(None, "dp"),
            P(None, "dp"),
            P(None, "dp"),
            P("dp", None, "heads"),
            P("dp", None, "heads"),
            P("dp", None, "heads"),
            P("heads", "dp"),
            P("heads", "dp"),
            P("heads", "dp"),
            P("dp", "heads"),
            P("dp", "heads"),
            P("dp", "heads"),
            P("heads", "dp"),
            P("heads", "dp"),
            P("heads", "dp"),
            P("dp", None),
            P("dp", None),
            P("dp", None),
            P(None, "dp"),
            P(None, "dp"),
            P(None, "dp"),
            P("dp"),
        ),
        check_vma=False,
    )
```

```python
import functools

import jax
import jax.numpy as jnp
from jax import lax
from jax.experimental import pallas as pl
from jax.experimental.pallas import tpu as pltpu
from jax.sharding import PartitionSpec as P

HEAD_DIM = 64
STEP = 10
BLOCK = 128
UNROLL = 16
ROW_SET = 8

low = jnp.bfloat16
f32 = jnp.float32

layer_eps = 1e-07
clip_level = 0.005
rate_steps = (0.1, 0.05, 0.05, 0.05, 0.05, 0.05, 0.05, 1.0)
beta_first = 0.9
beta_second = 0.999
adam_eps = 1e-08
weight_decay = 0.01


def dot_rows(a,b):
    return lax.dot_general(a,b,(((1,),(1,)),((),())),preferred_element_type=f32)
def dot_plain(a,b):
    return lax.dot_general(a,b,(((1,),(0,)),((),())),preferred_element_type=f32)
def dot_left(a,b):
    return lax.dot_general(a,b,(((0,),(0,)),((),())),preferred_element_type=f32)

def attend_head(group, head, length, qkv_ref, table_ref, probs_ref, mixed_ref, far_ref):
    seq = qkv_ref.shape[1]
    width = qkv_ref.shape[2] // 3
    heads = width // HEAD_DIM
    scale = (3 * HEAD_DIM) ** -0.5
    live = lax.broadcasted_iota(jnp.int32, (BLOCK, seq), 1) < length
    at = head * HEAD_DIM
    q = qkv_ref[group, :, at : at + HEAD_DIM]
    k = qkv_ref[group, :, width + at : width + at + HEAD_DIM]
    v = qkv_ref[group, :, 2 * width + at : 2 * width + at + HEAD_DIM]
    for block in range(seq // BLOCK):
        rows = slice(block * BLOCK, (block + 1) * BLOCK)
        window = slice(seq - BLOCK * (block + 1), 2 * seq - BLOCK * block)
        far = dot_rows(k[rows], table_ref[group, window, at : at + HEAD_DIM])
        far = pltpu.roll(far, seq, 1, stride=1, stride_axis=0)[:, :seq]
        far_ref[head, :, rows] = far.T
    for block in range(seq // BLOCK):
        rows = slice(block * BLOCK, (block + 1) * BLOCK)
        window = slice(seq - BLOCK * (block + 1), 2 * seq - BLOCK * block)
        near = dot_rows(q[rows], table_ref[group, window, width + at : width + at + HEAD_DIM])
        near = pltpu.roll(near, seq, 1, stride=1, stride_axis=0)[:, :seq]
        scores = (dot_rows(q[rows], k) + near + far_ref[head, rows, :]) * scale
        scores = jnp.where(live, scores, -1e9)
        top = jnp.max(scores, -1, keepdims=True)
        expo = jnp.exp(scores - top)
        probs = (expo * (1.0 / jnp.sum(expo, -1, keepdims=True))).astype(low)
        probs_ref[group * heads + head, rows, :] = probs
        mixed_ref[group, rows, at : at + HEAD_DIM] = dot_plain(probs, v).astype(low)


def attend_kernel(length_ref, qkv_ref, table_ref, probs_ref, mixed_ref, far_ref):
    for head in range(far_ref.shape[0]):
        attend_head(0, head, length_ref[0], qkv_ref, table_ref, probs_ref, mixed_ref, far_ref)


def attend(length, qkv, table):
    groups, seq, width3 = qkv.shape
    width = width3 // 3
    heads = width // HEAD_DIM
    return pl.pallas_call(
        attend_kernel,
        grid=(groups,),
        in_specs=[
            pl.BlockSpec(memory_space=pltpu.SMEM),
            pl.BlockSpec((1, seq, width3), lambda g: (g, 0, 0)),
            pl.BlockSpec((1, 2 * seq, 2 * width), lambda g: (g, 0, 0)),
        ],
        out_specs=[
            pl.BlockSpec((heads, seq, seq), lambda g: (g, 0, 0)),
            pl.BlockSpec((1, seq, width), lambda g: (g, 0, 0)),
        ],
        out_shape=[
            jax.ShapeDtypeStruct((groups * heads, seq, seq), low),
            jax.ShapeDtypeStruct((groups, seq, width), low),
        ],
        scratch_shapes=[pltpu.VMEM((heads, seq, seq), f32)],
        compiler_params=pltpu.CompilerParams(vmem_limit_bytes=48 << 20),
        name="attend",
    )(length, qkv, table)


def attend_back_head(
    group, head, qkv_ref, table_ref, probs_ref, up_ref, grad_ref, rel_ref, low_ref, sum_ref
):
    seq = qkv_ref.shape[1]
    width = qkv_ref.shape[2] // 3
    heads = width // HEAD_DIM
    scale = (3 * HEAD_DIM) ** -0.5
    row = lax.broadcasted_iota(jnp.int32, (BLOCK, BLOCK), 0)
    flip = row + lax.broadcasted_iota(jnp.int32, (BLOCK, BLOCK), 1) == BLOCK - 1
    flip = flip.astype(f32).astype(low)
    edge = jnp.zeros((BLOCK, BLOCK), f32)

    def shear(rows):
        return pltpu.roll(jnp.concatenate([rows, edge], 1), 1, 1, stride=1, stride_axis=0).astype(low)

    at = head * HEAD_DIM
    q = qkv_ref[group, :, at : at + HEAD_DIM]
    k = qkv_ref[group, :, width + at : width + at + HEAD_DIM]
    v = qkv_ref[group, :, 2 * width + at : 2 * width + at + HEAD_DIM]
    up = up_ref[group, :, at : at + HEAD_DIM]
    source = group * heads + head
    for block in range(seq // BLOCK):
        rows = slice(block * BLOCK, (block + 1) * BLOCK)
        probs = probs_ref[source, rows, :].astype(f32)
        pull = dot_rows(up[rows], v)
        inner = jnp.sum(probs * pull, -1, keepdims=True)
        low_ref[head, rows, :] = (probs * (pull - inner) * scale).astype(low)
    grad_v = dot_left(up, probs_ref[source]).T.astype(low)
    grad_ref[group, :, 2 * width + at : 2 * width + at + HEAD_DIM] = grad_v
    sum_ref[2 * head] = jnp.zeros(sum_ref.shape[1:], f32)
    sum_ref[2 * head + 1] = jnp.zeros(sum_ref.shape[1:], f32)
    for block in range(seq // BLOCK):
        rows = slice(block * BLOCK, (block + 1) * BLOCK)
        window = slice(seq - BLOCK * (block + 1), 2 * seq - BLOCK * block)
        turned = dot_plain(flip, low_ref[head, rows, :])
        near = shear(turned)
        grad_q = dot_plain(turned.astype(low), k) + dot_plain(
            near, table_ref[group, window, width + at : width + at + HEAD_DIM]
        )
        grad_ref[group, rows, at : at + HEAD_DIM] = dot_plain(flip, grad_q.astype(low)).astype(low)
        q_turned = dot_plain(flip, q[rows]).astype(low)
        sum_ref[2 * head + 1, :, window] += dot_left(q_turned, near)
        turned = dot_rows(flip, low_ref[head, :, rows])
        far = shear(turned)
        grad_k = dot_plain(turned.astype(low), q) + dot_plain(
            far, table_ref[group, window, at : at + HEAD_DIM]
        )
        grad_ref[group, rows, width + at : width + at + HEAD_DIM] = dot_plain(
            flip, grad_k.astype(low)
        ).astype(low)
        k_turned = dot_plain(flip, k[rows]).astype(low)
        sum_ref[2 * head, :, window] += dot_left(k_turned, far)
    rel_ref[group, :, at : at + HEAD_DIM] = sum_ref[2 * head].T.astype(low)
    rel_ref[group, :, width + at : width + at + HEAD_DIM] = sum_ref[2 * head + 1].T.astype(low)


def attend_back_kernel(*refs):
    for head in range(refs[-2].shape[0]):
        attend_back_head(0, head, *refs)


def attend_back(qkv, table, probs, up):
    groups, seq, width3 = qkv.shape
    width = width3 // 3
    heads = width // HEAD_DIM
    block = lambda *shape: pl.BlockSpec(shape, lambda g: (g, 0, 0))
    return pl.pallas_call(
        attend_back_kernel,
        grid=(groups,),
        in_specs=[
            block(1, seq, width3),
            block(1, 2 * seq, 2 * width),
            block(heads, seq, seq),
            block(1, seq, width),
        ],
        out_specs=[block(1, seq, width3), block(1, 2 * seq, 2 * width)],
        out_shape=[
            jax.ShapeDtypeStruct((groups, seq, width3), low),
            jax.ShapeDtypeStruct((groups, 2 * seq, 2 * width), low),
        ],
        scratch_shapes=[
            pltpu.VMEM((heads, seq, seq), low),
            pltpu.VMEM((2 * heads, HEAD_DIM, 2 * seq), f32),
        ],
        compiler_params=pltpu.CompilerParams(vmem_limit_bytes=48 << 20),
        name="attend_back",
    )(qkv, table, probs, up)


MESH = pl.DeviceIdType.MESH
ANYWHERE = pl.BlockSpec(memory_space=pl.ANY)
IN_VMEM = pl.BlockSpec(memory_space=pltpu.VMEM)


def place():
    owner, holder = lax.axis_index("dp"), lax.axis_index("heads")
    return owner // 2, owner % 2, holder // 2, holder % 2


def device(z, x, y, c):
    return (z * 2 + x, y * 2 + c)


def signal(target):
    pl.semaphore_signal(
        pltpu.get_barrier_semaphore(), inc=1, device_id=target, device_id_type=MESH
    )


def along_z(z):
    return [(z + step) % 4 for step in (2, 1, 3)]


def greet(z, x, y, c, line):
    signal(device(z, x, y, 1 - c))
    signal(device(z, x, 1 - y, c))
    if line:
        signal(device(z, 1 - x, y, c))
        for other in along_z(z):
            signal(device(other, x, y, c))
        pl.semaphore_wait(pltpu.get_barrier_semaphore(), 6)


def remote(source, target, send, recv, to):
    return pltpu.make_async_remote_copy(
        src_ref=source, dst_ref=target, send_sem=send, recv_sem=recv, device_id=to, device_id_type=MESH
    )


def sum_scratch(width, sizes):
    half = width // 2
    leads = (
        (2, 4, 2, width),
        (2, 4, 2, width),
        (4, 2, half),
        (2, 4, half),
        (4, half),
        (4, half),
        (4, width),
    )
    shapes = [pltpu.VMEM(lead + (size,), low) for lead in leads for size in sizes]
    count = len(sizes)
    return shapes + [
        pltpu.SemaphoreType.DMA((count, 2)),
        pltpu.SemaphoreType.DMA((count, 9)),
        pltpu.SemaphoreType.DMA((count, 10)),
    ]


def sum_stages(spot, grads, totals, chunks, refs):
    count = len(chunks)
    pair, own, first_a, first_b, second_a, second_b, column = [
        refs[count * part : count * (part + 1)] for part in range(7)
    ]
    local_sem, send_sem, recv_sem = refs[7 * count :]
    z, x, y, c = spot
    half = grads[0].shape[3] // 2
    upper, lower = pl.ds(0, half), pl.ds(half, half)
    core_to, y_to, x_to = device(z, x, y, 1 - c), device(z, x, 1 - y, c), device(z, 1 - x, y, c)

    def columns(part):
        return pl.ds(chunks[part][1], chunks[part][2])

    def source(part, row):
        return grads[chunks[part][0]].at[row, :, :, :, columns(part)]

    def link(part, slot, source, target, to):
        return remote(source, target, send_sem.at[part, slot], recv_sem.at[part, slot], to)

    def local(part, side):
        return pltpu.make_async_copy(
            source(part, side * 2 + c), own[part].at[side], local_sem.at[part, side]
        )

    def pair_copy(part, side):
        return link(part, side, source(part, side * 2 + 1 - c), pair[part].at[side], core_to)

    def first_copies(part):
        block = own[part]
        return (
            link(part, 2, block.at[1 - y, :, :, upper], first_a[part], y_to),
            link(part, 3, block.at[:, :, 1 - x, lower], first_b[part], x_to),
        )

    def second_copies(part):
        block = own[part]
        return (
            link(part, 4, block.at[y, :, 1 - x, upper], second_a[part], x_to),
            link(part, 5, block.at[1 - y, :, x, lower], second_b[part], y_to),
        )

    def line_copy(part, step, to):
        return remote(
            own[part].at[y, to, x],
            column[part].at[z],
            send_sem.at[part, 6 + step],
            recv_sem.at[part, 6 + z],
            device(to, x, y, c),
        )

    def line_arrival(part, step, source):
        return remote(
            own[part].at[y, z, x],
            column[part].at[source],
            send_sem.at[part, 6 + step],
            recv_sem.at[part, 6 + source],
            device(source, x, y, c),
        )

    def add(target, source):
        target[...] = (target[...].astype(f32) + source[...].astype(f32)).astype(low)

    def start_pair(part):
        for side in range(2):
            pair_copy(part, side).start()
            local(part, side).start()

    def stage_pair(part):
        for side in range(2):
            local(part, side).wait()
            pair_copy(part, side).wait()
        if part + 2 < count:
            start_pair(part + 2)

        def step(index, carry):
            side, rest = index // 8, index % 8
            add(own[part].at[side, rest // 2, rest % 2], pair[part].at[side, rest // 2, rest % 2])
            return carry

        lax.fori_loop(0, 16, step, 0)
        for copy in first_copies(part):
            copy.start()

    def stage_first(part):
        for copy in first_copies(part):
            copy.wait()

        def step(index, carry):
            add(own[part].at[y, index // 2, index % 2, upper], first_a[part].at[index // 2, index % 2])
            add(own[part].at[index % 2, index // 2, x, lower], first_b[part].at[index % 2, index // 2])
            return carry

        lax.fori_loop(0, 8, step, 0)
        for copy in second_copies(part):
            copy.start()

    def stage_second(part):
        for copy in second_copies(part):
            copy.wait()

        def step(index, carry):
            add(own[part].at[y, index, x, upper], second_a[part].at[index])
            add(own[part].at[y, index, x, lower], second_b[part].at[index])
            return carry

        lax.fori_loop(0, 4, step, 0)
        for step, to in enumerate(along_z(z)):
            line_copy(part, step, to).start()

    def stage_total(part):
        total = totals[chunks[part][0]].at[:, columns(part)]
        total[...] = own[part][y, z, x].astype(f32)
        for step, other in enumerate(along_z(z)):
            line_arrival(part, step, other).wait_recv()
            total[...] += column[part][other].astype(f32)
        for step, to in enumerate(along_z(z)):
            line_copy(part, step, to).wait_send()

    return start_pair, {
        "pair": stage_pair,
        "first": stage_first,
        "second": stage_second,
        "total": stage_total,
    }


def chunked(sizes, most=3 * BLOCK):
    return [
        (array, first, min(most, size - first))
        for array, size in enumerate(sizes)
        for first in range(0, size, most)
    ]


BACK_START = (("pair", 0),)
BACK_SLOTS = {
    0: (("pair", 1),),
    1: (("first", 0),),
    2: (("pair", 2),),
    3: (("first", 1), ("second", 0)),
    4: (("pair", 3),),
    5: (("first", 2), ("second", 1), ("total", 0)),
    6: (("pair", 4),),
    7: (("first", 3), ("second", 2), ("total", 1)),
    9: (("first", 4), ("second", 3), ("total", 2)),
    11: (("second", 4), ("total", 3)),
}
BACK_END = (("total", 4),)


def run_all(stages, steps):
    for name, chunk in steps:
        stages[name](chunk)


def attend_back_sums_kernel(count, chunks, *refs):
    inputs, grads = list(refs[:4]), refs[4 : 4 + count]
    outputs, totals = refs[4 + count : 6 + count], refs[6 + count : 6 + 2 * count]
    work, rest = refs[6 + 2 * count : 8 + 2 * count], refs[8 + 2 * count :]
    probs_ref, load_sem, *rest = rest
    probs_in, inputs[2] = inputs[2], probs_ref
    groups, heads = inputs[0].shape[0], work[0].shape[0]

    def load(group):
        part = pl.ds(group * heads, heads)
        return pltpu.make_async_copy(probs_in.at[part], probs_ref.at[part], load_sem.at[group])

    for group in range(groups):
        load(group).start()
    spot = place()
    greet(*spot, True)
    start_pair, stages = sum_stages(spot, grads, totals, chunks, rest)
    for chunk in range(2):
        start_pair(chunk)
    run_all(stages, BACK_START)

    def step(group, carry):
        load(group).wait()
        for head in range(heads):
            attend_back_head(group, head, *inputs, *outputs, *work)
            for slot, steps in BACK_SLOTS.items():
                if slot % heads == head:
                    pl.when(group == slot // heads)(functools.partial(run_all, stages, steps))
        return carry

    lax.fori_loop(0, groups, step, 0)
    run_all(stages, BACK_END)


def attend_back_sums(qkv, table, probs, up, grads, tag):
    groups, seq, width3 = qkv.shape
    width = width3 // 3
    heads = width // HEAD_DIM
    part = grads[0].shape[1] // 8
    sizes = [grad.shape[2] for grad in grads]
    chunks = chunked(sizes)
    return pl.pallas_call(
        functools.partial(attend_back_sums_kernel, len(grads), chunks),
        in_specs=[IN_VMEM, IN_VMEM, ANYWHERE, IN_VMEM] + [ANYWHERE] * len(grads),
        out_specs=[IN_VMEM] * (2 + len(grads)),
        out_shape=[
            jax.ShapeDtypeStruct((groups, seq, width3), low),
            jax.ShapeDtypeStruct((groups, 2 * seq, 2 * width), low),
        ]
        + [jax.ShapeDtypeStruct((part, size), f32) for size in sizes],
        scratch_shapes=[
            pltpu.VMEM((heads, seq, seq), low),
            pltpu.VMEM((2 * heads, HEAD_DIM, 2 * seq), f32),
            pltpu.VMEM(probs.shape, low),
            pltpu.SemaphoreType.DMA((groups,)),
        ]
        + sum_scratch(part, [chunk[2] for chunk in chunks]),
        compiler_params=pltpu.CompilerParams(
            collective_id=tag, has_side_effects=True, vmem_limit_bytes=60 << 20
        ),
        name="attend_back_sums",
    )(qkv, table, probs, up, *[grad.reshape(4, 4, 2, part, -1) for grad in grads])


def peers(z, x):
    return [((z + 2 - far) % 4, x if same else 1 - x) for far, same in PEER_ORDER]


PEER_ORDER = ((0, False), (0, True), (1, False), (1, True), (3, False), (3, True), (2, False))


def meet_owners(z, x, y, c):
    for peer_z, peer_x in peers(z, x):
        signal(device(peer_z, peer_x, y, c))


def share_facts_kernel(facts_ref, all_ref, local_sem, send_sem, recv_sem):
    z, x, y, c = place()
    meet_owners(z, x, y, c)
    pl.semaphore_wait(pltpu.get_barrier_semaphore(), 7)
    here = z * 2 + x
    keep = pltpu.make_async_copy(facts_ref, all_ref.at[here], local_sem)
    keep.start()
    copies = []
    for index, (peer_z, peer_x) in enumerate(peers(z, x)):
        copy = remote(
            facts_ref,
            all_ref.at[here],
            send_sem.at[index],
            recv_sem.at[here],
            device(peer_z, peer_x, y, c),
        )
        copy.start()
        copies.append(copy)
    for index, (peer_z, peer_x) in enumerate(peers(z, x)):
        there = peer_z * 2 + peer_x
        copies[index].wait_send()
        remote(
            facts_ref, all_ref.at[there], send_sem.at[index], recv_sem.at[there], device(z, x, y, c)
        ).wait_recv()
    keep.wait()


def share_facts(facts, tag):
    return pl.pallas_call(
        share_facts_kernel,
        in_specs=[IN_VMEM],
        out_specs=IN_VMEM,
        out_shape=jax.ShapeDtypeStruct((8,) + facts.shape, facts.dtype),
        scratch_shapes=[
            pltpu.SemaphoreType.DMA,
            pltpu.SemaphoreType.DMA((7,)),
            pltpu.SemaphoreType.DMA((8,)),
        ],
        compiler_params=pltpu.CompilerParams(collective_id=tag, has_side_effects=True),
        name="share_facts",
    )(facts)


def word_stages(spot, found_ref, words_ref, pair, side, send_sem, recv_sem, out_sem, in_sem):
    z, x, y, c = spot
    here = z * 2 + x
    targets = peers(z, x) + [(z, x)]
    core_to, y_to = device(z, x, y, 1 - c), device(z, x, 1 - y, c)

    def at_home(part):
        return targets[part][0] * 2 + targets[part][1]

    def pair_copy(part, row):
        to = at_home(part)
        return remote(
            found_ref.at[to, row * 2 + 1 - c],
            pair.at[row, to],
            send_sem.at[part, row],
            recv_sem.at[part, row],
            core_to,
        )

    def side_copy(part):
        to = at_home(part)
        return remote(
            pair.at[1 - y, to], side.at[to], send_sem.at[part, 2], recv_sem.at[part, 2], y_to
        )

    def out_copy(part):
        return remote(
            pair.at[y, at_home(part)],
            words_ref.at[here],
            out_sem.at[part],
            in_sem.at[here],
            device(targets[part][0], targets[part][1], y, c),
        )

    def start():
        for part in range(8):
            for row in range(2):
                pair_copy(part, row).start()

    def sideways(first, last):
        for part in range(first, last):
            to = at_home(part)
            for row in range(2):
                pair_copy(part, row).wait_recv()
                pair[row, to] = pair[row, to] + found_ref[to, row * 2 + c]
            side_copy(part).start()

    def outward(first, last):
        for part in range(first, last):
            to = at_home(part)
            side_copy(part).wait_recv()
            pair[y, to] = pair[y, to] + side[to]
            if part < 7:
                out_copy(part).start()
            else:
                words_ref[here] = pair[y, to]

    def finish():
        for part in range(8):
            for row in range(2):
                pair_copy(part, row).wait_send()
            side_copy(part).wait_send()
            if part < 7:
                out_copy(part).wait_send()
                there = at_home(part)
                remote(
                    pair.at[y, there], words_ref.at[there], out_sem.at[part], in_sem.at[there], core_to
                ).wait_recv()

    return start, sideways, outward, finish


def exchange_words_kernel(found_ref, words_ref, *refs):
    spot = place()
    meet_owners(*spot)
    greet(*spot, False)
    pl.semaphore_wait(pltpu.get_barrier_semaphore(), 9)
    start, sideways, outward, finish = word_stages(spot, found_ref, words_ref, *refs)
    start()
    sideways(0, 8)
    outward(0, 8)
    finish()


def exchange_words(found, tag):
    piece = found.shape[2:]
    return pl.pallas_call(
        exchange_words_kernel,
        in_specs=[IN_VMEM],
        out_specs=IN_VMEM,
        out_shape=jax.ShapeDtypeStruct((8,) + piece, low),
        scratch_shapes=[
            pltpu.VMEM((2, 8) + piece, low),
            pltpu.VMEM((8,) + piece, low),
            pltpu.SemaphoreType.DMA((8, 3)),
            pltpu.SemaphoreType.DMA((8, 3)),
            pltpu.SemaphoreType.DMA((8,)),
            pltpu.SemaphoreType.DMA((8,)),
        ],
        compiler_params=pltpu.CompilerParams(
            collective_id=tag, has_side_effects=True, vmem_limit_bytes=40 << 20
        ),
        name="exchange_words",
    )(found)


def return_stages(spot, grads_ref, sent_ref, refs):
    local_sem, out_sem, in_sem, send_sem, recv_sem = refs
    z, x, y, c = spot
    here = z * 2 + x
    own = y * 2 + c
    other = (1 - y) * 2 + c
    core_to, y_to = device(z, x, y, 1 - c), device(z, x, 1 - y, c)
    order = [(z, x)] + peers(z, x)[::-1]
    keep = pltpu.make_async_copy(grads_ref.at[here], sent_ref.at[here, own], local_sem)

    def out_copy(part, peer):
        return remote(
            grads_ref.at[peer[0] * 2 + peer[1]],
            sent_ref.at[here, own],
            out_sem.at[part],
            in_sem.at[here],
            device(peer[0], peer[1], y, c),
        )

    def in_copy(part, peer):
        there = peer[0] * 2 + peer[1]
        return remote(
            grads_ref.at[there], sent_ref.at[there, own], out_sem.at[part], in_sem.at[there], core_to
        )

    def pass_on(slot, row, there, to):
        block = sent_ref.at[there, row]
        return remote(block, block, send_sem.at[slot, there], recv_sem.at[row, there], to)

    def start():
        keep.start()
        for part, peer in enumerate(peers(z, x)):
            out_copy(part, peer).start()

    def forward(first, last):
        for part in range(first, last):
            there = order[part][0] * 2 + order[part][1]
            if part == 0:
                keep.wait()
            else:
                in_copy(part - 1, order[part]).wait_recv()
            pass_on(0, own, there, y_to).start()
            pass_on(1, own, there, core_to).start()

    def relay(first, last):
        for part in range(first, last):
            there = order[part][0] * 2 + order[part][1]
            pass_on(0, other, there, y_to).wait_recv()
            pass_on(2, other, there, core_to).start()

    def finish():
        for part, peer in enumerate(peers(z, x)):
            out_copy(part, peer).wait_send()
        for peer_z, peer_x in order:
            there = peer_z * 2 + peer_x
            pass_on(0, own, there, y_to).wait_send()
            pass_on(1, own, there, core_to).wait_send()
            pass_on(2, other, there, core_to).wait_send()
            pass_on(1, y * 2 + 1 - c, there, core_to).wait_recv()
            pass_on(2, (1 - y) * 2 + 1 - c, there, core_to).wait_recv()

    return start, forward, relay, finish


def return_scratch():
    return [
        pltpu.SemaphoreType.DMA,
        pltpu.SemaphoreType.DMA((7,)),
        pltpu.SemaphoreType.DMA((8,)),
        pltpu.SemaphoreType.DMA((3, 8)),
        pltpu.SemaphoreType.DMA((4, 8)),
    ]


def gather_stages(spot, pack_ref, all_ref, local_sem, send_sem, recv_sem, line_sem, core_sem):
    z, x, y, c = spot
    half = pack_ref.shape[0] // 2
    core_to, y_to, x_to = device(z, x, y, 1 - c), device(z, x, 1 - y, c), device(z, 1 - x, y, c)
    up_to, down_to = device(z + 1, x, y, c), device(z - 1, x, y, c)
    keep = pltpu.make_async_copy(pack_ref, all_ref.at[y * 2 + c, z * 2 + x], local_sem)
    CROSS, SIDE, UP, DOWN = range(4)
    targets = (x_to, y_to, up_to, down_to)

    def copy(kind, part, zz, xx, yy):
        at = lax.clamp(0, zz, 3) * 2 + xx
        block = all_ref.at[yy * 2 + c, at, pl.ds(part * half, half)]
        return remote(
            block, block, send_sem.at[kind, part, yy, at], recv_sem.at[part, yy, at], targets[kind]
        )

    def line_copy(kind, zz):
        zz = lax.clamp(0, zz, 3)
        block = all_ref.at[y * 2 + c, zz * 2 + x]
        return remote(block, block, line_sem.at[kind - UP, zz], line_sem.at[2, zz], targets[kind])

    def core_copy(zz, yy, column):
        zz = lax.clamp(0, zz, 3)
        block = all_ref.at[yy * 2 + column, pl.ds(zz * 2, 2)]
        return remote(block, block, core_sem.at[0, yy, zz], core_sem.at[1, yy, zz], core_to)

    def distances(far):
        if far == 0:
            return [(z, z >= 0, None)]
        return [(z - far, z >= far, UP), (z + far, z <= 3 - far, DOWN)]

    def along(way):
        if way is None:
            return [(UP, z < 3), (DOWN, z > 0)]
        return [(way, z < 3 if way == UP else z > 0)]

    def for_each(far, action):
        for zz, exists, way in distances(far):
            pl.when(exists)(functools.partial(action, zz, way))

    def onward(zz, way, action):
        for on, possible in along(way):
            pl.when(possible)(lambda on=on: action(line_copy(on, zz)))

    def line_one(zz, way):
        if way is None:
            keep.wait()
        else:
            line_copy(way, zz).wait_recv()
        onward(zz, way, lambda copy: copy.start())
        copy(CROSS, 0, zz, x, y).start()
        copy(SIDE, 1, zz, x, y).start()

    def rest_one(zz, way):
        copy(SIDE, 0, zz, x, y).start()
        copy(CROSS, 1, zz, x, y).start()

    def sides_one(zz, way):
        copy(CROSS, 0, zz, 1 - x, y).wait_recv()
        copy(SIDE, 0, zz, 1 - x, y).start()
        copy(SIDE, 1, zz, x, 1 - y).wait_recv()
        copy(CROSS, 1, zz, x, 1 - y).start()

    def corners_one(zz, way):
        for kind, part, xx, yy in (
            (SIDE, 0, x, 1 - y),
            (CROSS, 1, 1 - x, y),
            (SIDE, 0, 1 - x, 1 - y),
            (CROSS, 1, 1 - x, 1 - y),
        ):
            copy(kind, part, zz, xx, yy).wait_recv()
        for yy in range(2):
            core_copy(zz, yy, c).start()

    def finish_one(zz, way):
        onward(zz, way, lambda copy: copy.wait_send())
        for part in range(2):
            copy(CROSS, part, zz, x, y).wait_send()
            copy(SIDE, part, zz, x, y).wait_send()
        copy(SIDE, 0, zz, 1 - x, y).wait_send()
        copy(CROSS, 1, zz, x, 1 - y).wait_send()
        for yy in range(2):
            core_copy(zz, yy, c).wait_send()
            core_copy(zz, yy, 1 - c).wait_recv()

    steps = {
        "line": line_one,
        "rest": rest_one,
        "sides": sides_one,
        "corners": corners_one,
        "finish": finish_one,
    }
    return keep.start, {
        name: functools.partial(for_each, action=action) for name, action in steps.items()
    }


def gather_scratch():
    return [
        pltpu.SemaphoreType.DMA,
        pltpu.SemaphoreType.DMA((4, 2, 2, 8)),
        pltpu.SemaphoreType.DMA((2, 2, 8)),
        pltpu.SemaphoreType.DMA((3, 4)),
        pltpu.SemaphoreType.DMA((2, 2, 4)),
    ]


def finish_sums_kernel(
    width,
    losses_ref,
    squares_ref,
    *refs,
):
    sums, refs = refs[:4], refs[4:]
    total_ref, all_ref, facts, pair, side, cross, line, local_sem, send_sem, recv_sem, line_send, line_recv = refs
    z, x, y, c = place()
    core_to, y_to, x_to = device(z, x, y, 1 - c), device(z, x, 1 - y, c), device(z, 1 - x, y, c)
    column = [(z + step) % 4 for step in range(1, 4)]
    for target in (core_to, y_to, x_to, *[device(other, x, y, c) for other in column]):
        signal(target)
    own, other = y * 2 + c, (1 - y) * 2 + c
    all_ref[own, :, :width] = sums[2][:, :width]
    all_ref[own, :, width:] = sums[3][:, 3 * width :]
    squares = jnp.sum(squares_ref[...], 0, keepdims=True)
    for part in sums:
        for first in range(0, part.shape[1], BLOCK):
            values = part[:, first : first + BLOCK]
            squares += jnp.sum(values * values, 0, keepdims=True)
    facts[0:1] = squares
    facts[1:2] = jnp.broadcast_to(jnp.sum(losses_ref[...], 0, keepdims=True), squares.shape)
    facts[2:8] = jnp.zeros((6, BLOCK), f32)
    pl.semaphore_wait(pltpu.get_barrier_semaphore(), 6)
    swap_pair = remote(facts, pair, send_sem.at[0], recv_sem.at[0], core_to)
    swap_pair.start()
    block = all_ref.at[own]
    shared_side = remote(block, block, send_sem.at[3], recv_sem.at[3], y_to)
    shared_pair = remote(block, block, send_sem.at[4], recv_sem.at[4], core_to)
    swap_pair.wait()
    total_ref[...] = facts[...] + pair[...]
    swap_side = remote(total_ref, side, send_sem.at[1], recv_sem.at[1], y_to)
    swap_side.start()
    shared_side.start()
    shared_pair.start()
    swap_side.wait()
    total_ref[...] += side[...]
    swap_cross = remote(total_ref, cross, send_sem.at[2], recv_sem.at[2], x_to)
    swap_cross.start()
    swap_cross.wait()
    total_ref[...] += cross[...]
    line[z] = total_ref[...]
    lines = [
        remote(line.at[z], line.at[z], line_send.at[step], line_recv.at[z], device(to, x, y, c))
        for step, to in enumerate(column)
    ]
    for copy in lines:
        copy.start()
    shared_side.wait()
    relay = remote(all_ref.at[other], all_ref.at[other], send_sem.at[5], recv_sem.at[5], core_to)
    relay.start()
    for step, to in enumerate(column):
        lines[step].wait_send()
        remote(line.at[to], line.at[to], line_send.at[step], line_recv.at[to], core_to).wait_recv()
    total_ref[...] = (line[0] + line[1]) + (line[2] + line[3])
    shared_pair.wait()
    relay.wait()


def finish_sums(losses, squares, sums, width, tag):
    small = (8, BLOCK)
    return pl.pallas_call(
        functools.partial(finish_sums_kernel, width),
        in_specs=[IN_VMEM] * 6,
        out_specs=[IN_VMEM] * 2,
        out_shape=[
            jax.ShapeDtypeStruct(small, f32),
            jax.ShapeDtypeStruct((4, squares.shape[0], 2 * width), f32),
        ],
        scratch_shapes=[pltpu.VMEM(small, f32)] * 4
        + [
            pltpu.VMEM((4,) + small, f32),
            pltpu.SemaphoreType.DMA,
            pltpu.SemaphoreType.DMA((6,)),
            pltpu.SemaphoreType.DMA((6,)),
            pltpu.SemaphoreType.DMA((3,)),
            pltpu.SemaphoreType.DMA((4,)),
        ],
        compiler_params=pltpu.CompilerParams(collective_id=tag, has_side_effects=True),
        name="finish_sums",
    )(losses, squares, *sums)


def identity(size):
    rows = lax.broadcasted_iota(jnp.int32, (size, size), 0)
    columns = lax.broadcasted_iota(jnp.int32, (size, size), 1)
    return (rows == columns).astype(f32).astype(low)


def turn(values):
    return dot_rows(identity(values.shape[1]), values)


TABLES = 2


def lookup_kernel(counts_ref, keys_ref, weights_ref, words_ref, table_ref, rows_ref):
    width, slab = weights_ref.shape
    rows, _, seq = words_ref.shape
    shift = slab.bit_length()

    @pl.when(pl.program_id(0) == 0)
    def fill():
        def step(index, carry):
            first = pl.multiple_of(index * 9 * BLOCK, BLOCK)
            for part in range(9):
                at = first + part * BLOCK
                table_ref[pl.ds(at, BLOCK), :] = turn(weights_ref[:, pl.ds(at, BLOCK)].astype(low))
            return carry

        lax.fori_loop(0, slab // (9 * BLOCK), step, 0)
        table_ref[pl.ds(slab, 8), :] = jnp.zeros((8, width), f32)

    rows_ref[...] = jnp.zeros_like(rows_ref)

    def step(index, carry):
        for offset in range(UNROLL):
            key = keys_ref[0, 0, index * UNROLL + offset]
            spot, token = key & ((1 << shift) - 1), key >> shift
            rows_ref[pl.ds(token, 1), :] = table_ref[pl.ds(spot, 1), :]
        return carry

    lax.fori_loop(0, pl.cdiv(counts_ref[pl.program_id(0)], UNROLL), step, 0)
    for row in range(rows):
        values = rows_ref[row * seq : (row + 1) * seq, :].astype(low)
        words_ref[row] = dot_rows(identity(width), values).astype(low)


def lookup(counts, keys, weights, seq):
    steps, tokens = keys.shape
    width, slab = weights.shape
    rows = tokens // seq
    return pl.pallas_call(
        lookup_kernel,
        grid=(steps,),
        in_specs=[
            pl.BlockSpec(memory_space=pltpu.SMEM),
            pl.BlockSpec((1, 1, tokens), lambda step: (step, 0, 0), memory_space=pltpu.SMEM),
            pl.BlockSpec(weights.shape, lambda step: (0, 0)),
        ],
        out_specs=pl.BlockSpec((rows, width, seq), lambda step: (step, 0, 0)),
        out_shape=jax.ShapeDtypeStruct((steps * rows, width, seq), low),
        scratch_shapes=[pltpu.VMEM((slab + 8, width), f32), pltpu.VMEM((tokens + 8, width), f32)],
        compiler_params=pltpu.CompilerParams(vmem_limit_bytes=48 << 20),
        name="lookup",
    )(counts, keys[:, None], weights)


def deposit_kernel(counts_ref, keys_ref, grads_ref, total_ref, squares_ref, rows_ref, *tables):
    width, slab = total_ref.shape
    rows, _, seq = grads_ref.shape
    shift = slab.bit_length()

    @pl.when(pl.program_id(0) == 0)
    def clear():
        for table in tables:
            table[...] = jnp.zeros_like(table)
        rows_ref[pl.ds(rows * seq, 8), :] = jnp.zeros((8, width), f32)

    for row in range(rows):
        for first in range(0, seq, BLOCK):
            at = row * seq + first
            rows_ref[at : at + BLOCK, :] = turn(grads_ref[row, :, first : first + BLOCK])

    def step(index, carry):
        for offset in range(0, UNROLL, len(tables)):
            keys = [keys_ref[0, 0, index * UNROLL + offset + part] for part in range(len(tables))]
            spots = [key & ((1 << shift) - 1) for key in keys]
            sums = [
                table[pl.ds(spot, 1), :] + rows_ref[pl.ds(key >> shift, 1), :]
                for key, spot, table in zip(keys, spots, tables)
            ]
            for spot, table, value in zip(spots, tables, sums):
                table[pl.ds(spot, 1), :] = value
        return carry

    lax.fori_loop(0, pl.cdiv(counts_ref[pl.program_id(0)], UNROLL), step, 0)

    @pl.when(pl.program_id(0) == pl.num_programs(0) - 1)
    def finish():
        squares_ref[...] = jnp.zeros_like(squares_ref)

        def step(index, carry):
            first = pl.multiple_of(index * 9 * BLOCK, BLOCK)
            squares = jnp.zeros((width, BLOCK), f32)
            for part in range(9):
                at = pl.ds(first + part * BLOCK, BLOCK)
                block = sum(table[at, :] for table in tables).T
                total_ref[:, at] = block
                squares += block * block
            squares_ref[...] += squares
            return carry

        lax.fori_loop(0, slab // (9 * BLOCK), step, 0)


def deposit(counts, keys, grads, slab):
    steps, tokens = keys.shape
    _, width, seq = grads.shape
    rows = tokens // seq
    return pl.pallas_call(
        deposit_kernel,
        grid=(steps,),
        in_specs=[
            pl.BlockSpec(memory_space=pltpu.SMEM),
            pl.BlockSpec((1, 1, tokens), lambda step: (step, 0, 0), memory_space=pltpu.SMEM),
            pl.BlockSpec((rows, width, seq), lambda step: (step, 0, 0)),
        ],
        out_specs=[
            pl.BlockSpec((width, slab), lambda step: (0, 0)),
            pl.BlockSpec((width, BLOCK), lambda step: (0, 0)),
        ],
        out_shape=[
            jax.ShapeDtypeStruct((width, slab), f32),
            jax.ShapeDtypeStruct((width, BLOCK), f32),
        ],
        scratch_shapes=[pltpu.VMEM((tokens + 8, width), f32)]
        + [pltpu.VMEM((slab + 8, width), f32)] * TABLES,
        compiler_params=pltpu.CompilerParams(vmem_limit_bytes=60 << 20),
        name="deposit",
    )(counts, keys[:, None], grads)


def whiten(values):
    center = values - jnp.mean(values, -1, keepdims=True)
    rate = lax.rsqrt(jnp.mean(center * center, -1, keepdims=True) + layer_eps)
    return center * rate, rate


def unwhiten(upstream, gain, white, rate):
    scaled = upstream * gain
    inner = jnp.mean(scaled, -1, keepdims=True)
    along = jnp.mean(scaled * white, -1, keepdims=True)
    return (
        rate * (scaled - inner - white * along),
        jnp.sum(upstream * white, 0, keepdims=True),
        jnp.sum(upstream, 0, keepdims=True),
    )


def selection(length, entries):
    rows = lax.broadcasted_iota(jnp.int32, (2 * length, entries), 0)
    columns = lax.broadcasted_iota(jnp.int32, (2 * length, entries), 1)
    return (jnp.clip(length + entries // 2 - rows, 0, entries - 1) == columns).astype(f32).astype(low)


def prepare_kernel(*refs, between=lambda group: None):
    weights_ref, words_ref, vec_ref, white_ref, rate_ref, qkv_ref = refs[:6]
    rel_white_ref, rel_rate_ref, table_ref, low_ref, rel_ref = refs[6:]
    groups, model = weights_ref.shape[:2]
    seq = words_ref.shape[1]
    part = rel_ref.shape[0] // groups
    width = qkv_ref.shape[2] // 3
    terms = turn(weights_ref[0, :, 4 * BLOCK : 5 * BLOCK])
    half = BLOCK // 2
    vec_ref[...] = terms[half : half + 16] + terms[half + 16 : half + 32] + terms[half + 32 : half + 48]
    for group in range(groups):
        rows = slice(group * part, (group + 1) * part)
        entries = turn(weights_ref[group, :, 5 * BLOCK : 6 * BLOCK]) + turn(
            weights_ref[group, :, 6 * BLOCK : 7 * BLOCK]
        )
        white, rate = whiten(entries)
        rel_white_ref[rows, :] = white
        rel_rate_ref[rows, :] = rate
        rel_ref[rows, :] = (white * vec_ref[2:3] + vec_ref[3:4]).astype(low)
    for first in range(0, seq, BLOCK):
        rows = slice(first, first + BLOCK)
        white, rate = whiten(turn(words_ref[:, rows]))
        white_ref[rows, :] = white
        rate_ref[rows, :] = rate
        low_ref[rows, :] = (white * vec_ref[0:1] + vec_ref[1:2]).astype(low)
    chosen = selection(seq, rel_ref.shape[0])

    def step(group, carry):
        between(group)
        qkv_ref[group] = dot_plain(low_ref[...], weights_ref[group, :, : 3 * width]).astype(low)
        keys = dot_plain(rel_ref[...], weights_ref[group, :, : 2 * width]).astype(low)
        table_ref[group] = dot_plain(chosen, keys).astype(low)
        return carry

    lax.fori_loop(0, groups, step, 0)


def prepared(weights, seq, width, entries):
    groups, model = weights.shape[:2]
    outputs = [
        jax.ShapeDtypeStruct((16, model), f32),
        jax.ShapeDtypeStruct((seq, model), f32),
        jax.ShapeDtypeStruct((seq, 1), f32),
        jax.ShapeDtypeStruct((groups, seq, 3 * width), low),
        jax.ShapeDtypeStruct((entries, model), f32),
        jax.ShapeDtypeStruct((entries, 1), f32),
        jax.ShapeDtypeStruct((groups, 2 * seq, 2 * width), low),
    ]
    return outputs, [pltpu.VMEM((seq, model), low), pltpu.VMEM((entries, model), low)]


def prepare(weights, words, width, entries):
    outputs, scratch = prepared(weights, words.shape[1], width, entries)
    return pl.pallas_call(
        prepare_kernel,
        in_specs=[IN_VMEM] * 2,
        out_specs=[IN_VMEM] * 7,
        out_shape=outputs,
        scratch_shapes=scratch,
        compiler_params=pltpu.CompilerParams(vmem_limit_bytes=56 << 20),
        name="prepare",
    )(weights, words)


GATHER_SLOTS = {
    1: (("line", 2), ("rest", 1)),
    3: (("sides", 1),),
    5: (("line", 3), ("rest", 2)),
    6: (("sides", 2),),
    8: (("rest", 3), ("sides", 3), ("corners", 0)),
    10: (("corners", 1),),
}
GATHER_END = (
    ("corners", 2),
    ("corners", 3),
    ("finish", 0),
    ("finish", 1),
    ("finish", 2),
    ("finish", 3),
)


SAVED = (1, 3, 4, 6)


def attend_gather_kernel(length_ref, weights_ref, words_ref, pack_ref, *refs):
    outputs, probs_out, mixed_ref, all_ref = list(refs[:7]), refs[7], refs[8], refs[9]
    low_ref, rel_ref, far_ref, probs_ref, *kept, save_sem = refs[10:19]
    sems = refs[19:]
    saves = []
    for order, index in enumerate(SAVED):
        saves.append(pltpu.make_async_copy(kept[order], outputs[index], save_sem.at[order]))
        outputs[index] = kept[order]
    qkv_ref, table_ref = outputs[3], outputs[6]
    groups, heads = qkv_ref.shape[0], far_ref.shape[0]
    spot = place()
    greet(*spot, True)
    start, steps = gather_stages(spot, pack_ref, all_ref, *sems)
    start()
    run_all(steps, (("line", 0),))

    def between(group):
        pl.when(group == 0)(lambda: run_all(steps, (("rest", 0),)))
        pl.when(group == 2)(lambda: run_all(steps, (("line", 1), ("sides", 0))))

    prepare_kernel(weights_ref, words_ref, *outputs, low_ref, rel_ref, between=between)
    for copy in saves:
        copy.start()

    def save_probs(group):
        part = pl.ds(group * heads, heads)
        return pltpu.make_async_copy(
            probs_ref.at[part], probs_out.at[part], save_sem.at[len(SAVED) + group]
        )

    def step(group, carry):
        for head in range(heads):
            attend_head(group, head, length_ref[0], qkv_ref, table_ref, probs_ref, mixed_ref, far_ref)
            for slot, timed in GATHER_SLOTS.items():
                if slot % heads == head:
                    pl.when(group == slot // heads)(functools.partial(run_all, steps, timed))
        save_probs(group).start()
        return carry

    lax.fori_loop(0, groups, step, 0)
    run_all(steps, GATHER_END)
    for copy in saves:
        copy.wait()
    for group in range(groups):
        save_probs(group).wait()


def attend_gather(length, weights, words, pack, width, entries, tag):
    groups = weights.shape[0]
    seq = words.shape[1]
    heads = width // HEAD_DIM
    outputs, scratch = prepared(weights, seq, width, entries)
    return pl.pallas_call(
        attend_gather_kernel,
        in_specs=[pl.BlockSpec(memory_space=pltpu.SMEM), IN_VMEM, IN_VMEM, ANYWHERE],
        out_specs=[ANYWHERE if index in SAVED else IN_VMEM for index in range(7)]
        + [ANYWHERE, IN_VMEM, ANYWHERE],
        out_shape=outputs
        + [
            jax.ShapeDtypeStruct((groups * heads, seq, seq), low),
            jax.ShapeDtypeStruct((groups, seq, width), low),
            jax.ShapeDtypeStruct((4, 8) + pack.shape, low),
        ],
        scratch_shapes=scratch
        + [pltpu.VMEM((heads, seq, seq), f32), pltpu.VMEM((groups * heads, seq, seq), low)]
        + [pltpu.VMEM(outputs[index].shape, outputs[index].dtype) for index in SAVED]
        + [pltpu.SemaphoreType.DMA((len(SAVED) + groups,))]
        + gather_scratch(),
        compiler_params=pltpu.CompilerParams(
            collective_id=tag, has_side_effects=True, vmem_limit_bytes=56 << 20
        ),
        name="attend_gather",
    )(length, weights, words, pack)


def middle_kernel(
    weights_in,
    vec_ref,
    white_ref,
    mixed_ref,
    marks_ref,
    contract_save,
    expand_save,
    joint_out,
    mixed_out,
    sum_out,
    vec_out,
    loss_out,
    weights_ref,
    contract_out,
    expand_out,
    copy_sem,
    combine_ref,
    readout_ref,
    slope_ref,
    acts_ref,
    mid_ref,
    mid_white_ref,
    out_white_ref,
    gate_ref,
):
    groups, model = weights_ref.shape[:2]
    seq = white_ref.shape[0]
    width = mixed_ref.shape[2]
    hidden = acts_ref.shape[2]

    def load(group, first, last, sem):
        part = (group, slice(None), pl.ds(first, last - first))
        return pltpu.make_async_copy(weights_in.at[part], weights_ref.at[part], copy_sem.at[sem])

    def load_joint(group):
        return load(group, 2 * hidden, 2 * hidden + 2 * width, group)

    def load_group(group):
        return load(group, 0, 2 * hidden, groups + group)

    def save(group):
        return (
            pltpu.make_async_copy(
                contract_out.at[group], contract_save.at[group], copy_sem.at[2 * groups + group]
            ),
            pltpu.make_async_copy(
                expand_out.at[group], expand_save.at[group], copy_sem.at[3 * groups + group]
            ),
        )

    for group in range(groups):
        load_joint(group).start()
    for group in range(groups):
        load_group(group).start()
    for group in range(groups):
        load_joint(group).wait()
    vec = [vec_ref[row : row + 1] for row in range(11)]
    for group in range(groups):
        joint = weights_ref[group, :, 2 * hidden :]
        readout_ref[:, group * width : (group + 1) * width] = joint[:, :width]
        combine_ref[group] = joint[:, width:]
    total = white_ref[...] * vec[0] + vec[1]
    for group in range(groups):
        total += dot_rows(mixed_ref[group], combine_ref[group])
    mid_white, mid_rate = whiten(total)
    mid_white_ref[...] = mid_white
    hidden_mid = mid_white * vec[4] + vec[5]
    sum_out[...] = hidden_mid
    mid_ref[...] = hidden_mid.astype(low)

    def forward(group, carry):
        load_group(group).wait()
        gate = dot_plain(mid_ref[...], weights_ref[group, :, :hidden])
        share = 0.5 + 0.5 * lax.erf(gate * 0.5**0.5)
        acts_ref[group] = (gate * share).astype(low)
        slope_ref[group] = share + gate * jnp.exp(-0.5 * gate * gate) * (2.0 * jnp.pi) ** -0.5
        sum_out[...] += dot_rows(acts_ref[group], weights_ref[group, :, hidden : 2 * hidden])
        return carry

    lax.fori_loop(0, groups, forward, 0)
    out_white, out_rate = whiten(sum_out[...])
    out_white_ref[...] = out_white
    gate_ref[...] = (out_white * vec[6] + vec[7]).astype(low)
    dense = dot_plain(gate_ref[...], readout_ref[...])
    share = 0.5 + 0.5 * lax.erf(dense * 0.5**0.5)
    slope = share + dense * jnp.exp(-0.5 * dense * dense) * (2.0 * jnp.pi) ** -0.5
    white, rate = whiten(dense * share)
    head = white * vec[8] + vec[9]
    logits = jnp.sum(head * vec[10], -1, keepdims=True)
    weight, flags = marks_ref[:, 0:1], marks_ref[:, 1:2]
    losses = jnp.maximum(logits, 0.0) + jnp.log1p(jnp.exp(-jnp.abs(logits))) - flags * logits
    loss_out[...] = jnp.where(weight > 0.0, losses, 0.0)
    pull = (1.0 / (1.0 + jnp.exp(-logits)) - flags) * weight
    vec_out[6:7, :] = jnp.sum(head * pull, 0, keepdims=True)
    upstream, vec_out[4:5, :], vec_out[5:6, :] = unwhiten(pull * vec[10], vec[8], white, rate)
    dense_low = (upstream * slope).astype(low)
    turned = gate_ref[...].astype(f32).T.astype(low)
    for group in range(groups):
        joint_out[group, :, :width] = dot_plain(
            turned, dense_low[:, group * width : (group + 1) * width]
        ).astype(low)
    upstream, vec_out[2:3, :], vec_out[3:4, :] = unwhiten(
        dot_rows(dense_low, readout_ref[...]), vec[6], out_white_ref[...], out_rate
    )
    sum_out[...] = upstream
    gate_ref[...] = upstream.astype(low)
    upstream_turned = upstream.T.astype(low)
    mid_turned = mid_ref[...].astype(f32).T.astype(low)

    def backward(group, carry):
        contract_out[group] = dot_plain(upstream_turned, acts_ref[group]).astype(low)
        acts_ref[group] = (
            dot_plain(gate_ref[...], weights_ref[group, :, hidden : 2 * hidden]) * slope_ref[group]
        ).astype(low)
        expand_out[group] = dot_plain(mid_turned, acts_ref[group]).astype(low)
        sum_out[...] += dot_rows(acts_ref[group], weights_ref[group, :, :hidden])
        for copy in save(group):
            copy.start()
        return carry

    lax.fori_loop(0, groups, backward, 0)
    upstream, vec_out[0:1, :], vec_out[1:2, :] = unwhiten(
        sum_out[...], vec[4], mid_white_ref[...], mid_rate
    )
    vec_out[7:8, :] = jnp.zeros((1, model), f32)
    sum_out[...] = upstream
    gate_ref[...] = upstream.astype(low)
    turned = upstream.T.astype(low)
    for group in range(groups):
        mixed_out[group] = dot_plain(gate_ref[...], combine_ref[group]).astype(low)
        joint_out[group, :, width:] = dot_plain(turned, mixed_ref[group]).astype(low)
    for group in range(groups):
        for copy in save(group):
            copy.wait()


def middle(weights, vec, white, mixed, marks):
    groups, model = weights.shape[:2]
    seq, width = mixed.shape[1:]
    hidden = weights.shape[2] // 2 - width
    wide = pltpu.VMEM((seq, model), f32)
    outputs = [
        ((groups, model, hidden), low),
        ((groups, model, hidden), low),
        ((groups, model, 2 * width), low),
        ((groups, seq, width), low),
        ((seq, model), f32),
        ((8, model), f32),
        ((seq, 1), f32),
    ]
    return pl.pallas_call(
        middle_kernel,
        in_specs=[ANYWHERE] + [IN_VMEM] * 4,
        out_specs=[ANYWHERE] * 2 + [IN_VMEM] * 5,
        out_shape=[jax.ShapeDtypeStruct(*output) for output in outputs],
        scratch_shapes=[
            pltpu.VMEM(weights.shape, low),
            pltpu.VMEM((groups, model, hidden), low),
            pltpu.VMEM((groups, model, hidden), low),
            pltpu.SemaphoreType.DMA((4 * groups,)),
            pltpu.VMEM((groups, model, width), low),
            pltpu.VMEM((model, model), low),
            pltpu.VMEM((groups, seq, hidden), f32),
            pltpu.VMEM((groups, seq, hidden), low),
            pltpu.VMEM((seq, model), low),
            wide,
            wide,
            pltpu.VMEM((seq, model), low),
        ],
        compiler_params=pltpu.CompilerParams(vmem_limit_bytes=60 << 20),
        name="middle",
    )(weights, vec, white, mixed, marks)


def project_back_kernel(
    weights_ref,
    vec_ref,
    white_ref,
    rate_ref,
    rel_white_ref,
    rel_rate_ref,
    sum_ref,
    grads_ref,
    tables_ref,
    vec_grads_ref,
    words_out,
    project_out,
    total_ref,
    fold_ref,
    between=lambda point: None,
):
    groups, model = weights_ref.shape[:2]
    seq = white_ref.shape[0]
    width = grads_ref.shape[2] // 3
    entries = rel_white_ref.shape[0]
    part = entries // groups
    vec = [vec_ref[row : row + 1] for row in range(4)]

    def put(group, first, last, values):
        values = values.astype(low).reshape(project_out.shape[1:-1] + (last - first,))
        project_out[group, ..., first:last] = values

    total_ref[...] = sum_ref[...]
    for group in range(groups):
        total_ref[...] += dot_rows(grads_ref[group], weights_ref[group, :, : 3 * width])
    upstream, gain_grad, bias_grad = unwhiten(total_ref[...], vec[0], white_ref[...], rate_ref[...])
    turned = upstream.T.astype(low)
    words_out[...] = turned.reshape(words_out.shape)
    between("words")
    turned = (white_ref[...] * vec[0] + vec[1]).T.astype(low)
    rel_turned = (rel_white_ref[...] * vec[2] + vec[3]).T.astype(low)
    chosen = selection(seq, entries)
    rel_total = jnp.zeros((entries, model), f32)
    for group in range(groups):
        fold_ref[...] = dot_left(chosen, tables_ref[group]).astype(low)
        rel_total += dot_rows(fold_ref[...], weights_ref[group, :, : 2 * width])
        put(
            group,
            0,
            2 * width,
            dot_plain(turned, grads_ref[group, :, : 2 * width]) + dot_plain(rel_turned, fold_ref[...]),
        )
        put(group, 2 * width, 3 * width, dot_plain(turned, grads_ref[group, :, 2 * width :]))
        between(group)
    rel_up, rel_gain_grad, rel_bias_grad = unwhiten(
        rel_total, vec[2], rel_white_ref[...], rel_rate_ref[...]
    )
    turned = rel_up.T.astype(low)
    rows = [gain_grad, bias_grad, rel_gain_grad, rel_bias_grad]
    rows += [vec_grads_ref[row : row + 1] for row in range(7)]
    rows += [jnp.zeros((1, model), f32)]
    middle_column = 3 * width + BLOCK // 2
    for group in range(groups):
        put(group, middle_column, middle_column + part, turned[:, group * part : (group + 1) * part])
        three = jnp.concatenate(rows[3 * group : 3 * group + 3] + [jnp.zeros((BLOCK - 3, model), f32)], 0)
        put(group, 3 * width, middle_column, three.T[:, : BLOCK // 2])


def projected_back(weights, white, grads, rel_white):
    groups, model = weights.shape[:2]
    seq = white.shape[0]
    width = grads.shape[2] // 3
    entries = rel_white.shape[0]
    outputs = [
        jax.ShapeDtypeStruct((model, seq), low),
        jax.ShapeDtypeStruct((groups, model, 3 * width + BLOCK // 2 + entries // groups), low),
    ]
    return outputs, [pltpu.VMEM((seq, model), f32), pltpu.VMEM((entries, 2 * width), low)]


def project_back(weights, vec, white, rate, rel_white, rel_rate, total, grads, tables, vec_grads):
    outputs, scratch = projected_back(weights, white, grads, rel_white)
    return pl.pallas_call(
        project_back_kernel,
        in_specs=[IN_VMEM] * 10,
        out_specs=[IN_VMEM] * 2,
        out_shape=outputs,
        scratch_shapes=scratch,
        compiler_params=pltpu.CompilerParams(vmem_limit_bytes=56 << 20),
        name="project_back",
    )(weights, vec, white, rate, rel_white, rel_rate, total, grads, tables, vec_grads)


def project_return_kernel(chunks, *refs):
    inputs, (sent_ref, total_ref) = refs[:10], refs[10:12]
    words_ref, project_ref, *work = refs[12:16]
    spot = place()
    meet_owners(*spot)
    greet(*spot, False)
    pl.semaphore_wait(pltpu.get_barrier_semaphore(), 9)
    start_words, forward, relay, finish = return_stages(spot, words_ref, sent_ref, refs[16:21])
    start_sums, stages = sum_stages(spot, [project_ref], [total_ref], chunks, refs[21:])
    start_pair = start_sums

    def between(point):
        if point == "words":
            start_words()
        elif point == 1:
            forward(0, 2)
        elif point == 2:
            forward(2, 4)
        elif point == 3:
            start_pair(0)
            forward(4, 6)

    project_back_kernel(*inputs, words_ref, project_ref, *work, between=between)
    start_pair(1)
    run_all(stages, (("pair", 0),))
    forward(6, 8)
    run_all(stages, (("pair", 1),))
    relay(0, 4)
    run_all(stages, (("first", 0), ("first", 1)))
    relay(4, 8)
    run_all(stages, (("second", 0), ("second", 1), ("total", 0), ("total", 1)))
    finish()


def project_return(*inputs, tag):
    weights, white, rel_white, upstream = inputs[0], inputs[2], inputs[4], inputs[7]
    (words, project), scratch = projected_back(weights, white, upstream, rel_white)
    seq = words.shape[1]
    size = project.shape[2]
    part = words.shape[0] // 8
    chunks = chunked([size])
    return pl.pallas_call(
        functools.partial(project_return_kernel, chunks),
        in_specs=[IN_VMEM] * 10,
        out_specs=[IN_VMEM] * 2,
        out_shape=[
            jax.ShapeDtypeStruct((8, 4, part, seq), low),
            jax.ShapeDtypeStruct((part, size), f32),
        ],
        scratch_shapes=[
            pltpu.VMEM((8, part, seq), low),
            pltpu.VMEM((4, 4, 2, part, size), low),
        ]
        + scratch
        + return_scratch()
        + sum_scratch(part, [chunk[2] for chunk in chunks]),
        compiler_params=pltpu.CompilerParams(
            collective_id=tag, has_side_effects=True, vmem_limit_bytes=60 << 20
        ),
        name="project_return",
    )(*inputs)


def split_terms(values, count):
    terms = []
    for _ in range(count):
        term = lax.reduce_precision(values, 8, 7)
        terms.append(term.astype(low))
        values = values - term
    return terms


def adamw(weight, gradient, mean, square, rate_now):
    first = beta_first * mean + (1.0 - beta_first) * gradient
    second = beta_second * square + (1.0 - beta_second) * gradient * gradient
    mean_hat = first / (1.0 - beta_first**STEP)
    square_hat = second / (1.0 - beta_second**STEP)
    master = weight - rate_now * (
        mean_hat / (jnp.sqrt(square_hat) + adam_eps) + weight_decay * weight
    )
    return (first, second, master)


def update_kernel(width, *refs):
    facts_ref, shared_ref, *grads = refs[:7]
    weights, refs = refs[7:31], refs[31:]
    outputs, (factor_ref, bias_ref) = refs[:24], refs[24:26]
    squares = jnp.sum(facts_ref[0:1, :], 1, keepdims=True)
    factor = jnp.minimum(1.0, clip_level / jnp.sqrt(squares))

    def update(index, spot, gradient):
        weight, mean, square = [part.at[spot] for part in weights[3 * index : 3 * index + 3]]
        results = adamw(
            weight[...], gradient * factor, mean[...], square[...], rate_steps[index]
        )
        for part, value in zip(outputs[3 * index : 3 * index + 3], results):
            part.at[spot][...] = value

    everything = slice(None)
    update(0, (everything, everything), grads[0][...])

    contract, expand, joint, project = grads[1:]

    def at_step(step):
        return pl.when(pl.program_id(0) == step)

    @at_step(0)
    def norms():
        factor_ref[...] = jnp.broadcast_to(jnp.sqrt(squares), factor_ref.shape)
        count = weights[21].shape[0]
        for group in range(4):
            rows = shared_ref[group, :, BLOCK : 2 * BLOCK].T[BLOCK // 2 :]
            first = 3 * group
            last = min(first + 3, count)
            update(7, (slice(first, last), everything), rows[: last - first])
            if group == 1:
                bias_ref[...] = rows[0:1] * factor

    @at_step(1)
    def relative_table():
        for group in range(4):
            part = slice(group * BLOCK, (group + 1) * BLOCK)
            update(1, (everything, part), shared_ref[group, :, width + BLOCK // 2 :])

    @at_step(2)
    def readout_weights():
        for group in range(4):
            part = slice(group * width, (group + 1) * width)
            update(6, (everything, part), shared_ref[group, :, :width])

    @at_step(3)
    def project_weights():
        for kind in range(3):
            update(2, (kind,), project[:, kind * width : (kind + 1) * width])

    @at_step(4)
    def combine_weights():
        update(3, (everything, everything), joint[:, width:].T)

    @at_step(5)
    def expand_weights():
        update(4, (everything, everything), expand[...])

    @at_step(6)
    def contract_weights():
        update(5, (everything, everything), contract[...])


def update_all(facts, shared, grads, weights, width):
    rows, slab = grads[0].shape
    columns = 11 * BLOCK
    stripe = pl.BlockSpec((rows, columns), lambda step: (0, step))

    def full(array):
        return pl.BlockSpec(array.shape, functools.partial(lambda rank, step: (0,) * rank, array.ndim))

    in_specs = [full(facts), full(shared), stripe] + [full(grad) for grad in grads[1:]]
    in_specs += [stripe] * 3 + [full(weight) for weight in weights[3:]]
    results = [jax.ShapeDtypeStruct(weight.shape, f32) for weight in weights]
    results += [jax.ShapeDtypeStruct((1, BLOCK), f32), jax.ShapeDtypeStruct((1, rows), f32)]
    return pl.pallas_call(
        functools.partial(update_kernel, width),
        grid=(slab // columns,),
        in_specs=in_specs,
        out_specs=[stripe] * 3 + [full(result) for result in results[3:]],
        out_shape=results,
        compiler_params=pltpu.CompilerParams(vmem_limit_bytes=62 << 20),
        name="update_all",
    )(facts, shared, *grads, *weights)


def per_device(
    token_ids,
    row_lengths,
    replaced,
    embedding,
    relative,
    project,
    combine,
    expand,
    contract,
    readout,
    vectors,
    embedding_mean,
    relative_mean,
    project_mean,
    combine_mean,
    expand_mean,
    contract_mean,
    readout_mean,
    vectors_mean,
    embedding_square,
    relative_square,
    project_square,
    combine_square,
    expand_square,
    contract_square,
    readout_square,
    vectors_square,
):
    pieces = lax.axis_size("heads")
    holder = lax.axis_index("heads")
    owners = lax.axis_size("dp")
    row_count, seq_len = token_ids.shape
    width = vectors.shape[1]
    model = width * owners
    everyone = ("heads", "dp")
    head_width = project.shape[2]
    hidden = expand.shape[1]
    vocab_slab = embedding.shape[1]
    span_part = relative.shape[0] // pieces
    vector_count = vectors.shape[0]
    direct = owners == 8 and pieces == 4

    own_relative = lax.dynamic_slice_in_dim(relative, holder * span_part, span_part, 0).T
    own_readout = lax.dynamic_slice_in_dim(readout, holder * head_width, head_width, 1)
    vector_terms = [
        jnp.pad(term, ((0, 0), (0, 16 - vector_count))) for term in split_terms(vectors.T, 3)
    ]
    high, rest = split_terms(own_relative, 2)
    first_pack = jnp.concatenate(
        [
            project.reshape(width, 3 * head_width).astype(low),
            *vector_terms,
            jnp.zeros((width, 16), low),
            high,
            rest,
        ],
        1,
    )
    second_pack = jnp.concatenate(
        [
            expand.astype(low),
            contract.T.astype(low),
            own_readout.astype(low),
            combine.T.astype(low),
        ],
        1,
    )
    first_all = lax.all_gather(first_pack, everyone, axis=0, tiled=True)
    first_all = first_all.reshape(pieces, model, -1)

    length_row = jnp.pad(row_lengths[None, :], ((0, 0), (0, seq_len - row_count)))
    facts = jnp.concatenate([token_ids, jnp.pad(length_row, ((0, 8 - 1 - row_count), (0, 0)))], 0)
    all_facts = share_facts(facts, 1) if direct else lax.all_gather(facts, "dp")
    all_ids = all_facts[:, :row_count].reshape(owners * row_count, seq_len)
    all_lengths = all_facts[:, row_count, :row_count].reshape(-1)
    token_total = jnp.sum(all_lengths).astype(f32)
    local_ids = all_ids - holder * vocab_slab
    inside = (local_ids >= 0) & (local_ids < vocab_slab)
    inside = inside & (jnp.arange(seq_len)[None] < all_lengths[:, None])
    inside = inside.reshape(-1, ROW_SET * seq_len)
    counts = jnp.sum(inside.astype(jnp.int32), 1)
    shift = vocab_slab.bit_length()
    keys = jnp.arange(ROW_SET * seq_len, dtype=jnp.int32)[None] << shift
    keys = jnp.where(
        inside,
        keys + local_ids.reshape(inside.shape),
        ((ROW_SET * seq_len) << shift) + vocab_slab,
    )
    keys = lax.sort(keys.T, dimension=0, is_stable=False).T

    found = lookup(counts, keys, embedding, seq_len)
    found = found.reshape(owners, row_count, width, seq_len)
    if direct:
        found = exchange_words(found, 2)
    else:
        found = lax.psum_scatter(found, "heads", scatter_dimension=1, tiled=True)[:, 0]
        found = lax.all_to_all(found, "dp", 0, 0, tiled=True)
    own_length = lax.dynamic_slice_in_dim(row_lengths, holder, 1)
    own_live = jnp.arange(seq_len) < own_length
    own_flags = lax.dynamic_slice_in_dim(replaced, holder, 1)[0].astype(f32)
    marks = jnp.stack([jnp.where(own_live, 1.0 / token_total, 0.0), own_flags], 1)

    entries = relative.shape[0]
    words = found.reshape(model, seq_len)
    if direct:
        *ready, probs, mixed, second_all = attend_gather(
            own_length, first_all, words, second_pack, head_width, entries, 3
        )
    else:
        ready = prepare(first_all, words, head_width, entries)
        probs, mixed = attend(own_length, ready[3], ready[6])
        second_all = lax.all_gather(second_pack, everyone, axis=0, tiled=True)
    vec_full, white, rate, qkv, rel_white, rel_rate, rel_table = ready
    second_all = second_all.reshape(pieces, model, -1)
    grad_contract, grad_expand, grad_joint, grad_mixed, grad_sum, grad_vec, losses = middle(
        second_all, vec_full, white, mixed, marks
    )
    back = (first_all, vec_full, white, rate, rel_white, rel_rate, grad_sum)
    if direct:
        qkv_grads, rel_table_grads, *sums = attend_back_sums(
            qkv, rel_table, probs, grad_mixed, [grad_contract, grad_expand, grad_joint], 4
        )
        sent, project_sum = project_return(*back, qkv_grads, rel_table_grads, grad_vec, tag=5)
        sums.append(project_sum)
    else:
        qkv_grads, rel_table_grads = attend_back(qkv, rel_table, probs, grad_mixed)
        sent, grad_project = project_back(*back, qkv_grads, rel_table_grads, grad_vec)
        sent = sent.reshape(owners, width, seq_len)
        sent = lax.all_to_all(sent, "dp", 0, 0, tiled=True)
        sent = lax.all_gather(sent, "heads", axis=0)
        sent = sent.transpose(1, 0, 2, 3)
        sums = [
            lax.psum_scatter(
                part.reshape(pieces * model, -1), everyone, scatter_dimension=0, tiled=True
            ).astype(f32)
            for part in (grad_contract, grad_expand, grad_joint, grad_project)
        ]
    sent = sent.reshape(owners * row_count, width, seq_len)
    grad_embedding, own_squares = deposit(counts, keys, sent, vocab_slab)

    weights = (embedding, relative, project, combine, expand, contract, readout, vectors)
    means = (
        embedding_mean,
        relative_mean,
        project_mean,
        combine_mean,
        expand_mean,
        contract_mean,
        readout_mean,
        vectors_mean,
    )
    squares = (
        embedding_square,
        relative_square,
        project_square,
        combine_square,
        expand_square,
        contract_square,
        readout_square,
        vectors_square,
    )
    if direct:
        turns = {1: (1, 0), 2: (1, 0, 2), 5: (1, 0)}
        flat = [
            part.transpose(turns[index]) if index in turns else part
            for index, parts in enumerate(zip(weights, means, squares))
            for part in parts
        ]
        all_facts, shared = finish_sums(losses, own_squares, sums, head_width, 6)
        *flat, norm_row, bias_row = update_all(
            all_facts, shared, [grad_embedding, *sums], flat, head_width
        )
        flat = [
            part.transpose(turns[index // 3]) if index // 3 in turns else part
            for index, part in enumerate(flat)
        ]
        return (all_facts[1, 0], token_total, norm_row[0, 0], *flat, bias_row[0])

    squares_local = sum(jnp.sum(part * part) for part in sums) + jnp.sum(own_squares)
    shared = jnp.concatenate([sums[2][:, :head_width], sums[3][:, 3 * head_width :]], 1)
    squares_total, loss_sum = lax.psum((squares_local, jnp.sum(losses)), everyone)
    shared = lax.all_gather(shared, "heads", axis=0)
    grad_norm = jnp.sqrt(squares_total)
    factor = jnp.minimum(1.0, clip_level / grad_norm)
    grad_readout = shared[:, :, :head_width].transpose(1, 0, 2).reshape(width, model)
    at = head_width + BLOCK // 2
    grad_relative = shared[:, :, at:].transpose(0, 2, 1).reshape(entries, width)
    grad_vec = shared[:, :, head_width : head_width + 3].transpose(0, 2, 1).reshape(-1, width)
    grad_vec = grad_vec[:vector_count]
    gradients = (
        grad_embedding,
        grad_relative,
        sums[3][:, : 3 * head_width].reshape(width, 3, head_width),
        sums[2][:, head_width:].T,
        sums[1],
        sums[0].T,
        grad_readout,
        grad_vec,
    )
    updates = [
        adamw(weight, gradient * factor, mean, square, rate_now)
        for weight, gradient, mean, square, rate_now in zip(
            weights, gradients, means, squares, rate_steps
        )
    ]
    flat = [part for parts in updates for part in parts]
    return (loss_sum, token_total, grad_norm, *flat, grad_vec[3] * factor)


def solution(mesh):
    placed = (
        P("dp", None),
        P("dp"),
        P("dp", None),
        P("dp", "heads"),
        P(None, "dp"),
        P("dp", None, "heads"),
        P("heads", "dp"),
        P("dp", "heads"),
        P("heads", "dp"),
        P("dp", None),
        P(None, "dp"),
        P("dp", "heads"),
        P(None, "dp"),
        P("dp", None, "heads"),
        P("heads", "dp"),
        P("dp", "heads"),
        P("heads", "dp"),
        P("dp", None),
        P(None, "dp"),
        P("dp", "heads"),
        P(None, "dp"),
        P("dp", None, "heads"),
        P("heads", "dp"),
        P("dp", "heads"),
        P("heads", "dp"),
        P("dp", None),
        P(None, "dp"),
    )
    return jax.shard_map(
        per_device,
        mesh=mesh,
        in_specs=placed,
        out_specs=(
            P(),
            P(),
            P(),
            P("dp", "heads"),
            P("dp", "heads"),
            P("dp", "heads"),
            P(None, "dp"),
            P(None, "dp"),
            P(None, "dp"),
            P("dp", None, "heads"),
            P("dp", None, "heads"),
            P("dp", None, "heads"),
            P("heads", "dp"),
            P("heads", "dp"),
            P("heads", "dp"),
            P("dp", "heads"),
            P("dp", "heads"),
            P("dp", "heads"),
            P("heads", "dp"),
            P("heads", "dp"),
            P("heads", "dp"),
            P("dp", None),
            P("dp", None),
            P("dp", None),
            P(None, "dp"),
            P(None, "dp"),
            P(None, "dp"),
            P("dp"),
        ),
        check_vma=False,
    )
```

```python
import functools

import jax
import jax.numpy as jnp
from jax import lax
from jax.experimental import pallas as pl
from jax.experimental.pallas import tpu as pltpu
from jax.sharding import PartitionSpec as P

HEAD_DIM = 64
STEP = 10
BLOCK = 128
UNROLL = 16
ROW_SET = 8

low = jnp.bfloat16
f32 = jnp.float32

layer_eps = 1e-07
clip_level = 0.005
rate_steps = (0.1, 0.05, 0.05, 0.05, 0.05, 0.05, 0.05, 1.0)
beta_first = 0.9
beta_second = 0.999
adam_eps = 1e-08
weight_decay = 0.01


def dot_rows(a,b):
    return lax.dot_general(a,b,(((1,),(1,)),((),())),preferred_element_type=f32)
def dot_plain(a,b):
    return lax.dot_general(a,b,(((1,),(0,)),((),())),preferred_element_type=f32)
def dot_left(a,b):
    return lax.dot_general(a,b,(((0,),(0,)),((),())),preferred_element_type=f32)

def attend_head(group, head, length, qkv_ref, table_ref, probs_ref, mixed_ref, far_ref):
    seq = qkv_ref.shape[1]
    width = qkv_ref.shape[2] // 3
    heads = width // HEAD_DIM
    scale = (3 * HEAD_DIM) ** -0.5
    live = lax.broadcasted_iota(jnp.int32, (BLOCK, seq), 1) < length
    at = head * HEAD_DIM
    q = qkv_ref[group, :, at : at + HEAD_DIM]
    k = qkv_ref[group, :, width + at : width + at + HEAD_DIM]
    v = qkv_ref[group, :, 2 * width + at : 2 * width + at + HEAD_DIM]
    for block in range(seq // BLOCK):
        rows = slice(block * BLOCK, (block + 1) * BLOCK)
        window = slice(seq - BLOCK * (block + 1), 2 * seq - BLOCK * block)
        far = dot_rows(k[rows], table_ref[group, window, at : at + HEAD_DIM])
        far = pltpu.roll(far, seq, 1, stride=1, stride_axis=0)[:, :seq]
        far_ref[head, :, rows] = far.T
    for block in range(seq // BLOCK):
        rows = slice(block * BLOCK, (block + 1) * BLOCK)
        window = slice(seq - BLOCK * (block + 1), 2 * seq - BLOCK * block)
        near = dot_rows(q[rows], table_ref[group, window, width + at : width + at + HEAD_DIM])
        near = pltpu.roll(near, seq, 1, stride=1, stride_axis=0)[:, :seq]
        scores = (dot_rows(q[rows], k) + near + far_ref[head, rows, :]) * scale
        scores = jnp.where(live, scores, -1e9)
        top = jnp.max(scores, -1, keepdims=True)
        expo = jnp.exp(scores - top)
        probs = (expo * (1.0 / jnp.sum(expo, -1, keepdims=True))).astype(low)
        probs_ref[group * heads + head, rows, :] = probs
        mixed_ref[group, rows, at : at + HEAD_DIM] = dot_plain(probs, v).astype(low)


def attend_kernel(length_ref, qkv_ref, table_ref, probs_ref, mixed_ref, far_ref):
    for head in range(far_ref.shape[0]):
        attend_head(0, head, length_ref[0], qkv_ref, table_ref, probs_ref, mixed_ref, far_ref)


def attend(length, qkv, table):
    groups, seq, width3 = qkv.shape
    width = width3 // 3
    heads = width // HEAD_DIM
    return pl.pallas_call(
        attend_kernel,
        grid=(groups,),
        in_specs=[
            pl.BlockSpec(memory_space=pltpu.SMEM),
            pl.BlockSpec((1, seq, width3), lambda g: (g, 0, 0)),
            pl.BlockSpec((1, 2 * seq, 2 * width), lambda g: (g, 0, 0)),
        ],
        out_specs=[
            pl.BlockSpec((heads, seq, seq), lambda g: (g, 0, 0)),
            pl.BlockSpec((1, seq, width), lambda g: (g, 0, 0)),
        ],
        out_shape=[
            jax.ShapeDtypeStruct((groups * heads, seq, seq), low),
            jax.ShapeDtypeStruct((groups, seq, width), low),
        ],
        scratch_shapes=[pltpu.VMEM((heads, seq, seq), f32)],
        compiler_params=pltpu.CompilerParams(vmem_limit_bytes=48 << 20),
        name="attend",
    )(length, qkv, table)


def attend_back_head(
    group, head, qkv_ref, table_ref, probs_ref, up_ref, grad_ref, rel_ref, low_ref, sum_ref
):
    seq = qkv_ref.shape[1]
    width = qkv_ref.shape[2] // 3
    heads = width // HEAD_DIM
    scale = (3 * HEAD_DIM) ** -0.5
    row = lax.broadcasted_iota(jnp.int32, (BLOCK, BLOCK), 0)
    flip = row + lax.broadcasted_iota(jnp.int32, (BLOCK, BLOCK), 1) == BLOCK - 1
    flip = flip.astype(f32).astype(low)
    edge = jnp.zeros((BLOCK, BLOCK), f32)

    def shear(rows):
        return pltpu.roll(jnp.concatenate([rows, edge], 1), 1, 1, stride=1, stride_axis=0).astype(low)

    at = head * HEAD_DIM
    q = qkv_ref[group, :, at : at + HEAD_DIM]
    k = qkv_ref[group, :, width + at : width + at + HEAD_DIM]
    v = qkv_ref[group, :, 2 * width + at : 2 * width + at + HEAD_DIM]
    up = up_ref[group, :, at : at + HEAD_DIM]
    source = group * heads + head
    for block in range(seq // BLOCK):
        rows = slice(block * BLOCK, (block + 1) * BLOCK)
        probs = probs_ref[source, rows, :].astype(f32)
        pull = dot_rows(up[rows], v)
        inner = jnp.sum(probs * pull, -1, keepdims=True)
        low_ref[head, rows, :] = (probs * (pull - inner) * scale).astype(low)
    grad_v = dot_left(up, probs_ref[source]).T.astype(low)
    grad_ref[group, :, 2 * width + at : 2 * width + at + HEAD_DIM] = grad_v
    sum_ref[2 * head] = jnp.zeros(sum_ref.shape[1:], f32)
    sum_ref[2 * head + 1] = jnp.zeros(sum_ref.shape[1:], f32)
    for block in range(seq // BLOCK):
        rows = slice(block * BLOCK, (block + 1) * BLOCK)
        window = slice(seq - BLOCK * (block + 1), 2 * seq - BLOCK * block)
        turned = dot_plain(flip, low_ref[head, rows, :])
        near = shear(turned)
        grad_q = dot_plain(turned.astype(low), k) + dot_plain(
            near, table_ref[group, window, width + at : width + at + HEAD_DIM]
        )
        grad_ref[group, rows, at : at + HEAD_DIM] = dot_plain(flip, grad_q.astype(low)).astype(low)
        q_turned = dot_plain(flip, q[rows]).astype(low)
        sum_ref[2 * head + 1, :, window] += dot_left(q_turned, near)
        turned = dot_rows(flip, low_ref[head, :, rows])
        far = shear(turned)
        grad_k = dot_plain(turned.astype(low), q) + dot_plain(
            far, table_ref[group, window, at : at + HEAD_DIM]
        )
        grad_ref[group, rows, width + at : width + at + HEAD_DIM] = dot_plain(
            flip, grad_k.astype(low)
        ).astype(low)
        k_turned = dot_plain(flip, k[rows]).astype(low)
        sum_ref[2 * head, :, window] += dot_left(k_turned, far)
    rel_ref[group, :, at : at + HEAD_DIM] = sum_ref[2 * head].T.astype(low)
    rel_ref[group, :, width + at : width + at + HEAD_DIM] = sum_ref[2 * head + 1].T.astype(low)


def attend_back_kernel(*refs):
    for head in range(refs[-2].shape[0]):
        attend_back_head(0, head, *refs)


def attend_back(qkv, table, probs, up):
    groups, seq, width3 = qkv.shape
    width = width3 // 3
    heads = width // HEAD_DIM
    block = lambda *shape: pl.BlockSpec(shape, lambda g: (g, 0, 0))
    return pl.pallas_call(
        attend_back_kernel,
        grid=(groups,),
        in_specs=[
            block(1, seq, width3),
            block(1, 2 * seq, 2 * width),
            block(heads, seq, seq),
            block(1, seq, width),
        ],
        out_specs=[block(1, seq, width3), block(1, 2 * seq, 2 * width)],
        out_shape=[
            jax.ShapeDtypeStruct((groups, seq, width3), low),
            jax.ShapeDtypeStruct((groups, 2 * seq, 2 * width), low),
        ],
        scratch_shapes=[
            pltpu.VMEM((heads, seq, seq), low),
            pltpu.VMEM((2 * heads, HEAD_DIM, 2 * seq), f32),
        ],
        compiler_params=pltpu.CompilerParams(vmem_limit_bytes=48 << 20),
        name="attend_back",
    )(qkv, table, probs, up)


MESH = pl.DeviceIdType.MESH
ANYWHERE = pl.BlockSpec(memory_space=pl.ANY)
IN_VMEM = pl.BlockSpec(memory_space=pltpu.VMEM)


def place():
    owner, holder = lax.axis_index("dp"), lax.axis_index("heads")
    return owner // 2, owner % 2, holder // 2, holder % 2


def device(z, x, y, c):
    return (z * 2 + x, y * 2 + c)


def signal(target):
    pl.semaphore_signal(
        pltpu.get_barrier_semaphore(), inc=1, device_id=target, device_id_type=MESH
    )


def along_z(z):
    return [(z + step) % 4 for step in (2, 1, 3)]


def greet(z, x, y, c, line):
    signal(device(z, x, y, 1 - c))
    signal(device(z, x, 1 - y, c))
    if line:
        signal(device(z, 1 - x, y, c))
        for other in along_z(z):
            signal(device(other, x, y, c))
        pl.semaphore_wait(pltpu.get_barrier_semaphore(), 6)


def remote(source, target, send, recv, to):
    return pltpu.make_async_remote_copy(
        src_ref=source, dst_ref=target, send_sem=send, recv_sem=recv, device_id=to, device_id_type=MESH
    )


def sum_scratch(width, sizes):
    half = width // 2
    leads = (
        (2, 4, 2, width),
        (2, 4, 2, width),
        (4, 2, half),
        (2, 4, half),
        (4, half),
        (4, half),
        (4, width),
    )
    shapes = [pltpu.VMEM(lead + (size,), low) for lead in leads for size in sizes]
    count = len(sizes)
    return shapes + [
        pltpu.SemaphoreType.DMA((count, 2)),
        pltpu.SemaphoreType.DMA((count, 9)),
        pltpu.SemaphoreType.DMA((count, 10)),
    ]


def sum_stages(spot, grads, totals, chunks, refs, resident=False):
    count = len(chunks)
    pair, own, first_a, first_b, second_a, second_b, column = [
        refs[count * part : count * (part + 1)] for part in range(7)
    ]
    local_sem, send_sem, recv_sem = refs[7 * count :]
    z, x, y, c = spot
    half = grads[0].shape[3] // 2
    upper, lower = pl.ds(0, half), pl.ds(half, half)
    core_to, y_to, x_to = device(z, x, y, 1 - c), device(z, x, 1 - y, c), device(z, 1 - x, y, c)

    def columns(part):
        return pl.ds(chunks[part][1], chunks[part][2])

    def source(part, row):
        return grads[chunks[part][0]].at[row, :, :, :, columns(part)]

    def link(part, slot, source, target, to):
        return remote(source, target, send_sem.at[part, slot], recv_sem.at[part, slot], to)

    def local(part, side):
        return pltpu.make_async_copy(
            source(part, side * 2 + c), own[part].at[side], local_sem.at[part, side]
        )

    def pair_copy(part, side):
        return link(part, side, source(part, side * 2 + 1 - c), pair[part].at[side], core_to)

    def first_copies(part):
        block = own[part]
        return (
            link(part, 2, block.at[1 - y, :, :, upper], first_a[part], y_to),
            link(part, 3, block.at[:, :, 1 - x, lower], first_b[part], x_to),
        )

    def second_copies(part):
        block = own[part]
        return (
            link(part, 4, block.at[y, :, 1 - x, upper], second_a[part], x_to),
            link(part, 5, block.at[1 - y, :, x, lower], second_b[part], y_to),
        )

    def line_copy(part, step, to):
        return remote(
            own[part].at[y, to, x],
            column[part].at[z],
            send_sem.at[part, 6 + step],
            recv_sem.at[part, 6 + z],
            device(to, x, y, c),
        )

    def line_arrival(part, step, source):
        return remote(
            own[part].at[y, z, x],
            column[part].at[source],
            send_sem.at[part, 6 + step],
            recv_sem.at[part, 6 + source],
            device(source, x, y, c),
        )

    def add(target, source):
        target[...] = (target[...].astype(f32) + source[...].astype(f32)).astype(low)

    def start_pair(part):
        for side in range(2):
            pair_copy(part, side).start()
            if not resident:
                local(part, side).start()

    def stage_pair(part):
        for side in range(2):
            if not resident:
                local(part, side).wait()
            pair_copy(part, side).wait()
        if part + 2 < count:
            start_pair(part + 2)

        def step(index, carry):
            side, rest = index // 8, index % 8
            spot = (side, rest // 2, rest % 2)
            kept = own[part].at[spot]
            if resident:
                array, first, size = chunks[part]
                kept = grads[array].at[side * 2 + c, rest // 2, rest % 2, :, pl.ds(first, size)]
            total = kept[...].astype(f32) + pair[part].at[spot][...].astype(f32)
            own[part].at[spot][...] = total.astype(low)
            return carry

        lax.fori_loop(0, 16, step, 0)
        for copy in first_copies(part):
            copy.start()

    def stage_first(part):
        for copy in first_copies(part):
            copy.wait()

        def step(index, carry):
            add(own[part].at[y, index // 2, index % 2, upper], first_a[part].at[index // 2, index % 2])
            add(own[part].at[index % 2, index // 2, x, lower], first_b[part].at[index % 2, index // 2])
            return carry

        lax.fori_loop(0, 8, step, 0)
        for copy in second_copies(part):
            copy.start()

    def stage_second(part):
        for copy in second_copies(part):
            copy.wait()

        def step(index, carry):
            add(own[part].at[y, index, x, upper], second_a[part].at[index])
            add(own[part].at[y, index, x, lower], second_b[part].at[index])
            return carry

        lax.fori_loop(0, 4, step, 0)
        for step, to in enumerate(along_z(z)):
            line_copy(part, step, to).start()

    def stage_total(part):
        total = totals[chunks[part][0]].at[:, columns(part)]
        total[...] = own[part][y, z, x].astype(f32)
        for step, other in enumerate(along_z(z)):
            line_arrival(part, step, other).wait_recv()
            total[...] += column[part][other].astype(f32)
        for step, to in enumerate(along_z(z)):
            line_copy(part, step, to).wait_send()

    return start_pair, {
        "pair": stage_pair,
        "first": stage_first,
        "second": stage_second,
        "total": stage_total,
    }


def chunked(sizes, most=3 * BLOCK):
    return [
        (array, first, min(most, size - first))
        for array, size in enumerate(sizes)
        for first in range(0, size, most)
    ]


BACK_START = (("pair", 0),)
BACK_SLOTS = {
    0: (("pair", 1),),
    1: (("first", 0),),
    2: (("pair", 2),),
    3: (("first", 1), ("second", 0)),
    4: (("pair", 3),),
    5: (("first", 2), ("second", 1), ("total", 0)),
    6: (("pair", 4),),
    7: (("first", 3), ("second", 2), ("total", 1)),
    9: (("first", 4), ("second", 3), ("total", 2)),
    11: (("second", 4), ("total", 3)),
}
BACK_END = (("total", 4),)


def run_all(stages, steps):
    for name, chunk in steps:
        stages[name](chunk)


def attend_back_sums_kernel(count, chunks, *refs):
    inputs, grads = list(refs[:4]), refs[4 : 4 + count]
    outputs, totals = refs[4 + count : 6 + count], refs[6 + count : 6 + 2 * count]
    work, rest = refs[6 + 2 * count : 8 + 2 * count], refs[8 + 2 * count :]
    probs_ref, load_sem, *rest = rest
    probs_in, inputs[2] = inputs[2], probs_ref
    groups, heads = inputs[0].shape[0], work[0].shape[0]

    def load(group):
        part = pl.ds(group * heads, heads)
        return pltpu.make_async_copy(probs_in.at[part], probs_ref.at[part], load_sem.at[group])

    for group in range(groups):
        load(group).start()
    spot = place()
    greet(*spot, True)
    start_pair, stages = sum_stages(spot, grads, totals, chunks, rest)
    for chunk in range(2):
        start_pair(chunk)
    run_all(stages, BACK_START)

    def step(group, carry):
        load(group).wait()
        for head in range(heads):
            attend_back_head(group, head, *inputs, *outputs, *work)
            for slot, steps in BACK_SLOTS.items():
                if slot % heads == head:
                    pl.when(group == slot // heads)(functools.partial(run_all, stages, steps))
        return carry

    lax.fori_loop(0, groups, step, 0)
    run_all(stages, BACK_END)


def attend_back_sums(qkv, table, probs, up, grads, tag):
    groups, seq, width3 = qkv.shape
    width = width3 // 3
    heads = width // HEAD_DIM
    part = grads[0].shape[1] // 8
    sizes = [grad.shape[2] for grad in grads]
    chunks = chunked(sizes)
    return pl.pallas_call(
        functools.partial(attend_back_sums_kernel, len(grads), chunks),
        in_specs=[IN_VMEM, IN_VMEM, ANYWHERE, IN_VMEM] + [ANYWHERE] * len(grads),
        out_specs=[IN_VMEM] * (2 + len(grads)),
        out_shape=[
            jax.ShapeDtypeStruct((groups, seq, width3), low),
            jax.ShapeDtypeStruct((groups, 2 * seq, 2 * width), low),
        ]
        + [jax.ShapeDtypeStruct((part, size), f32) for size in sizes],
        scratch_shapes=[
            pltpu.VMEM((heads, seq, seq), low),
            pltpu.VMEM((2 * heads, HEAD_DIM, 2 * seq), f32),
            pltpu.VMEM(probs.shape, low),
            pltpu.SemaphoreType.DMA((groups,)),
        ]
        + sum_scratch(part, [chunk[2] for chunk in chunks]),
        compiler_params=pltpu.CompilerParams(
            collective_id=tag, has_side_effects=True, vmem_limit_bytes=60 << 20
        ),
        name="attend_back_sums",
    )(qkv, table, probs, up, *[grad.reshape(4, 4, 2, part, -1) for grad in grads])


def peers(z, x):
    return [((z + 2 - far) % 4, x if same else 1 - x) for far, same in PEER_ORDER]


PEER_ORDER = ((0, False), (0, True), (1, False), (1, True), (3, False), (3, True), (2, False))


def meet_owners(z, x, y, c):
    for peer_z, peer_x in peers(z, x):
        signal(device(peer_z, peer_x, y, c))


def share_facts_kernel(facts_ref, all_ref, local_sem, send_sem, recv_sem):
    z, x, y, c = place()
    meet_owners(z, x, y, c)
    pl.semaphore_wait(pltpu.get_barrier_semaphore(), 7)
    here = z * 2 + x
    keep = pltpu.make_async_copy(facts_ref, all_ref.at[here], local_sem)
    keep.start()
    copies = []
    for index, (peer_z, peer_x) in enumerate(peers(z, x)):
        copy = remote(
            facts_ref,
            all_ref.at[here],
            send_sem.at[index],
            recv_sem.at[here],
            device(peer_z, peer_x, y, c),
        )
        copy.start()
        copies.append(copy)
    for index, (peer_z, peer_x) in enumerate(peers(z, x)):
        there = peer_z * 2 + peer_x
        copies[index].wait_send()
        remote(
            facts_ref, all_ref.at[there], send_sem.at[index], recv_sem.at[there], device(z, x, y, c)
        ).wait_recv()
    keep.wait()


def share_facts(facts, tag):
    return pl.pallas_call(
        share_facts_kernel,
        in_specs=[IN_VMEM],
        out_specs=IN_VMEM,
        out_shape=jax.ShapeDtypeStruct((8,) + facts.shape, facts.dtype),
        scratch_shapes=[
            pltpu.SemaphoreType.DMA,
            pltpu.SemaphoreType.DMA((7,)),
            pltpu.SemaphoreType.DMA((8,)),
        ],
        compiler_params=pltpu.CompilerParams(collective_id=tag, has_side_effects=True),
        name="share_facts",
    )(facts)


def word_stages(spot, found_ref, words_ref, pair, side, send_sem, recv_sem, out_sem, in_sem):
    z, x, y, c = spot
    here = z * 2 + x
    targets = peers(z, x) + [(z, x)]
    core_to, y_to = device(z, x, y, 1 - c), device(z, x, 1 - y, c)

    def at_home(part):
        return targets[part][0] * 2 + targets[part][1]

    def pair_copy(part, row):
        to = at_home(part)
        return remote(
            found_ref.at[to, row * 2 + 1 - c],
            pair.at[row, to],
            send_sem.at[part, row],
            recv_sem.at[part, row],
            core_to,
        )

    def side_copy(part):
        to = at_home(part)
        return remote(
            pair.at[1 - y, to], side.at[to], send_sem.at[part, 2], recv_sem.at[part, 2], y_to
        )

    def out_copy(part):
        return remote(
            pair.at[y, at_home(part)],
            words_ref.at[here],
            out_sem.at[part],
            in_sem.at[here],
            device(targets[part][0], targets[part][1], y, c),
        )

    def start():
        for part in range(8):
            for row in range(2):
                pair_copy(part, row).start()

    def sideways(first, last):
        for part in range(first, last):
            to = at_home(part)
            for row in range(2):
                pair_copy(part, row).wait_recv()
                pair[row, to] = pair[row, to] + found_ref[to, row * 2 + c]
            side_copy(part).start()

    def outward(first, last):
        for part in range(first, last):
            to = at_home(part)
            side_copy(part).wait_recv()
            pair[y, to] = pair[y, to] + side[to]
            if part < 7:
                out_copy(part).start()
            else:
                words_ref[here] = pair[y, to]

    def finish():
        for part in range(8):
            for row in range(2):
                pair_copy(part, row).wait_send()
            side_copy(part).wait_send()
            if part < 7:
                out_copy(part).wait_send()
                there = at_home(part)
                remote(
                    pair.at[y, there], words_ref.at[there], out_sem.at[part], in_sem.at[there], core_to
                ).wait_recv()

    return start, sideways, outward, finish


def exchange_words_kernel(found_ref, words_ref, *refs):
    spot = place()
    meet_owners(*spot)
    greet(*spot, False)
    pl.semaphore_wait(pltpu.get_barrier_semaphore(), 9)
    start, sideways, outward, finish = word_stages(spot, found_ref, words_ref, *refs)
    start()
    sideways(0, 8)
    outward(0, 8)
    finish()


def exchange_words(found, tag):
    piece = found.shape[2:]
    return pl.pallas_call(
        exchange_words_kernel,
        in_specs=[IN_VMEM],
        out_specs=IN_VMEM,
        out_shape=jax.ShapeDtypeStruct((8,) + piece, low),
        scratch_shapes=[
            pltpu.VMEM((2, 8) + piece, low),
            pltpu.VMEM((8,) + piece, low),
            pltpu.SemaphoreType.DMA((8, 3)),
            pltpu.SemaphoreType.DMA((8, 3)),
            pltpu.SemaphoreType.DMA((8,)),
            pltpu.SemaphoreType.DMA((8,)),
        ],
        compiler_params=pltpu.CompilerParams(
            collective_id=tag, has_side_effects=True, vmem_limit_bytes=40 << 20
        ),
        name="exchange_words",
    )(found)


def return_stages(spot, grads_ref, sent_ref, refs):
    local_sem, out_sem, in_sem, send_sem, recv_sem = refs
    z, x, y, c = spot
    here = z * 2 + x
    own = y * 2 + c
    other = (1 - y) * 2 + c
    core_to, y_to = device(z, x, y, 1 - c), device(z, x, 1 - y, c)
    order = [(z, x)] + peers(z, x)[::-1]
    keep = pltpu.make_async_copy(grads_ref.at[here], sent_ref.at[here, own], local_sem)

    def out_copy(part, peer):
        return remote(
            grads_ref.at[peer[0] * 2 + peer[1]],
            sent_ref.at[here, own],
            out_sem.at[part],
            in_sem.at[here],
            device(peer[0], peer[1], y, c),
        )

    def in_copy(part, peer):
        there = peer[0] * 2 + peer[1]
        return remote(
            grads_ref.at[there], sent_ref.at[there, own], out_sem.at[part], in_sem.at[there], core_to
        )

    def pass_on(slot, row, there, to, source=None):
        block = sent_ref.at[there, row]
        source = block if source is None else source
        return remote(source, block, send_sem.at[slot, there], recv_sem.at[row, there], to)

    def start():
        keep.start()
        for part, peer in enumerate(peers(z, x)):
            out_copy(part, peer).start()

    def forward(first, last):
        for part in range(first, last):
            there = order[part][0] * 2 + order[part][1]
            source = grads_ref.at[here]
            if part > 0:
                in_copy(part - 1, order[part]).wait_recv()
                source = None
            pass_on(0, own, there, y_to, source).start()
            pass_on(1, own, there, core_to, source).start()

    def relay(first, last):
        for part in range(first, last):
            there = order[part][0] * 2 + order[part][1]
            pass_on(0, other, there, y_to).wait_recv()
            pass_on(2, other, there, core_to).start()

    def finish():
        keep.wait()
        for part, peer in enumerate(peers(z, x)):
            out_copy(part, peer).wait_send()
        for peer_z, peer_x in order:
            there = peer_z * 2 + peer_x
            pass_on(0, own, there, y_to).wait_send()
            pass_on(1, own, there, core_to).wait_send()
            pass_on(2, other, there, core_to).wait_send()
            pass_on(1, y * 2 + 1 - c, there, core_to).wait_recv()
            pass_on(2, (1 - y) * 2 + 1 - c, there, core_to).wait_recv()

    return start, forward, relay, finish


def return_scratch():
    return [
        pltpu.SemaphoreType.DMA,
        pltpu.SemaphoreType.DMA((7,)),
        pltpu.SemaphoreType.DMA((8,)),
        pltpu.SemaphoreType.DMA((3, 8)),
        pltpu.SemaphoreType.DMA((4, 8)),
    ]


def gather_stages(spot, pack_ref, all_ref, local_sem, send_sem, recv_sem, line_sem, core_sem):
    z, x, y, c = spot
    half = pack_ref.shape[0] // 2
    core_to, y_to, x_to = device(z, x, y, 1 - c), device(z, x, 1 - y, c), device(z, 1 - x, y, c)
    up_to, down_to = device(z + 1, x, y, c), device(z - 1, x, y, c)
    keep = pltpu.make_async_copy(pack_ref, all_ref.at[y * 2 + c, z * 2 + x], local_sem)
    CROSS, SIDE, UP, DOWN = range(4)
    targets = (x_to, y_to, up_to, down_to)

    def copy(kind, part, zz, xx, yy, own=False):
        at = lax.clamp(0, zz, 3) * 2 + xx
        rows = pl.ds(part * half, half)
        block = all_ref.at[yy * 2 + c, at, rows]
        source = pack_ref.at[rows] if own else block
        return remote(
            source, block, send_sem.at[kind, part, yy, at], recv_sem.at[part, yy, at], targets[kind]
        )

    def line_copy(kind, zz, own=False):
        zz = lax.clamp(0, zz, 3)
        block = all_ref.at[y * 2 + c, zz * 2 + x]
        source = pack_ref if own else block
        return remote(source, block, line_sem.at[kind - UP, zz], line_sem.at[2, zz], targets[kind])

    def core_copy(zz, yy, column):
        zz = lax.clamp(0, zz, 3)
        block = all_ref.at[yy * 2 + column, pl.ds(zz * 2, 2)]
        return remote(block, block, core_sem.at[0, yy, zz], core_sem.at[1, yy, zz], core_to)

    def distances(far):
        if far == 0:
            return [(z, z >= 0, None)]
        return [(z - far, z >= far, UP), (z + far, z <= 3 - far, DOWN)]

    def along(way):
        if way is None:
            return [(UP, z < 3), (DOWN, z > 0)]
        return [(way, z < 3 if way == UP else z > 0)]

    def for_each(far, action):
        for zz, exists, way in distances(far):
            pl.when(exists)(functools.partial(action, zz, way))

    def onward(zz, way, action):
        for on, possible in along(way):
            pl.when(possible)(lambda on=on: action(line_copy(on, zz, way is None)))

    def line_one(zz, way):
        own = way is None
        if not own:
            line_copy(way, zz).wait_recv()
        onward(zz, way, lambda copy: copy.start())
        copy(CROSS, 0, zz, x, y, own).start()
        copy(SIDE, 1, zz, x, y, own).start()

    def rest_one(zz, way):
        own = way is None
        copy(SIDE, 0, zz, x, y, own).start()
        copy(CROSS, 1, zz, x, y, own).start()

    def sides_one(zz, way):
        copy(CROSS, 0, zz, 1 - x, y).wait_recv()
        copy(SIDE, 0, zz, 1 - x, y).start()
        copy(SIDE, 1, zz, x, 1 - y).wait_recv()
        copy(CROSS, 1, zz, x, 1 - y).start()

    def corners_one(zz, way):
        for kind, part, xx, yy in (
            (SIDE, 0, x, 1 - y),
            (CROSS, 1, 1 - x, y),
            (SIDE, 0, 1 - x, 1 - y),
            (CROSS, 1, 1 - x, 1 - y),
        ):
            copy(kind, part, zz, xx, yy).wait_recv()
        if way is None:
            keep.wait()
        for yy in range(2):
            core_copy(zz, yy, c).start()

    def finish_one(zz, way):
        onward(zz, way, lambda copy: copy.wait_send())
        for part in range(2):
            copy(CROSS, part, zz, x, y).wait_send()
            copy(SIDE, part, zz, x, y).wait_send()
        copy(SIDE, 0, zz, 1 - x, y).wait_send()
        copy(CROSS, 1, zz, x, 1 - y).wait_send()
        for yy in range(2):
            core_copy(zz, yy, c).wait_send()
            core_copy(zz, yy, 1 - c).wait_recv()

    steps = {
        "line": line_one,
        "rest": rest_one,
        "sides": sides_one,
        "corners": corners_one,
        "finish": finish_one,
    }
    return keep.start, {
        name: functools.partial(for_each, action=action) for name, action in steps.items()
    }


def gather_scratch():
    return [
        pltpu.SemaphoreType.DMA,
        pltpu.SemaphoreType.DMA((4, 2, 2, 8)),
        pltpu.SemaphoreType.DMA((2, 2, 8)),
        pltpu.SemaphoreType.DMA((3, 4)),
        pltpu.SemaphoreType.DMA((2, 2, 4)),
    ]


def finish_sums_kernel(
    width,
    losses_ref,
    squares_ref,
    *refs,
):
    sums, refs = refs[:4], refs[4:]
    total_ref, all_ref, facts, pair, side, cross, line, local_sem, send_sem, recv_sem, line_send, line_recv = refs
    z, x, y, c = place()
    core_to, y_to, x_to = device(z, x, y, 1 - c), device(z, x, 1 - y, c), device(z, 1 - x, y, c)
    column = [(z + step) % 4 for step in range(1, 4)]
    for target in (core_to, y_to, x_to, *[device(other, x, y, c) for other in column]):
        signal(target)
    own, other = y * 2 + c, (1 - y) * 2 + c
    all_ref[own, :, :width] = sums[2][:, :width]
    all_ref[own, :, width:] = sums[3][:, 3 * width :]
    squares = jnp.sum(squares_ref[...], 0, keepdims=True)
    for part in sums:
        for first in range(0, part.shape[1], BLOCK):
            values = part[:, first : first + BLOCK]
            squares += jnp.sum(values * values, 0, keepdims=True)
    facts[0:1] = squares
    facts[1:2] = jnp.broadcast_to(jnp.sum(losses_ref[...], 0, keepdims=True), squares.shape)
    facts[2:8] = jnp.zeros((6, BLOCK), f32)
    pl.semaphore_wait(pltpu.get_barrier_semaphore(), 6)
    swap_pair = remote(facts, pair, send_sem.at[0], recv_sem.at[0], core_to)
    swap_pair.start()
    block = all_ref.at[own]
    shared_side = remote(block, block, send_sem.at[3], recv_sem.at[3], y_to)
    shared_pair = remote(block, block, send_sem.at[4], recv_sem.at[4], core_to)
    swap_pair.wait()
    total_ref[...] = facts[...] + pair[...]
    swap_side = remote(total_ref, side, send_sem.at[1], recv_sem.at[1], y_to)
    swap_side.start()
    shared_side.start()
    shared_pair.start()
    swap_side.wait()
    total_ref[...] += side[...]
    swap_cross = remote(total_ref, cross, send_sem.at[2], recv_sem.at[2], x_to)
    swap_cross.start()
    swap_cross.wait()
    total_ref[...] += cross[...]
    line[z] = total_ref[...]
    lines = [
        remote(line.at[z], line.at[z], line_send.at[step], line_recv.at[z], device(to, x, y, c))
        for step, to in enumerate(column)
    ]
    for copy in lines:
        copy.start()
    shared_side.wait()
    relay = remote(all_ref.at[other], all_ref.at[other], send_sem.at[5], recv_sem.at[5], core_to)
    relay.start()
    for step, to in enumerate(column):
        lines[step].wait_send()
        remote(line.at[to], line.at[to], line_send.at[step], line_recv.at[to], core_to).wait_recv()
    total_ref[...] = (line[0] + line[1]) + (line[2] + line[3])
    shared_pair.wait()
    relay.wait()


def finish_sums(losses, squares, sums, width, tag):
    small = (8, BLOCK)
    return pl.pallas_call(
        functools.partial(finish_sums_kernel, width),
        in_specs=[IN_VMEM] * 6,
        out_specs=[IN_VMEM] * 2,
        out_shape=[
            jax.ShapeDtypeStruct(small, f32),
            jax.ShapeDtypeStruct((4, squares.shape[0], 2 * width), f32),
        ],
        scratch_shapes=[pltpu.VMEM(small, f32)] * 4
        + [
            pltpu.VMEM((4,) + small, f32),
            pltpu.SemaphoreType.DMA,
            pltpu.SemaphoreType.DMA((6,)),
            pltpu.SemaphoreType.DMA((6,)),
            pltpu.SemaphoreType.DMA((3,)),
            pltpu.SemaphoreType.DMA((4,)),
        ],
        compiler_params=pltpu.CompilerParams(collective_id=tag, has_side_effects=True),
        name="finish_sums",
    )(losses, squares, *sums)


def identity(size):
    rows = lax.broadcasted_iota(jnp.int32, (size, size), 0)
    columns = lax.broadcasted_iota(jnp.int32, (size, size), 1)
    return (rows == columns).astype(f32).astype(low)


def turn(values):
    return dot_rows(identity(values.shape[1]), values)


TABLES = 2


def lookup_kernel(counts_ref, keys_ref, weights_ref, words_ref, table_ref, rows_ref):
    width, slab = weights_ref.shape
    rows, _, seq = words_ref.shape
    shift = slab.bit_length()

    @pl.when(pl.program_id(0) == 0)
    def fill():
        def step(index, carry):
            first = pl.multiple_of(index * 9 * BLOCK, BLOCK)
            for part in range(9):
                at = first + part * BLOCK
                table_ref[pl.ds(at, BLOCK), :] = turn(weights_ref[:, pl.ds(at, BLOCK)].astype(low))
            return carry

        lax.fori_loop(0, slab // (9 * BLOCK), step, 0)
        table_ref[pl.ds(slab, 8), :] = jnp.zeros((8, width), f32)

    rows_ref[...] = jnp.zeros_like(rows_ref)

    def step(index, carry):
        for offset in range(UNROLL):
            key = keys_ref[0, 0, index * UNROLL + offset]
            spot, token = key & ((1 << shift) - 1), key >> shift
            rows_ref[pl.ds(token, 1), :] = table_ref[pl.ds(spot, 1), :]
        return carry

    lax.fori_loop(0, pl.cdiv(counts_ref[pl.program_id(0)], UNROLL), step, 0)
    for row in range(rows):
        values = rows_ref[row * seq : (row + 1) * seq, :].astype(low)
        words_ref[row] = dot_rows(identity(width), values).astype(low)


def lookup(counts, keys, weights, seq):
    steps, tokens = keys.shape
    width, slab = weights.shape
    rows = tokens // seq
    return pl.pallas_call(
        lookup_kernel,
        grid=(steps,),
        in_specs=[
            pl.BlockSpec(memory_space=pltpu.SMEM),
            pl.BlockSpec((1, 1, tokens), lambda step: (step, 0, 0), memory_space=pltpu.SMEM),
            pl.BlockSpec(weights.shape, lambda step: (0, 0)),
        ],
        out_specs=pl.BlockSpec((rows, width, seq), lambda step: (step, 0, 0)),
        out_shape=jax.ShapeDtypeStruct((steps * rows, width, seq), low),
        scratch_shapes=[pltpu.VMEM((slab + 8, width), f32), pltpu.VMEM((tokens + 8, width), f32)],
        compiler_params=pltpu.CompilerParams(vmem_limit_bytes=48 << 20),
        name="lookup",
    )(counts, keys[:, None], weights)


def deposit_kernel(counts_ref, keys_ref, grads_ref, total_ref, squares_ref, rows_ref, *tables):
    width, slab = total_ref.shape
    rows, _, seq = grads_ref.shape
    shift = slab.bit_length()

    @pl.when(pl.program_id(0) == 0)
    def clear():
        for table in tables:
            table[...] = jnp.zeros_like(table)
        rows_ref[pl.ds(rows * seq, 8), :] = jnp.zeros((8, width), f32)

    for row in range(rows):
        for first in range(0, seq, BLOCK):
            at = row * seq + first
            rows_ref[at : at + BLOCK, :] = turn(grads_ref[row, :, first : first + BLOCK])

    def step(index, carry):
        for offset in range(0, UNROLL, len(tables)):
            keys = [keys_ref[0, 0, index * UNROLL + offset + part] for part in range(len(tables))]
            spots = [key & ((1 << shift) - 1) for key in keys]
            sums = [
                table[pl.ds(spot, 1), :] + rows_ref[pl.ds(key >> shift, 1), :]
                for key, spot, table in zip(keys, spots, tables)
            ]
            for spot, table, value in zip(spots, tables, sums):
                table[pl.ds(spot, 1), :] = value
        return carry

    lax.fori_loop(0, pl.cdiv(counts_ref[pl.program_id(0)], UNROLL), step, 0)

    @pl.when(pl.program_id(0) == pl.num_programs(0) - 1)
    def finish():
        squares_ref[...] = jnp.zeros_like(squares_ref)

        def step(index, carry):
            first = pl.multiple_of(index * 9 * BLOCK, BLOCK)
            squares = jnp.zeros((width, BLOCK), f32)
            for part in range(9):
                at = pl.ds(first + part * BLOCK, BLOCK)
                block = sum(table[at, :] for table in tables).T
                total_ref[:, at] = block
                squares += block * block
            squares_ref[...] += squares
            return carry

        lax.fori_loop(0, slab // (9 * BLOCK), step, 0)


def deposit(counts, keys, grads, slab):
    steps, tokens = keys.shape
    _, width, seq = grads.shape
    rows = tokens // seq
    return pl.pallas_call(
        deposit_kernel,
        grid=(steps,),
        in_specs=[
            pl.BlockSpec(memory_space=pltpu.SMEM),
            pl.BlockSpec((1, 1, tokens), lambda step: (step, 0, 0), memory_space=pltpu.SMEM),
            pl.BlockSpec((rows, width, seq), lambda step: (step, 0, 0)),
        ],
        out_specs=[
            pl.BlockSpec((width, slab), lambda step: (0, 0)),
            pl.BlockSpec((width, BLOCK), lambda step: (0, 0)),
        ],
        out_shape=[
            jax.ShapeDtypeStruct((width, slab), f32),
            jax.ShapeDtypeStruct((width, BLOCK), f32),
        ],
        scratch_shapes=[pltpu.VMEM((tokens + 8, width), f32)]
        + [pltpu.VMEM((slab + 8, width), f32)] * TABLES,
        compiler_params=pltpu.CompilerParams(vmem_limit_bytes=60 << 20),
        name="deposit",
    )(counts, keys[:, None], grads)


def whiten(values):
    center = values - jnp.mean(values, -1, keepdims=True)
    rate = lax.rsqrt(jnp.mean(center * center, -1, keepdims=True) + layer_eps)
    return center * rate, rate


def unwhiten(upstream, gain, white, rate):
    scaled = upstream * gain
    inner = jnp.mean(scaled, -1, keepdims=True)
    along = jnp.mean(scaled * white, -1, keepdims=True)
    return (
        rate * (scaled - inner - white * along),
        jnp.sum(upstream * white, 0, keepdims=True),
        jnp.sum(upstream, 0, keepdims=True),
    )


def selection(length, entries):
    rows = lax.broadcasted_iota(jnp.int32, (2 * length, entries), 0)
    columns = lax.broadcasted_iota(jnp.int32, (2 * length, entries), 1)
    return (jnp.clip(length + entries // 2 - rows, 0, entries - 1) == columns).astype(f32).astype(low)


def prepare_kernel(*refs, between=lambda group: None):
    weights_ref, words_ref, vec_ref, white_ref, rate_ref, qkv_ref = refs[:6]
    rel_white_ref, rel_rate_ref, table_ref, low_ref, rel_ref = refs[6:]
    groups, model = weights_ref.shape[:2]
    seq = words_ref.shape[1]
    part = rel_ref.shape[0] // groups
    width = qkv_ref.shape[2] // 3
    terms = turn(weights_ref[0, :, 4 * BLOCK : 5 * BLOCK])
    half = BLOCK // 2
    vec_ref[...] = terms[half : half + 16] + terms[half + 16 : half + 32] + terms[half + 32 : half + 48]
    for group in range(groups):
        rows = slice(group * part, (group + 1) * part)
        entries = turn(weights_ref[group, :, 5 * BLOCK : 6 * BLOCK]) + turn(
            weights_ref[group, :, 6 * BLOCK : 7 * BLOCK]
        )
        white, rate = whiten(entries)
        rel_white_ref[rows, :] = white
        rel_rate_ref[rows, :] = rate
        rel_ref[rows, :] = (white * vec_ref[2:3] + vec_ref[3:4]).astype(low)
    for first in range(0, seq, BLOCK):
        rows = slice(first, first + BLOCK)
        white, rate = whiten(turn(words_ref[:, rows]))
        white_ref[rows, :] = white
        rate_ref[rows, :] = rate
        low_ref[rows, :] = (white * vec_ref[0:1] + vec_ref[1:2]).astype(low)
    chosen = selection(seq, rel_ref.shape[0])

    def step(group, carry):
        between(group)
        qkv_ref[group] = dot_plain(low_ref[...], weights_ref[group, :, : 3 * width]).astype(low)
        keys = dot_plain(rel_ref[...], weights_ref[group, :, : 2 * width]).astype(low)
        table_ref[group] = dot_plain(chosen, keys).astype(low)
        return carry

    lax.fori_loop(0, groups, step, 0)


def prepared(weights, seq, width, entries):
    groups, model = weights.shape[:2]
    outputs = [
        jax.ShapeDtypeStruct((16, model), f32),
        jax.ShapeDtypeStruct((seq, model), f32),
        jax.ShapeDtypeStruct((seq, 1), f32),
        jax.ShapeDtypeStruct((groups, seq, 3 * width), low),
        jax.ShapeDtypeStruct((entries, model), f32),
        jax.ShapeDtypeStruct((entries, 1), f32),
        jax.ShapeDtypeStruct((groups, 2 * seq, 2 * width), low),
    ]
    return outputs, [pltpu.VMEM((seq, model), low), pltpu.VMEM((entries, model), low)]


def prepare(weights, words, width, entries):
    outputs, scratch = prepared(weights, words.shape[1], width, entries)
    return pl.pallas_call(
        prepare_kernel,
        in_specs=[IN_VMEM] * 2,
        out_specs=[IN_VMEM] * 7,
        out_shape=outputs,
        scratch_shapes=scratch,
        compiler_params=pltpu.CompilerParams(vmem_limit_bytes=56 << 20),
        name="prepare",
    )(weights, words)


GATHER_SLOTS = {
    1: (("line", 2), ("rest", 1)),
    3: (("sides", 1),),
    5: (("line", 3), ("rest", 2)),
    6: (("sides", 2),),
    8: (("rest", 3), ("sides", 3), ("corners", 0)),
    10: (("corners", 1),),
}
GATHER_END = (
    ("corners", 2),
    ("corners", 3),
    ("finish", 0),
    ("finish", 1),
    ("finish", 2),
    ("finish", 3),
)


SAVED = (1, 3, 4, 6)


def attend_gather_kernel(length_ref, weights_ref, words_ref, pack_ref, *refs):
    outputs, probs_out, mixed_ref, all_ref = list(refs[:7]), refs[7], refs[8], refs[9]
    low_ref, rel_ref, far_ref, probs_ref, *kept, save_sem = refs[10:19]
    sems = refs[19:]
    saves = []
    for order, index in enumerate(SAVED):
        saves.append(pltpu.make_async_copy(kept[order], outputs[index], save_sem.at[order]))
        outputs[index] = kept[order]
    qkv_ref, table_ref = outputs[3], outputs[6]
    groups, heads = qkv_ref.shape[0], far_ref.shape[0]
    spot = place()
    greet(*spot, True)
    start, steps = gather_stages(spot, pack_ref, all_ref, *sems)
    start()
    run_all(steps, (("line", 0),))

    def between(group):
        pl.when(group == 0)(lambda: run_all(steps, (("rest", 0),)))
        pl.when(group == 2)(lambda: run_all(steps, (("line", 1), ("sides", 0))))

    prepare_kernel(weights_ref, words_ref, *outputs, low_ref, rel_ref, between=between)
    for copy in saves:
        copy.start()

    def save_probs(group):
        part = pl.ds(group * heads, heads)
        return pltpu.make_async_copy(
            probs_ref.at[part], probs_out.at[part], save_sem.at[len(SAVED) + group]
        )

    def step(group, carry):
        for head in range(heads):
            attend_head(group, head, length_ref[0], qkv_ref, table_ref, probs_ref, mixed_ref, far_ref)
            for slot, timed in GATHER_SLOTS.items():
                if slot % heads == head:
                    pl.when(group == slot // heads)(functools.partial(run_all, steps, timed))
        save_probs(group).start()
        return carry

    lax.fori_loop(0, groups, step, 0)
    run_all(steps, GATHER_END)
    for copy in saves:
        copy.wait()
    for group in range(groups):
        save_probs(group).wait()


def attend_gather(length, weights, words, pack, width, entries, tag):
    groups = weights.shape[0]
    seq = words.shape[1]
    heads = width // HEAD_DIM
    outputs, scratch = prepared(weights, seq, width, entries)
    return pl.pallas_call(
        attend_gather_kernel,
        in_specs=[pl.BlockSpec(memory_space=pltpu.SMEM), IN_VMEM, IN_VMEM, ANYWHERE],
        out_specs=[ANYWHERE if index in SAVED else IN_VMEM for index in range(7)]
        + [ANYWHERE, IN_VMEM, ANYWHERE],
        out_shape=outputs
        + [
            jax.ShapeDtypeStruct((groups * heads, seq, seq), low),
            jax.ShapeDtypeStruct((groups, seq, width), low),
            jax.ShapeDtypeStruct((4, 8) + pack.shape, low),
        ],
        scratch_shapes=scratch
        + [pltpu.VMEM((heads, seq, seq), f32), pltpu.VMEM((groups * heads, seq, seq), low)]
        + [pltpu.VMEM(outputs[index].shape, outputs[index].dtype) for index in SAVED]
        + [pltpu.SemaphoreType.DMA((len(SAVED) + groups,))]
        + gather_scratch(),
        compiler_params=pltpu.CompilerParams(
            collective_id=tag, has_side_effects=True, vmem_limit_bytes=56 << 20
        ),
        name="attend_gather",
    )(length, weights, words, pack)


def middle_kernel(
    weights_in,
    vec_ref,
    white_ref,
    mixed_ref,
    marks_ref,
    contract_save,
    expand_save,
    joint_out,
    mixed_out,
    sum_out,
    vec_out,
    loss_out,
    weights_ref,
    contract_out,
    expand_out,
    copy_sem,
    combine_ref,
    readout_ref,
    slope_ref,
    acts_ref,
    mid_ref,
    mid_white_ref,
    out_white_ref,
    gate_ref,
):
    groups, model = weights_ref.shape[:2]
    seq = white_ref.shape[0]
    width = mixed_ref.shape[2]
    hidden = acts_ref.shape[2]

    def load(group, first, last, sem):
        part = (group, slice(None), pl.ds(first, last - first))
        return pltpu.make_async_copy(weights_in.at[part], weights_ref.at[part], copy_sem.at[sem])

    def load_joint(group):
        return load(group, 2 * hidden, 2 * hidden + 2 * width, group)

    def load_group(group):
        return load(group, 0, 2 * hidden, groups + group)

    def save(group):
        return (
            pltpu.make_async_copy(
                contract_out.at[group], contract_save.at[group], copy_sem.at[2 * groups + group]
            ),
            pltpu.make_async_copy(
                expand_out.at[group], expand_save.at[group], copy_sem.at[3 * groups + group]
            ),
        )

    for group in range(groups):
        load_joint(group).start()
    for group in range(groups):
        load_group(group).start()
    for group in range(groups):
        load_joint(group).wait()
    vec = [vec_ref[row : row + 1] for row in range(11)]
    for group in range(groups):
        joint = weights_ref[group, :, 2 * hidden :]
        readout_ref[:, group * width : (group + 1) * width] = joint[:, :width]
        combine_ref[group] = joint[:, width:]
    total = white_ref[...] * vec[0] + vec[1]
    for group in range(groups):
        total += dot_rows(mixed_ref[group], combine_ref[group])
    mid_white, mid_rate = whiten(total)
    mid_white_ref[...] = mid_white
    hidden_mid = mid_white * vec[4] + vec[5]
    sum_out[...] = hidden_mid
    mid_ref[...] = hidden_mid.astype(low)

    def forward(group, carry):
        load_group(group).wait()
        gate = dot_plain(mid_ref[...], weights_ref[group, :, :hidden])
        share = 0.5 + 0.5 * lax.erf(gate * 0.5**0.5)
        acts_ref[group] = (gate * share).astype(low)
        slope_ref[group] = share + gate * jnp.exp(-0.5 * gate * gate) * (2.0 * jnp.pi) ** -0.5
        sum_out[...] += dot_rows(acts_ref[group], weights_ref[group, :, hidden : 2 * hidden])
        return carry

    lax.fori_loop(0, groups, forward, 0)
    out_white, out_rate = whiten(sum_out[...])
    out_white_ref[...] = out_white
    gate_ref[...] = (out_white * vec[6] + vec[7]).astype(low)
    dense = dot_plain(gate_ref[...], readout_ref[...])
    share = 0.5 + 0.5 * lax.erf(dense * 0.5**0.5)
    slope = share + dense * jnp.exp(-0.5 * dense * dense) * (2.0 * jnp.pi) ** -0.5
    white, rate = whiten(dense * share)
    head = white * vec[8] + vec[9]
    logits = jnp.sum(head * vec[10], -1, keepdims=True)
    weight, flags = marks_ref[:, 0:1], marks_ref[:, 1:2]
    losses = jnp.maximum(logits, 0.0) + jnp.log1p(jnp.exp(-jnp.abs(logits))) - flags * logits
    loss_out[...] = jnp.where(weight > 0.0, losses, 0.0)
    pull = (1.0 / (1.0 + jnp.exp(-logits)) - flags) * weight
    vec_out[6:7, :] = jnp.sum(head * pull, 0, keepdims=True)
    upstream, vec_out[4:5, :], vec_out[5:6, :] = unwhiten(pull * vec[10], vec[8], white, rate)
    dense_low = (upstream * slope).astype(low)
    turned = gate_ref[...].astype(f32).T.astype(low)
    for group in range(groups):
        joint_out[group, :, :width] = dot_plain(
            turned, dense_low[:, group * width : (group + 1) * width]
        ).astype(low)
    upstream, vec_out[2:3, :], vec_out[3:4, :] = unwhiten(
        dot_rows(dense_low, readout_ref[...]), vec[6], out_white_ref[...], out_rate
    )
    sum_out[...] = upstream
    gate_ref[...] = upstream.astype(low)
    upstream_turned = upstream.T.astype(low)
    mid_turned = mid_ref[...].astype(f32).T.astype(low)

    def backward(group, carry):
        contract_out[group] = dot_plain(upstream_turned, acts_ref[group]).astype(low)
        acts_ref[group] = (
            dot_plain(gate_ref[...], weights_ref[group, :, hidden : 2 * hidden]) * slope_ref[group]
        ).astype(low)
        expand_out[group] = dot_plain(mid_turned, acts_ref[group]).astype(low)
        sum_out[...] += dot_rows(acts_ref[group], weights_ref[group, :, :hidden])
        for copy in save(group):
            copy.start()
        return carry

    lax.fori_loop(0, groups, backward, 0)
    upstream, vec_out[0:1, :], vec_out[1:2, :] = unwhiten(
        sum_out[...], vec[4], mid_white_ref[...], mid_rate
    )
    vec_out[7:8, :] = jnp.zeros((1, model), f32)
    sum_out[...] = upstream
    gate_ref[...] = upstream.astype(low)
    turned = upstream.T.astype(low)
    for group in range(groups):
        mixed_out[group] = dot_plain(gate_ref[...], combine_ref[group]).astype(low)
        joint_out[group, :, width:] = dot_plain(turned, mixed_ref[group]).astype(low)
    for group in range(groups):
        for copy in save(group):
            copy.wait()


def middle(weights, vec, white, mixed, marks):
    groups, model = weights.shape[:2]
    seq, width = mixed.shape[1:]
    hidden = weights.shape[2] // 2 - width
    wide = pltpu.VMEM((seq, model), f32)
    outputs = [
        ((groups, model, hidden), low),
        ((groups, model, hidden), low),
        ((groups, model, 2 * width), low),
        ((groups, seq, width), low),
        ((seq, model), f32),
        ((8, model), f32),
        ((seq, 1), f32),
    ]
    return pl.pallas_call(
        middle_kernel,
        in_specs=[ANYWHERE] + [IN_VMEM] * 4,
        out_specs=[ANYWHERE] * 2 + [IN_VMEM] * 5,
        out_shape=[jax.ShapeDtypeStruct(*output) for output in outputs],
        scratch_shapes=[
            pltpu.VMEM(weights.shape, low),
            pltpu.VMEM((groups, model, hidden), low),
            pltpu.VMEM((groups, model, hidden), low),
            pltpu.SemaphoreType.DMA((4 * groups,)),
            pltpu.VMEM((groups, model, width), low),
            pltpu.VMEM((model, model), low),
            pltpu.VMEM((groups, seq, hidden), f32),
            pltpu.VMEM((groups, seq, hidden), low),
            pltpu.VMEM((seq, model), low),
            wide,
            wide,
            pltpu.VMEM((seq, model), low),
        ],
        compiler_params=pltpu.CompilerParams(vmem_limit_bytes=60 << 20),
        name="middle",
    )(weights, vec, white, mixed, marks)


def project_back_kernel(
    weights_ref,
    vec_ref,
    white_ref,
    rate_ref,
    rel_white_ref,
    rel_rate_ref,
    sum_ref,
    grads_ref,
    tables_ref,
    vec_grads_ref,
    words_out,
    project_out,
    total_ref,
    fold_ref,
    between=lambda point: None,
):
    groups, model = weights_ref.shape[:2]
    seq = white_ref.shape[0]
    width = grads_ref.shape[2] // 3
    entries = rel_white_ref.shape[0]
    part = entries // groups
    vec = [vec_ref[row : row + 1] for row in range(4)]

    def put(group, first, last, values):
        values = values.astype(low).reshape(project_out.shape[1:-1] + (last - first,))
        project_out[group, ..., first:last] = values

    turned = (white_ref[...] * vec[0] + vec[1]).T.astype(low)
    rel_turned = (rel_white_ref[...] * vec[2] + vec[3]).T.astype(low)
    chosen = selection(seq, entries)
    rel_total = jnp.zeros((entries, model), f32)
    for group in range(groups):
        fold_ref[...] = dot_left(chosen, tables_ref[group]).astype(low)
        rel_total += dot_rows(fold_ref[...], weights_ref[group, :, : 2 * width])
        put(
            group,
            0,
            2 * width,
            dot_plain(turned, grads_ref[group, :, : 2 * width]) + dot_plain(rel_turned, fold_ref[...]),
        )
        put(group, 2 * width, 3 * width, dot_plain(turned, grads_ref[group, :, 2 * width :]))
        between(group)
    total_ref[...] = sum_ref[...]
    for group in range(groups):
        total_ref[...] += dot_rows(grads_ref[group], weights_ref[group, :, : 3 * width])
    upstream, gain_grad, bias_grad = unwhiten(total_ref[...], vec[0], white_ref[...], rate_ref[...])
    turned = upstream.T.astype(low)
    words_out[...] = turned.reshape(words_out.shape)
    between("words")
    rel_up, rel_gain_grad, rel_bias_grad = unwhiten(
        rel_total, vec[2], rel_white_ref[...], rel_rate_ref[...]
    )
    turned = rel_up.T.astype(low)
    rows = [gain_grad, bias_grad, rel_gain_grad, rel_bias_grad]
    rows += [vec_grads_ref[row : row + 1] for row in range(7)]
    rows += [jnp.zeros((1, model), f32)]
    middle_column = 3 * width + BLOCK // 2
    for group in range(groups):
        put(group, middle_column, middle_column + part, turned[:, group * part : (group + 1) * part])
        three = jnp.concatenate(rows[3 * group : 3 * group + 3] + [jnp.zeros((BLOCK - 3, model), f32)], 0)
        put(group, 3 * width, middle_column, three.T[:, : BLOCK // 2])


def projected_back(weights, white, grads, rel_white):
    groups, model = weights.shape[:2]
    seq = white.shape[0]
    width = grads.shape[2] // 3
    entries = rel_white.shape[0]
    outputs = [
        jax.ShapeDtypeStruct((model, seq), low),
        jax.ShapeDtypeStruct((groups, model, 3 * width + BLOCK // 2 + entries // groups), low),
    ]
    return outputs, [pltpu.VMEM((seq, model), f32), pltpu.VMEM((entries, 2 * width), low)]


def project_back(weights, vec, white, rate, rel_white, rel_rate, total, grads, tables, vec_grads):
    outputs, scratch = projected_back(weights, white, grads, rel_white)
    return pl.pallas_call(
        project_back_kernel,
        in_specs=[IN_VMEM] * 10,
        out_specs=[IN_VMEM] * 2,
        out_shape=outputs,
        scratch_shapes=scratch,
        compiler_params=pltpu.CompilerParams(vmem_limit_bytes=56 << 20),
        name="project_back",
    )(weights, vec, white, rate, rel_white, rel_rate, total, grads, tables, vec_grads)


def project_return_kernel(chunks, *refs):
    inputs, (sent_ref, total_ref) = refs[:10], refs[10:12]
    words_ref, project_ref, *work = refs[12:16]
    spot = place()
    meet_owners(*spot)
    greet(*spot, False)
    pl.semaphore_wait(pltpu.get_barrier_semaphore(), 9)
    start_words, forward, relay, finish = return_stages(spot, words_ref, sent_ref, refs[16:21])
    start_sums, stages = sum_stages(
        spot, [project_ref], [total_ref], chunks, refs[21:], resident=True
    )
    start_pair = start_sums

    def between(point):
        if point == "words":
            start_words()
            run_all(stages, (("pair", 0),))
        elif point == 3:
            start_pair(0)

    project_back_kernel(*inputs, words_ref, project_ref, *work, between=between)
    start_pair(1)
    run_all(stages, (("pair", 1),))
    forward(0, 2)
    run_all(stages, (("first", 0),))
    forward(2, 8)
    run_all(stages, (("first", 1), ("second", 0)))
    relay(0, 4)
    run_all(stages, (("second", 1),))
    relay(4, 8)
    run_all(stages, (("total", 0), ("total", 1)))
    finish()


def project_return(*inputs, tag):
    weights, white, rel_white, upstream = inputs[0], inputs[2], inputs[4], inputs[7]
    (words, project), scratch = projected_back(weights, white, upstream, rel_white)
    seq = words.shape[1]
    size = project.shape[2]
    part = words.shape[0] // 8
    chunks = [(0, 0, 4 * BLOCK), (0, 4 * BLOCK, size - 4 * BLOCK)]
    return pl.pallas_call(
        functools.partial(project_return_kernel, chunks),
        in_specs=[IN_VMEM] * 10,
        out_specs=[IN_VMEM] * 2,
        out_shape=[
            jax.ShapeDtypeStruct((8, 4, part, seq), low),
            jax.ShapeDtypeStruct((part, size), f32),
        ],
        scratch_shapes=[
            pltpu.VMEM((8, part, seq), low),
            pltpu.VMEM((4, 4, 2, part, size), low),
        ]
        + scratch
        + return_scratch()
        + sum_scratch(part, [chunk[2] for chunk in chunks]),
        compiler_params=pltpu.CompilerParams(
            collective_id=tag, has_side_effects=True, vmem_limit_bytes=60 << 20
        ),
        name="project_return",
    )(*inputs)


def split_terms(values, count):
    terms = []
    for _ in range(count):
        term = lax.reduce_precision(values, 8, 7)
        terms.append(term.astype(low))
        values = values - term
    return terms


def adamw(weight, gradient, mean, square, rate_now):
    first = beta_first * mean + (1.0 - beta_first) * gradient
    second = beta_second * square + (1.0 - beta_second) * gradient * gradient
    mean_hat = first / (1.0 - beta_first**STEP)
    square_hat = second / (1.0 - beta_second**STEP)
    master = weight - rate_now * (
        mean_hat / (jnp.sqrt(square_hat) + adam_eps) + weight_decay * weight
    )
    return (first, second, master)


def update_kernel(width, *refs):
    facts_ref, shared_ref, *grads = refs[:7]
    weights, refs = refs[7:31], refs[31:]
    outputs, (norm_ref, loss_ref, bias_ref) = refs[:24], refs[24:27]
    squares = jnp.sum(facts_ref[0:1, :], 1, keepdims=True)
    factor = jnp.minimum(1.0, clip_level / jnp.sqrt(squares))

    def update(index, spot, gradient):
        weight, mean, square = [part.at[spot] for part in weights[3 * index : 3 * index + 3]]
        results = adamw(
            weight[...], gradient * factor, mean[...], square[...], rate_steps[index]
        )
        for part, value in zip(outputs[3 * index : 3 * index + 3], results):
            part.at[spot][...] = value

    everything = slice(None)
    update(0, (everything, everything), grads[0][...])

    contract, expand, joint, project = grads[1:]

    def at_step(step):
        return pl.when(pl.program_id(0) == step)

    @at_step(0)
    def norms():
        norm_ref[...] = jnp.sqrt(squares)
        loss_ref[...] = facts_ref[1:2, 0:1]
        count = weights[21].shape[0]
        for group in range(4):
            rows = shared_ref[group, :, BLOCK : 2 * BLOCK].T[BLOCK // 2 :]
            first = 3 * group
            last = min(first + 3, count)
            update(7, (slice(first, last), everything), rows[: last - first])
            if group == 1:
                bias_ref[...] = rows[0:1] * factor

    @at_step(1)
    def relative_table():
        for group in range(4):
            part = slice(group * BLOCK, (group + 1) * BLOCK)
            update(1, (everything, part), shared_ref[group, :, width + BLOCK // 2 :])

    @at_step(2)
    def readout_weights():
        for group in range(4):
            part = slice(group * width, (group + 1) * width)
            update(6, (everything, part), shared_ref[group, :, :width])

    @at_step(3)
    def project_weights():
        for kind in range(3):
            update(2, (kind,), project[:, kind * width : (kind + 1) * width])

    @at_step(4)
    def combine_weights():
        update(3, (everything, everything), joint[:, width:].T)

    @at_step(5)
    def expand_weights():
        update(4, (everything, everything), expand[...])

    @at_step(6)
    def contract_weights():
        update(5, (everything, everything), contract[...])


def update_all(facts, shared, grads, weights, width):
    rows, slab = grads[0].shape
    columns = 11 * BLOCK
    stripe = pl.BlockSpec((rows, columns), lambda step: (0, step))

    def full(array):
        return pl.BlockSpec(array.shape, functools.partial(lambda rank, step: (0,) * rank, array.ndim))

    in_specs = [full(facts), full(shared), stripe] + [full(grad) for grad in grads[1:]]
    in_specs += [stripe] * 3 + [full(weight) for weight in weights[3:]]
    results = [jax.ShapeDtypeStruct(weight.shape, f32) for weight in weights]
    results += [jax.ShapeDtypeStruct(shape, f32) for shape in ((1, 1), (1, 1), (1, rows))]
    return pl.pallas_call(
        functools.partial(update_kernel, width),
        grid=(slab // columns,),
        in_specs=in_specs,
        out_specs=[stripe] * 3 + [full(result) for result in results[3:]],
        out_shape=results,
        compiler_params=pltpu.CompilerParams(vmem_limit_bytes=62 << 20),
        name="update_all",
    )(facts, shared, *grads, *weights)


def per_device(
    token_ids,
    row_lengths,
    replaced,
    embedding,
    relative,
    project,
    combine,
    expand,
    contract,
    readout,
    vectors,
    embedding_mean,
    relative_mean,
    project_mean,
    combine_mean,
    expand_mean,
    contract_mean,
    readout_mean,
    vectors_mean,
    embedding_square,
    relative_square,
    project_square,
    combine_square,
    expand_square,
    contract_square,
    readout_square,
    vectors_square,
):
    pieces = lax.axis_size("heads")
    holder = lax.axis_index("heads")
    owners = lax.axis_size("dp")
    row_count, seq_len = token_ids.shape
    width = vectors.shape[1]
    model = width * owners
    everyone = ("heads", "dp")
    head_width = project.shape[2]
    hidden = expand.shape[1]
    vocab_slab = embedding.shape[1]
    span_part = relative.shape[0] // pieces
    vector_count = vectors.shape[0]
    direct = owners == 8 and pieces == 4

    own_relative = lax.dynamic_slice_in_dim(relative, holder * span_part, span_part, 0).T
    own_readout = lax.dynamic_slice_in_dim(readout, holder * head_width, head_width, 1)
    vector_terms = [
        jnp.pad(term, ((0, 0), (0, 16 - vector_count))) for term in split_terms(vectors.T, 3)
    ]
    high, rest = split_terms(own_relative, 2)
    first_pack = jnp.concatenate(
        [
            project.reshape(width, 3 * head_width).astype(low),
            *vector_terms,
            jnp.zeros((width, 16), low),
            high,
            rest,
        ],
        1,
    )
    second_pack = jnp.concatenate(
        [
            expand.astype(low),
            contract.T.astype(low),
            own_readout.astype(low),
            combine.T.astype(low),
        ],
        1,
    )
    first_all = lax.all_gather(first_pack, everyone, axis=0, tiled=True)
    first_all = first_all.reshape(pieces, model, -1)

    length_row = jnp.pad(row_lengths[None, :], ((0, 0), (0, seq_len - row_count)))
    facts = jnp.concatenate([token_ids, jnp.pad(length_row, ((0, 8 - 1 - row_count), (0, 0)))], 0)
    all_facts = share_facts(facts, 1) if direct else lax.all_gather(facts, "dp")
    all_ids = all_facts[:, :row_count].reshape(owners * row_count, seq_len)
    all_lengths = all_facts[:, row_count, :row_count].reshape(-1)
    local_ids = all_ids - holder * vocab_slab
    inside = (local_ids >= 0) & (local_ids < vocab_slab)
    inside = inside & (jnp.arange(seq_len)[None] < all_lengths[:, None])
    inside = inside.reshape(-1, ROW_SET * seq_len)
    counts = jnp.sum(inside.astype(jnp.int32), 1)
    shift = vocab_slab.bit_length()
    keys = jnp.arange(ROW_SET * seq_len, dtype=jnp.int32)[None] << shift
    keys = jnp.where(
        inside,
        keys + local_ids.reshape(inside.shape),
        ((ROW_SET * seq_len) << shift) + vocab_slab,
    )
    keys = lax.sort(keys.T, dimension=0, is_stable=False).T

    found = lookup(counts, keys, embedding, seq_len)
    found = found.reshape(owners, row_count, width, seq_len)
    if direct:
        found = exchange_words(found, 2)
    else:
        found = lax.psum_scatter(found, "heads", scatter_dimension=1, tiled=True)[:, 0]
        found = lax.all_to_all(found, "dp", 0, 0, tiled=True)
    all_lengths, row_lengths, replaced, found = lax.optimization_barrier(
        (all_lengths, row_lengths, replaced, found)
    )
    token_total = jnp.sum(all_lengths).astype(f32)
    own_length = lax.dynamic_slice_in_dim(row_lengths, holder, 1)
    own_live = jnp.arange(seq_len) < own_length
    own_flags = lax.dynamic_slice_in_dim(replaced, holder, 1)[0].astype(f32)
    marks = jnp.stack([jnp.where(own_live, 1.0 / token_total, 0.0), own_flags], 1)

    entries = relative.shape[0]
    words = found.reshape(model, seq_len)
    if direct:
        *ready, probs, mixed, second_all = attend_gather(
            own_length, first_all, words, second_pack, head_width, entries, 3
        )
    else:
        ready = prepare(first_all, words, head_width, entries)
        probs, mixed = attend(own_length, ready[3], ready[6])
        second_all = lax.all_gather(second_pack, everyone, axis=0, tiled=True)
    vec_full, white, rate, qkv, rel_white, rel_rate, rel_table = ready
    second_all = second_all.reshape(pieces, model, -1)
    grad_contract, grad_expand, grad_joint, grad_mixed, grad_sum, grad_vec, losses = middle(
        second_all, vec_full, white, mixed, marks
    )
    back = (first_all, vec_full, white, rate, rel_white, rel_rate, grad_sum)
    if direct:
        qkv_grads, rel_table_grads, *sums = attend_back_sums(
            qkv, rel_table, probs, grad_mixed, [grad_contract, grad_expand, grad_joint], 4
        )
        sent, project_sum = project_return(*back, qkv_grads, rel_table_grads, grad_vec, tag=5)
        sums.append(project_sum)
    else:
        qkv_grads, rel_table_grads = attend_back(qkv, rel_table, probs, grad_mixed)
        sent, grad_project = project_back(*back, qkv_grads, rel_table_grads, grad_vec)
        sent = sent.reshape(owners, width, seq_len)
        sent = lax.all_to_all(sent, "dp", 0, 0, tiled=True)
        sent = lax.all_gather(sent, "heads", axis=0)
        sent = sent.transpose(1, 0, 2, 3)
        sums = [
            lax.psum_scatter(
                part.reshape(pieces * model, -1), everyone, scatter_dimension=0, tiled=True
            ).astype(f32)
            for part in (grad_contract, grad_expand, grad_joint, grad_project)
        ]
    sent = sent.reshape(owners * row_count, width, seq_len)
    grad_embedding, own_squares = deposit(counts, keys, sent, vocab_slab)

    weights = (embedding, relative, project, combine, expand, contract, readout, vectors)
    means = (
        embedding_mean,
        relative_mean,
        project_mean,
        combine_mean,
        expand_mean,
        contract_mean,
        readout_mean,
        vectors_mean,
    )
    squares = (
        embedding_square,
        relative_square,
        project_square,
        combine_square,
        expand_square,
        contract_square,
        readout_square,
        vectors_square,
    )
    if direct:
        turns = {1: (1, 0), 2: (1, 0, 2), 5: (1, 0)}
        flat = [
            part.transpose(turns[index]) if index in turns else part
            for index, parts in enumerate(zip(weights, means, squares))
            for part in parts
        ]
        all_facts, shared = finish_sums(losses, own_squares, sums, head_width, 6)
        *flat, norm, loss_sum, bias_row = update_all(
            all_facts, shared, [grad_embedding, *sums], flat, head_width
        )
        flat = [
            part.transpose(turns[index // 3]) if index // 3 in turns else part
            for index, part in enumerate(flat)
        ]
        return (loss_sum[0, 0], token_total, norm[0, 0], *flat, bias_row[0])

    squares_local = sum(jnp.sum(part * part) for part in sums) + jnp.sum(own_squares)
    shared = jnp.concatenate([sums[2][:, :head_width], sums[3][:, 3 * head_width :]], 1)
    squares_total, loss_sum = lax.psum((squares_local, jnp.sum(losses)), everyone)
    shared = lax.all_gather(shared, "heads", axis=0)
    grad_norm = jnp.sqrt(squares_total)
    factor = jnp.minimum(1.0, clip_level / grad_norm)
    grad_readout = shared[:, :, :head_width].transpose(1, 0, 2).reshape(width, model)
    at = head_width + BLOCK // 2
    grad_relative = shared[:, :, at:].transpose(0, 2, 1).reshape(entries, width)
    grad_vec = shared[:, :, head_width : head_width + 3].transpose(0, 2, 1).reshape(-1, width)
    grad_vec = grad_vec[:vector_count]
    gradients = (
        grad_embedding,
        grad_relative,
        sums[3][:, : 3 * head_width].reshape(width, 3, head_width),
        sums[2][:, head_width:].T,
        sums[1],
        sums[0].T,
        grad_readout,
        grad_vec,
    )
    updates = [
        adamw(weight, gradient * factor, mean, square, rate_now)
        for weight, gradient, mean, square, rate_now in zip(
            weights, gradients, means, squares, rate_steps
        )
    ]
    flat = [part for parts in updates for part in parts]
    return (loss_sum, token_total, grad_norm, *flat, grad_vec[3] * factor)


def solution(mesh):
    placed = (
        P("dp", None),
        P("dp"),
        P("dp", None),
        P("dp", "heads"),
        P(None, "dp"),
        P("dp", None, "heads"),
        P("heads", "dp"),
        P("dp", "heads"),
        P("heads", "dp"),
        P("dp", None),
        P(None, "dp"),
        P("dp", "heads"),
        P(None, "dp"),
        P("dp", None, "heads"),
        P("heads", "dp"),
        P("dp", "heads"),
        P("heads", "dp"),
        P("dp", None),
        P(None, "dp"),
        P("dp", "heads"),
        P(None, "dp"),
        P("dp", None, "heads"),
        P("heads", "dp"),
        P("dp", "heads"),
        P("heads", "dp"),
        P("dp", None),
        P(None, "dp"),
    )
    return jax.shard_map(
        per_device,
        mesh=mesh,
        in_specs=placed,
        out_specs=(
            P(),
            P(),
            P(),
            P("dp", "heads"),
            P("dp", "heads"),
            P("dp", "heads"),
            P(None, "dp"),
            P(None, "dp"),
            P(None, "dp"),
            P("dp", None, "heads"),
            P("dp", None, "heads"),
            P("dp", None, "heads"),
            P("heads", "dp"),
            P("heads", "dp"),
            P("heads", "dp"),
            P("dp", "heads"),
            P("dp", "heads"),
            P("dp", "heads"),
            P("heads", "dp"),
            P("heads", "dp"),
            P("heads", "dp"),
            P("dp", None),
            P("dp", None),
            P("dp", None),
            P(None, "dp"),
            P(None, "dp"),
            P(None, "dp"),
            P("dp"),
        ),
        check_vma=False,
    )
```

```python
import functools

import jax
import jax.numpy as jnp
from jax import lax
from jax.experimental import pallas as pl
from jax.experimental.pallas import tpu as pltpu
from jax.sharding import PartitionSpec as P

HEAD_DIM = 64
STEP = 10
BLOCK = 128
UNROLL = 16
ROW_SET = 8

low = jnp.bfloat16
f32 = jnp.float32

layer_eps = 1e-07
clip_level = 0.005
rate_steps = (0.1, 0.05, 0.05, 0.05, 0.05, 0.05, 0.05, 1.0)
beta_first = 0.9
beta_second = 0.999
adam_eps = 1e-08
weight_decay = 0.01


def dot_rows(a,b):
    return lax.dot_general(a,b,(((1,),(1,)),((),())),preferred_element_type=f32)
def dot_plain(a,b):
    return lax.dot_general(a,b,(((1,),(0,)),((),())),preferred_element_type=f32)
def dot_left(a,b):
    return lax.dot_general(a,b,(((0,),(0,)),((),())),preferred_element_type=f32)

def attend_head(group, head, length, qkv_ref, table_ref, probs_ref, mixed_ref, far_ref):
    seq = qkv_ref.shape[1]
    width = qkv_ref.shape[2] // 3
    heads = width // HEAD_DIM
    scale = (3 * HEAD_DIM) ** -0.5
    live = lax.broadcasted_iota(jnp.int32, (BLOCK, seq), 1) < length
    at = head * HEAD_DIM
    q = qkv_ref[group, :, at : at + HEAD_DIM]
    k = qkv_ref[group, :, width + at : width + at + HEAD_DIM]
    v = qkv_ref[group, :, 2 * width + at : 2 * width + at + HEAD_DIM]
    for block in range(seq // BLOCK):
        rows = slice(block * BLOCK, (block + 1) * BLOCK)
        window = slice(seq - BLOCK * (block + 1), 2 * seq - BLOCK * block)
        far = dot_rows(k[rows], table_ref[group, window, at : at + HEAD_DIM])
        far = pltpu.roll(far, seq, 1, stride=1, stride_axis=0)[:, :seq]
        far_ref[head, :, rows] = far.T
    for block in range(seq // BLOCK):
        rows = slice(block * BLOCK, (block + 1) * BLOCK)
        window = slice(seq - BLOCK * (block + 1), 2 * seq - BLOCK * block)
        near = dot_rows(q[rows], table_ref[group, window, width + at : width + at + HEAD_DIM])
        near = pltpu.roll(near, seq, 1, stride=1, stride_axis=0)[:, :seq]
        scores = (dot_rows(q[rows], k) + near + far_ref[head, rows, :]) * scale
        scores = jnp.where(live, scores, -1e9)
        top = jnp.max(scores, -1, keepdims=True)
        expo = jnp.exp(scores - top)
        probs = (expo * (1.0 / jnp.sum(expo, -1, keepdims=True))).astype(low)
        probs_ref[group * heads + head, rows, :] = probs
        mixed_ref[group, rows, at : at + HEAD_DIM] = dot_plain(probs, v).astype(low)


def attend_kernel(length_ref, qkv_ref, table_ref, probs_ref, mixed_ref, far_ref):
    for head in range(far_ref.shape[0]):
        attend_head(0, head, length_ref[0], qkv_ref, table_ref, probs_ref, mixed_ref, far_ref)


def attend(length, qkv, table):
    groups, seq, width3 = qkv.shape
    width = width3 // 3
    heads = width // HEAD_DIM
    return pl.pallas_call(
        attend_kernel,
        grid=(groups,),
        in_specs=[
            pl.BlockSpec(memory_space=pltpu.SMEM),
            pl.BlockSpec((1, seq, width3), lambda g: (g, 0, 0)),
            pl.BlockSpec((1, 2 * seq, 2 * width), lambda g: (g, 0, 0)),
        ],
        out_specs=[
            pl.BlockSpec((heads, seq, seq), lambda g: (g, 0, 0)),
            pl.BlockSpec((1, seq, width), lambda g: (g, 0, 0)),
        ],
        out_shape=[
            jax.ShapeDtypeStruct((groups * heads, seq, seq), low),
            jax.ShapeDtypeStruct((groups, seq, width), low),
        ],
        scratch_shapes=[pltpu.VMEM((heads, seq, seq), f32)],
        compiler_params=pltpu.CompilerParams(vmem_limit_bytes=48 << 20),
        name="attend",
    )(length, qkv, table)


def attend_back_head(
    group, head, qkv_ref, table_ref, probs_ref, up_ref, grad_ref, rel_ref, low_ref, sum_ref
):
    seq = qkv_ref.shape[1]
    width = qkv_ref.shape[2] // 3
    heads = width // HEAD_DIM
    scale = (3 * HEAD_DIM) ** -0.5
    row = lax.broadcasted_iota(jnp.int32, (BLOCK, BLOCK), 0)
    flip = row + lax.broadcasted_iota(jnp.int32, (BLOCK, BLOCK), 1) == BLOCK - 1
    flip = flip.astype(f32).astype(low)
    edge = jnp.zeros((BLOCK, BLOCK), f32)

    def shear(rows):
        return pltpu.roll(jnp.concatenate([rows, edge], 1), 1, 1, stride=1, stride_axis=0).astype(low)

    at = head * HEAD_DIM
    q = qkv_ref[group, :, at : at + HEAD_DIM]
    k = qkv_ref[group, :, width + at : width + at + HEAD_DIM]
    v = qkv_ref[group, :, 2 * width + at : 2 * width + at + HEAD_DIM]
    up = up_ref[group, :, at : at + HEAD_DIM]
    source = group * heads + head
    for block in range(seq // BLOCK):
        rows = slice(block * BLOCK, (block + 1) * BLOCK)
        probs = probs_ref[source, rows, :].astype(f32)
        pull = dot_rows(up[rows], v)
        inner = jnp.sum(probs * pull, -1, keepdims=True)
        low_ref[head, rows, :] = (probs * (pull - inner) * scale).astype(low)
    grad_v = dot_left(up, probs_ref[source]).T.astype(low)
    grad_ref[group, :, 2 * width + at : 2 * width + at + HEAD_DIM] = grad_v
    sum_ref[2 * head] = jnp.zeros(sum_ref.shape[1:], f32)
    sum_ref[2 * head + 1] = jnp.zeros(sum_ref.shape[1:], f32)
    for block in range(seq // BLOCK):
        rows = slice(block * BLOCK, (block + 1) * BLOCK)
        window = slice(seq - BLOCK * (block + 1), 2 * seq - BLOCK * block)
        turned = dot_plain(flip, low_ref[head, rows, :])
        near = shear(turned)
        grad_q = dot_plain(turned.astype(low), k) + dot_plain(
            near, table_ref[group, window, width + at : width + at + HEAD_DIM]
        )
        grad_ref[group, rows, at : at + HEAD_DIM] = dot_plain(flip, grad_q.astype(low)).astype(low)
        q_turned = dot_plain(flip, q[rows]).astype(low)
        sum_ref[2 * head + 1, :, window] += dot_left(q_turned, near)
        turned = dot_rows(flip, low_ref[head, :, rows])
        far = shear(turned)
        grad_k = dot_plain(turned.astype(low), q) + dot_plain(
            far, table_ref[group, window, at : at + HEAD_DIM]
        )
        grad_ref[group, rows, width + at : width + at + HEAD_DIM] = dot_plain(
            flip, grad_k.astype(low)
        ).astype(low)
        k_turned = dot_plain(flip, k[rows]).astype(low)
        sum_ref[2 * head, :, window] += dot_left(k_turned, far)
    rel_ref[group, :, at : at + HEAD_DIM] = sum_ref[2 * head].T.astype(low)
    rel_ref[group, :, width + at : width + at + HEAD_DIM] = sum_ref[2 * head + 1].T.astype(low)


def attend_back_kernel(*refs):
    for head in range(refs[-2].shape[0]):
        attend_back_head(0, head, *refs)


def attend_back(qkv, table, probs, up):
    groups, seq, width3 = qkv.shape
    width = width3 // 3
    heads = width // HEAD_DIM
    block = lambda *shape: pl.BlockSpec(shape, lambda g: (g, 0, 0))
    return pl.pallas_call(
        attend_back_kernel,
        grid=(groups,),
        in_specs=[
            block(1, seq, width3),
            block(1, 2 * seq, 2 * width),
            block(heads, seq, seq),
            block(1, seq, width),
        ],
        out_specs=[block(1, seq, width3), block(1, 2 * seq, 2 * width)],
        out_shape=[
            jax.ShapeDtypeStruct((groups, seq, width3), low),
            jax.ShapeDtypeStruct((groups, 2 * seq, 2 * width), low),
        ],
        scratch_shapes=[
            pltpu.VMEM((heads, seq, seq), low),
            pltpu.VMEM((2 * heads, HEAD_DIM, 2 * seq), f32),
        ],
        compiler_params=pltpu.CompilerParams(vmem_limit_bytes=48 << 20),
        name="attend_back",
    )(qkv, table, probs, up)


MESH = pl.DeviceIdType.MESH
ANYWHERE = pl.BlockSpec(memory_space=pl.ANY)
IN_VMEM = pl.BlockSpec(memory_space=pltpu.VMEM)


def place():
    owner, holder = lax.axis_index("dp"), lax.axis_index("heads")
    return owner // 2, owner % 2, holder // 2, holder % 2


def device(z, x, y, c):
    return (z * 2 + x, y * 2 + c)


def signal(target):
    pl.semaphore_signal(
        pltpu.get_barrier_semaphore(), inc=1, device_id=target, device_id_type=MESH
    )


def along_z(z):
    return [(z + step) % 4 for step in (2, 1, 3)]


def greet(z, x, y, c, line):
    signal(device(z, x, y, 1 - c))
    signal(device(z, x, 1 - y, c))
    if line:
        signal(device(z, 1 - x, y, c))
        for other in along_z(z):
            signal(device(other, x, y, c))
        pl.semaphore_wait(pltpu.get_barrier_semaphore(), 6)


def remote(source, target, send, recv, to):
    return pltpu.make_async_remote_copy(
        src_ref=source, dst_ref=target, send_sem=send, recv_sem=recv, device_id=to, device_id_type=MESH
    )


def sum_scratch(width, sizes):
    half = width // 2
    leads = (
        (2, 4, 2, width),
        (2, 4, 2, width),
        (4, 2, half),
        (2, 4, half),
        (4, half),
        (4, half),
        (4, width),
    )
    shapes = [pltpu.VMEM(lead + (size,), low) for lead in leads for size in sizes]
    count = len(sizes)
    return shapes + [
        pltpu.SemaphoreType.DMA((count, 2)),
        pltpu.SemaphoreType.DMA((count, 9)),
        pltpu.SemaphoreType.DMA((count, 10)),
    ]


def sum_stages(spot, grads, totals, chunks, refs, resident=False):
    count = len(chunks)
    pair, own, first_a, first_b, second_a, second_b, column = [
        refs[count * part : count * (part + 1)] for part in range(7)
    ]
    local_sem, send_sem, recv_sem = refs[7 * count :]
    z, x, y, c = spot
    half = grads[0].shape[3] // 2
    upper, lower = pl.ds(0, half), pl.ds(half, half)
    core_to, y_to, x_to = device(z, x, y, 1 - c), device(z, x, 1 - y, c), device(z, 1 - x, y, c)

    def columns(part):
        return pl.ds(chunks[part][1], chunks[part][2])

    def source(part, row):
        return grads[chunks[part][0]].at[row, :, :, :, columns(part)]

    def link(part, slot, source, target, to):
        return remote(source, target, send_sem.at[part, slot], recv_sem.at[part, slot], to)

    def local(part, side):
        return pltpu.make_async_copy(
            source(part, side * 2 + c), own[part].at[side], local_sem.at[part, side]
        )

    def pair_copy(part, side):
        return link(part, side, source(part, side * 2 + 1 - c), pair[part].at[side], core_to)

    def first_copies(part):
        block = own[part]
        return (
            link(part, 2, block.at[1 - y, :, :, upper], first_a[part], y_to),
            link(part, 3, block.at[:, :, 1 - x, lower], first_b[part], x_to),
        )

    def second_copies(part):
        block = own[part]
        return (
            link(part, 4, block.at[y, :, 1 - x, upper], second_a[part], x_to),
            link(part, 5, block.at[1 - y, :, x, lower], second_b[part], y_to),
        )

    def line_copy(part, step, to):
        return remote(
            own[part].at[y, to, x],
            column[part].at[z],
            send_sem.at[part, 6 + step],
            recv_sem.at[part, 6 + z],
            device(to, x, y, c),
        )

    def line_arrival(part, step, source):
        return remote(
            own[part].at[y, z, x],
            column[part].at[source],
            send_sem.at[part, 6 + step],
            recv_sem.at[part, 6 + source],
            device(source, x, y, c),
        )

    def add(target, source):
        target[...] = (target[...].astype(f32) + source[...].astype(f32)).astype(low)

    def start_pair(part):
        for side in range(2):
            pair_copy(part, side).start()
            if not resident:
                local(part, side).start()

    def stage_pair(part):
        for side in range(2):
            if not resident:
                local(part, side).wait()
            pair_copy(part, side).wait()
        if part + 2 < count:
            start_pair(part + 2)

        def step(index, carry):
            side, rest = index // 8, index % 8
            spot = (side, rest // 2, rest % 2)
            kept = own[part].at[spot]
            if resident:
                array, first, size = chunks[part]
                kept = grads[array].at[side * 2 + c, rest // 2, rest % 2, :, pl.ds(first, size)]
            total = kept[...].astype(f32) + pair[part].at[spot][...].astype(f32)
            own[part].at[spot][...] = total.astype(low)
            return carry

        lax.fori_loop(0, 16, step, 0)
        for copy in first_copies(part):
            copy.start()

    def stage_first(part):
        for copy in first_copies(part):
            copy.wait()

        def step(index, carry):
            add(own[part].at[y, index // 2, index % 2, upper], first_a[part].at[index // 2, index % 2])
            add(own[part].at[index % 2, index // 2, x, lower], first_b[part].at[index % 2, index // 2])
            return carry

        lax.fori_loop(0, 8, step, 0)
        for copy in second_copies(part):
            copy.start()

    def stage_second(part):
        for copy in second_copies(part):
            copy.wait()

        def step(index, carry):
            add(own[part].at[y, index, x, upper], second_a[part].at[index])
            add(own[part].at[y, index, x, lower], second_b[part].at[index])
            return carry

        lax.fori_loop(0, 4, step, 0)
        for step, to in enumerate(along_z(z)):
            line_copy(part, step, to).start()

    def stage_total(part):
        total = totals[chunks[part][0]].at[:, columns(part)]
        total[...] = own[part][y, z, x].astype(f32)
        for step, other in enumerate(along_z(z)):
            line_arrival(part, step, other).wait_recv()
            total[...] += column[part][other].astype(f32)
        for step, to in enumerate(along_z(z)):
            line_copy(part, step, to).wait_send()

    return start_pair, {
        "pair": stage_pair,
        "first": stage_first,
        "second": stage_second,
        "total": stage_total,
    }


def chunked(sizes, most=3 * BLOCK):
    return [
        (array, first, min(most, size - first))
        for array, size in enumerate(sizes)
        for first in range(0, size, most)
    ]


BACK_START = (("pair", 0),)
BACK_SLOTS = {
    0: (("pair", 1),),
    1: (("first", 0),),
    2: (("pair", 2),),
    3: (("first", 1), ("second", 0)),
    4: (("pair", 3),),
    5: (("first", 2), ("second", 1), ("total", 0)),
    6: (("pair", 4),),
    7: (("first", 3), ("second", 2), ("total", 1)),
    9: (("first", 4), ("second", 3), ("total", 2)),
    11: (("second", 4), ("total", 3)),
}
BACK_END = (("total", 4),)


def run_all(stages, steps):
    for name, chunk in steps:
        stages[name](chunk)


def attend_back_sums_kernel(count, chunks, *refs):
    inputs, grads = list(refs[:4]), refs[4 : 4 + count]
    outputs, totals = refs[4 + count : 6 + count], refs[6 + count : 6 + 2 * count]
    work, rest = refs[6 + 2 * count : 8 + 2 * count], refs[8 + 2 * count :]
    probs_ref, load_sem, *rest = rest
    probs_in, inputs[2] = inputs[2], probs_ref
    groups, heads = inputs[0].shape[0], work[0].shape[0]

    def load(group):
        part = pl.ds(group * heads, heads)
        return pltpu.make_async_copy(probs_in.at[part], probs_ref.at[part], load_sem.at[group])

    for group in range(groups):
        load(group).start()
    spot = place()
    greet(*spot, True)
    start_pair, stages = sum_stages(spot, grads, totals, chunks, rest)
    for chunk in range(2):
        start_pair(chunk)
    run_all(stages, BACK_START)

    def step(group, carry):
        load(group).wait()
        for head in range(heads):
            attend_back_head(group, head, *inputs, *outputs, *work)
            for slot, steps in BACK_SLOTS.items():
                if slot % heads == head:
                    pl.when(group == slot // heads)(functools.partial(run_all, stages, steps))
        return carry

    lax.fori_loop(0, groups, step, 0)
    run_all(stages, BACK_END)


def attend_back_sums(qkv, table, probs, up, grads, tag):
    groups, seq, width3 = qkv.shape
    width = width3 // 3
    heads = width // HEAD_DIM
    part = grads[0].shape[1] // 8
    sizes = [grad.shape[2] for grad in grads]
    chunks = chunked(sizes)
    return pl.pallas_call(
        functools.partial(attend_back_sums_kernel, len(grads), chunks),
        in_specs=[IN_VMEM, IN_VMEM, ANYWHERE, IN_VMEM] + [ANYWHERE] * len(grads),
        out_specs=[IN_VMEM] * (2 + len(grads)),
        out_shape=[
            jax.ShapeDtypeStruct((groups, seq, width3), low),
            jax.ShapeDtypeStruct((groups, 2 * seq, 2 * width), low),
        ]
        + [jax.ShapeDtypeStruct((part, size), f32) for size in sizes],
        scratch_shapes=[
            pltpu.VMEM((heads, seq, seq), low),
            pltpu.VMEM((2 * heads, HEAD_DIM, 2 * seq), f32),
            pltpu.VMEM(probs.shape, low),
            pltpu.SemaphoreType.DMA((groups,)),
        ]
        + sum_scratch(part, [chunk[2] for chunk in chunks]),
        compiler_params=pltpu.CompilerParams(
            collective_id=tag, has_side_effects=True, vmem_limit_bytes=60 << 20
        ),
        name="attend_back_sums",
    )(qkv, table, probs, up, *[grad.reshape(4, 4, 2, part, -1) for grad in grads])


def peers(z, x):
    return [((z + 2 - far) % 4, x if same else 1 - x) for far, same in PEER_ORDER]


PEER_ORDER = ((0, False), (0, True), (1, False), (1, True), (3, False), (3, True), (2, False))


def meet_owners(z, x, y, c):
    for peer_z, peer_x in peers(z, x):
        signal(device(peer_z, peer_x, y, c))


def share_facts_kernel(facts_ref, all_ref, local_sem, send_sem, recv_sem):
    z, x, y, c = place()
    meet_owners(z, x, y, c)
    pl.semaphore_wait(pltpu.get_barrier_semaphore(), 7)
    here = z * 2 + x
    keep = pltpu.make_async_copy(facts_ref, all_ref.at[here], local_sem)
    keep.start()
    copies = []
    for index, (peer_z, peer_x) in enumerate(peers(z, x)):
        copy = remote(
            facts_ref,
            all_ref.at[here],
            send_sem.at[index],
            recv_sem.at[here],
            device(peer_z, peer_x, y, c),
        )
        copy.start()
        copies.append(copy)
    for index, (peer_z, peer_x) in enumerate(peers(z, x)):
        there = peer_z * 2 + peer_x
        copies[index].wait_send()
        remote(
            facts_ref, all_ref.at[there], send_sem.at[index], recv_sem.at[there], device(z, x, y, c)
        ).wait_recv()
    keep.wait()


def share_facts(facts, tag):
    return pl.pallas_call(
        share_facts_kernel,
        in_specs=[IN_VMEM],
        out_specs=IN_VMEM,
        out_shape=jax.ShapeDtypeStruct((8,) + facts.shape, facts.dtype),
        scratch_shapes=[
            pltpu.SemaphoreType.DMA,
            pltpu.SemaphoreType.DMA((7,)),
            pltpu.SemaphoreType.DMA((8,)),
        ],
        compiler_params=pltpu.CompilerParams(collective_id=tag, has_side_effects=True),
        name="share_facts",
    )(facts)


def word_stages(spot, found_ref, words_ref, pair, side, send_sem, recv_sem, out_sem, in_sem):
    z, x, y, c = spot
    here = z * 2 + x
    targets = peers(z, x) + [(z, x)]
    core_to, y_to = device(z, x, y, 1 - c), device(z, x, 1 - y, c)

    def at_home(part):
        return targets[part][0] * 2 + targets[part][1]

    def pair_copy(part, row):
        to = at_home(part)
        return remote(
            found_ref.at[to, row * 2 + 1 - c],
            pair.at[row, to],
            send_sem.at[part, row],
            recv_sem.at[part, row],
            core_to,
        )

    def side_copy(part):
        to = at_home(part)
        return remote(
            pair.at[1 - y, to], side.at[to], send_sem.at[part, 2], recv_sem.at[part, 2], y_to
        )

    def out_copy(part):
        return remote(
            pair.at[y, at_home(part)],
            words_ref.at[here],
            out_sem.at[part],
            in_sem.at[here],
            device(targets[part][0], targets[part][1], y, c),
        )

    def start():
        for part in range(8):
            for row in range(2):
                pair_copy(part, row).start()

    def sideways(first, last):
        for part in range(first, last):
            to = at_home(part)
            for row in range(2):
                pair_copy(part, row).wait_recv()
                pair[row, to] = pair[row, to] + found_ref[to, row * 2 + c]
            side_copy(part).start()

    def outward(first, last):
        for part in range(first, last):
            to = at_home(part)
            side_copy(part).wait_recv()
            pair[y, to] = pair[y, to] + side[to]
            if part < 7:
                out_copy(part).start()
            else:
                words_ref[here] = pair[y, to]

    def finish():
        for part in range(8):
            for row in range(2):
                pair_copy(part, row).wait_send()
            side_copy(part).wait_send()
            if part < 7:
                out_copy(part).wait_send()
                there = at_home(part)
                remote(
                    pair.at[y, there], words_ref.at[there], out_sem.at[part], in_sem.at[there], core_to
                ).wait_recv()

    return start, sideways, outward, finish


def exchange_words_kernel(found_ref, words_ref, *refs):
    spot = place()
    meet_owners(*spot)
    greet(*spot, False)
    pl.semaphore_wait(pltpu.get_barrier_semaphore(), 9)
    start, sideways, outward, finish = word_stages(spot, found_ref, words_ref, *refs)
    start()
    sideways(0, 8)
    outward(0, 8)
    finish()


def exchange_words(found, tag):
    piece = found.shape[2:]
    return pl.pallas_call(
        exchange_words_kernel,
        in_specs=[IN_VMEM],
        out_specs=IN_VMEM,
        out_shape=jax.ShapeDtypeStruct((8,) + piece, low),
        scratch_shapes=[
            pltpu.VMEM((2, 8) + piece, low),
            pltpu.VMEM((8,) + piece, low),
            pltpu.SemaphoreType.DMA((8, 3)),
            pltpu.SemaphoreType.DMA((8, 3)),
            pltpu.SemaphoreType.DMA((8,)),
            pltpu.SemaphoreType.DMA((8,)),
        ],
        compiler_params=pltpu.CompilerParams(
            collective_id=tag, has_side_effects=True, vmem_limit_bytes=40 << 20
        ),
        name="exchange_words",
    )(found)


def return_stages(spot, grads_ref, sent_ref, refs):
    local_sem, out_sem, in_sem, send_sem, recv_sem = refs
    z, x, y, c = spot
    here = z * 2 + x
    own = y * 2 + c
    other = (1 - y) * 2 + c
    core_to, y_to = device(z, x, y, 1 - c), device(z, x, 1 - y, c)
    order = [(z, x)] + peers(z, x)[::-1]
    keep = pltpu.make_async_copy(grads_ref.at[here], sent_ref.at[here, own], local_sem)

    def out_copy(part, peer):
        return remote(
            grads_ref.at[peer[0] * 2 + peer[1]],
            sent_ref.at[here, own],
            out_sem.at[part],
            in_sem.at[here],
            device(peer[0], peer[1], y, c),
        )

    def in_copy(part, peer):
        there = peer[0] * 2 + peer[1]
        return remote(
            grads_ref.at[there], sent_ref.at[there, own], out_sem.at[part], in_sem.at[there], core_to
        )

    def pass_on(slot, row, there, to, source=None):
        block = sent_ref.at[there, row]
        source = block if source is None else source
        return remote(source, block, send_sem.at[slot, there], recv_sem.at[row, there], to)

    def start():
        keep.start()
        for part, peer in enumerate(peers(z, x)):
            out_copy(part, peer).start()

    def forward(first, last):
        for part in range(first, last):
            there = order[part][0] * 2 + order[part][1]
            source = grads_ref.at[here]
            if part > 0:
                in_copy(part - 1, order[part]).wait_recv()
                source = None
            pass_on(0, own, there, y_to, source).start()
            pass_on(1, own, there, core_to, source).start()

    def relay(first, last):
        for part in range(first, last):
            there = order[part][0] * 2 + order[part][1]
            pass_on(0, other, there, y_to).wait_recv()
            pass_on(2, other, there, core_to).start()

    def finish():
        keep.wait()
        for part, peer in enumerate(peers(z, x)):
            out_copy(part, peer).wait_send()
        for peer_z, peer_x in order:
            there = peer_z * 2 + peer_x
            pass_on(0, own, there, y_to).wait_send()
            pass_on(1, own, there, core_to).wait_send()
            pass_on(2, other, there, core_to).wait_send()
            pass_on(1, y * 2 + 1 - c, there, core_to).wait_recv()
            pass_on(2, (1 - y) * 2 + 1 - c, there, core_to).wait_recv()

    return start, forward, relay, finish


def return_scratch():
    return [
        pltpu.SemaphoreType.DMA,
        pltpu.SemaphoreType.DMA((7,)),
        pltpu.SemaphoreType.DMA((8,)),
        pltpu.SemaphoreType.DMA((3, 8)),
        pltpu.SemaphoreType.DMA((4, 8)),
    ]


def gather_stages(spot, pack_ref, all_ref, local_sem, send_sem, recv_sem, line_sem, core_sem):
    z, x, y, c = spot
    half = pack_ref.shape[0] // 2
    core_to, y_to, x_to = device(z, x, y, 1 - c), device(z, x, 1 - y, c), device(z, 1 - x, y, c)
    up_to, down_to = device(z + 1, x, y, c), device(z - 1, x, y, c)
    keep = pltpu.make_async_copy(pack_ref, all_ref.at[y * 2 + c, z * 2 + x], local_sem)
    CROSS, SIDE, UP, DOWN = range(4)
    targets = (x_to, y_to, up_to, down_to)

    def copy(kind, part, zz, xx, yy, own=False):
        at = lax.clamp(0, zz, 3) * 2 + xx
        rows = pl.ds(part * half, half)
        block = all_ref.at[yy * 2 + c, at, rows]
        source = pack_ref.at[rows] if own else block
        return remote(
            source, block, send_sem.at[kind, part, yy, at], recv_sem.at[part, yy, at], targets[kind]
        )

    def line_copy(kind, zz, own=False):
        zz = lax.clamp(0, zz, 3)
        block = all_ref.at[y * 2 + c, zz * 2 + x]
        source = pack_ref if own else block
        return remote(source, block, line_sem.at[kind - UP, zz], line_sem.at[2, zz], targets[kind])

    def core_copy(zz, yy, column):
        zz = lax.clamp(0, zz, 3)
        block = all_ref.at[yy * 2 + column, pl.ds(zz * 2, 2)]
        return remote(block, block, core_sem.at[0, yy, zz], core_sem.at[1, yy, zz], core_to)

    def distances(far):
        if far == 0:
            return [(z, z >= 0, None)]
        return [(z - far, z >= far, UP), (z + far, z <= 3 - far, DOWN)]

    def along(way):
        if way is None:
            return [(UP, z < 3), (DOWN, z > 0)]
        return [(way, z < 3 if way == UP else z > 0)]

    def for_each(far, action):
        for zz, exists, way in distances(far):
            pl.when(exists)(functools.partial(action, zz, way))

    def onward(zz, way, action):
        for on, possible in along(way):
            pl.when(possible)(lambda on=on: action(line_copy(on, zz, way is None)))

    def line_one(zz, way):
        own = way is None
        if not own:
            line_copy(way, zz).wait_recv()
        onward(zz, way, lambda copy: copy.start())
        copy(CROSS, 0, zz, x, y, own).start()
        copy(SIDE, 1, zz, x, y, own).start()

    def rest_one(zz, way):
        own = way is None
        copy(SIDE, 0, zz, x, y, own).start()
        copy(CROSS, 1, zz, x, y, own).start()

    def sides_one(zz, way):
        copy(CROSS, 0, zz, 1 - x, y).wait_recv()
        copy(SIDE, 0, zz, 1 - x, y).start()
        copy(SIDE, 1, zz, x, 1 - y).wait_recv()
        copy(CROSS, 1, zz, x, 1 - y).start()

    def corners_one(zz, way):
        for kind, part, xx, yy in (
            (SIDE, 0, x, 1 - y),
            (CROSS, 1, 1 - x, y),
            (SIDE, 0, 1 - x, 1 - y),
            (CROSS, 1, 1 - x, 1 - y),
        ):
            copy(kind, part, zz, xx, yy).wait_recv()
        if way is None:
            keep.wait()
        for yy in range(2):
            core_copy(zz, yy, c).start()

    def finish_one(zz, way):
        onward(zz, way, lambda copy: copy.wait_send())
        for part in range(2):
            copy(CROSS, part, zz, x, y).wait_send()
            copy(SIDE, part, zz, x, y).wait_send()
        copy(SIDE, 0, zz, 1 - x, y).wait_send()
        copy(CROSS, 1, zz, x, 1 - y).wait_send()
        for yy in range(2):
            core_copy(zz, yy, c).wait_send()
            core_copy(zz, yy, 1 - c).wait_recv()

    steps = {
        "line": line_one,
        "rest": rest_one,
        "sides": sides_one,
        "corners": corners_one,
        "finish": finish_one,
    }
    return keep.start, {
        name: functools.partial(for_each, action=action) for name, action in steps.items()
    }


def gather_scratch():
    return [
        pltpu.SemaphoreType.DMA,
        pltpu.SemaphoreType.DMA((4, 2, 2, 8)),
        pltpu.SemaphoreType.DMA((2, 2, 8)),
        pltpu.SemaphoreType.DMA((3, 4)),
        pltpu.SemaphoreType.DMA((2, 2, 4)),
    ]


def finish_sums_kernel(
    width,
    losses_ref,
    squares_ref,
    *refs,
):
    sums, refs = refs[:4], refs[4:]
    total_ref, all_ref, facts, quad, line, shared_send, shared_recv, send_sem, quad_recv, line_recv = refs
    z, x, y, c = place()
    here, own, other = z * 2 + x, y * 2 + c, (1 - y) * 2 + c
    core_to, y_to = device(z, x, y, 1 - c), device(z, x, 1 - y, c)
    mates = [(1 - y, 1 - c), (1 - y, c), (y, 1 - c)]
    meet_owners(z, x, y, c)
    for mate_y, mate_c in mates:
        signal(device(z, x, mate_y, mate_c))
    all_ref[own, :, :width] = sums[2][:, :width]
    all_ref[own, :, width:] = sums[3][:, 3 * width :]
    squares = jnp.sum(squares_ref[...], 0, keepdims=True)
    for part in sums:
        for first in range(0, part.shape[1], BLOCK):
            values = part[:, first : first + BLOCK]
            squares += jnp.sum(values * values, 0, keepdims=True)
    facts[0:1] = squares
    facts[1:2] = jnp.broadcast_to(jnp.sum(losses_ref[...], 0, keepdims=True), squares.shape)
    facts[2:8] = jnp.zeros((6, BLOCK), f32)
    quad[own] = facts[...]

    def quad_copy(step, source, to):
        block = quad.at[source]
        return remote(block, block, send_sem.at[step], quad_recv.at[source], to)

    def line_copy(step, source, to):
        block = line.at[source]
        return remote(block, block, send_sem.at[3 + step], line_recv.at[source], to)

    def shared_copy(step, source, to):
        block = all_ref.at[source]
        return remote(block, block, shared_send.at[step], shared_recv.at[source], to)

    pl.semaphore_wait(pltpu.get_barrier_semaphore(), 10)
    for step, mate in enumerate(mates):
        quad_copy(step, own, device(z, x, *mate)).start()
    shared_copy(0, own, y_to).start()
    shared_copy(1, own, core_to).start()
    for step, (mate_y, mate_c) in enumerate(mates):
        quad_copy(step, mate_y * 2 + mate_c, core_to).wait_recv()
    line[here] = (quad[0] + quad[1]) + (quad[2] + quad[3])
    for step, (peer_z, peer_x) in enumerate(peers(z, x)):
        line_copy(step, here, device(peer_z, peer_x, y, c)).start()
    shared_copy(0, other, y_to).wait_recv()
    shared_copy(2, other, core_to).start()
    for step, (peer_z, peer_x) in enumerate(peers(z, x)):
        line_copy(step, peer_z * 2 + peer_x, core_to).wait_recv()
    total = line[0]
    for index in range(1, 8):
        total = total + line[index]
    total_ref[...] = total
    shared_copy(1, y * 2 + 1 - c, core_to).wait_recv()
    shared_copy(2, (1 - y) * 2 + 1 - c, core_to).wait_recv()
    for step, mate in enumerate(mates):
        quad_copy(step, own, device(z, x, *mate)).wait_send()
    for step, (peer_z, peer_x) in enumerate(peers(z, x)):
        line_copy(step, here, device(peer_z, peer_x, y, c)).wait_send()
    shared_copy(0, own, y_to).wait_send()
    shared_copy(1, own, core_to).wait_send()
    shared_copy(2, other, core_to).wait_send()


def finish_sums(losses, squares, sums, width, tag):
    small = (8, BLOCK)
    return pl.pallas_call(
        functools.partial(finish_sums_kernel, width),
        in_specs=[IN_VMEM] * 6,
        out_specs=[IN_VMEM] * 2,
        out_shape=[
            jax.ShapeDtypeStruct(small, f32),
            jax.ShapeDtypeStruct((4, squares.shape[0], 2 * width), f32),
        ],
        scratch_shapes=[
            pltpu.VMEM(small, f32),
            pltpu.VMEM((4,) + small, f32),
            pltpu.VMEM((8,) + small, f32),
            pltpu.SemaphoreType.DMA((3,)),
            pltpu.SemaphoreType.DMA((4,)),
            pltpu.SemaphoreType.DMA((10,)),
            pltpu.SemaphoreType.DMA((4,)),
            pltpu.SemaphoreType.DMA((8,)),
        ],
        compiler_params=pltpu.CompilerParams(collective_id=tag, has_side_effects=True),
        name="finish_sums",
    )(losses, squares, *sums)


def identity(size):
    rows = lax.broadcasted_iota(jnp.int32, (size, size), 0)
    columns = lax.broadcasted_iota(jnp.int32, (size, size), 1)
    return (rows == columns).astype(f32).astype(low)


def turn(values):
    return dot_rows(identity(values.shape[1]), values)


TABLES = 2


def lookup_kernel(counts_ref, keys_ref, weights_ref, words_ref, table_ref, rows_ref):
    width, slab = weights_ref.shape
    rows, _, seq = words_ref.shape
    shift = slab.bit_length()

    @pl.when(pl.program_id(0) == 0)
    def fill():
        def step(index, carry):
            first = pl.multiple_of(index * 9 * BLOCK, BLOCK)
            for part in range(9):
                at = first + part * BLOCK
                table_ref[pl.ds(at, BLOCK), :] = turn(weights_ref[:, pl.ds(at, BLOCK)].astype(low))
            return carry

        lax.fori_loop(0, slab // (9 * BLOCK), step, 0)
        table_ref[pl.ds(slab, 8), :] = jnp.zeros((8, width), f32)

    rows_ref[...] = jnp.zeros_like(rows_ref)

    def step(index, carry):
        for offset in range(UNROLL):
            key = keys_ref[0, 0, index * UNROLL + offset]
            spot, token = key & ((1 << shift) - 1), key >> shift
            rows_ref[pl.ds(token, 1), :] = table_ref[pl.ds(spot, 1), :]
        return carry

    lax.fori_loop(0, pl.cdiv(counts_ref[pl.program_id(0)], UNROLL), step, 0)
    for row in range(rows):
        values = rows_ref[row * seq : (row + 1) * seq, :].astype(low)
        words_ref[row] = dot_rows(identity(width), values).astype(low)


def lookup(counts, keys, weights, seq):
    steps, tokens = keys.shape
    width, slab = weights.shape
    rows = tokens // seq
    return pl.pallas_call(
        lookup_kernel,
        grid=(steps,),
        in_specs=[
            pl.BlockSpec(memory_space=pltpu.SMEM),
            pl.BlockSpec((1, 1, tokens), lambda step: (step, 0, 0), memory_space=pltpu.SMEM),
            pl.BlockSpec(weights.shape, lambda step: (0, 0)),
        ],
        out_specs=pl.BlockSpec((rows, width, seq), lambda step: (step, 0, 0)),
        out_shape=jax.ShapeDtypeStruct((steps * rows, width, seq), low),
        scratch_shapes=[pltpu.VMEM((slab + 8, width), f32), pltpu.VMEM((tokens + 8, width), f32)],
        compiler_params=pltpu.CompilerParams(vmem_limit_bytes=48 << 20),
        name="lookup",
    )(counts, keys[:, None], weights)


def deposit_kernel(counts_ref, keys_ref, grads_ref, total_ref, squares_ref, rows_ref, *tables):
    width, slab = total_ref.shape
    rows, _, seq = grads_ref.shape
    shift = slab.bit_length()

    @pl.when(pl.program_id(0) == 0)
    def clear():
        for table in tables:
            table[...] = jnp.zeros_like(table)
        rows_ref[pl.ds(rows * seq, 8), :] = jnp.zeros((8, width), f32)

    for row in range(rows):
        for first in range(0, seq, BLOCK):
            at = row * seq + first
            rows_ref[at : at + BLOCK, :] = turn(grads_ref[row, :, first : first + BLOCK])

    def step(index, carry):
        for offset in range(0, UNROLL, len(tables)):
            keys = [keys_ref[0, 0, index * UNROLL + offset + part] for part in range(len(tables))]
            spots = [key & ((1 << shift) - 1) for key in keys]
            sums = [
                table[pl.ds(spot, 1), :] + rows_ref[pl.ds(key >> shift, 1), :]
                for key, spot, table in zip(keys, spots, tables)
            ]
            for spot, table, value in zip(spots, tables, sums):
                table[pl.ds(spot, 1), :] = value
        return carry

    lax.fori_loop(0, pl.cdiv(counts_ref[pl.program_id(0)], UNROLL), step, 0)

    @pl.when(pl.program_id(0) == pl.num_programs(0) - 1)
    def finish():
        squares_ref[...] = jnp.zeros_like(squares_ref)

        def step(index, carry):
            first = pl.multiple_of(index * 9 * BLOCK, BLOCK)
            squares = jnp.zeros((width, BLOCK), f32)
            for part in range(9):
                at = pl.ds(first + part * BLOCK, BLOCK)
                block = sum(table[at, :] for table in tables).T
                total_ref[:, at] = block
                squares += block * block
            squares_ref[...] += squares
            return carry

        lax.fori_loop(0, slab // (9 * BLOCK), step, 0)


def deposit(counts, keys, grads, slab):
    steps, tokens = keys.shape
    _, width, seq = grads.shape
    rows = tokens // seq
    return pl.pallas_call(
        deposit_kernel,
        grid=(steps,),
        in_specs=[
            pl.BlockSpec(memory_space=pltpu.SMEM),
            pl.BlockSpec((1, 1, tokens), lambda step: (step, 0, 0), memory_space=pltpu.SMEM),
            pl.BlockSpec((rows, width, seq), lambda step: (step, 0, 0)),
        ],
        out_specs=[
            pl.BlockSpec((width, slab), lambda step: (0, 0)),
            pl.BlockSpec((width, BLOCK), lambda step: (0, 0)),
        ],
        out_shape=[
            jax.ShapeDtypeStruct((width, slab), f32),
            jax.ShapeDtypeStruct((width, BLOCK), f32),
        ],
        scratch_shapes=[pltpu.VMEM((tokens + 8, width), f32)]
        + [pltpu.VMEM((slab + 8, width), f32)] * TABLES,
        compiler_params=pltpu.CompilerParams(vmem_limit_bytes=60 << 20),
        name="deposit",
    )(counts, keys[:, None], grads)


def whiten(values):
    center = values - jnp.mean(values, -1, keepdims=True)
    rate = lax.rsqrt(jnp.mean(center * center, -1, keepdims=True) + layer_eps)
    return center * rate, rate


def unwhiten(upstream, gain, white, rate):
    scaled = upstream * gain
    inner = jnp.mean(scaled, -1, keepdims=True)
    along = jnp.mean(scaled * white, -1, keepdims=True)
    return (
        rate * (scaled - inner - white * along),
        jnp.sum(upstream * white, 0, keepdims=True),
        jnp.sum(upstream, 0, keepdims=True),
    )


def selection(length, entries):
    rows = lax.broadcasted_iota(jnp.int32, (2 * length, entries), 0)
    columns = lax.broadcasted_iota(jnp.int32, (2 * length, entries), 1)
    return (jnp.clip(length + entries // 2 - rows, 0, entries - 1) == columns).astype(f32).astype(low)


def prepare_kernel(*refs, between=lambda group: None):
    weights_ref, words_ref, vec_ref, white_ref, rate_ref, qkv_ref = refs[:6]
    rel_white_ref, rel_rate_ref, table_ref, low_ref, rel_ref = refs[6:]
    groups, model = weights_ref.shape[:2]
    seq = words_ref.shape[1]
    part = rel_ref.shape[0] // groups
    width = qkv_ref.shape[2] // 3
    terms = turn(weights_ref[0, :, 4 * BLOCK : 5 * BLOCK])
    half = BLOCK // 2
    vec_ref[...] = terms[half : half + 16] + terms[half + 16 : half + 32] + terms[half + 32 : half + 48]
    for group in range(groups):
        rows = slice(group * part, (group + 1) * part)
        entries = turn(weights_ref[group, :, 5 * BLOCK : 6 * BLOCK]) + turn(
            weights_ref[group, :, 6 * BLOCK : 7 * BLOCK]
        )
        white, rate = whiten(entries)
        rel_white_ref[rows, :] = white
        rel_rate_ref[rows, :] = rate
        rel_ref[rows, :] = (white * vec_ref[2:3] + vec_ref[3:4]).astype(low)
    for first in range(0, seq, BLOCK):
        rows = slice(first, first + BLOCK)
        white, rate = whiten(turn(words_ref[:, rows]))
        white_ref[rows, :] = white
        rate_ref[rows, :] = rate
        low_ref[rows, :] = (white * vec_ref[0:1] + vec_ref[1:2]).astype(low)
    chosen = selection(seq, rel_ref.shape[0])

    def step(group, carry):
        between(group)
        qkv_ref[group] = dot_plain(low_ref[...], weights_ref[group, :, : 3 * width]).astype(low)
        keys = dot_plain(rel_ref[...], weights_ref[group, :, : 2 * width]).astype(low)
        table_ref[group] = dot_plain(chosen, keys).astype(low)
        return carry

    lax.fori_loop(0, groups, step, 0)


def prepared(weights, seq, width, entries):
    groups, model = weights.shape[:2]
    outputs = [
        jax.ShapeDtypeStruct((16, model), f32),
        jax.ShapeDtypeStruct((seq, model), f32),
        jax.ShapeDtypeStruct((seq, 1), f32),
        jax.ShapeDtypeStruct((groups, seq, 3 * width), low),
        jax.ShapeDtypeStruct((entries, model), f32),
        jax.ShapeDtypeStruct((entries, 1), f32),
        jax.ShapeDtypeStruct((groups, 2 * seq, 2 * width), low),
    ]
    return outputs, [pltpu.VMEM((seq, model), low), pltpu.VMEM((entries, model), low)]


def prepare(weights, words, width, entries):
    outputs, scratch = prepared(weights, words.shape[1], width, entries)
    return pl.pallas_call(
        prepare_kernel,
        in_specs=[IN_VMEM] * 2,
        out_specs=[IN_VMEM] * 7,
        out_shape=outputs,
        scratch_shapes=scratch,
        compiler_params=pltpu.CompilerParams(vmem_limit_bytes=56 << 20),
        name="prepare",
    )(weights, words)


GATHER_SLOTS = {
    1: (("line", 2), ("rest", 1)),
    3: (("sides", 1),),
    5: (("line", 3), ("rest", 2)),
    6: (("sides", 2),),
    8: (("rest", 3), ("sides", 3), ("corners", 0)),
    10: (("corners", 1),),
}
GATHER_END = (
    ("corners", 2),
    ("corners", 3),
    ("finish", 0),
    ("finish", 1),
    ("finish", 2),
    ("finish", 3),
)


SAVED = (1, 3, 4, 6)


def attend_gather_kernel(length_ref, weights_ref, words_ref, pack_ref, *refs):
    outputs, probs_out, mixed_ref, all_ref = list(refs[:7]), refs[7], refs[8], refs[9]
    low_ref, rel_ref, far_ref, probs_ref, *kept, save_sem = refs[10:19]
    sems = refs[19:]
    saves = []
    for order, index in enumerate(SAVED):
        saves.append(pltpu.make_async_copy(kept[order], outputs[index], save_sem.at[order]))
        outputs[index] = kept[order]
    qkv_ref, table_ref = outputs[3], outputs[6]
    groups, heads = qkv_ref.shape[0], far_ref.shape[0]
    spot = place()
    greet(*spot, True)
    start, steps = gather_stages(spot, pack_ref, all_ref, *sems)
    start()
    run_all(steps, (("line", 0),))

    def between(group):
        pl.when(group == 0)(lambda: run_all(steps, (("rest", 0),)))
        pl.when(group == 2)(lambda: run_all(steps, (("line", 1), ("sides", 0))))

    prepare_kernel(weights_ref, words_ref, *outputs, low_ref, rel_ref, between=between)
    for copy in saves:
        copy.start()

    def save_probs(group):
        part = pl.ds(group * heads, heads)
        return pltpu.make_async_copy(
            probs_ref.at[part], probs_out.at[part], save_sem.at[len(SAVED) + group]
        )

    def step(group, carry):
        for head in range(heads):
            attend_head(group, head, length_ref[0], qkv_ref, table_ref, probs_ref, mixed_ref, far_ref)
            for slot, timed in GATHER_SLOTS.items():
                if slot % heads == head:
                    pl.when(group == slot // heads)(functools.partial(run_all, steps, timed))
        save_probs(group).start()
        return carry

    lax.fori_loop(0, groups, step, 0)
    run_all(steps, GATHER_END)
    for copy in saves:
        copy.wait()
    for group in range(groups):
        save_probs(group).wait()


def attend_gather(length, weights, words, pack, width, entries, tag):
    groups = weights.shape[0]
    seq = words.shape[1]
    heads = width // HEAD_DIM
    outputs, scratch = prepared(weights, seq, width, entries)
    return pl.pallas_call(
        attend_gather_kernel,
        in_specs=[pl.BlockSpec(memory_space=pltpu.SMEM), IN_VMEM, IN_VMEM, ANYWHERE],
        out_specs=[ANYWHERE if index in SAVED else IN_VMEM for index in range(7)]
        + [ANYWHERE, IN_VMEM, ANYWHERE],
        out_shape=outputs
        + [
            jax.ShapeDtypeStruct((groups * heads, seq, seq), low),
            jax.ShapeDtypeStruct((groups, seq, width), low),
            jax.ShapeDtypeStruct((4, 8) + pack.shape, low),
        ],
        scratch_shapes=scratch
        + [pltpu.VMEM((heads, seq, seq), f32), pltpu.VMEM((groups * heads, seq, seq), low)]
        + [pltpu.VMEM(outputs[index].shape, outputs[index].dtype) for index in SAVED]
        + [pltpu.SemaphoreType.DMA((len(SAVED) + groups,))]
        + gather_scratch(),
        compiler_params=pltpu.CompilerParams(
            collective_id=tag, has_side_effects=True, vmem_limit_bytes=56 << 20
        ),
        name="attend_gather",
    )(length, weights, words, pack)


def middle_kernel(
    weights_in,
    vec_ref,
    white_ref,
    mixed_ref,
    marks_ref,
    contract_save,
    expand_save,
    joint_out,
    mixed_out,
    sum_out,
    vec_out,
    loss_out,
    weights_ref,
    contract_out,
    expand_out,
    copy_sem,
    combine_ref,
    readout_ref,
    slope_ref,
    acts_ref,
    mid_ref,
    mid_white_ref,
    out_white_ref,
    gate_ref,
):
    groups, model = weights_ref.shape[:2]
    seq = white_ref.shape[0]
    width = mixed_ref.shape[2]
    hidden = acts_ref.shape[2]

    def load(group, first, last, sem):
        part = (group, slice(None), pl.ds(first, last - first))
        return pltpu.make_async_copy(weights_in.at[part], weights_ref.at[part], copy_sem.at[sem])

    def load_joint(group):
        return load(group, 2 * hidden, 2 * hidden + 2 * width, group)

    def load_group(group):
        return load(group, 0, 2 * hidden, groups + group)

    def save(group):
        return (
            pltpu.make_async_copy(
                contract_out.at[group], contract_save.at[group], copy_sem.at[2 * groups + group]
            ),
            pltpu.make_async_copy(
                expand_out.at[group], expand_save.at[group], copy_sem.at[3 * groups + group]
            ),
        )

    for group in range(groups):
        load_joint(group).start()
    for group in range(groups):
        load_group(group).start()
    for group in range(groups):
        load_joint(group).wait()
    vec = [vec_ref[row : row + 1] for row in range(11)]
    for group in range(groups):
        joint = weights_ref[group, :, 2 * hidden :]
        readout_ref[:, group * width : (group + 1) * width] = joint[:, :width]
        combine_ref[group] = joint[:, width:]
    total = white_ref[...] * vec[0] + vec[1]
    for group in range(groups):
        total += dot_rows(mixed_ref[group], combine_ref[group])
    mid_white, mid_rate = whiten(total)
    mid_white_ref[...] = mid_white
    hidden_mid = mid_white * vec[4] + vec[5]
    sum_out[...] = hidden_mid
    mid_ref[...] = hidden_mid.astype(low)

    def forward(group, carry):
        load_group(group).wait()
        gate = dot_plain(mid_ref[...], weights_ref[group, :, :hidden])
        share = 0.5 + 0.5 * lax.erf(gate * 0.5**0.5)
        acts_ref[group] = (gate * share).astype(low)
        slope_ref[group] = share + gate * jnp.exp(-0.5 * gate * gate) * (2.0 * jnp.pi) ** -0.5
        sum_out[...] += dot_rows(acts_ref[group], weights_ref[group, :, hidden : 2 * hidden])
        return carry

    lax.fori_loop(0, groups, forward, 0)
    out_white, out_rate = whiten(sum_out[...])
    out_white_ref[...] = out_white
    gate_ref[...] = (out_white * vec[6] + vec[7]).astype(low)
    dense = dot_plain(gate_ref[...], readout_ref[...])
    share = 0.5 + 0.5 * lax.erf(dense * 0.5**0.5)
    slope = share + dense * jnp.exp(-0.5 * dense * dense) * (2.0 * jnp.pi) ** -0.5
    white, rate = whiten(dense * share)
    head = white * vec[8] + vec[9]
    logits = jnp.sum(head * vec[10], -1, keepdims=True)
    weight, flags = marks_ref[:, 0:1], marks_ref[:, 1:2]
    losses = jnp.maximum(logits, 0.0) + jnp.log1p(jnp.exp(-jnp.abs(logits))) - flags * logits
    loss_out[...] = jnp.where(weight > 0.0, losses, 0.0)
    pull = (1.0 / (1.0 + jnp.exp(-logits)) - flags) * weight
    vec_out[6:7, :] = jnp.sum(head * pull, 0, keepdims=True)
    upstream, vec_out[4:5, :], vec_out[5:6, :] = unwhiten(pull * vec[10], vec[8], white, rate)
    dense_low = (upstream * slope).astype(low)
    turned = gate_ref[...].astype(f32).T.astype(low)
    for group in range(groups):
        joint_out[group, :, :width] = dot_plain(
            turned, dense_low[:, group * width : (group + 1) * width]
        ).astype(low)
    upstream, vec_out[2:3, :], vec_out[3:4, :] = unwhiten(
        dot_rows(dense_low, readout_ref[...]), vec[6], out_white_ref[...], out_rate
    )
    sum_out[...] = upstream
    gate_ref[...] = upstream.astype(low)
    upstream_turned = upstream.T.astype(low)
    mid_turned = mid_ref[...].astype(f32).T.astype(low)

    def backward(group, carry):
        contract_out[group] = dot_plain(upstream_turned, acts_ref[group]).astype(low)
        acts_ref[group] = (
            dot_plain(gate_ref[...], weights_ref[group, :, hidden : 2 * hidden]) * slope_ref[group]
        ).astype(low)
        expand_out[group] = dot_plain(mid_turned, acts_ref[group]).astype(low)
        sum_out[...] += dot_rows(acts_ref[group], weights_ref[group, :, :hidden])
        for copy in save(group):
            copy.start()
        return carry

    lax.fori_loop(0, groups, backward, 0)
    upstream, vec_out[0:1, :], vec_out[1:2, :] = unwhiten(
        sum_out[...], vec[4], mid_white_ref[...], mid_rate
    )
    vec_out[7:8, :] = jnp.zeros((1, model), f32)
    sum_out[...] = upstream
    gate_ref[...] = upstream.astype(low)
    turned = upstream.T.astype(low)
    for group in range(groups):
        mixed_out[group] = dot_plain(gate_ref[...], combine_ref[group]).astype(low)
        joint_out[group, :, width:] = dot_plain(turned, mixed_ref[group]).astype(low)
    for group in range(groups):
        for copy in save(group):
            copy.wait()


def middle(weights, vec, white, mixed, marks):
    groups, model = weights.shape[:2]
    seq, width = mixed.shape[1:]
    hidden = weights.shape[2] // 2 - width
    wide = pltpu.VMEM((seq, model), f32)
    outputs = [
        ((groups, model, hidden), low),
        ((groups, model, hidden), low),
        ((groups, model, 2 * width), low),
        ((groups, seq, width), low),
        ((seq, model), f32),
        ((8, model), f32),
        ((seq, 1), f32),
    ]
    return pl.pallas_call(
        middle_kernel,
        in_specs=[ANYWHERE] + [IN_VMEM] * 4,
        out_specs=[ANYWHERE] * 2 + [IN_VMEM] * 5,
        out_shape=[jax.ShapeDtypeStruct(*output) for output in outputs],
        scratch_shapes=[
            pltpu.VMEM(weights.shape, low),
            pltpu.VMEM((groups, model, hidden), low),
            pltpu.VMEM((groups, model, hidden), low),
            pltpu.SemaphoreType.DMA((4 * groups,)),
            pltpu.VMEM((groups, model, width), low),
            pltpu.VMEM((model, model), low),
            pltpu.VMEM((groups, seq, hidden), f32),
            pltpu.VMEM((groups, seq, hidden), low),
            pltpu.VMEM((seq, model), low),
            wide,
            wide,
            pltpu.VMEM((seq, model), low),
        ],
        compiler_params=pltpu.CompilerParams(vmem_limit_bytes=60 << 20),
        name="middle",
    )(weights, vec, white, mixed, marks)


def project_back_kernel(
    weights_ref,
    vec_ref,
    white_ref,
    rate_ref,
    rel_white_ref,
    rel_rate_ref,
    sum_ref,
    grads_ref,
    tables_ref,
    vec_grads_ref,
    words_out,
    project_out,
    total_ref,
    fold_ref,
    between=lambda point: None,
):
    groups, model = weights_ref.shape[:2]
    seq = white_ref.shape[0]
    width = grads_ref.shape[2] // 3
    entries = rel_white_ref.shape[0]
    part = entries // groups
    vec = [vec_ref[row : row + 1] for row in range(4)]

    def put(group, first, last, values):
        values = values.astype(low).reshape(project_out.shape[1:-1] + (last - first,))
        project_out[group, ..., first:last] = values

    turned = (white_ref[...] * vec[0] + vec[1]).T.astype(low)
    rel_turned = (rel_white_ref[...] * vec[2] + vec[3]).T.astype(low)
    chosen = selection(seq, entries)
    rel_total = jnp.zeros((entries, model), f32)
    for group in range(groups):
        fold_ref[...] = dot_left(chosen, tables_ref[group]).astype(low)
        rel_total += dot_rows(fold_ref[...], weights_ref[group, :, : 2 * width])
        put(
            group,
            0,
            2 * width,
            dot_plain(turned, grads_ref[group, :, : 2 * width]) + dot_plain(rel_turned, fold_ref[...]),
        )
        put(group, 2 * width, 3 * width, dot_plain(turned, grads_ref[group, :, 2 * width :]))
        between(group)
    total_ref[...] = sum_ref[...]
    for group in range(groups):
        total_ref[...] += dot_rows(grads_ref[group], weights_ref[group, :, : 3 * width])
    upstream, gain_grad, bias_grad = unwhiten(total_ref[...], vec[0], white_ref[...], rate_ref[...])
    turned = upstream.T.astype(low)
    words_out[...] = turned.reshape(words_out.shape)
    between("words")
    rel_up, rel_gain_grad, rel_bias_grad = unwhiten(
        rel_total, vec[2], rel_white_ref[...], rel_rate_ref[...]
    )
    turned = rel_up.T.astype(low)
    rows = [gain_grad, bias_grad, rel_gain_grad, rel_bias_grad]
    rows += [vec_grads_ref[row : row + 1] for row in range(7)]
    rows += [jnp.zeros((1, model), f32)]
    middle_column = 3 * width + BLOCK // 2
    for group in range(groups):
        put(group, middle_column, middle_column + part, turned[:, group * part : (group + 1) * part])
        three = jnp.concatenate(rows[3 * group : 3 * group + 3] + [jnp.zeros((BLOCK - 3, model), f32)], 0)
        put(group, 3 * width, middle_column, three.T[:, : BLOCK // 2])


def projected_back(weights, white, grads, rel_white):
    groups, model = weights.shape[:2]
    seq = white.shape[0]
    width = grads.shape[2] // 3
    entries = rel_white.shape[0]
    outputs = [
        jax.ShapeDtypeStruct((model, seq), low),
        jax.ShapeDtypeStruct((groups, model, 3 * width + BLOCK // 2 + entries // groups), low),
    ]
    return outputs, [pltpu.VMEM((seq, model), f32), pltpu.VMEM((entries, 2 * width), low)]


def project_back(weights, vec, white, rate, rel_white, rel_rate, total, grads, tables, vec_grads):
    outputs, scratch = projected_back(weights, white, grads, rel_white)
    return pl.pallas_call(
        project_back_kernel,
        in_specs=[IN_VMEM] * 10,
        out_specs=[IN_VMEM] * 2,
        out_shape=outputs,
        scratch_shapes=scratch,
        compiler_params=pltpu.CompilerParams(vmem_limit_bytes=56 << 20),
        name="project_back",
    )(weights, vec, white, rate, rel_white, rel_rate, total, grads, tables, vec_grads)


def project_return_kernel(chunks, *refs):
    inputs, (sent_ref, total_ref) = refs[:10], refs[10:12]
    words_ref, project_ref, *work = refs[12:16]
    spot = place()
    meet_owners(*spot)
    greet(*spot, False)
    pl.semaphore_wait(pltpu.get_barrier_semaphore(), 9)
    start_words, forward, relay, finish = return_stages(spot, words_ref, sent_ref, refs[16:21])
    start_sums, stages = sum_stages(
        spot, [project_ref], [total_ref], chunks, refs[21:], resident=True
    )
    start_pair = start_sums

    def between(point):
        if point == "words":
            start_words()
            run_all(stages, (("pair", 0),))
        elif point == 3:
            start_pair(0)

    project_back_kernel(*inputs, words_ref, project_ref, *work, between=between)
    start_pair(1)
    run_all(stages, (("pair", 1),))
    forward(0, 2)
    run_all(stages, (("first", 0),))
    forward(2, 8)
    run_all(stages, (("first", 1), ("second", 0)))
    relay(0, 4)
    run_all(stages, (("second", 1),))
    relay(4, 8)
    run_all(stages, (("total", 0), ("total", 1)))
    finish()


def project_return(*inputs, tag):
    weights, white, rel_white, upstream = inputs[0], inputs[2], inputs[4], inputs[7]
    (words, project), scratch = projected_back(weights, white, upstream, rel_white)
    seq = words.shape[1]
    size = project.shape[2]
    part = words.shape[0] // 8
    chunks = [(0, 0, 4 * BLOCK), (0, 4 * BLOCK, size - 4 * BLOCK)]
    return pl.pallas_call(
        functools.partial(project_return_kernel, chunks),
        in_specs=[IN_VMEM] * 10,
        out_specs=[IN_VMEM] * 2,
        out_shape=[
            jax.ShapeDtypeStruct((8, 4, part, seq), low),
            jax.ShapeDtypeStruct((part, size), f32),
        ],
        scratch_shapes=[
            pltpu.VMEM((8, part, seq), low),
            pltpu.VMEM((4, 4, 2, part, size), low),
        ]
        + scratch
        + return_scratch()
        + sum_scratch(part, [chunk[2] for chunk in chunks]),
        compiler_params=pltpu.CompilerParams(
            collective_id=tag, has_side_effects=True, vmem_limit_bytes=60 << 20
        ),
        name="project_return",
    )(*inputs)


def split_terms(values, count):
    terms = []
    for _ in range(count):
        term = lax.reduce_precision(values, 8, 7)
        terms.append(term.astype(low))
        values = values - term
    return terms


def adamw(weight, gradient, mean, square, rate_now):
    first = beta_first * mean + (1.0 - beta_first) * gradient
    second = beta_second * square + (1.0 - beta_second) * gradient * gradient
    mean_hat = first / (1.0 - beta_first**STEP)
    square_hat = second / (1.0 - beta_second**STEP)
    master = weight - rate_now * (
        mean_hat / (jnp.sqrt(square_hat) + adam_eps) + weight_decay * weight
    )
    return (first, second, master)


def update_kernel(width, *refs):
    facts_ref, shared_ref, *grads = refs[:7]
    weights, refs = refs[7:31], refs[31:]
    outputs, (norm_ref, loss_ref, bias_ref) = refs[:24], refs[24:27]
    squares = jnp.sum(facts_ref[0:1, :], 1, keepdims=True)
    factor = jnp.minimum(1.0, clip_level / jnp.sqrt(squares))

    def update(index, spot, gradient):
        weight, mean, square = [part.at[spot] for part in weights[3 * index : 3 * index + 3]]
        results = adamw(
            weight[...], gradient * factor, mean[...], square[...], rate_steps[index]
        )
        for part, value in zip(outputs[3 * index : 3 * index + 3], results):
            part.at[spot][...] = value

    everything = slice(None)
    update(0, (everything, everything), grads[0][...])

    contract, expand, joint, project = grads[1:]

    def at_step(step):
        return pl.when(pl.program_id(0) == step)

    @at_step(0)
    def norms():
        norm_ref[...] = jnp.sqrt(squares)
        loss_ref[...] = facts_ref[1:2, 0:1]
        count = weights[21].shape[0]
        for group in range(4):
            rows = shared_ref[group, :, BLOCK : 2 * BLOCK].T[BLOCK // 2 :]
            first = 3 * group
            last = min(first + 3, count)
            update(7, (slice(first, last), everything), rows[: last - first])
            if group == 1:
                bias_ref[...] = rows[0:1] * factor

    @at_step(1)
    def relative_table():
        for group in range(4):
            part = slice(group * BLOCK, (group + 1) * BLOCK)
            update(1, (everything, part), shared_ref[group, :, width + BLOCK // 2 :])

    @at_step(2)
    def readout_weights():
        for group in range(4):
            part = slice(group * width, (group + 1) * width)
            update(6, (everything, part), shared_ref[group, :, :width])

    @at_step(3)
    def project_weights():
        for kind in range(3):
            update(2, (kind,), project[:, kind * width : (kind + 1) * width])

    @at_step(4)
    def combine_weights():
        update(3, (everything, everything), joint[:, width:].T)

    @at_step(5)
    def expand_weights():
        update(4, (everything, everything), expand[...])

    @at_step(6)
    def contract_weights():
        update(5, (everything, everything), contract[...])


def update_all(facts, shared, grads, weights, width):
    rows, slab = grads[0].shape
    columns = 11 * BLOCK
    stripe = pl.BlockSpec((rows, columns), lambda step: (0, step))

    def full(array):
        return pl.BlockSpec(array.shape, functools.partial(lambda rank, step: (0,) * rank, array.ndim))

    in_specs = [full(facts), full(shared), stripe] + [full(grad) for grad in grads[1:]]
    in_specs += [stripe] * 3 + [full(weight) for weight in weights[3:]]
    results = [jax.ShapeDtypeStruct(weight.shape, f32) for weight in weights]
    results += [jax.ShapeDtypeStruct(shape, f32) for shape in ((1, 1), (1, 1), (1, rows))]
    return pl.pallas_call(
        functools.partial(update_kernel, width),
        grid=(slab // columns,),
        in_specs=in_specs,
        out_specs=[stripe] * 3 + [full(result) for result in results[3:]],
        out_shape=results,
        compiler_params=pltpu.CompilerParams(vmem_limit_bytes=62 << 20),
        name="update_all",
    )(facts, shared, *grads, *weights)


def per_device(
    token_ids,
    row_lengths,
    replaced,
    embedding,
    relative,
    project,
    combine,
    expand,
    contract,
    readout,
    vectors,
    embedding_mean,
    relative_mean,
    project_mean,
    combine_mean,
    expand_mean,
    contract_mean,
    readout_mean,
    vectors_mean,
    embedding_square,
    relative_square,
    project_square,
    combine_square,
    expand_square,
    contract_square,
    readout_square,
    vectors_square,
):
    pieces = lax.axis_size("heads")
    holder = lax.axis_index("heads")
    owners = lax.axis_size("dp")
    row_count, seq_len = token_ids.shape
    width = vectors.shape[1]
    model = width * owners
    everyone = ("heads", "dp")
    head_width = project.shape[2]
    hidden = expand.shape[1]
    vocab_slab = embedding.shape[1]
    span_part = relative.shape[0] // pieces
    vector_count = vectors.shape[0]
    direct = owners == 8 and pieces == 4

    own_relative = lax.dynamic_slice_in_dim(relative, holder * span_part, span_part, 0).T
    own_readout = lax.dynamic_slice_in_dim(readout, holder * head_width, head_width, 1)
    vector_terms = [
        jnp.pad(term, ((0, 0), (0, 16 - vector_count))) for term in split_terms(vectors.T, 3)
    ]
    high, rest = split_terms(own_relative, 2)
    first_pack = jnp.concatenate(
        [
            project.reshape(width, 3 * head_width).astype(low),
            *vector_terms,
            jnp.zeros((width, 16), low),
            high,
            rest,
        ],
        1,
    )
    second_pack = jnp.concatenate(
        [
            expand.astype(low),
            contract.T.astype(low),
            own_readout.astype(low),
            combine.T.astype(low),
        ],
        1,
    )
    first_all = lax.all_gather(first_pack, everyone, axis=0, tiled=True)
    first_all = first_all.reshape(pieces, model, -1)

    length_row = jnp.pad(row_lengths[None, :], ((0, 0), (0, seq_len - row_count)))
    facts = jnp.concatenate([token_ids, jnp.pad(length_row, ((0, 8 - 1 - row_count), (0, 0)))], 0)
    all_facts = share_facts(facts, 1) if direct else lax.all_gather(facts, "dp")
    all_ids = all_facts[:, :row_count].reshape(owners * row_count, seq_len)
    all_lengths = all_facts[:, row_count, :row_count].reshape(-1)
    local_ids = all_ids - holder * vocab_slab
    inside = (local_ids >= 0) & (local_ids < vocab_slab)
    inside = inside & (jnp.arange(seq_len)[None] < all_lengths[:, None])
    inside = inside.reshape(-1, ROW_SET * seq_len)
    counts = jnp.sum(inside.astype(jnp.int32), 1)
    shift = vocab_slab.bit_length()
    keys = jnp.arange(ROW_SET * seq_len, dtype=jnp.int32)[None] << shift
    keys = jnp.where(
        inside,
        keys + local_ids.reshape(inside.shape),
        ((ROW_SET * seq_len) << shift) + vocab_slab,
    )
    keys = lax.sort(keys.T, dimension=0, is_stable=False).T

    found = lookup(counts, keys, embedding, seq_len)
    found = found.reshape(owners, row_count, width, seq_len)
    if direct:
        found = exchange_words(found, 2)
    else:
        found = lax.psum_scatter(found, "heads", scatter_dimension=1, tiled=True)[:, 0]
        found = lax.all_to_all(found, "dp", 0, 0, tiled=True)
    all_lengths, row_lengths, replaced, found = lax.optimization_barrier(
        (all_lengths, row_lengths, replaced, found)
    )
    token_total = jnp.sum(all_lengths).astype(f32)
    own_length = lax.dynamic_slice_in_dim(row_lengths, holder, 1)
    own_live = jnp.arange(seq_len) < own_length
    own_flags = lax.dynamic_slice_in_dim(replaced, holder, 1)[0].astype(f32)
    marks = jnp.stack([jnp.where(own_live, 1.0 / token_total, 0.0), own_flags], 1)

    entries = relative.shape[0]
    words = found.reshape(model, seq_len)
    if direct:
        *ready, probs, mixed, second_all = attend_gather(
            own_length, first_all, words, second_pack, head_width, entries, 3
        )
    else:
        ready = prepare(first_all, words, head_width, entries)
        probs, mixed = attend(own_length, ready[3], ready[6])
        second_all = lax.all_gather(second_pack, everyone, axis=0, tiled=True)
    vec_full, white, rate, qkv, rel_white, rel_rate, rel_table = ready
    second_all = second_all.reshape(pieces, model, -1)
    grad_contract, grad_expand, grad_joint, grad_mixed, grad_sum, grad_vec, losses = middle(
        second_all, vec_full, white, mixed, marks
    )
    back = (first_all, vec_full, white, rate, rel_white, rel_rate, grad_sum)
    if direct:
        qkv_grads, rel_table_grads, *sums = attend_back_sums(
            qkv, rel_table, probs, grad_mixed, [grad_contract, grad_expand, grad_joint], 4
        )
        sent, project_sum = project_return(*back, qkv_grads, rel_table_grads, grad_vec, tag=5)
        sums.append(project_sum)
    else:
        qkv_grads, rel_table_grads = attend_back(qkv, rel_table, probs, grad_mixed)
        sent, grad_project = project_back(*back, qkv_grads, rel_table_grads, grad_vec)
        sent = sent.reshape(owners, width, seq_len)
        sent = lax.all_to_all(sent, "dp", 0, 0, tiled=True)
        sent = lax.all_gather(sent, "heads", axis=0)
        sent = sent.transpose(1, 0, 2, 3)
        sums = [
            lax.psum_scatter(
                part.reshape(pieces * model, -1), everyone, scatter_dimension=0, tiled=True
            ).astype(f32)
            for part in (grad_contract, grad_expand, grad_joint, grad_project)
        ]
    sent = sent.reshape(owners * row_count, width, seq_len)
    grad_embedding, own_squares = deposit(counts, keys, sent, vocab_slab)

    weights = (embedding, relative, project, combine, expand, contract, readout, vectors)
    means = (
        embedding_mean,
        relative_mean,
        project_mean,
        combine_mean,
        expand_mean,
        contract_mean,
        readout_mean,
        vectors_mean,
    )
    squares = (
        embedding_square,
        relative_square,
        project_square,
        combine_square,
        expand_square,
        contract_square,
        readout_square,
        vectors_square,
    )
    if direct:
        turns = {1: (1, 0), 2: (1, 0, 2), 5: (1, 0)}
        flat = [
            part.transpose(turns[index]) if index in turns else part
            for index, parts in enumerate(zip(weights, means, squares))
            for part in parts
        ]
        all_facts, shared = finish_sums(losses, own_squares, sums, head_width, 6)
        *flat, norm, loss_sum, bias_row = update_all(
            all_facts, shared, [grad_embedding, *sums], flat, head_width
        )
        flat = [
            part.transpose(turns[index // 3]) if index // 3 in turns else part
            for index, part in enumerate(flat)
        ]
        return (loss_sum[0, 0], token_total, norm[0, 0], *flat, bias_row[0])

    squares_local = sum(jnp.sum(part * part) for part in sums) + jnp.sum(own_squares)
    shared = jnp.concatenate([sums[2][:, :head_width], sums[3][:, 3 * head_width :]], 1)
    squares_total, loss_sum = lax.psum((squares_local, jnp.sum(losses)), everyone)
    shared = lax.all_gather(shared, "heads", axis=0)
    grad_norm = jnp.sqrt(squares_total)
    factor = jnp.minimum(1.0, clip_level / grad_norm)
    grad_readout = shared[:, :, :head_width].transpose(1, 0, 2).reshape(width, model)
    at = head_width + BLOCK // 2
    grad_relative = shared[:, :, at:].transpose(0, 2, 1).reshape(entries, width)
    grad_vec = shared[:, :, head_width : head_width + 3].transpose(0, 2, 1).reshape(-1, width)
    grad_vec = grad_vec[:vector_count]
    gradients = (
        grad_embedding,
        grad_relative,
        sums[3][:, : 3 * head_width].reshape(width, 3, head_width),
        sums[2][:, head_width:].T,
        sums[1],
        sums[0].T,
        grad_readout,
        grad_vec,
    )
    updates = [
        adamw(weight, gradient * factor, mean, square, rate_now)
        for weight, gradient, mean, square, rate_now in zip(
            weights, gradients, means, squares, rate_steps
        )
    ]
    flat = [part for parts in updates for part in parts]
    return (loss_sum, token_total, grad_norm, *flat, grad_vec[3] * factor)


def solution(mesh):
    placed = (
        P("dp", None),
        P("dp"),
        P("dp", None),
        P("dp", "heads"),
        P(None, "dp"),
        P("dp", None, "heads"),
        P("heads", "dp"),
        P("dp", "heads"),
        P("heads", "dp"),
        P("dp", None),
        P(None, "dp"),
        P("dp", "heads"),
        P(None, "dp"),
        P("dp", None, "heads"),
        P("heads", "dp"),
        P("dp", "heads"),
        P("heads", "dp"),
        P("dp", None),
        P(None, "dp"),
        P("dp", "heads"),
        P(None, "dp"),
        P("dp", None, "heads"),
        P("heads", "dp"),
        P("dp", "heads"),
        P("heads", "dp"),
        P("dp", None),
        P(None, "dp"),
    )
    return jax.shard_map(
        per_device,
        mesh=mesh,
        in_specs=placed,
        out_specs=(
            P(),
            P(),
            P(),
            P("dp", "heads"),
            P("dp", "heads"),
            P("dp", "heads"),
            P(None, "dp"),
            P(None, "dp"),
            P(None, "dp"),
            P("dp", None, "heads"),
            P("dp", None, "heads"),
            P("dp", None, "heads"),
            P("heads", "dp"),
            P("heads", "dp"),
            P("heads", "dp"),
            P("dp", "heads"),
            P("dp", "heads"),
            P("dp", "heads"),
            P("heads", "dp"),
            P("heads", "dp"),
            P("heads", "dp"),
            P("dp", None),
            P("dp", None),
            P("dp", None),
            P(None, "dp"),
            P(None, "dp"),
            P(None, "dp"),
            P("dp"),
        ),
        check_vma=False,
    )
```
